128 devices in a mesh: cuts: 128 (over z, y, x, core).
Axes of the slice: x: 4, y: 4, z: 4, core: 2. Of those that a mesh axis runs over, the one named last changes fastest.
Arguments:
- field: float32 [2, 16, 128, 128, 128], P(None, None, 'cuts'), may hold values from -6 to 6
- phase_bins: int32 [16, 128, 8192], P(None, 'cuts'), may hold values from 0 to 15
- phase_jitter: float32 [16, 128, 8192], P(None, 'cuts'), may hold values from 0 to 1
- energy: float32 [16, 128, 8192], P(None, 'cuts'), may hold values from -6 to 6
- profile: float32 [128, 128], replicated, may hold values from 0.1 to 1
- delays: int32 [16, 64, 1], replicated, may hold values from 0 to 127; in each aligned block of 1024 rows (0 to 1023, 1024 to 2047, ..., all dimensions but the last counted through in order) at most 20 rows name the same one
Outputs:
- field_out: float32 [2, 16, 128, 128, 128], P(None, None, 'cuts')
- phase_out: float32 [16, 128, 8192], P(None, 'cuts')
- energy_out: float32 [16, 128, 8192], P(None, 'cuts')
The draws below stay inside these ranges and needn't reach their ends.
Inputs may be any that keep to these rules, and one draw needn't show every extreme that they name: `delays`: over all pairs (k, j) no delay value is named more than 20 times, a bound that some block reaches; every value 0 to 127 is named.
All inputs are finite; a program needn't handle non-finite values.
Results may differ from the reference program's by a relative error of at most 0.0003.
Values sent between devices are 32-bit elements; how exact they have to be, the bound alone decides.
No kernel may reach another device: no remote copies, remote signals or barrier semaphores. Data moves between devices by JAX's collectives and lax.ppermute only.
A program may use at most 64 MiB of HBM per device.

```python
import math
import jax
import jax.numpy as jnp
import numpy as np

GRID = 128
NP = 8192
BLOCK = 128
NBINS = 16
NPER = 2
SL_DEV = 16
NBS = 64
CAPP = 20
N_CUTS = 128


def set_ends(result, own_key, low, largest):
    longest = result.shape.index(max(result.shape))
    spots = []
    for shift in (0, 1):
        where = [jax.random.randint(jax.random.fold_in(own_key, axis), (), 0, length) for axis, length in enumerate(result.shape)]
        where[longest] = (where[longest] + shift) % result.shape[longest]
        spots.append(tuple(where))
    return result.at[spots[0]].set(low).at[spots[1]].set(largest)


def block_levels(key, extent, shards, least, top_value):
    def one(dim, blocks):
        heights = jax.random.uniform(jax.random.fold_in(jax.random.fold_in(key, 6), dim), (blocks,), jnp.float32, least / len(shards), top_value / len(shards))
        return jnp.repeat(jnp.exp(heights), extent[dim] // blocks).reshape((-1,) + (1,) * (len(extent) - dim - 1))

    factor_of = one(*shards[0])
    for cut in shards[1:]:
        factor_of = factor_of * one(*cut)
    return factor_of


def assign_block(rng, own, number, rows, count, top, reach, skew):
    ranking = jax.random.permutation(rng, count)
    crowded, common = shares(count, rows * top, reach, skew, True), shares(count, rows * top, reach, skew, False)
    places = jnp.arange(count)

    def named(tallies, offset_by):
        used = int((tallies > 0).sum())
        fixed = max(1, used // 4)
        passed = fixed + (places - fixed + offset_by * (used - fixed)) % max(1, count - fixed)
        return jnp.zeros((count,), jnp.int32).at[ranking[jnp.where(places < fixed, places, passed)]].set(jnp.asarray(tallies, jnp.int32))

    tallies = jnp.where(number % 4 == 0, named(crowded, number // 4), named(common, number - number // 4 - 1))
    mixed = jax.random.permutation(jax.random.fold_in(own, 3), count)
    giver, taker = mixed[0:count // 2 * 2:2], mixed[1:count // 2 * 2:2]
    room = jnp.minimum(tallies[giver] - 1, reach - tallies[taker]) // 2
    room = jnp.where((giver == ranking[0]) | (taker == ranking[0]) | (tallies[taker] == 0), 0, jnp.maximum(room, 0))
    passed = jax.random.randint(jax.random.fold_in(own, 4), (count // 2,), 0, 1 << 20) % (room + 1)
    tallies = tallies.at[giver].add(-passed).at[taker].add(passed)
    items = jnp.searchsorted(jnp.cumsum(tallies), jnp.arange(rows * top), side="right").astype(jnp.int32)
    listing = items.reshape(top, rows).T
    listing = listing[jax.random.permutation(jax.random.fold_in(own, 1), rows)]
    offset_by = jax.random.randint(jax.random.fold_in(own, 2), (rows, 1), 0, top)
    return jnp.take_along_axis(listing, (jnp.arange(top)[None, :] + offset_by) % top, axis=1)


def shares(number_of, total, limit, lean, full):
    portions = [(1 << 20) // math.isqrt(rank ** lean) + 1 for rank in range(1, number_of + 1)]
    largest = limit if full else min(limit, max(-(-total // number_of), total * portions[0] // sum(portions)))
    least = 1 if total - largest >= number_of - 1 else 0
    counts, surplus = [largest] + [least] * (number_of - 1), total - largest - least * (number_of - 1)
    while surplus > 0:
        movable = [i for i in range(1, number_of) if counts[i] < largest] or [i for i in range(1, number_of) if counts[i] < limit]
        mass, budget = sum([portions[i] for i in movable]), surplus
        for i in movable:
            addition = min(limit - counts[i], max(1, budget * portions[i] // mass), surplus)
            counts[i] = counts[i] + addition
            surplus = surplus - addition
    return np.array(counts)


def noise(key, extent, width, most, pieces=(), kind=jnp.bfloat16):
    drawn = jax.random.normal(key, extent, jnp.float32) * width
    if len(pieces) > 0:
        drawn = block_levels(key, extent, pieces, -0.22, 0.18) * drawn
    return jnp.clip(drawn, min=-most, max=most).astype(kind)


def setup_inputs(seed: int = 0) -> dict:
    key_of = jax.random.split(jax.random.key(seed), 7)
    field = noise(key_of[0], (2, SL_DEV, N_CUTS, GRID, GRID), 1.0, 6.0, ((2, 128),), jnp.float32)
    phase_bins = set_ends(jax.random.randint(key_of[1], (SL_DEV, N_CUTS, NP), 0, NBINS), jax.random.fold_in(key_of[1], 1), 0, NBINS - 1).astype(jnp.int32)
    phase_jitter = jnp.clip(1.0 * jax.random.uniform(key_of[2], (SL_DEV, N_CUTS, NP), jnp.float32) ** block_levels(key_of[2], (SL_DEV, N_CUTS, NP), ((1, 128),), -0.2, 0.2), 0.0, 1.0)
    energy = noise(key_of[3], (SL_DEV, N_CUTS, NP), 1.0, 6.0, ((1, 128),), jnp.float32)
    profile = jnp.clip(jnp.exp(jax.random.uniform(key_of[4], (GRID, GRID), jnp.float32, math.log(0.1), math.log(1.0))), 0.1, 1.0)
    delays_keys = jax.random.split(jax.random.fold_in(key_of[5], 1), SL_DEV * NBS // (SL_DEV * NBS))
    delays_turns = jax.random.permutation(jax.random.fold_in(key_of[5], 3), SL_DEV * NBS // (SL_DEV * NBS))
    delays = jax.vmap(lambda own, number: assign_block(jax.random.fold_in(key_of[5], 2), own, number, SL_DEV * NBS, N_CUTS, 1, CAPP, 1))(delays_keys, delays_turns).reshape((SL_DEV, NBS, 1))
    return {"field": field, "phase_bins": phase_bins, "phase_jitter": phase_jitter, "energy": energy, "profile": profile, "delays": delays}


KAPPA = 1.0
OMEGA = 1.0
GAIN = 16.0
PHASE_COEF = 20.0


def transfer_phase():
    index_line = jnp.arange(GRID)
    freq = (((index_line + GRID // 2) % GRID) - GRID // 2).astype(jnp.float32) / GRID
    return PHASE_COEF * (freq[:, None] ** 2 + freq[None, :] ** 2)


def one_period(field_re, field_im, phases, energies, profile, angle):
    amp_re = jnp.sum(profile * field_re, axis=(1, 2)) / GRID
    amp_im = jnp.sum(profile * field_im, axis=(1, 2)) / GRID
    energies = energies - KAPPA * (amp_re[:, None] * jnp.cos(phases) - amp_im[:, None] * jnp.sin(phases))
    phases = phases + OMEGA * energies
    bunch_re = jnp.mean(jnp.cos(phases), axis=1)
    bunch_im = -jnp.mean(jnp.sin(phases), axis=1)
    field_re = field_re + GAIN * bunch_re[:, None, None] * profile
    field_im = field_im + GAIN * bunch_im[:, None, None] * profile
    spectrum = jnp.fft.fft2(field_re + 1j * field_im)
    spectrum = spectrum * (jnp.cos(angle) - 1j * jnp.sin(angle))
    back = jnp.fft.ifft2(spectrum)
    field_re = jnp.real(back).astype(field_re.dtype)
    field_im = jnp.imag(back).astype(field_re.dtype)
    zero_slice = jnp.zeros_like(field_re[:1])
    field_re = jnp.concatenate([zero_slice, field_re[:-1]], axis=0)
    field_im = jnp.concatenate([zero_slice, field_im[:-1]], axis=0)
    return field_re, field_im, phases, energies


def reference(field, phase_bins, phase_jitter, energy, profile, delays):
    slices = SL_DEV * N_CUTS
    field_re = field[0].reshape(slices, GRID, GRID)
    field_im = field[1].reshape(slices, GRID, GRID)
    phases = (2.0 * math.pi / NBINS) * (phase_bins.astype(field.dtype) + phase_jitter)
    phases = phases.reshape(slices, NP)
    energies = energy.reshape(slices, NP)
    angle = transfer_phase().astype(field.dtype)
    for period in range(NPER):
        field_re, field_im, phases, energies = one_period(field_re, field_im, phases, energies, profile, angle)
    field_out = jnp.stack([field_re, field_im]).reshape(2, SL_DEV, N_CUTS, GRID, GRID)
    delay_table = delays[:, :, 0].astype(jnp.int32)
    source = (jnp.arange(N_CUTS, dtype=jnp.int32)[None, :, None] - delay_table[:, None, :]) % N_CUTS
    source = source[:, :, :, None]
    phase_blocks = phases.reshape(SL_DEV, N_CUTS, NBS, BLOCK)
    energy_blocks = energies.reshape(SL_DEV, N_CUTS, NBS, BLOCK)
    phase_out = jnp.take_along_axis(phase_blocks, source, axis=1).reshape(SL_DEV, N_CUTS, NP)
    energy_out = jnp.take_along_axis(energy_blocks, source, axis=1).reshape(SL_DEV, N_CUTS, NP)
    return field_out, phase_out, energy_out
```

```python
import functools
import math

import jax
import jax.numpy as jnp
import ml_dtypes
import numpy as np
from jax import lax
from jax.experimental import pallas as pl
from jax.experimental.pallas import tpu as pltpu
from jax.sharding import PartitionSpec as P

BLOCK = 128
NBINS = 16
KAPPA = 1.0
OMEGA = 1.0
GAIN = 16.0
PHASE_COEF = 20.0
GRID = 128
GROUPS = 16
NBS = 64
COUNT = GROUPS * NBS
PEERS = 128
CAP = 20
ROWS = PEERS * CAP
BATCH = 16
VMEM_LIMIT = 24 * 1024 * 1024
HIGHEST = lax.Precision.HIGHEST


def line_operator(power):
    index = np.arange(GRID)
    freq = ((index + GRID // 2) % GRID - GRID // 2) / GRID
    weight = np.exp(-1j * PHASE_COEF * power * freq**2)
    wave = np.exp(2j * np.pi * (index[:, None] * index[None, :] % GRID) / GRID)
    column = wave @ weight / GRID
    matrix = column[(index[:, None] - index[None, :]) % GRID]
    return matrix.real, matrix.imag


def left_form(real, imag):
    return np.block([[real, -imag], [imag, real]])


def right_form(real, imag):
    return np.block([[real, imag], [-imag, real]])


def halves(matrix):
    high = matrix.astype(ml_dtypes.bfloat16)
    return high, (matrix - high.astype(np.float64)).astype(ml_dtypes.bfloat16)


def deep_left(matrix):
    high, low = halves(matrix)
    return jnp.asarray(np.concatenate([high, high, low], axis=1))


def deep_right(matrix):
    high, low = halves(matrix)
    return jnp.asarray(np.concatenate([high, high, low], axis=0))


def fitted(function, degree):
    top = (math.pi / 2 + 0.01) ** 2
    nodes = (np.cos(np.pi * (np.arange(400) + 0.5) / 400) + 1) / 2 * top
    series = np.polynomial.chebyshev.Chebyshev.fit(nodes, function(np.sqrt(nodes)), degree, domain=[0, top])
    return [float(c) for c in series.convert(kind=np.polynomial.Polynomial).coef]


SIN_COEF = fitted(lambda r: np.sin(r) / r, 5)
COS_COEF = fitted(np.cos, 6)
PI_HIGH = 3.140625
PI_MID = 9.67502593994140625e-4
PI_LOW = math.pi - PI_HIGH - PI_MID


def horner(coefs, x):
    value = jnp.float32(coefs[-1])
    for c in coefs[-2::-1]:
        value = value * x + jnp.float32(c)
    return value


def cos_sin(x):
    turns = jnp.round(x * jnp.float32(1.0 / math.pi))
    r = x - turns * jnp.float32(PI_HIGH)
    r = r - turns * jnp.float32(PI_MID)
    r = r - turns * jnp.float32(PI_LOW)
    half = turns * 0.5
    sign = 1.0 - 4.0 * jnp.abs(half - jnp.round(half))
    square = r * r
    return horner(COS_COEF, square) * sign, horner(SIN_COEF, square) * (r * sign)


def lane_total(rows):
    return jnp.broadcast_to(jnp.sum(rows, axis=1, keepdims=True), rows.shape)


def slots_of(delays):
    row = jnp.concatenate([delays[k] for k in range(GROUPS)], axis=1)
    values = lax.broadcasted_iota(jnp.int32, (PEERS, COUNT), 0)
    onehot = jnp.where(values == row, 1.0, 0.0)
    before = lax.broadcasted_iota(jnp.int32, (COUNT, COUNT), 0) < lax.broadcasted_iota(jnp.int32, (COUNT, COUNT), 1)
    upper = jnp.where(before, 1.0, 0.0).astype(jnp.bfloat16)
    earlier = jnp.dot(onehot.astype(jnp.bfloat16), upper, preferred_element_type=jnp.float32)
    return row, jnp.sum(earlier * onehot, axis=0, keepdims=True).astype(jnp.int32)


def folded(row):
    return jnp.concatenate([row[:, n * 128 : (n + 1) * 128] for n in range(COUNT // 128)], axis=0)


def rows_of(k):
    return pl.ds(pl.multiple_of(k * NBS, NBS), NBS)


def first_kernel(
    field_hbm, profile_hbm, bins_hbm, jitter_hbm, energy_hbm, delays_hbm, left_hbm, right_hbm,
    phases, energies, small, beam, places,
    field, profile, bins, jitter, energy, delays, left, right, acc, sems,
):
    pairs = [
        (profile_hbm, profile), (left_hbm, left), (right_hbm, right), (delays_hbm, delays),
        (field_hbm, field), (bins_hbm, bins), (jitter_hbm, jitter), (energy_hbm, energy),
    ]
    copies = [pltpu.make_async_copy(src, dst, sems.at[n]) for n, (src, dst) in enumerate(pairs)]
    for copy in copies:
        copy.start()
    for copy in copies[:4]:
        copy.wait()
    p = profile[...]
    half = jnp.dot(left[...], p, precision=HIGHEST, preferred_element_type=jnp.float32)
    both = jnp.concatenate([half[:GRID], half[GRID:]], axis=1)
    spread = jnp.dot(both, right[...], precision=HIGHEST, preferred_element_type=jnp.float32)
    beam[0] = spread[:, :GRID]
    beam[2] = p
    beam[1] = spread[:, GRID:]
    row, slot = slots_of(delays)
    places[0:1] = row
    places[1:2] = slot
    copies[4].wait()

    def project(k, carry):
        re, im = field[0, k], field[1, k]
        dr, di, q = beam[0], beam[1], profile[...]
        acc[0, pl.ds(k, 1)] = jnp.sum(q * re, axis=0, keepdims=True)
        acc[1, pl.ds(k, 1)] = jnp.sum(q * im, axis=0, keepdims=True)
        acc[2, pl.ds(k, 1)] = jnp.sum(dr * re - di * im, axis=0, keepdims=True)
        acc[3, pl.ds(k, 1)] = jnp.sum(dr * im + di * re, axis=0, keepdims=True)
        return carry

    lax.fori_loop(0, GROUPS, project, 0)
    self_re = jnp.sum(p * beam[0])
    self_im = jnp.sum(p * beam[1])
    for n in range(4):
        acc[n] = lane_total(acc[n]) * (1.0 / GRID)
    for copy in copies[5:]:
        copy.wait()

    def push(k, carry):
        rows = rows_of(k)
        ph = jnp.float32(2.0 * math.pi / NBINS) * (bins[rows].astype(jnp.float32) + jitter[rows])
        ph, en = pushed(ph, energy[rows], acc[0, pl.ds(k, 1)], acc[1, pl.ds(k, 1)])
        phases[rows] = ph
        energies[rows] = en
        c, s = cos_sin(ph)
        small[2, pl.ds(k, 1)] = jnp.sum(c, axis=0, keepdims=True)
        small[3, pl.ds(k, 1)] = jnp.sum(s, axis=0, keepdims=True)
        return carry

    lax.fori_loop(0, GROUPS, push, 0)
    bre = lane_total(small[2]) * (1.0 / (NBS * BLOCK))
    bim = lane_total(small[3]) * (-1.0 / (NBS * BLOCK))
    small[2] = bre
    small[3] = bim
    gain = GAIN / GRID
    small[0] = acc[2] + gain * (bre * self_re - bim * self_im)
    small[1] = acc[3] + gain * (bre * self_im + bim * self_re)


def pushed(ph, en, amp_re, amp_im):
    c, s = cos_sin(ph)
    en = en - KAPPA * (amp_re * c - amp_im * s)
    return ph + OMEGA * en, en


def carried(value, flag):
    rolled = jnp.concatenate([jnp.zeros_like(value[:1]), value[:-1]], axis=0)
    return jnp.where(flag, rolled, value)


def second_kernel(
    mine, phases1, energies1, arrived, places, send_hbm, small, acc, phases, energies, send, index_v, index, sems
):
    me = mine[0]
    index_v[...] = folded(((me + places[0:1]) % PEERS) * (2 * CAP) + places[1:2])
    to_scalar = pltpu.make_async_copy(index_v, index, sems.at[0])
    to_scalar.start()
    for n in range(4):
        acc[n] = carried(arrived[n], me == 0)

    def push(k, carry):
        rows = rows_of(k)
        ph, en = pushed(phases1[rows], energies1[rows], acc[0, pl.ds(k, 1)], acc[1, pl.ds(k, 1)])
        phases[rows] = ph
        energies[rows] = en
        c, s = cos_sin(ph)
        small[0, pl.ds(k, 1)] = jnp.sum(c, axis=0, keepdims=True)
        small[1, pl.ds(k, 1)] = jnp.sum(s, axis=0, keepdims=True)
        return carry

    lax.fori_loop(0, GROUPS, push, 0)
    small[0] = lane_total(small[0]) * (1.0 / (NBS * BLOCK))
    small[1] = lane_total(small[1]) * (-1.0 / (NBS * BLOCK))
    small[2] = acc[2]
    small[3] = acc[3]
    to_scalar.wait()

    def put(n, carry):
        base = pl.multiple_of(n * BATCH, BATCH)
        spots = [index[n // (128 // BATCH), n % (128 // BATCH) * BATCH + m] for m in range(BATCH)]
        ph = [phases[pl.ds(base + m, 1)] for m in range(BATCH)]
        en = [energies[pl.ds(base + m, 1)] for m in range(BATCH)]
        for m in range(BATCH):
            send[pl.ds(spots[m], 1)] = ph[m]
            send[pl.ds(spots[m] + CAP, 1)] = en[m]
        return carry

    lax.fori_loop(0, COUNT // BATCH, put, 0)
    out = pltpu.make_async_copy(send, send_hbm, sems.at[0])
    out.start()
    out.wait()


def wide_halves(x):
    high = x.astype(jnp.bfloat16)
    return high, (x - high.astype(jnp.float32)).astype(jnp.bfloat16)


def pick_kernel(mine, recv, places, phases, energies, index_v, index, sems):
    me = mine[0]
    index_v[...] = folded(((me - places[0:1] + PEERS) % PEERS) * (2 * CAP) + places[1:2])
    to_scalar = pltpu.make_async_copy(index_v, index, sems.at[0])
    to_scalar.start()
    to_scalar.wait()

    def get(n, carry):
        base = pl.multiple_of(n * BATCH, BATCH)
        spots = [index[n // (128 // BATCH), n % (128 // BATCH) * BATCH + m] for m in range(BATCH)]
        ph = [recv[pl.ds(spot, 1)] for spot in spots]
        en = [recv[pl.ds(spot + CAP, 1)] for spot in spots]
        for m in range(BATCH):
            phases[pl.ds(base + m, 1)] = ph[m]
            energies[pl.ds(base + m, 1)] = en[m]
        return carry

    lax.fori_loop(0, COUNT // BATCH, get, 0)


SLAB = 4
PIECES = ((0, 2), (2, 4), (4, 16))


def field_kernel(mine, piece_a, piece_b, piece_c, small, beam, left, right, out_hbm, acc, out, sems):
    me = mine[0]
    for n in range(4):
        acc[n] = GAIN * carried(small[n], me == 0)

    def plane(c, k):
        for piece, (low, high) in zip((piece_a, piece_b, piece_c), PIECES):
            if low <= k < high:
                return piece[c, k - low]
        return jnp.zeros((GRID, GRID), jnp.float32)

    late = me < 2
    p = beam[2]
    dr, di = beam[0], beam[1]
    copies = []
    for slab in range(GROUPS // SLAB):
        ks = range(slab * SLAB, (slab + 1) * SLAB)
        rows = []
        for k in ks:
            parts = [jnp.where(late, plane(c, k - 1), plane(c, k)) + acc[2 + c, k : k + 1] * p for c in range(2)]
            rows.append(jnp.concatenate(parts, axis=1))
        hi, lo = wide_halves(jnp.concatenate(rows, axis=0))
        half = jnp.dot(jnp.concatenate([hi, lo, hi], axis=1), right[...], preferred_element_type=jnp.float32)
        cols = []
        for m in range(SLAB):
            mid = half[m * GRID : (m + 1) * GRID]
            cols.append(jnp.concatenate([mid[:, :GRID], mid[:, GRID:]], axis=0))
        hi, lo = wide_halves(jnp.concatenate(cols, axis=1))
        full = jnp.dot(left[...], jnp.concatenate([hi, lo, hi], axis=0), preferred_element_type=jnp.float32)
        for m, k in enumerate(ks):
            cr, ci = acc[0, k : k + 1], acc[1, k : k + 1]
            out[0, k] = full[:GRID, m * GRID : (m + 1) * GRID] + (cr * dr - ci * di)
            out[1, k] = full[GRID:, m * GRID : (m + 1) * GRID] + (cr * di + ci * dr)
        for c in range(2):
            span = pl.ds(slab * SLAB, SLAB)
            copies.append(pltpu.make_async_copy(out.at[c, span], out_hbm.at[c, span], sems.at[2 * slab + c]))
            copies[-1].start()
    for copy in copies:
        copy.wait()


def shifted(value, axis, steps):
    count = lax.axis_size(axis)
    pairs = [(source, (source + steps) % count) for source in range(count)]
    return lax.ppermute(value, axis, pairs)


def shape(*dims, dtype=jnp.float32):
    return jax.ShapeDtypeStruct(dims, dtype)


def whole():
    return pl.BlockSpec(memory_space=pltpu.VMEM)


def vmem(*dims, dtype=jnp.float32):
    return pltpu.VMEM(dims, dtype)


def in_hbm(value):
    return pltpu.with_memory_space_constraint(value, pltpu.HBM)


def exchange(send):
    return lax.all_to_all(send.reshape(PEERS, 2 * CAP, BLOCK), "cuts", split_axis=0, concat_axis=0, tiled=True)


def per_device(field, phase_bins, phase_jitter, energy, profile, delays):
    params = pltpu.CompilerParams(vmem_limit_bytes=VMEM_LIMIT)
    scalar = pl.BlockSpec(memory_space=pltpu.SMEM)
    remain = pl.BlockSpec(memory_space=pltpu.HBM)
    field = field.reshape(2, GROUPS, GRID, GRID)
    bins = phase_bins.reshape(COUNT, BLOCK)
    jitter = phase_jitter.reshape(COUNT, BLOCK)
    energies = energy.reshape(COUNT, BLOCK)
    mine = lax.axis_index("cuts").reshape(1)
    one, two = line_operator(1), line_operator(2)
    left_one = jnp.asarray(np.concatenate(one, axis=0), jnp.float32)
    right_one = jnp.asarray(right_form(*one), jnp.float32)
    sources = [field[:, low:high] for low, high in PIECES]
    field_a = shifted(sources[0], "cuts", 2)
    operands = [field, profile, bins, jitter, energies, delays.reshape(GROUPS, 1, NBS), left_one, right_one]
    phases1, energies1, small1, beam, places = pl.pallas_call(
        first_kernel,
        out_shape=(
            shape(COUNT, BLOCK),
            shape(COUNT, BLOCK),
            shape(4, GROUPS, 128),
            shape(3, GRID, GRID),
            shape(8, COUNT, dtype=jnp.int32),
        ),
        in_specs=[remain] * 8,
        out_specs=(whole(),) * 5,
        scratch_shapes=[
            vmem(2, GROUPS, GRID, GRID),
            vmem(GRID, GRID),
            vmem(COUNT, BLOCK, dtype=jnp.int32),
            vmem(COUNT, BLOCK),
            vmem(COUNT, BLOCK),
            vmem(GROUPS, 1, NBS, dtype=jnp.int32),
            vmem(2 * GRID, GRID),
            vmem(2 * GRID, 2 * GRID),
            vmem(4, GROUPS, 128),
            pltpu.SemaphoreType.DMA((8,)),
        ],
        compiler_params=params,
        name="project_push",
    )(*[in_hbm(value) for value in operands])
    arrived1 = shifted(small1, "cuts", 1)
    arrived1, field_a, source_b, source_c = lax.optimization_barrier((arrived1, field_a, sources[1], sources[2]))
    field_b = shifted(source_b, "cuts", 2)
    send, small2 = pl.pallas_call(
        second_kernel,
        out_shape=(pltpu.HBM((2 * ROWS, BLOCK), jnp.float32), shape(4, GROUPS, 128)),
        in_specs=[scalar] + [whole()] * 4,
        out_specs=(remain, whole()),
        scratch_shapes=[
            vmem(4, GROUPS, 128),
            vmem(COUNT, BLOCK),
            vmem(COUNT, BLOCK),
            vmem(2 * ROWS, BLOCK),
            vmem(8, 128, dtype=jnp.int32),
            pltpu.SMEM((8, 128), jnp.int32),
            pltpu.SemaphoreType.DMA((1,)),
        ],
        compiler_params=params,
        name="push_place",
    )(mine, phases1, energies1, arrived1, places)
    arrived2 = shifted(small2, "cuts", 1)
    send, field_b, source_c = lax.optimization_barrier((send, field_b, source_c))
    field_c = shifted(source_c, "cuts", 2)
    fits = jnp.max(delays) < PEERS
    recv = lax.cond(fits, exchange, lambda rows: jnp.zeros((PEERS, 2 * CAP, BLOCK), jnp.float32), send)
    phase_out, energy_out = pl.pallas_call(
        pick_kernel,
        out_shape=(shape(COUNT, BLOCK), shape(COUNT, BLOCK)),
        in_specs=[scalar] + [whole()] * 2,
        out_specs=(whole(),) * 2,
        scratch_shapes=[
            vmem(8, 128, dtype=jnp.int32),
            pltpu.SMEM((8, 128), jnp.int32),
            pltpu.SemaphoreType.DMA((1,)),
        ],
        compiler_params=params,
        name="pick",
    )(mine, recv.reshape(2 * ROWS, BLOCK), places)
    out = pl.pallas_call(
        field_kernel,
        out_shape=shape(2, GROUPS, GRID, GRID),
        in_specs=[scalar] + [whole()] * 7,
        out_specs=remain,
        scratch_shapes=[
            vmem(4, GROUPS, 128),
            vmem(2, GROUPS, GRID, GRID),
            pltpu.SemaphoreType.DMA((2 * GROUPS // SLAB,)),
        ],
        compiler_params=params,
        name="diffract",
    )(mine, field_a, field_b, field_c, arrived2, beam, deep_left(left_form(*two)), deep_right(right_form(*two)))
    return (
        out.reshape(2, GROUPS, 1, GRID, GRID),
        phase_out.reshape(GROUPS, 1, NBS * BLOCK),
        energy_out.reshape(GROUPS, 1, NBS * BLOCK),
    )


def solution(mesh):
    return jax.shard_map(
        per_device,
        mesh=mesh,
        in_specs=(
            P(None, None, "cuts", None, None),
            P(None, "cuts", None),
            P(None, "cuts", None),
            P(None, "cuts", None),
            P(),
            P(),
        ),
        out_specs=(P(None, None, "cuts", None, None), P(None, "cuts", None), P(None, "cuts", None)),
        check_vma=False,
    )
```

```python
import functools
import math

import jax
import jax.numpy as jnp
import ml_dtypes
import numpy as np
from jax import lax
from jax.experimental import pallas as pl
from jax.experimental.pallas import tpu as pltpu
from jax.sharding import PartitionSpec as P

BLOCK = 128
NBINS = 16
KAPPA = 1.0
OMEGA = 1.0
GAIN = 16.0
PHASE_COEF = 20.0
GRID = 128
GROUPS = 16
NBS = 64
COUNT = GROUPS * NBS
PEERS = 128
CAP = 20
MESSAGE = 2 * CAP + 1
ROWS = PEERS * MESSAGE
BATCH = 16
VMEM_LIMIT = 24 * 1024 * 1024
HIGHEST = lax.Precision.HIGHEST


def line_operator(power):
    index = np.arange(GRID)
    freq = ((index + GRID // 2) % GRID - GRID // 2) / GRID
    weight = np.exp(-1j * PHASE_COEF * power * freq**2)
    wave = np.exp(2j * np.pi * (index[:, None] * index[None, :] % GRID) / GRID)
    column = wave @ weight / GRID
    matrix = column[(index[:, None] - index[None, :]) % GRID]
    return matrix.real, matrix.imag


def left_form(real, imag):
    return np.block([[real, -imag], [imag, real]])


def right_form(real, imag):
    return np.block([[real, imag], [-imag, real]])


def halves(matrix):
    high = matrix.astype(ml_dtypes.bfloat16)
    return high, (matrix - high.astype(np.float64)).astype(ml_dtypes.bfloat16)


def deep_left(matrix):
    high, low = halves(matrix)
    return jnp.asarray(np.concatenate([high, high, low], axis=1))


def deep_right(matrix):
    high, low = halves(matrix)
    return jnp.asarray(np.concatenate([high, high, low], axis=0))


def fitted(function, degree):
    top = (math.pi / 2 + 0.01) ** 2
    nodes = (np.cos(np.pi * (np.arange(400) + 0.5) / 400) + 1) / 2 * top
    series = np.polynomial.chebyshev.Chebyshev.fit(nodes, function(np.sqrt(nodes)), degree, domain=[0, top])
    return [float(c) for c in series.convert(kind=np.polynomial.Polynomial).coef]


SIN_COEF = fitted(lambda r: np.sin(r) / r, 5)
COS_COEF = fitted(np.cos, 6)
PI_HIGH = 3.140625
PI_MID = 9.67502593994140625e-4
PI_LOW = math.pi - PI_HIGH - PI_MID


def horner(coefs, x):
    value = jnp.float32(coefs[-1])
    for c in coefs[-2::-1]:
        value = value * x + jnp.float32(c)
    return value


def cos_sin(x):
    turns = jnp.round(x * jnp.float32(1.0 / math.pi))
    r = x - turns * jnp.float32(PI_HIGH)
    r = r - turns * jnp.float32(PI_MID)
    r = r - turns * jnp.float32(PI_LOW)
    half = turns * 0.5
    sign = 1.0 - 4.0 * jnp.abs(half - jnp.round(half))
    square = r * r
    return horner(COS_COEF, square) * sign, horner(SIN_COEF, square) * (r * sign)


def lane_total(rows):
    return jnp.broadcast_to(jnp.sum(rows, axis=1, keepdims=True), rows.shape)


def slots_of(delays):
    row = jnp.concatenate([delays[k] for k in range(GROUPS)], axis=1)
    values = lax.broadcasted_iota(jnp.int32, (PEERS, COUNT), 0)
    onehot = jnp.where(values == row, 1.0, 0.0)
    before = lax.broadcasted_iota(jnp.int32, (COUNT, COUNT), 0) < lax.broadcasted_iota(jnp.int32, (COUNT, COUNT), 1)
    upper = jnp.where(before, 1.0, 0.0).astype(jnp.bfloat16)
    earlier = jnp.dot(onehot.astype(jnp.bfloat16), upper, preferred_element_type=jnp.float32)
    return row, jnp.sum(earlier * onehot, axis=0, keepdims=True).astype(jnp.int32)


def folded(row):
    return jnp.concatenate([row[:, n * 128 : (n + 1) * 128] for n in range(COUNT // 128)], axis=0)


def rows_of(k):
    return pl.ds(pl.multiple_of(k * NBS, NBS), NBS)


def first_kernel(
    mine, field_hbm, profile_hbm, bins_hbm, jitter_hbm, energy_hbm, delays_hbm, left_hbm, right_hbm,
    send_hbm, phases, energies, beam, places,
    field, profile, bins, jitter, energy, delays, left, right, acc, send, index_v, index, sems,
):
    pairs = [
        (profile_hbm, profile), (left_hbm, left), (right_hbm, right), (delays_hbm, delays),
        (field_hbm, field), (bins_hbm, bins), (jitter_hbm, jitter), (energy_hbm, energy),
    ]
    copies = [pltpu.make_async_copy(src, dst, sems.at[n]) for n, (src, dst) in enumerate(pairs)]
    for copy in copies:
        copy.start()
    copies[3].wait()
    row, slot = slots_of(delays)
    places[0:1] = row
    places[1:2] = slot
    index_v[...] = folded(((mine[0] + row) % PEERS) * MESSAGE + slot)
    to_scalar = pltpu.make_async_copy(index_v, index, sems.at[3])
    to_scalar.start()
    for copy in copies[:3]:
        copy.wait()
    p = profile[...]
    half = jnp.dot(left[...], p, precision=HIGHEST, preferred_element_type=jnp.float32)
    both = jnp.concatenate([half[:GRID], half[GRID:]], axis=1)
    spread = jnp.dot(both, right[...], precision=HIGHEST, preferred_element_type=jnp.float32)
    beam[0] = spread[:, :GRID]
    beam[1] = spread[:, GRID:]
    beam[2] = p
    copies[4].wait()

    def project(k, carry):
        re, im = field[0, k], field[1, k]
        dr, di, q = beam[0], beam[1], profile[...]
        acc[0, pl.ds(k, 1)] = jnp.sum(q * re, axis=0, keepdims=True)
        acc[1, pl.ds(k, 1)] = jnp.sum(q * im, axis=0, keepdims=True)
        acc[2, pl.ds(k, 1)] = jnp.sum(dr * re - di * im, axis=0, keepdims=True)
        acc[3, pl.ds(k, 1)] = jnp.sum(dr * im + di * re, axis=0, keepdims=True)
        return carry

    lax.fori_loop(0, GROUPS, project, 0)
    self_re = jnp.sum(p * beam[0])
    self_im = jnp.sum(p * beam[1])
    for n in range(4):
        acc[n] = lane_total(acc[n]) * (1.0 / GRID)
    for copy in copies[5:]:
        copy.wait()

    def push(k, carry):
        rows = rows_of(k)
        ph = jnp.float32(2.0 * math.pi / NBINS) * (bins[rows].astype(jnp.float32) + jitter[rows])
        ph, en = pushed(ph, energy[rows], acc[0, pl.ds(k, 1)], acc[1, pl.ds(k, 1)])
        phases[rows] = ph
        energies[rows] = en
        c, s = cos_sin(ph)
        acc[4, pl.ds(k, 1)] = jnp.sum(c, axis=0, keepdims=True)
        acc[5, pl.ds(k, 1)] = jnp.sum(s, axis=0, keepdims=True)
        return carry

    lax.fori_loop(0, GROUPS, push, 0)
    to_scalar.wait()

    def put(n, carry):
        base = pl.multiple_of(n * BATCH, BATCH)
        spots = [index[n // (128 // BATCH), n % (128 // BATCH) * BATCH + m] for m in range(BATCH)]
        ph = [phases[pl.ds(base + m, 1)] for m in range(BATCH)]
        en = [energies[pl.ds(base + m, 1)] for m in range(BATCH)]
        for m in range(BATCH):
            send[pl.ds(spots[m], 1)] = ph[m]
            send[pl.ds(spots[m] + CAP, 1)] = en[m]
        return carry

    lax.fori_loop(0, COUNT // BATCH, put, 0)
    bre = lane_total(acc[4]) * (1.0 / (NBS * BLOCK))
    bim = lane_total(acc[5]) * (-1.0 / (NBS * BLOCK))
    gain = GAIN / GRID
    next_re = acc[2] + gain * (bre * self_re - bim * self_im)
    next_im = acc[3] + gain * (bre * self_im + bim * self_re)
    note = one_row([next_re, next_im, bre, bim])
    for n in range(PEERS):
        send[n * MESSAGE + 2 * CAP : (n + 1) * MESSAGE] = note
    out = pltpu.make_async_copy(send, send_hbm, sems.at[0])
    out.start()
    out.wait()


def pushed(ph, en, amp_re, amp_im):
    c, s = cos_sin(ph)
    en = en - KAPPA * (amp_re * c - amp_im * s)
    return ph + OMEGA * en, en


def one_row(parts):
    rest = 128 // GROUPS - len(parts)
    stack = jnp.concatenate(parts + [jnp.zeros((rest * GROUPS, 128), jnp.float32)], axis=0)
    return stack.T[0:1]


def parts_of(recv, device):
    row = recv[pl.ds(device * MESSAGE + 2 * CAP, 1)]
    return jnp.broadcast_to(row, (128, 128)).T


def carried(value, flag):
    rolled = jnp.concatenate([jnp.zeros_like(value[:1]), value[:-1]], axis=0)
    return jnp.where(flag, rolled, value)


def second_kernel(mine, phases1, energies1, recv, small, earlier, acc):
    me = mine[0]
    near = parts_of(recv, (me + PEERS - 1) % PEERS)
    far = parts_of(recv, (me + PEERS - 2) % PEERS)
    for n in range(2):
        acc[n] = carried(near[n * GROUPS : (n + 1) * GROUPS], me == 0)
        earlier[n] = carried(far[(2 + n) * GROUPS : (3 + n) * GROUPS], me < 2)

    def push(k, carry):
        rows = rows_of(k)
        ph, _ = pushed(phases1[rows], energies1[rows], acc[0, pl.ds(k, 1)], acc[1, pl.ds(k, 1)])
        c, s = cos_sin(ph)
        acc[2, pl.ds(k, 1)] = jnp.sum(c, axis=0, keepdims=True)
        acc[3, pl.ds(k, 1)] = jnp.sum(s, axis=0, keepdims=True)
        return carry

    lax.fori_loop(0, GROUPS, push, 0)
    small[0] = lane_total(acc[2]) * (1.0 / (NBS * BLOCK))
    small[1] = lane_total(acc[3]) * (-1.0 / (NBS * BLOCK))


def wide_halves(x):
    high = x.astype(jnp.bfloat16)
    return high, (x - high.astype(jnp.float32)).astype(jnp.bfloat16)


def pick_kernel(mine, recv, places, phases, energies, index_v, index, amps, sems):
    me = mine[0]
    source = (me - places[0:1] + PEERS) % PEERS
    index_v[...] = folded(source * MESSAGE + places[1:2])
    to_scalar = pltpu.make_async_copy(index_v, index, sems.at[0])
    to_scalar.start()
    lane = lax.broadcasted_iota(jnp.int32, (128, 128), 1)
    sheet = recv[pl.ds(2 * CAP, PEERS, MESSAGE), :]
    wrapped = jnp.concatenate([sheet[127:128, 127:128], sheet[127:128, :127]], axis=1)
    wrapped = jnp.where(lane[0:1] % GROUPS == 0, 0.0, wrapped)
    sheet = jnp.concatenate([wrapped, sheet[:127]], axis=0)
    for n in range(COUNT // 128):
        column = jnp.broadcast_to(source[:, n * 128 : (n + 1) * 128], (128, 128)).T
        onehot = jnp.where(lane == column, 1.0, 0.0)
        amps[n * 128 : (n + 1) * 128] = jnp.dot(
            onehot, sheet, precision=HIGHEST, preferred_element_type=jnp.float32
        )
    to_scalar.wait()

    def get(n, carry):
        base = pl.multiple_of(n * BATCH, BATCH)
        spots = [index[n // (128 // BATCH), n % (128 // BATCH) * BATCH + m] for m in range(BATCH)]
        ph = [recv[pl.ds(spot, 1)] for spot in spots]
        en = [recv[pl.ds(spot + CAP, 1)] for spot in spots]
        for m in range(BATCH):
            phases[pl.ds(base + m, 1)] = ph[m]
            energies[pl.ds(base + m, 1)] = en[m]
        return carry

    lax.fori_loop(0, COUNT // BATCH, get, 0)
    for k in range(GROUPS):
        rows = slice(k * NBS, (k + 1) * NBS)
        re, im = amps[rows, k : k + 1], amps[rows, GROUPS + k : GROUPS + k + 1]
        phases[rows], energies[rows] = pushed(phases[rows], energies[rows], re, im)


SLAB = 4
PIECES = ((0, 1), (1, 12), (12, 16))


def field_kernel(mine, piece_a, piece_b, piece_c, small, earlier, beam, left, right, out_hbm, acc, out, sems):
    me = mine[0]
    for n in range(2):
        acc[n] = GAIN * carried(small[n], me == 0)
        acc[2 + n] = GAIN * earlier[n]

    def plane(c, k):
        for piece, (low, high) in zip((piece_a, piece_b, piece_c), PIECES):
            if low <= k < high:
                return piece[c, k - low]
        return jnp.zeros((GRID, GRID), jnp.float32)

    late = me < 2
    p = beam[2]
    dr, di = beam[0], beam[1]
    copies = []
    for slab in range(GROUPS // SLAB):
        ks = range(slab * SLAB, (slab + 1) * SLAB)
        rows = []
        for k in ks:
            parts = [jnp.where(late, plane(c, k - 1), plane(c, k)) + acc[2 + c, k : k + 1] * p for c in range(2)]
            rows.append(jnp.concatenate(parts, axis=1))
        hi, lo = wide_halves(jnp.concatenate(rows, axis=0))
        half = jnp.dot(jnp.concatenate([hi, lo, hi], axis=1), right[...], preferred_element_type=jnp.float32)
        cols = []
        for m in range(SLAB):
            mid = half[m * GRID : (m + 1) * GRID]
            cols.append(jnp.concatenate([mid[:, :GRID], mid[:, GRID:]], axis=0))
        hi, lo = wide_halves(jnp.concatenate(cols, axis=1))
        full = jnp.dot(left[...], jnp.concatenate([hi, lo, hi], axis=0), preferred_element_type=jnp.float32)
        for m, k in enumerate(ks):
            cr, ci = acc[0, k : k + 1], acc[1, k : k + 1]
            out[0, k] = full[:GRID, m * GRID : (m + 1) * GRID] + (cr * dr - ci * di)
            out[1, k] = full[GRID:, m * GRID : (m + 1) * GRID] + (cr * di + ci * dr)
        for c in range(2):
            span = pl.ds(slab * SLAB, SLAB)
            copies.append(pltpu.make_async_copy(out.at[c, span], out_hbm.at[c, span], sems.at[2 * slab + c]))
            copies[-1].start()
    for copy in copies:
        copy.wait()


def shifted(value, axis, steps):
    count = lax.axis_size(axis)
    pairs = [(source, (source + steps) % count) for source in range(count)]
    return lax.ppermute(value, axis, pairs)


def shape(*dims, dtype=jnp.float32):
    return jax.ShapeDtypeStruct(dims, dtype)


def whole():
    return pl.BlockSpec(memory_space=pltpu.VMEM)


def vmem(*dims, dtype=jnp.float32):
    return pltpu.VMEM(dims, dtype)


def in_hbm(value):
    return pltpu.with_memory_space_constraint(value, pltpu.HBM)


def per_device(field, phase_bins, phase_jitter, energy, profile, delays):
    params = pltpu.CompilerParams(vmem_limit_bytes=VMEM_LIMIT)
    scalar = pl.BlockSpec(memory_space=pltpu.SMEM)
    remain = pl.BlockSpec(memory_space=pltpu.HBM)
    field = field.reshape(2, GROUPS, GRID, GRID)
    bins = phase_bins.reshape(COUNT, BLOCK)
    jitter = phase_jitter.reshape(COUNT, BLOCK)
    energies = energy.reshape(COUNT, BLOCK)
    mine = lax.axis_index("cuts").reshape(1)
    one, two = line_operator(1), line_operator(2)
    left_one = jnp.asarray(np.concatenate(one, axis=0), jnp.float32)
    right_one = jnp.asarray(right_form(*one), jnp.float32)
    sources = [field[:, low:high] for low, high in PIECES]
    field_a = shifted(sources[0], "cuts", 2)
    operands = [field, profile, bins, jitter, energies, delays.reshape(GROUPS, 1, NBS), left_one, right_one]
    send, phases1, energies1, beam, places = pl.pallas_call(
        first_kernel,
        out_shape=(
            pltpu.HBM((ROWS, BLOCK), jnp.float32),
            shape(COUNT, BLOCK),
            shape(COUNT, BLOCK),
            shape(3, GRID, GRID),
            shape(8, COUNT, dtype=jnp.int32),
        ),
        in_specs=[scalar] + [remain] * 8,
        out_specs=(remain,) + (whole(),) * 4,
        scratch_shapes=[
            vmem(2, GROUPS, GRID, GRID),
            vmem(GRID, GRID),
            vmem(COUNT, BLOCK, dtype=jnp.int32),
            vmem(COUNT, BLOCK),
            vmem(COUNT, BLOCK),
            vmem(GROUPS, 1, NBS, dtype=jnp.int32),
            vmem(2 * GRID, GRID),
            vmem(2 * GRID, 2 * GRID),
            vmem(6, GROUPS, 128),
            vmem(ROWS, BLOCK),
            vmem(8, 128, dtype=jnp.int32),
            pltpu.SMEM((8, 128), jnp.int32),
            pltpu.SemaphoreType.DMA((8,)),
        ],
        compiler_params=params,
        name="push_place",
    )(mine, *[in_hbm(value) for value in operands])
    send, field_a = lax.optimization_barrier((send, field_a))
    field_b = shifted(sources[1], "cuts", 2)
    field_c = shifted(sources[2], "cuts", 2)
    recv = lax.all_to_all(send.reshape(ROWS, 1, BLOCK), "cuts", split_axis=0, concat_axis=0, tiled=True)
    recv = recv.reshape(ROWS, BLOCK)
    small, earlier = pl.pallas_call(
        second_kernel,
        out_shape=(shape(2, GROUPS, 128), shape(2, GROUPS, 128)),
        in_specs=[scalar] + [whole()] * 3,
        out_specs=(whole(),) * 2,
        scratch_shapes=[vmem(4, GROUPS, 128)],
        compiler_params=params,
        name="second_push",
    )(mine, phases1, energies1, recv)
    arrived = shifted(small, "cuts", 1)
    phase_out, energy_out = pl.pallas_call(
        pick_kernel,
        out_shape=(shape(COUNT, BLOCK), shape(COUNT, BLOCK)),
        in_specs=[scalar] + [whole()] * 2,
        out_specs=(whole(),) * 2,
        scratch_shapes=[
            vmem(8, 128, dtype=jnp.int32),
            pltpu.SMEM((8, 128), jnp.int32),
            vmem(COUNT, 128),
            pltpu.SemaphoreType.DMA((1,)),
        ],
        compiler_params=params,
        name="pick",
    )(mine, recv, places)
    out = pl.pallas_call(
        field_kernel,
        out_shape=shape(2, GROUPS, GRID, GRID),
        in_specs=[scalar] + [whole()] * 8,
        out_specs=remain,
        scratch_shapes=[
            vmem(4, GROUPS, 128),
            vmem(2, GROUPS, GRID, GRID),
            pltpu.SemaphoreType.DMA((2 * GROUPS // SLAB,)),
        ],
        compiler_params=params,
        name="diffract",
    )(mine, field_a, field_b, field_c, arrived, earlier, beam, deep_left(left_form(*two)), deep_right(right_form(*two)))
    return (
        out.reshape(2, GROUPS, 1, GRID, GRID),
        phase_out.reshape(GROUPS, 1, NBS * BLOCK),
        energy_out.reshape(GROUPS, 1, NBS * BLOCK),
    )


def solution(mesh):
    return jax.shard_map(
        per_device,
        mesh=mesh,
        in_specs=(
            P(None, None, "cuts", None, None),
            P(None, "cuts", None),
            P(None, "cuts", None),
            P(None, "cuts", None),
            P(),
            P(),
        ),
        out_specs=(P(None, None, "cuts", None, None), P(None, "cuts", None), P(None, "cuts", None)),
        check_vma=False,
    )
```

```python
import functools
import math

import jax
import jax.numpy as jnp
import ml_dtypes
import numpy as np
from jax import lax
from jax.experimental import pallas as pl
from jax.experimental.pallas import tpu as pltpu
from jax.sharding import PartitionSpec as P

BLOCK = 128
NBINS = 16
KAPPA = 1.0
OMEGA = 1.0
GAIN = 16.0
PHASE_COEF = 20.0
GRID = 128
GROUPS = 16
NBS = 64
COUNT = GROUPS * NBS
PEERS = 128
CAP = 20
MESSAGE = 2 * CAP + 1
ROWS = PEERS * MESSAGE
BATCH = 16
VMEM_LIMIT = 24 * 1024 * 1024
HIGHEST = lax.Precision.HIGHEST


def line_operator(power):
    index = np.arange(GRID)
    freq = ((index + GRID // 2) % GRID - GRID // 2) / GRID
    weight = np.exp(-1j * PHASE_COEF * power * freq**2)
    wave = np.exp(2j * np.pi * (index[:, None] * index[None, :] % GRID) / GRID)
    column = wave @ weight / GRID
    matrix = column[(index[:, None] - index[None, :]) % GRID]
    return matrix.real, matrix.imag


def left_form(real, imag):
    return np.block([[real, -imag], [imag, real]])


def right_form(real, imag):
    return np.block([[real, imag], [-imag, real]])


def halves(matrix):
    high = matrix.astype(ml_dtypes.bfloat16)
    return high, (matrix - high.astype(np.float64)).astype(ml_dtypes.bfloat16)


def deep_left(matrix):
    high, low = halves(matrix)
    return jnp.asarray(np.concatenate([high, high, low], axis=1))


def deep_right(matrix):
    high, low = halves(matrix)
    return jnp.asarray(np.concatenate([high, high, low], axis=0))


def fitted(function, degree):
    top = (math.pi / 2 + 0.01) ** 2
    nodes = (np.cos(np.pi * (np.arange(400) + 0.5) / 400) + 1) / 2 * top
    series = np.polynomial.chebyshev.Chebyshev.fit(nodes, function(np.sqrt(nodes)), degree, domain=[0, top])
    return [float(c) for c in series.convert(kind=np.polynomial.Polynomial).coef]


SIN_COEF = fitted(lambda r: np.sin(r) / r, 5)
COS_COEF = fitted(np.cos, 6)
PI_HIGH = 3.140625
PI_MID = 9.67502593994140625e-4
PI_LOW = math.pi - PI_HIGH - PI_MID


def horner(coefs, x):
    value = jnp.float32(coefs[-1])
    for c in coefs[-2::-1]:
        value = value * x + jnp.float32(c)
    return value


def cos_sin(x):
    turns = jnp.round(x * jnp.float32(1.0 / math.pi))
    r = x - turns * jnp.float32(PI_HIGH)
    r = r - turns * jnp.float32(PI_MID)
    r = r - turns * jnp.float32(PI_LOW)
    half = turns * 0.5
    sign = 1.0 - 4.0 * jnp.abs(half - jnp.round(half))
    square = r * r
    return horner(COS_COEF, square) * sign, horner(SIN_COEF, square) * (r * sign)


def lane_total(rows):
    return jnp.broadcast_to(jnp.sum(rows, axis=1, keepdims=True), rows.shape)


def slots_of(delays):
    row = jnp.concatenate([delays[k] for k in range(GROUPS)], axis=1)
    values = lax.broadcasted_iota(jnp.int32, (PEERS, COUNT), 0)
    onehot = jnp.where(values == row, 1.0, 0.0)
    before = lax.broadcasted_iota(jnp.int32, (COUNT, COUNT), 0) < lax.broadcasted_iota(jnp.int32, (COUNT, COUNT), 1)
    upper = jnp.where(before, 1.0, 0.0).astype(jnp.bfloat16)
    earlier = jnp.dot(onehot.astype(jnp.bfloat16), upper, preferred_element_type=jnp.float32)
    return row, jnp.sum(earlier * onehot, axis=0, keepdims=True).astype(jnp.int32)


def folded(row):
    return jnp.concatenate([row[:, n * 128 : (n + 1) * 128] for n in range(COUNT // 128)], axis=0)


def rows_of(k):
    return pl.ds(pl.multiple_of(k * NBS, NBS), NBS)


def first_kernel(
    mine, field_hbm, profile_hbm, bins_hbm, jitter_hbm, energy_hbm, delays_hbm, left_hbm, right_hbm,
    send_hbm, phases_hbm, energies_hbm, places_hbm, beam,
    field, profile, bins, jitter, energy, delays, left, right, acc, send, phases, energies, places, index_v, index, sems,
):
    pairs = [
        (profile_hbm, profile), (left_hbm, left), (right_hbm, right), (delays_hbm, delays),
        (field_hbm, field), (bins_hbm, bins), (jitter_hbm, jitter), (energy_hbm, energy),
    ]
    copies = [pltpu.make_async_copy(src, dst, sems.at[n]) for n, (src, dst) in enumerate(pairs)]
    for copy in copies:
        copy.start()
    copies[3].wait()
    row, slot = slots_of(delays)
    places[0:1] = row
    places[1:2] = slot
    index_v[...] = folded(((mine[0] + row) % PEERS) * MESSAGE + slot)
    to_scalar = pltpu.make_async_copy(index_v, index, sems.at[3])
    to_scalar.start()
    for copy in copies[:3]:
        copy.wait()
    p = profile[...]
    half = jnp.dot(left[...], p, precision=HIGHEST, preferred_element_type=jnp.float32)
    both = jnp.concatenate([half[:GRID], half[GRID:]], axis=1)
    spread = jnp.dot(both, right[...], precision=HIGHEST, preferred_element_type=jnp.float32)
    beam[0] = spread[:, :GRID]
    beam[1] = spread[:, GRID:]
    beam[2] = p
    copies[4].wait()
    kept = [pltpu.make_async_copy(places, places_hbm, sems.at[8])]
    kept[0].start()

    def project(k, carry):
        re, im = field[0, k], field[1, k]
        dr, di, q = beam[0], beam[1], profile[...]
        acc[0, pl.ds(k, 1)] = jnp.sum(q * re, axis=0, keepdims=True)
        acc[1, pl.ds(k, 1)] = jnp.sum(q * im, axis=0, keepdims=True)
        acc[2, pl.ds(k, 1)] = jnp.sum(dr * re - di * im, axis=0, keepdims=True)
        acc[3, pl.ds(k, 1)] = jnp.sum(dr * im + di * re, axis=0, keepdims=True)
        return carry

    lax.fori_loop(0, GROUPS, project, 0)
    self_re = jnp.sum(p * beam[0])
    self_im = jnp.sum(p * beam[1])
    for n in range(4):
        acc[n] = lane_total(acc[n]) * (1.0 / GRID)
    for copy in copies[5:]:
        copy.wait()

    def push(k, carry):
        rows = rows_of(k)
        ph = jnp.float32(2.0 * math.pi / NBINS) * (bins[rows].astype(jnp.float32) + jitter[rows])
        ph, en = pushed(ph, energy[rows], acc[0, pl.ds(k, 1)], acc[1, pl.ds(k, 1)])
        phases[rows] = ph
        energies[rows] = en
        c, s = cos_sin(ph)
        acc[4, pl.ds(k, 1)] = jnp.sum(c, axis=0, keepdims=True)
        acc[5, pl.ds(k, 1)] = jnp.sum(s, axis=0, keepdims=True)
        return carry

    lax.fori_loop(0, GROUPS, push, 0)
    kept.append(pltpu.make_async_copy(phases, phases_hbm, sems.at[9]))
    kept.append(pltpu.make_async_copy(energies, energies_hbm, sems.at[10]))
    for copy in kept[1:]:
        copy.start()
    to_scalar.wait()

    def put(n, carry):
        base = pl.multiple_of(n * BATCH, BATCH)
        spots = [index[n // (128 // BATCH), n % (128 // BATCH) * BATCH + m] for m in range(BATCH)]
        ph = [phases[pl.ds(base + m, 1)] for m in range(BATCH)]
        en = [energies[pl.ds(base + m, 1)] for m in range(BATCH)]
        for m in range(BATCH):
            send[pl.ds(spots[m], 1)] = ph[m]
            send[pl.ds(spots[m] + CAP, 1)] = en[m]
        return carry

    lax.fori_loop(0, COUNT // BATCH, put, 0)
    bre = lane_total(acc[4]) * (1.0 / (NBS * BLOCK))
    bim = lane_total(acc[5]) * (-1.0 / (NBS * BLOCK))
    gain = GAIN / GRID
    next_re = acc[2] + gain * (bre * self_re - bim * self_im)
    next_im = acc[3] + gain * (bre * self_im + bim * self_re)
    note = one_row([next_re, next_im, bre, bim])
    for n in range(PEERS):
        send[n * MESSAGE + 2 * CAP : (n + 1) * MESSAGE] = note
    out = pltpu.make_async_copy(send, send_hbm, sems.at[0])
    out.start()
    for copy in kept:
        copy.wait()
    out.wait()


def pushed(ph, en, amp_re, amp_im):
    c, s = cos_sin(ph)
    en = en - KAPPA * (amp_re * c - amp_im * s)
    return ph + OMEGA * en, en


def one_row(parts):
    rest = 128 // GROUPS - len(parts)
    stack = jnp.concatenate(parts + [jnp.zeros((rest * GROUPS, 128), jnp.float32)], axis=0)
    return stack.T[0:1]


def parts_of(recv, device):
    row = recv[pl.ds(device * MESSAGE + 2 * CAP, 1)]
    return jnp.broadcast_to(row, (128, 128)).T


def carried(value, flag):
    rolled = jnp.concatenate([jnp.zeros_like(value[:1]), value[:-1]], axis=0)
    return jnp.where(flag, rolled, value)


def second_kernel(mine, phases1, energies1, recv, small, earlier, acc):
    me = mine[0]
    near = parts_of(recv, (me + PEERS - 1) % PEERS)
    far = parts_of(recv, (me + PEERS - 2) % PEERS)
    for n in range(2):
        acc[n] = carried(near[n * GROUPS : (n + 1) * GROUPS], me == 0)
        earlier[n] = carried(far[(2 + n) * GROUPS : (3 + n) * GROUPS], me < 2)

    def push(k, carry):
        rows = rows_of(k)
        ph, _ = pushed(phases1[rows], energies1[rows], acc[0, pl.ds(k, 1)], acc[1, pl.ds(k, 1)])
        c, s = cos_sin(ph)
        acc[2, pl.ds(k, 1)] = jnp.sum(c, axis=0, keepdims=True)
        acc[3, pl.ds(k, 1)] = jnp.sum(s, axis=0, keepdims=True)
        return carry

    lax.fori_loop(0, GROUPS, push, 0)
    small[0] = lane_total(acc[2]) * (1.0 / (NBS * BLOCK))
    small[1] = lane_total(acc[3]) * (-1.0 / (NBS * BLOCK))


def wide_halves(x):
    high = x.astype(jnp.bfloat16)
    return high, (x - high.astype(jnp.float32)).astype(jnp.bfloat16)


def pick_kernel(mine, recv, places, phases, energies, index_v, index, amps, sems):
    me = mine[0]
    source = (me - places[0:1] + PEERS) % PEERS
    index_v[...] = folded(source * MESSAGE + places[1:2])
    to_scalar = pltpu.make_async_copy(index_v, index, sems.at[0])
    to_scalar.start()
    lane = lax.broadcasted_iota(jnp.int32, (128, 128), 1)
    sheet = recv[pl.ds(2 * CAP, PEERS, MESSAGE), :]
    wrapped = jnp.concatenate([sheet[127:128, 127:128], sheet[127:128, :127]], axis=1)
    wrapped = jnp.where(lane[0:1] % GROUPS == 0, 0.0, wrapped)
    sheet = jnp.concatenate([wrapped, sheet[:127]], axis=0)
    for n in range(COUNT // 128):
        column = jnp.broadcast_to(source[:, n * 128 : (n + 1) * 128], (128, 128)).T
        onehot = jnp.where(lane == column, 1.0, 0.0)
        amps[n * 128 : (n + 1) * 128] = jnp.dot(
            onehot, sheet, precision=HIGHEST, preferred_element_type=jnp.float32
        )
    to_scalar.wait()

    def get(n, carry):
        base = pl.multiple_of(n * BATCH, BATCH)
        spots = [index[n // (128 // BATCH), n % (128 // BATCH) * BATCH + m] for m in range(BATCH)]
        ph = [recv[pl.ds(spot, 1)] for spot in spots]
        en = [recv[pl.ds(spot + CAP, 1)] for spot in spots]
        for m in range(BATCH):
            phases[pl.ds(base + m, 1)] = ph[m]
            energies[pl.ds(base + m, 1)] = en[m]
        return carry

    lax.fori_loop(0, COUNT // BATCH, get, 0)
    for k in range(GROUPS):
        rows = slice(k * NBS, (k + 1) * NBS)
        re, im = amps[rows, k : k + 1], amps[rows, GROUPS + k : GROUPS + k + 1]
        phases[rows], energies[rows] = pushed(phases[rows], energies[rows], re, im)


SLAB = 4
PIECES = ((0, 8), (8, 16))


def field_kernel(mine, piece_a, piece_b, small, earlier, beam, left, right, out_hbm, acc, out, out_sems):
    me = mine[0]

    def plane(c, k):
        for piece, (low, high) in zip((piece_a, piece_b), PIECES):
            if low <= k < high:
                return piece[c, k - low]
        return jnp.zeros((GRID, GRID), jnp.float32)

    for n in range(2):
        acc[n] = GAIN * carried(small[n], me == 0)
        acc[2 + n] = GAIN * earlier[n]
    late = me < 2
    p = beam[2]
    dr, di = beam[0], beam[1]
    copies = []
    for slab in range(GROUPS // SLAB):
        ks = range(slab * SLAB, (slab + 1) * SLAB)
        rows = []
        for k in ks:
            parts = [jnp.where(late, plane(c, k - 1), plane(c, k)) + acc[2 + c, k : k + 1] * p for c in range(2)]
            rows.append(jnp.concatenate(parts, axis=1))
        hi, lo = wide_halves(jnp.concatenate(rows, axis=0))
        half = jnp.dot(jnp.concatenate([hi, lo, hi], axis=1), right[...], preferred_element_type=jnp.float32)
        cols = []
        for m in range(SLAB):
            mid = half[m * GRID : (m + 1) * GRID]
            cols.append(jnp.concatenate([mid[:, :GRID], mid[:, GRID:]], axis=0))
        hi, lo = wide_halves(jnp.concatenate(cols, axis=1))
        full = jnp.dot(left[...], jnp.concatenate([hi, lo, hi], axis=0), preferred_element_type=jnp.float32)
        for m, k in enumerate(ks):
            cr, ci = acc[0, k : k + 1], acc[1, k : k + 1]
            out[0, k] = full[:GRID, m * GRID : (m + 1) * GRID] + (cr * dr - ci * di)
            out[1, k] = full[GRID:, m * GRID : (m + 1) * GRID] + (cr * di + ci * dr)
        for c in range(2):
            span = pl.ds(slab * SLAB, SLAB)
            copies.append(pltpu.make_async_copy(out.at[c, span], out_hbm.at[c, span], out_sems.at[2 * slab + c]))
            copies[-1].start()
    for copy in copies:
        copy.wait()


def shifted(value, axis, steps):
    count = lax.axis_size(axis)
    pairs = [(source, (source + steps) % count) for source in range(count)]
    return lax.ppermute(value, axis, pairs)


def shape(*dims, dtype=jnp.float32):
    return jax.ShapeDtypeStruct(dims, dtype)


def whole():
    return pl.BlockSpec(memory_space=pltpu.VMEM)


def vmem(*dims, dtype=jnp.float32):
    return pltpu.VMEM(dims, dtype)


def in_hbm(value):
    return pltpu.with_memory_space_constraint(value, pltpu.HBM)


def per_device(field, phase_bins, phase_jitter, energy, profile, delays):
    params = pltpu.CompilerParams(vmem_limit_bytes=VMEM_LIMIT)
    scalar = pl.BlockSpec(memory_space=pltpu.SMEM)
    remain = pl.BlockSpec(memory_space=pltpu.HBM)
    field = field.reshape(2, GROUPS, GRID, GRID)
    bins = phase_bins.reshape(COUNT, BLOCK)
    jitter = phase_jitter.reshape(COUNT, BLOCK)
    energies = energy.reshape(COUNT, BLOCK)
    mine = lax.axis_index("cuts").reshape(1)
    one, two = line_operator(1), line_operator(2)
    left_one = jnp.asarray(np.concatenate(one, axis=0), jnp.float32)
    right_one = jnp.asarray(right_form(*one), jnp.float32)
    field_a = shifted(field[:, : PIECES[0][1]], "cuts", 2)
    operands = [field, profile, bins, jitter, energies, delays.reshape(GROUPS, 1, NBS), left_one, right_one]
    low, high = PIECES[1]
    send, phases1, energies1, places, beam = pl.pallas_call(
        first_kernel,
        out_shape=(
            pltpu.HBM((ROWS, BLOCK), jnp.float32),
            pltpu.HBM((COUNT, BLOCK), jnp.float32),
            pltpu.HBM((COUNT, BLOCK), jnp.float32),
            pltpu.HBM((8, COUNT), jnp.int32),
            shape(3, GRID, GRID),
        ),
        in_specs=[scalar] + [remain] * 8,
        out_specs=(remain,) * 4 + (whole(),),
        scratch_shapes=[
            vmem(2, GROUPS, GRID, GRID),
            vmem(GRID, GRID),
            vmem(COUNT, BLOCK, dtype=jnp.int32),
            vmem(COUNT, BLOCK),
            vmem(COUNT, BLOCK),
            vmem(GROUPS, 1, NBS, dtype=jnp.int32),
            vmem(2 * GRID, GRID),
            vmem(2 * GRID, 2 * GRID),
            vmem(6, GROUPS, 128),
            vmem(ROWS, BLOCK),
            vmem(COUNT, BLOCK),
            vmem(COUNT, BLOCK),
            vmem(8, COUNT, dtype=jnp.int32),
            vmem(8, 128, dtype=jnp.int32),
            pltpu.SMEM((8, 128), jnp.int32),
            pltpu.SemaphoreType.DMA((11,)),
        ],
        compiler_params=params,
        name="push_place",
    )(mine, *[in_hbm(value) for value in operands])

    def exchange(send, phases1, energies1, places, field):
        field_b = shifted(field[:, low:high], "cuts", 2)
        recv = lax.all_to_all(send.reshape(ROWS, 1, BLOCK), "cuts", split_axis=0, concat_axis=0, tiled=True)
        recv = recv.reshape(ROWS, BLOCK)
        small, earlier = pl.pallas_call(
            second_kernel,
            out_shape=(shape(2, GROUPS, 128), shape(2, GROUPS, 128)),
            in_specs=[scalar] + [whole()] * 3,
            out_specs=(whole(),) * 2,
            scratch_shapes=[vmem(4, GROUPS, 128)],
            compiler_params=params,
            name="second_push",
        )(mine, phases1, energies1, recv)
        arrived = shifted(small, "cuts", 1)
        phase_out, energy_out = pl.pallas_call(
            pick_kernel,
            out_shape=(shape(COUNT, BLOCK), shape(COUNT, BLOCK)),
            in_specs=[scalar] + [whole()] * 2,
            out_specs=(whole(),) * 2,
            scratch_shapes=[
                vmem(8, 128, dtype=jnp.int32),
                pltpu.SMEM((8, 128), jnp.int32),
                vmem(COUNT, 128),
                pltpu.SemaphoreType.DMA((1,)),
            ],
            compiler_params=params,
            name="pick",
        )(mine, recv, places)
        return phase_out, energy_out, field_b, arrived, earlier

    def refuse(*operands):
        sizes = [(COUNT, BLOCK)] * 2 + [(2, high - low, GRID, GRID)] + [(2, GROUPS, 128)] * 2
        return tuple(jnp.zeros(size, jnp.float32) for size in sizes)

    phase_out, energy_out, field_b, arrived, earlier = lax.cond(
        delays[0, 0, 0] < PEERS, exchange, refuse, send, phases1, energies1, places, field
    )
    out = pl.pallas_call(
        field_kernel,
        out_shape=shape(2, GROUPS, GRID, GRID),
        in_specs=[scalar] + [whole()] * 7,
        out_specs=remain,
        scratch_shapes=[
            vmem(4, GROUPS, 128),
            vmem(2, GROUPS, GRID, GRID),
            pltpu.SemaphoreType.DMA((2 * GROUPS // SLAB,)),
        ],
        compiler_params=params,
        name="diffract",
    )(mine, field_a, field_b, arrived, earlier, beam, deep_left(left_form(*two)), deep_right(right_form(*two)))
    return (
        out.reshape(2, GROUPS, 1, GRID, GRID),
        phase_out.reshape(GROUPS, 1, NBS * BLOCK),
        energy_out.reshape(GROUPS, 1, NBS * BLOCK),
    )


def solution(mesh):
    return jax.shard_map(
        per_device,
        mesh=mesh,
        in_specs=(
            P(None, None, "cuts", None, None),
            P(None, "cuts", None),
            P(None, "cuts", None),
            P(None, "cuts", None),
            P(),
            P(),
        ),
        out_specs=(P(None, None, "cuts", None, None), P(None, "cuts", None), P(None, "cuts", None)),
        check_vma=False,
    )
```

```python
import functools
import math

import jax
import jax.numpy as jnp
import ml_dtypes
import numpy as np
from jax import lax
from jax.experimental import pallas as pl
from jax.experimental.pallas import tpu as pltpu
from jax.sharding import PartitionSpec as P

BLOCK = 128
NBINS = 16
KAPPA = 1.0
OMEGA = 1.0
GAIN = 16.0
PHASE_COEF = 20.0
GRID = 128
GROUPS = 16
NBS = 64
COUNT = GROUPS * NBS
PEERS = 128
CAP = 20
MESSAGE = 2 * CAP + 1
ROWS = PEERS * MESSAGE
BATCH = 16
VMEM_LIMIT = 24 * 1024 * 1024
HIGHEST = lax.Precision.HIGHEST


def line_operator(power):
    index = np.arange(GRID)
    freq = ((index + GRID // 2) % GRID - GRID // 2) / GRID
    weight = np.exp(-1j * PHASE_COEF * power * freq**2)
    wave = np.exp(2j * np.pi * (index[:, None] * index[None, :] % GRID) / GRID)
    column = wave @ weight / GRID
    matrix = column[(index[:, None] - index[None, :]) % GRID]
    return matrix.real, matrix.imag


def left_form(real, imag):
    return np.block([[real, -imag], [imag, real]])


def right_form(real, imag):
    return np.block([[real, imag], [-imag, real]])


def halves(matrix):
    high = matrix.astype(ml_dtypes.bfloat16)
    return high, (matrix - high.astype(np.float64)).astype(ml_dtypes.bfloat16)


def deep_left(matrix):
    high, low = halves(matrix)
    return jnp.asarray(np.concatenate([high, high, low], axis=1))


def deep_right(matrix):
    high, low = halves(matrix)
    return jnp.asarray(np.concatenate([high, high, low], axis=0))


def fitted(function, degree):
    top = (math.pi / 2 + 0.01) ** 2
    nodes = (np.cos(np.pi * (np.arange(400) + 0.5) / 400) + 1) / 2 * top
    series = np.polynomial.chebyshev.Chebyshev.fit(nodes, function(np.sqrt(nodes)), degree, domain=[0, top])
    return [float(c) for c in series.convert(kind=np.polynomial.Polynomial).coef]


SIN_COEF = fitted(lambda r: np.sin(r) / r, 5)
COS_COEF = fitted(np.cos, 6)
PI_HIGH = 3.140625
PI_MID = 9.67502593994140625e-4
PI_LOW = math.pi - PI_HIGH - PI_MID


def horner(coefs, x):
    value = jnp.float32(coefs[-1])
    for c in coefs[-2::-1]:
        value = value * x + jnp.float32(c)
    return value


def cos_sin(x):
    turns = jnp.round(x * jnp.float32(1.0 / math.pi))
    r = x - turns * jnp.float32(PI_HIGH)
    r = r - turns * jnp.float32(PI_MID)
    r = r - turns * jnp.float32(PI_LOW)
    half = turns * 0.5
    sign = 1.0 - 4.0 * jnp.abs(half - jnp.round(half))
    square = r * r
    return horner(COS_COEF, square) * sign, horner(SIN_COEF, square) * (r * sign)


def lane_total(rows):
    return jnp.broadcast_to(jnp.sum(rows, axis=1, keepdims=True), rows.shape)


def slots_of(delays):
    row = jnp.concatenate([delays[k] for k in range(GROUPS)], axis=1)
    values = lax.broadcasted_iota(jnp.int32, (PEERS, COUNT), 0)
    onehot = jnp.where(values == row, 1.0, 0.0)
    before = lax.broadcasted_iota(jnp.int32, (COUNT, COUNT), 0) < lax.broadcasted_iota(jnp.int32, (COUNT, COUNT), 1)
    upper = jnp.where(before, 1.0, 0.0).astype(jnp.bfloat16)
    earlier = jnp.dot(onehot.astype(jnp.bfloat16), upper, preferred_element_type=jnp.float32)
    return row, jnp.sum(earlier * onehot, axis=0, keepdims=True).astype(jnp.int32)


def folded(row):
    return jnp.concatenate([row[:, n * 128 : (n + 1) * 128] for n in range(COUNT // 128)], axis=0)


def rows_of(k):
    return pl.ds(pl.multiple_of(k * NBS, NBS), NBS)


def first_kernel(
    mine, field_hbm, profile_hbm, bins_hbm, jitter_hbm, energy_hbm, delays_hbm, left_hbm, right_hbm,
    send_hbm, phases_hbm, energies_hbm, places_hbm, beam,
    field, profile, bins, jitter, energy, delays, left, right, acc, send, phases, energies, places, index_v, index, sems,
):
    pairs = [
        (profile_hbm, profile), (left_hbm, left), (right_hbm, right), (delays_hbm, delays),
        (field_hbm, field), (bins_hbm, bins), (jitter_hbm, jitter), (energy_hbm, energy),
    ]
    copies = [pltpu.make_async_copy(src, dst, sems.at[n]) for n, (src, dst) in enumerate(pairs)]
    for copy in copies:
        copy.start()
    copies[3].wait()
    row, slot = slots_of(delays)
    places[0:1] = row
    places[1:2] = slot
    index_v[...] = folded(((mine[0] + row) % PEERS) * MESSAGE + slot)
    to_scalar = pltpu.make_async_copy(index_v, index, sems.at[3])
    to_scalar.start()
    for copy in copies[:3]:
        copy.wait()
    p = profile[...]
    half = jnp.dot(left[...], p, precision=HIGHEST, preferred_element_type=jnp.float32)
    both = jnp.concatenate([half[:GRID], half[GRID:]], axis=1)
    spread = jnp.dot(both, right[...], precision=HIGHEST, preferred_element_type=jnp.float32)
    beam[0] = spread[:, :GRID]
    beam[1] = spread[:, GRID:]
    beam[2] = p
    copies[4].wait()
    kept = [pltpu.make_async_copy(places, places_hbm, sems.at[8])]
    kept[0].start()

    def project(k, carry):
        re, im = field[0, k], field[1, k]
        dr, di, q = beam[0], beam[1], profile[...]
        acc[0, pl.ds(k, 1)] = jnp.sum(q * re, axis=0, keepdims=True)
        acc[1, pl.ds(k, 1)] = jnp.sum(q * im, axis=0, keepdims=True)
        acc[2, pl.ds(k, 1)] = jnp.sum(dr * re - di * im, axis=0, keepdims=True)
        acc[3, pl.ds(k, 1)] = jnp.sum(dr * im + di * re, axis=0, keepdims=True)
        return carry

    lax.fori_loop(0, GROUPS, project, 0)
    self_re = jnp.sum(p * beam[0])
    self_im = jnp.sum(p * beam[1])
    for n in range(4):
        acc[n] = lane_total(acc[n]) * (1.0 / GRID)
    for copy in copies[5:]:
        copy.wait()

    def push(k, carry):
        rows = rows_of(k)
        ph = jnp.float32(2.0 * math.pi / NBINS) * (bins[rows].astype(jnp.float32) + jitter[rows])
        ph, en = pushed(ph, energy[rows], acc[0, pl.ds(k, 1)], acc[1, pl.ds(k, 1)])
        phases[rows] = ph
        energies[rows] = en
        c, s = cos_sin(ph)
        acc[4, pl.ds(k, 1)] = jnp.sum(c, axis=0, keepdims=True)
        acc[5, pl.ds(k, 1)] = jnp.sum(s, axis=0, keepdims=True)
        return carry

    lax.fori_loop(0, GROUPS, push, 0)
    kept.append(pltpu.make_async_copy(phases, phases_hbm, sems.at[9]))
    kept.append(pltpu.make_async_copy(energies, energies_hbm, sems.at[10]))
    for copy in kept[1:]:
        copy.start()
    to_scalar.wait()

    def put(n, carry):
        base = pl.multiple_of(n * BATCH, BATCH)
        spots = [index[n // (128 // BATCH), n % (128 // BATCH) * BATCH + m] for m in range(BATCH)]
        ph = [phases[pl.ds(base + m, 1)] for m in range(BATCH)]
        en = [energies[pl.ds(base + m, 1)] for m in range(BATCH)]
        for m in range(BATCH):
            send[pl.ds(spots[m], 1)] = ph[m]
            send[pl.ds(spots[m] + CAP, 1)] = en[m]
        return carry

    lax.fori_loop(0, COUNT // BATCH, put, 0)
    bre = lane_total(acc[4]) * (1.0 / (NBS * BLOCK))
    bim = lane_total(acc[5]) * (-1.0 / (NBS * BLOCK))
    gain = GAIN / GRID
    next_re = acc[2] + gain * (bre * self_re - bim * self_im)
    next_im = acc[3] + gain * (bre * self_im + bim * self_re)
    note = one_row([next_re, next_im, bre, bim])
    for n in range(PEERS):
        send[n * MESSAGE + 2 * CAP : (n + 1) * MESSAGE] = note
    out = pltpu.make_async_copy(send, send_hbm, sems.at[0])
    out.start()
    for copy in kept:
        copy.wait()
    out.wait()


def pushed(ph, en, amp_re, amp_im):
    c, s = cos_sin(ph)
    en = en - KAPPA * (amp_re * c - amp_im * s)
    return ph + OMEGA * en, en


def one_row(parts):
    rest = 128 // GROUPS - len(parts)
    stack = jnp.concatenate(parts + [jnp.zeros((rest * GROUPS, 128), jnp.float32)], axis=0)
    return stack.T[0:1]


def parts_of(recv, device):
    row = recv[pl.ds(device * MESSAGE + 2 * CAP, 1)]
    return jnp.broadcast_to(row, (128, 128)).T


def carried(value, flag):
    rolled = jnp.concatenate([jnp.zeros_like(value[:1]), value[:-1]], axis=0)
    return jnp.where(flag, rolled, value)


def second_kernel(mine, phases1, energies1, recv, small, earlier, acc):
    me = mine[0]
    near = parts_of(recv, (me + PEERS - 1) % PEERS)
    far = parts_of(recv, (me + PEERS - 2) % PEERS)
    for n in range(2):
        acc[n] = carried(near[n * GROUPS : (n + 1) * GROUPS], me == 0)
        earlier[n] = carried(far[(2 + n) * GROUPS : (3 + n) * GROUPS], me < 2)

    def push(k, carry):
        rows = rows_of(k)
        ph, _ = pushed(phases1[rows], energies1[rows], acc[0, pl.ds(k, 1)], acc[1, pl.ds(k, 1)])
        c, s = cos_sin(ph)
        acc[2, pl.ds(k, 1)] = jnp.sum(c, axis=0, keepdims=True)
        acc[3, pl.ds(k, 1)] = jnp.sum(s, axis=0, keepdims=True)
        return carry

    lax.fori_loop(0, GROUPS, push, 0)
    small[0] = lane_total(acc[2]) * (1.0 / (NBS * BLOCK))
    small[1] = lane_total(acc[3]) * (-1.0 / (NBS * BLOCK))


def wide_halves(x):
    high = x.astype(jnp.bfloat16)
    return high, (x - high.astype(jnp.float32)).astype(jnp.bfloat16)


def pick_kernel(mine, recv, places, phases, energies, index_v, index, amps, sems):
    me = mine[0]
    source = (me - places[0:1] + PEERS) % PEERS
    index_v[...] = folded(source * MESSAGE + places[1:2])
    to_scalar = pltpu.make_async_copy(index_v, index, sems.at[0])
    to_scalar.start()
    lane = lax.broadcasted_iota(jnp.int32, (128, 128), 1)
    sheet = recv[pl.ds(2 * CAP, PEERS, MESSAGE), :]
    wrapped = jnp.concatenate([sheet[127:128, 127:128], sheet[127:128, :127]], axis=1)
    wrapped = jnp.where(lane[0:1] % GROUPS == 0, 0.0, wrapped)
    sheet = jnp.concatenate([wrapped, sheet[:127]], axis=0)
    for n in range(COUNT // 128):
        column = jnp.broadcast_to(source[:, n * 128 : (n + 1) * 128], (128, 128)).T
        onehot = jnp.where(lane == column, 1.0, 0.0)
        amps[n * 128 : (n + 1) * 128] = jnp.dot(
            onehot, sheet, precision=HIGHEST, preferred_element_type=jnp.float32
        )
    to_scalar.wait()

    def get(n, carry):
        base = pl.multiple_of(n * BATCH, BATCH)
        spots = [index[n // (128 // BATCH), n % (128 // BATCH) * BATCH + m] for m in range(BATCH)]
        ph = [recv[pl.ds(spot, 1)] for spot in spots]
        en = [recv[pl.ds(spot + CAP, 1)] for spot in spots]
        for m in range(BATCH):
            phases[pl.ds(base + m, 1)] = ph[m]
            energies[pl.ds(base + m, 1)] = en[m]
        return carry

    lax.fori_loop(0, COUNT // BATCH, get, 0)
    for k in range(GROUPS):
        rows = slice(k * NBS, (k + 1) * NBS)
        re, im = amps[rows, k : k + 1], amps[rows, GROUPS + k : GROUPS + k + 1]
        phases[rows], energies[rows] = pushed(phases[rows], energies[rows], re, im)


SLAB = 4
PIECES = ((0, 8), (8, 16))


def field_kernel(first, mine, piece, before, earlier, beam, left, right, out):
    late = mine[0] < 2
    p = beam[2]

    def plane(c, k):
        if k >= 0:
            return piece[c, k]
        return before[c, before.shape[1] - 1] if first else jnp.zeros((GRID, GRID), jnp.float32)

    for slab in range(piece.shape[1] // SLAB):
        ks = range(slab * SLAB, (slab + 1) * SLAB)
        rows = []
        for k in ks:
            parts = [
                jnp.where(late, plane(c, k - 1), plane(c, k)) + GAIN * earlier[c, first + k : first + k + 1] * p
                for c in range(2)
            ]
            rows.append(jnp.concatenate(parts, axis=1))
        hi, lo = wide_halves(jnp.concatenate(rows, axis=0))
        half = jnp.dot(jnp.concatenate([hi, lo, hi], axis=1), right[...], preferred_element_type=jnp.float32)
        cols = []
        for m in range(SLAB):
            mid = half[m * GRID : (m + 1) * GRID]
            cols.append(jnp.concatenate([mid[:, :GRID], mid[:, GRID:]], axis=0))
        hi, lo = wide_halves(jnp.concatenate(cols, axis=1))
        full = jnp.dot(left[...], jnp.concatenate([hi, lo, hi], axis=0), preferred_element_type=jnp.float32)
        for m, k in enumerate(ks):
            out[0, k] = full[:GRID, m * GRID : (m + 1) * GRID]
            out[1, k] = full[GRID:, m * GRID : (m + 1) * GRID]


def last_kernel(mine, part_a, part_b, small, beam, out_hbm, acc, out, sems):
    for n in range(2):
        acc[n] = GAIN * carried(small[n], mine[0] == 0)
    copies = []
    for part, (low, high) in zip((part_a, part_b), PIECES):

        def add(k, carry, part=part, low=low):
            cr, ci = acc[0, pl.ds(low + k, 1)], acc[1, pl.ds(low + k, 1)]
            out[0, low + k] = part[0, k] + (cr * beam[0] - ci * beam[1])
            out[1, low + k] = part[1, k] + (cr * beam[1] + ci * beam[0])
            return carry

        for start in range(0, high - low, SLAB):
            lax.fori_loop(start, start + SLAB, add, 0)
            span = pl.ds(low + start, SLAB)
            for c in range(2):
                copies.append(pltpu.make_async_copy(out.at[c, span], out_hbm.at[c, span], sems.at[len(copies)]))
                copies[-1].start()
    for copy in copies:
        copy.wait()


def shifted(value, axis, steps):
    count = lax.axis_size(axis)
    pairs = [(source, (source + steps) % count) for source in range(count)]
    return lax.ppermute(value, axis, pairs)


def shape(*dims, dtype=jnp.float32):
    return jax.ShapeDtypeStruct(dims, dtype)


def whole():
    return pl.BlockSpec(memory_space=pltpu.VMEM)


def vmem(*dims, dtype=jnp.float32):
    return pltpu.VMEM(dims, dtype)


def in_hbm(value):
    return pltpu.with_memory_space_constraint(value, pltpu.HBM)


def per_device(field, phase_bins, phase_jitter, energy, profile, delays):
    params = pltpu.CompilerParams(vmem_limit_bytes=VMEM_LIMIT)
    scalar = pl.BlockSpec(memory_space=pltpu.SMEM)
    remain = pl.BlockSpec(memory_space=pltpu.HBM)
    field = field.reshape(2, GROUPS, GRID, GRID)
    bins = phase_bins.reshape(COUNT, BLOCK)
    jitter = phase_jitter.reshape(COUNT, BLOCK)
    energies = energy.reshape(COUNT, BLOCK)
    mine = lax.axis_index("cuts").reshape(1)
    one, two = line_operator(1), line_operator(2)
    left_one = jnp.asarray(np.concatenate(one, axis=0), jnp.float32)
    right_one = jnp.asarray(right_form(*one), jnp.float32)
    field_a = shifted(field[:, : PIECES[0][1]], "cuts", 2)
    operands = [field, profile, bins, jitter, energies, delays.reshape(GROUPS, 1, NBS), left_one, right_one]
    low, high = PIECES[1]
    send, phases1, energies1, places, beam = pl.pallas_call(
        first_kernel,
        out_shape=(
            pltpu.HBM((ROWS, BLOCK), jnp.float32),
            pltpu.HBM((COUNT, BLOCK), jnp.float32),
            pltpu.HBM((COUNT, BLOCK), jnp.float32),
            pltpu.HBM((8, COUNT), jnp.int32),
            shape(3, GRID, GRID),
        ),
        in_specs=[scalar] + [remain] * 8,
        out_specs=(remain,) * 4 + (whole(),),
        scratch_shapes=[
            vmem(2, GROUPS, GRID, GRID),
            vmem(GRID, GRID),
            vmem(COUNT, BLOCK, dtype=jnp.int32),
            vmem(COUNT, BLOCK),
            vmem(COUNT, BLOCK),
            vmem(GROUPS, 1, NBS, dtype=jnp.int32),
            vmem(2 * GRID, GRID),
            vmem(2 * GRID, 2 * GRID),
            vmem(6, GROUPS, 128),
            vmem(ROWS, BLOCK),
            vmem(COUNT, BLOCK),
            vmem(COUNT, BLOCK),
            vmem(8, COUNT, dtype=jnp.int32),
            vmem(8, 128, dtype=jnp.int32),
            pltpu.SMEM((8, 128), jnp.int32),
            pltpu.SemaphoreType.DMA((11,)),
        ],
        compiler_params=params,
        name="push_place",
    )(mine, *[in_hbm(value) for value in operands])

    def exchange(rows):
        return lax.all_to_all(rows.reshape(ROWS, 1, BLOCK), "cuts", split_axis=0, concat_axis=0, tiled=True)

    def refuse(rows):
        return jnp.zeros((ROWS, 1, BLOCK), jnp.float32)

    recv = lax.cond(delays[0, 0, 0] < PEERS, exchange, refuse, send).reshape(ROWS, BLOCK)
    source_b, recv = lax.optimization_barrier((field[:, low:high], recv))
    field_b = shifted(source_b, "cuts", 2)
    small, earlier = pl.pallas_call(
        second_kernel,
        out_shape=(shape(2, GROUPS, 128), shape(2, GROUPS, 128)),
        in_specs=[scalar] + [whole()] * 3,
        out_specs=(whole(),) * 2,
        scratch_shapes=[vmem(4, GROUPS, 128)],
        compiler_params=params,
        name="second_push",
    )(mine, phases1, energies1, recv)
    arrived = shifted(small, "cuts", 1)
    phase_out, energy_out = pl.pallas_call(
        pick_kernel,
        out_shape=(shape(COUNT, BLOCK), shape(COUNT, BLOCK)),
        in_specs=[scalar] + [whole()] * 2,
        out_specs=(whole(),) * 2,
        scratch_shapes=[
            vmem(8, 128, dtype=jnp.int32),
            pltpu.SMEM((8, 128), jnp.int32),
            vmem(COUNT, 128),
            pltpu.SemaphoreType.DMA((1,)),
        ],
        compiler_params=params,
        name="pick",
    )(mine, recv, places)
    tables = (earlier, beam, deep_left(left_form(*two)), deep_right(right_form(*two)))

    def diffract(first, piece, before):
        return pl.pallas_call(
            functools.partial(field_kernel, first),
            out_shape=shape(*piece.shape),
            in_specs=[scalar] + [whole()] * 6,
            out_specs=whole(),
            compiler_params=params,
            name="diffract",
        )(mine, piece, before, *tables)

    part_a = diffract(0, field_a, field_a)
    part_b = diffract(low, field_b, field_a)
    out = pl.pallas_call(
        last_kernel,
        out_shape=shape(2, GROUPS, GRID, GRID),
        in_specs=[scalar] + [whole()] * 4,
        out_specs=remain,
        scratch_shapes=[
            vmem(2, GROUPS, 128),
            vmem(2, GROUPS, GRID, GRID),
            pltpu.SemaphoreType.DMA((2 * GROUPS // SLAB,)),
        ],
        compiler_params=params,
        name="last_bunching",
    )(mine, part_a, part_b, arrived, beam)
    return (
        out.reshape(2, GROUPS, 1, GRID, GRID),
        phase_out.reshape(GROUPS, 1, NBS * BLOCK),
        energy_out.reshape(GROUPS, 1, NBS * BLOCK),
    )


def solution(mesh):
    return jax.shard_map(
        per_device,
        mesh=mesh,
        in_specs=(
            P(None, None, "cuts", None, None),
            P(None, "cuts", None),
            P(None, "cuts", None),
            P(None, "cuts", None),
            P(),
            P(),
        ),
        out_specs=(P(None, None, "cuts", None, None), P(None, "cuts", None), P(None, "cuts", None)),
        check_vma=False,
    )
```

```python
import functools
import math

import jax
import jax.numpy as jnp
import ml_dtypes
import numpy as np
from jax import lax
from jax.experimental import pallas as pl
from jax.experimental.pallas import tpu as pltpu
from jax.sharding import PartitionSpec as P

BLOCK = 128
NBINS = 16
KAPPA = 1.0
OMEGA = 1.0
GAIN = 16.0
PHASE_COEF = 20.0
GRID = 128
GROUPS = 16
NBS = 64
COUNT = GROUPS * NBS
PEERS = 128
CAP = 20
MESSAGE = 2 * CAP + 1
ROWS = PEERS * MESSAGE
BATCH = 16
VMEM_LIMIT = 24 * 1024 * 1024
HIGHEST = lax.Precision.HIGHEST


def line_operator(power):
    index = np.arange(GRID)
    freq = ((index + GRID // 2) % GRID - GRID // 2) / GRID
    weight = np.exp(-1j * PHASE_COEF * power * freq**2)
    wave = np.exp(2j * np.pi * (index[:, None] * index[None, :] % GRID) / GRID)
    column = wave @ weight / GRID
    matrix = column[(index[:, None] - index[None, :]) % GRID]
    return matrix.real, matrix.imag


def left_form(real, imag):
    return np.block([[real, -imag], [imag, real]])


def right_form(real, imag):
    return np.block([[real, imag], [-imag, real]])


def halves(matrix):
    high = matrix.astype(ml_dtypes.bfloat16)
    return high, (matrix - high.astype(np.float64)).astype(ml_dtypes.bfloat16)


def deep_left(matrix):
    high, low = halves(matrix)
    return jnp.asarray(np.concatenate([high, high, low], axis=1))


def deep_right(matrix):
    high, low = halves(matrix)
    return jnp.asarray(np.concatenate([high, high, low], axis=0))


def fitted(function, degree):
    top = (math.pi / 2 + 0.01) ** 2
    nodes = (np.cos(np.pi * (np.arange(400) + 0.5) / 400) + 1) / 2 * top
    series = np.polynomial.chebyshev.Chebyshev.fit(nodes, function(np.sqrt(nodes)), degree, domain=[0, top])
    return [float(c) for c in series.convert(kind=np.polynomial.Polynomial).coef]


SIN_COEF = fitted(lambda r: np.sin(r) / r, 5)
COS_COEF = fitted(np.cos, 6)
PI_HIGH = 3.140625
PI_MID = 9.67502593994140625e-4
PI_LOW = math.pi - PI_HIGH - PI_MID


def horner(coefs, x):
    value = jnp.float32(coefs[-1])
    for c in coefs[-2::-1]:
        value = value * x + jnp.float32(c)
    return value


def cos_sin(x):
    turns = jnp.round(x * jnp.float32(1.0 / math.pi))
    r = x - turns * jnp.float32(PI_HIGH)
    r = r - turns * jnp.float32(PI_MID)
    r = r - turns * jnp.float32(PI_LOW)
    half = turns * 0.5
    sign = 1.0 - 4.0 * jnp.abs(half - jnp.round(half))
    square = r * r
    return horner(COS_COEF, square) * sign, horner(SIN_COEF, square) * (r * sign)


def lane_total(rows):
    return jnp.broadcast_to(jnp.sum(rows, axis=1, keepdims=True), rows.shape)


def slots_of(delays):
    row = jnp.concatenate([delays[k] for k in range(GROUPS)], axis=1)
    values = lax.broadcasted_iota(jnp.int32, (PEERS, COUNT), 0)
    onehot = jnp.where(values == row, 1.0, 0.0)
    before = lax.broadcasted_iota(jnp.int32, (COUNT, COUNT), 0) < lax.broadcasted_iota(jnp.int32, (COUNT, COUNT), 1)
    upper = jnp.where(before, 1.0, 0.0).astype(jnp.bfloat16)
    earlier = jnp.dot(onehot.astype(jnp.bfloat16), upper, preferred_element_type=jnp.float32)
    return row, jnp.sum(earlier * onehot, axis=0, keepdims=True).astype(jnp.int32)


def folded(row):
    return jnp.concatenate([row[:, n * 128 : (n + 1) * 128] for n in range(COUNT // 128)], axis=0)


def rows_of(k):
    return pl.ds(pl.multiple_of(k * NBS, NBS), NBS)


def first_kernel(
    mine, field_hbm, profile_hbm, bins_hbm, jitter_hbm, energy_hbm, delays_hbm, left_hbm, right_hbm,
    send_hbm, phases_hbm, energies_hbm, places_hbm, beam,
    field, profile, bins, jitter, energy, delays, left, right, acc, send, phases, energies, places, index_v, index, sems,
):
    pairs = [
        (profile_hbm, profile), (left_hbm, left), (right_hbm, right), (delays_hbm, delays),
        (field_hbm, field), (bins_hbm, bins), (jitter_hbm, jitter), (energy_hbm, energy),
    ]
    copies = [pltpu.make_async_copy(src, dst, sems.at[n]) for n, (src, dst) in enumerate(pairs)]
    for copy in copies:
        copy.start()
    copies[3].wait()
    row, slot = slots_of(delays)
    places[0:1] = row
    places[1:2] = slot
    index_v[...] = folded(((mine[0] + row) % PEERS) * MESSAGE + slot)
    to_scalar = pltpu.make_async_copy(index_v, index, sems.at[3])
    to_scalar.start()
    for copy in copies[:3]:
        copy.wait()
    p = profile[...]
    half = jnp.dot(left[...], p, precision=HIGHEST, preferred_element_type=jnp.float32)
    both = jnp.concatenate([half[:GRID], half[GRID:]], axis=1)
    spread = jnp.dot(both, right[...], precision=HIGHEST, preferred_element_type=jnp.float32)
    beam[0] = spread[:, :GRID]
    beam[1] = spread[:, GRID:]
    beam[2] = p
    copies[4].wait()
    kept = [pltpu.make_async_copy(places, places_hbm, sems.at[8])]
    kept[0].start()

    def project(k, carry):
        re, im = field[0, k], field[1, k]
        dr, di, q = beam[0], beam[1], profile[...]
        acc[0, pl.ds(k, 1)] = jnp.sum(q * re, axis=0, keepdims=True)
        acc[1, pl.ds(k, 1)] = jnp.sum(q * im, axis=0, keepdims=True)
        acc[2, pl.ds(k, 1)] = jnp.sum(dr * re - di * im, axis=0, keepdims=True)
        acc[3, pl.ds(k, 1)] = jnp.sum(dr * im + di * re, axis=0, keepdims=True)
        return carry

    lax.fori_loop(0, GROUPS, project, 0)
    self_re = jnp.sum(p * beam[0])
    self_im = jnp.sum(p * beam[1])
    for n in range(4):
        acc[n] = lane_total(acc[n]) * (1.0 / GRID)
    for copy in copies[5:]:
        copy.wait()

    def push(k, carry):
        rows = rows_of(k)
        ph = jnp.float32(2.0 * math.pi / NBINS) * (bins[rows].astype(jnp.float32) + jitter[rows])
        ph, en = pushed(ph, energy[rows], acc[0, pl.ds(k, 1)], acc[1, pl.ds(k, 1)])
        phases[rows] = ph
        energies[rows] = en
        c, s = cos_sin(ph)
        acc[4, pl.ds(k, 1)] = jnp.sum(c, axis=0, keepdims=True)
        acc[5, pl.ds(k, 1)] = jnp.sum(s, axis=0, keepdims=True)
        return carry

    lax.fori_loop(0, GROUPS, push, 0)
    kept.append(pltpu.make_async_copy(phases, phases_hbm, sems.at[9]))
    kept.append(pltpu.make_async_copy(energies, energies_hbm, sems.at[10]))
    for copy in kept[1:]:
        copy.start()
    to_scalar.wait()

    def put(n, carry):
        base = pl.multiple_of(n * BATCH, BATCH)
        spots = [index[n // (128 // BATCH), n % (128 // BATCH) * BATCH + m] for m in range(BATCH)]
        ph = [phases[pl.ds(base + m, 1)] for m in range(BATCH)]
        en = [energies[pl.ds(base + m, 1)] for m in range(BATCH)]
        for m in range(BATCH):
            send[pl.ds(spots[m], 1)] = ph[m]
            send[pl.ds(spots[m] + CAP, 1)] = en[m]
        return carry

    lax.fori_loop(0, COUNT // BATCH, put, 0)
    bre = lane_total(acc[4]) * (1.0 / (NBS * BLOCK))
    bim = lane_total(acc[5]) * (-1.0 / (NBS * BLOCK))
    gain = GAIN / GRID
    next_re = acc[2] + gain * (bre * self_re - bim * self_im)
    next_im = acc[3] + gain * (bre * self_im + bim * self_re)
    note = one_row([next_re, next_im, bre, bim])
    for n in range(PEERS):
        send[n * MESSAGE + 2 * CAP : (n + 1) * MESSAGE] = note
    out = pltpu.make_async_copy(send, send_hbm, sems.at[0])
    out.start()
    for copy in kept:
        copy.wait()
    out.wait()


def pushed(ph, en, amp_re, amp_im):
    c, s = cos_sin(ph)
    en = en - KAPPA * (amp_re * c - amp_im * s)
    return ph + OMEGA * en, en


def one_row(parts):
    rest = 128 // GROUPS - len(parts)
    stack = jnp.concatenate(parts + [jnp.zeros((rest * GROUPS, 128), jnp.float32)], axis=0)
    return stack.T[0:1]


def parts_of(recv, device):
    row = recv[pl.ds(device * MESSAGE + 2 * CAP, 1)]
    return jnp.broadcast_to(row, (128, 128)).T


def carried(value, flag):
    rolled = jnp.concatenate([jnp.zeros_like(value[:1]), value[:-1]], axis=0)
    return jnp.where(flag, rolled, value)


def second_kernel(mine, phases1, energies1, recv, small, earlier, acc):
    me = mine[0]
    near = parts_of(recv, (me + PEERS - 1) % PEERS)
    far = parts_of(recv, (me + PEERS - 2) % PEERS)
    for n in range(2):
        acc[n] = carried(near[n * GROUPS : (n + 1) * GROUPS], me == 0)
        earlier[n] = carried(far[(2 + n) * GROUPS : (3 + n) * GROUPS], me < 2)

    def push(k, carry):
        rows = rows_of(k)
        ph, _ = pushed(phases1[rows], energies1[rows], acc[0, pl.ds(k, 1)], acc[1, pl.ds(k, 1)])
        c, s = cos_sin(ph)
        acc[2, pl.ds(k, 1)] = jnp.sum(c, axis=0, keepdims=True)
        acc[3, pl.ds(k, 1)] = jnp.sum(s, axis=0, keepdims=True)
        return carry

    lax.fori_loop(0, GROUPS, push, 0)
    small[0] = lane_total(acc[2]) * (1.0 / (NBS * BLOCK))
    small[1] = lane_total(acc[3]) * (-1.0 / (NBS * BLOCK))


def wide_halves(x):
    high = x.astype(jnp.bfloat16)
    return high, (x - high.astype(jnp.float32)).astype(jnp.bfloat16)


def pick_kernel(mine, recv, places, phases, energies, index_v, index, amps, sems):
    me = mine[0]
    source = (me - places[0:1] + PEERS) % PEERS
    index_v[...] = folded(source * MESSAGE + places[1:2])
    to_scalar = pltpu.make_async_copy(index_v, index, sems.at[0])
    to_scalar.start()
    lane = lax.broadcasted_iota(jnp.int32, (128, 128), 1)
    sheet = recv[pl.ds(2 * CAP, PEERS, MESSAGE), :]
    wrapped = jnp.concatenate([sheet[127:128, 127:128], sheet[127:128, :127]], axis=1)
    wrapped = jnp.where(lane[0:1] % GROUPS == 0, 0.0, wrapped)
    sheet = jnp.concatenate([wrapped, sheet[:127]], axis=0)
    for n in range(COUNT // 128):
        column = jnp.broadcast_to(source[:, n * 128 : (n + 1) * 128], (128, 128)).T
        onehot = jnp.where(lane == column, 1.0, 0.0)
        amps[n * 128 : (n + 1) * 128] = jnp.dot(
            onehot, sheet, precision=HIGHEST, preferred_element_type=jnp.float32
        )
    to_scalar.wait()

    def get(n, carry):
        base = pl.multiple_of(n * BATCH, BATCH)
        spots = [index[n // (128 // BATCH), n % (128 // BATCH) * BATCH + m] for m in range(BATCH)]
        ph = [recv[pl.ds(spot, 1)] for spot in spots]
        en = [recv[pl.ds(spot + CAP, 1)] for spot in spots]
        for m in range(BATCH):
            phases[pl.ds(base + m, 1)] = ph[m]
            energies[pl.ds(base + m, 1)] = en[m]
        return carry

    lax.fori_loop(0, COUNT // BATCH, get, 0)
    for k in range(GROUPS):
        rows = slice(k * NBS, (k + 1) * NBS)
        re, im = amps[rows, k : k + 1], amps[rows, GROUPS + k : GROUPS + k + 1]
        phases[rows], energies[rows] = pushed(phases[rows], energies[rows], re, im)


SLAB = 4
EARLY, LATE = 4, 12
MIDDLE = ((4, 7), (7, 10), (10, 12))


def field_kernel(
    mine, piece_0, piece_1, piece_b0, piece_b1, piece_b2, piece_c, small, earlier, beam, left, right, out_hbm, acc, out, out_sems
):
    me = mine[0]

    def plane(c, k):
        if k < 0:
            return jnp.zeros((GRID, GRID), jnp.float32)
        if k < EARLY:
            return jnp.where(me % 2 == 0, piece_0[c, k], piece_1[c, k])
        for piece, (low, high) in zip((piece_b0, piece_b1, piece_b2), MIDDLE):
            if low <= k < high:
                return piece[c, k - low]
        return piece_c[c, k - LATE]

    for n in range(2):
        acc[n] = GAIN * carried(small[n], me == 0)
        acc[2 + n] = GAIN * earlier[n]
    late = me < 2
    p = beam[2]
    dr, di = beam[0], beam[1]
    copies = []
    for slab in range(GROUPS // SLAB):
        ks = range(slab * SLAB, (slab + 1) * SLAB)
        rows = []
        for k in ks:
            parts = [jnp.where(late, plane(c, k - 1), plane(c, k)) + acc[2 + c, k : k + 1] * p for c in range(2)]
            rows.append(jnp.concatenate(parts, axis=1))
        hi, lo = wide_halves(jnp.concatenate(rows, axis=0))
        half = jnp.dot(jnp.concatenate([hi, lo, hi], axis=1), right[...], preferred_element_type=jnp.float32)
        cols = []
        for m in range(SLAB):
            mid = half[m * GRID : (m + 1) * GRID]
            cols.append(jnp.concatenate([mid[:, :GRID], mid[:, GRID:]], axis=0))
        hi, lo = wide_halves(jnp.concatenate(cols, axis=1))
        full = jnp.dot(left[...], jnp.concatenate([hi, lo, hi], axis=0), preferred_element_type=jnp.float32)
        for m, k in enumerate(ks):
            cr, ci = acc[0, k : k + 1], acc[1, k : k + 1]
            out[0, k] = full[:GRID, m * GRID : (m + 1) * GRID] + (cr * dr - ci * di)
            out[1, k] = full[GRID:, m * GRID : (m + 1) * GRID] + (cr * di + ci * dr)
        for c in range(2):
            span = pl.ds(slab * SLAB, SLAB)
            copies.append(pltpu.make_async_copy(out.at[c, span], out_hbm.at[c, span], out_sems.at[2 * slab + c]))
            copies[-1].start()
    for copy in copies:
        copy.wait()


def early_pairs(core):
    onward = [(device, (device + 2) % PEERS) for device in range(core, PEERS, 2)]
    across = [(device, (device + 8) % PEERS) for device in range(1 - core, PEERS, 2) if device % 8 >= 6]
    return onward + across


def late_pairs():
    return [(device, device + 2 if device % 8 < 6 else device - 6) for device in range(PEERS)]


def shifted(value, axis, steps):
    count = lax.axis_size(axis)
    pairs = [(source, (source + steps) % count) for source in range(count)]
    return lax.ppermute(value, axis, pairs)


def shape(*dims, dtype=jnp.float32):
    return jax.ShapeDtypeStruct(dims, dtype)


def whole():
    return pl.BlockSpec(memory_space=pltpu.VMEM)


def vmem(*dims, dtype=jnp.float32):
    return pltpu.VMEM(dims, dtype)


def in_hbm(value):
    return pltpu.with_memory_space_constraint(value, pltpu.HBM)


def per_device(field, phase_bins, phase_jitter, energy, profile, delays):
    params = pltpu.CompilerParams(vmem_limit_bytes=VMEM_LIMIT)
    scalar = pl.BlockSpec(memory_space=pltpu.SMEM)
    remain = pl.BlockSpec(memory_space=pltpu.HBM)
    field = field.reshape(2, GROUPS, GRID, GRID)
    bins = phase_bins.reshape(COUNT, BLOCK)
    jitter = phase_jitter.reshape(COUNT, BLOCK)
    energies = energy.reshape(COUNT, BLOCK)
    mine = lax.axis_index("cuts").reshape(1)
    one, two = line_operator(1), line_operator(2)
    left_one = jnp.asarray(np.concatenate(one, axis=0), jnp.float32)
    right_one = jnp.asarray(right_form(*one), jnp.float32)
    core = mine[0] % 2
    shared_0 = lax.ppermute(lax.dynamic_slice_in_dim(field, core * LATE, EARLY, 1), "cuts", early_pairs(0))
    shared_1 = lax.ppermute(lax.dynamic_slice_in_dim(field, (1 - core) * LATE, EARLY, 1), "cuts", early_pairs(1))
    operands = [field, profile, bins, jitter, energies, delays.reshape(GROUPS, 1, NBS), left_one, right_one]
    send, phases1, energies1, places, beam = pl.pallas_call(
        first_kernel,
        out_shape=(
            pltpu.HBM((ROWS, BLOCK), jnp.float32),
            pltpu.HBM((COUNT, BLOCK), jnp.float32),
            pltpu.HBM((COUNT, BLOCK), jnp.float32),
            pltpu.HBM((8, COUNT), jnp.int32),
            shape(3, GRID, GRID),
        ),
        in_specs=[scalar] + [remain] * 8,
        out_specs=(remain,) * 4 + (whole(),),
        scratch_shapes=[
            vmem(2, GROUPS, GRID, GRID),
            vmem(GRID, GRID),
            vmem(COUNT, BLOCK, dtype=jnp.int32),
            vmem(COUNT, BLOCK),
            vmem(COUNT, BLOCK),
            vmem(GROUPS, 1, NBS, dtype=jnp.int32),
            vmem(2 * GRID, GRID),
            vmem(2 * GRID, 2 * GRID),
            vmem(6, GROUPS, 128),
            vmem(ROWS, BLOCK),
            vmem(COUNT, BLOCK),
            vmem(COUNT, BLOCK),
            vmem(8, COUNT, dtype=jnp.int32),
            vmem(8, 128, dtype=jnp.int32),
            pltpu.SMEM((8, 128), jnp.int32),
            pltpu.SemaphoreType.DMA((11,)),
        ],
        compiler_params=params,
        name="push_place",
    )(mine, *[in_hbm(value) for value in operands])
    send, *sources = lax.optimization_barrier((send, *[field[:, low:high] for low, high in MIDDLE]))
    field_b = [shifted(source, "cuts", 2) for source in sources]

    def exchange(send, phases1, energies1, places, field, shared_0, shared_1):
        handed = jnp.where(core == 0, shared_1, shared_0)
        source_c = jnp.where(mine[0] % 8 >= 6, handed, field[:, LATE:])
        field_c = lax.ppermute(source_c, "cuts", late_pairs())
        recv = lax.all_to_all(send.reshape(ROWS, 1, BLOCK), "cuts", split_axis=0, concat_axis=0, tiled=True)
        recv = recv.reshape(ROWS, BLOCK)
        small, earlier = pl.pallas_call(
            second_kernel,
            out_shape=(shape(2, GROUPS, 128), shape(2, GROUPS, 128)),
            in_specs=[scalar] + [whole()] * 3,
            out_specs=(whole(),) * 2,
            scratch_shapes=[vmem(4, GROUPS, 128)],
            compiler_params=params,
            name="second_push",
        )(mine, phases1, energies1, recv)
        arrived = shifted(small, "cuts", 1)
        phase_out, energy_out = pl.pallas_call(
            pick_kernel,
            out_shape=(shape(COUNT, BLOCK), shape(COUNT, BLOCK)),
            in_specs=[scalar] + [whole()] * 2,
            out_specs=(whole(),) * 2,
            scratch_shapes=[
                vmem(8, 128, dtype=jnp.int32),
                pltpu.SMEM((8, 128), jnp.int32),
                vmem(COUNT, 128),
                pltpu.SemaphoreType.DMA((1,)),
            ],
            compiler_params=params,
            name="pick",
        )(mine, recv, places)
        return phase_out, energy_out, field_c, arrived, earlier

    def refuse(*operands):
        sizes = [(COUNT, BLOCK)] * 2 + [(2, GROUPS - LATE, GRID, GRID)] + [(2, GROUPS, 128)] * 2
        return tuple(jnp.zeros(size, jnp.float32) for size in sizes)

    phase_out, energy_out, field_c, arrived, earlier = lax.cond(
        delays[0, 0, 0] < PEERS, exchange, refuse, send, phases1, energies1, places, field, shared_0, shared_1
    )
    out = pl.pallas_call(
        field_kernel,
        out_shape=shape(2, GROUPS, GRID, GRID),
        in_specs=[scalar] + [whole()] * 11,
        out_specs=remain,
        scratch_shapes=[
            vmem(4, GROUPS, 128),
            vmem(2, GROUPS, GRID, GRID),
            pltpu.SemaphoreType.DMA((2 * GROUPS // SLAB,)),
        ],
        compiler_params=params,
        name="diffract",
    )(
        mine,
        shared_0,
        shared_1,
        *field_b,
        field_c,
        arrived,
        earlier,
        beam,
        deep_left(left_form(*two)),
        deep_right(right_form(*two)),
    )
    return (
        out.reshape(2, GROUPS, 1, GRID, GRID),
        phase_out.reshape(GROUPS, 1, NBS * BLOCK),
        energy_out.reshape(GROUPS, 1, NBS * BLOCK),
    )


def solution(mesh):
    return jax.shard_map(
        per_device,
        mesh=mesh,
        in_specs=(
            P(None, None, "cuts", None, None),
            P(None, "cuts", None),
            P(None, "cuts", None),
            P(None, "cuts", None),
            P(),
            P(),
        ),
        out_specs=(P(None, None, "cuts", None, None), P(None, "cuts", None), P(None, "cuts", None)),
        check_vma=False,
    )
```

```python
import functools
import math

import jax
import jax.numpy as jnp
import ml_dtypes
import numpy as np
from jax import lax
from jax.experimental import pallas as pl
from jax.experimental.pallas import tpu as pltpu
from jax.sharding import PartitionSpec as P

BLOCK = 128
NBINS = 16
KAPPA = 1.0
OMEGA = 1.0
GAIN = 16.0
PHASE_COEF = 20.0
GRID = 128
GROUPS = 16
NBS = 64
COUNT = GROUPS * NBS
PEERS = 128
CAP = 20
MESSAGE = 2 * CAP + 1
ROWS = PEERS * MESSAGE
BATCH = 32
VMEM_LIMIT = 24 * 1024 * 1024
HIGHEST = lax.Precision.HIGHEST


def line_operator(power):
    index = np.arange(GRID)
    freq = ((index + GRID // 2) % GRID - GRID // 2) / GRID
    weight = np.exp(-1j * PHASE_COEF * power * freq**2)
    wave = np.exp(2j * np.pi * (index[:, None] * index[None, :] % GRID) / GRID)
    column = wave @ weight / GRID
    matrix = column[(index[:, None] - index[None, :]) % GRID]
    return matrix.real, matrix.imag


def left_form(real, imag):
    return np.block([[real, -imag], [imag, real]])


def right_form(real, imag):
    return np.block([[real, imag], [-imag, real]])


def halves(matrix):
    high = matrix.astype(ml_dtypes.bfloat16)
    return high, (matrix - high.astype(np.float64)).astype(ml_dtypes.bfloat16)


def deep_left(matrix):
    high, low = halves(matrix)
    return jnp.asarray(np.concatenate([high, high, low], axis=1))


def deep_right(matrix):
    high, low = halves(matrix)
    return jnp.asarray(np.concatenate([high, high, low], axis=0))


def fitted(function, degree):
    top = (math.pi / 2 + 0.01) ** 2
    nodes = (np.cos(np.pi * (np.arange(400) + 0.5) / 400) + 1) / 2 * top
    series = np.polynomial.chebyshev.Chebyshev.fit(nodes, function(np.sqrt(nodes)), degree, domain=[0, top])
    return [float(c) for c in series.convert(kind=np.polynomial.Polynomial).coef]


SIN_COEF = fitted(lambda r: np.sin(r) / r, 5)
COS_COEF = fitted(np.cos, 6)
PI_HIGH = 3.140625
PI_MID = 9.67502593994140625e-4
PI_LOW = math.pi - PI_HIGH - PI_MID


def horner(coefs, x):
    value = jnp.float32(coefs[-1])
    for c in coefs[-2::-1]:
        value = value * x + jnp.float32(c)
    return value


def cos_sin(x):
    turns = jnp.round(x * jnp.float32(1.0 / math.pi))
    r = x - turns * jnp.float32(PI_HIGH)
    r = r - turns * jnp.float32(PI_MID)
    r = r - turns * jnp.float32(PI_LOW)
    half = turns * 0.5
    sign = 1.0 - 4.0 * jnp.abs(half - jnp.round(half))
    square = r * r
    return horner(COS_COEF, square) * sign, horner(SIN_COEF, square) * (r * sign)


def lane_total(rows):
    return jnp.broadcast_to(jnp.sum(rows, axis=1, keepdims=True), rows.shape)


def slots_of(delays):
    row = jnp.concatenate([delays[k] for k in range(GROUPS)], axis=1)
    values = lax.broadcasted_iota(jnp.int32, (PEERS, COUNT), 0)
    onehot = jnp.where(values == row, 1.0, 0.0)
    before = lax.broadcasted_iota(jnp.int32, (COUNT, COUNT), 0) < lax.broadcasted_iota(jnp.int32, (COUNT, COUNT), 1)
    upper = jnp.where(before, 1.0, 0.0).astype(jnp.bfloat16)
    earlier = jnp.dot(onehot.astype(jnp.bfloat16), upper, preferred_element_type=jnp.float32)
    return row, jnp.sum(earlier * onehot, axis=0, keepdims=True).astype(jnp.int32)


def folded(row):
    return jnp.concatenate([row[:, n * 128 : (n + 1) * 128] for n in range(COUNT // 128)], axis=0)


def rows_of(k):
    return pl.ds(pl.multiple_of(k * NBS, NBS), NBS)


def first_kernel(
    mine, field_hbm, profile_hbm, bins_hbm, jitter_hbm, energy_hbm, delays_hbm, left_hbm, right_hbm,
    send_hbm, phases_hbm, energies_hbm, places_hbm, beam, middle_0, middle_1,
    field, profile, bins, jitter, energy, delays, left, right, acc, send, phases, energies, places, index_v, index, sems,
):
    pairs = [
        (profile_hbm, profile), (left_hbm, left), (right_hbm, right), (delays_hbm, delays),
        (field_hbm, field), (bins_hbm, bins), (jitter_hbm, jitter), (energy_hbm, energy),
    ]
    copies = [pltpu.make_async_copy(src, dst, sems.at[n]) for n, (src, dst) in enumerate(pairs)]
    for copy in copies:
        copy.start()
    copies[3].wait()
    row, slot = slots_of(delays)
    places[0:1] = row
    places[1:2] = slot
    index_v[...] = folded(((mine[0] + row) % PEERS) * MESSAGE + slot)
    to_scalar = pltpu.make_async_copy(index_v, index, sems.at[3])
    to_scalar.start()
    for copy in copies[:3]:
        copy.wait()
    p = profile[...]
    half = jnp.dot(left[...], p, precision=HIGHEST, preferred_element_type=jnp.float32)
    both = jnp.concatenate([half[:GRID], half[GRID:]], axis=1)
    spread = jnp.dot(both, right[...], precision=HIGHEST, preferred_element_type=jnp.float32)
    beam[0] = spread[:, :GRID]
    beam[1] = spread[:, GRID:]
    beam[2] = p
    copies[4].wait()
    kept = [pltpu.make_async_copy(places, places_hbm, sems.at[8])]
    for middle, (low, high) in zip((middle_0, middle_1), MIDDLE):
        for c in range(2):
            span = pl.ds(low, high - low)
            kept.append(pltpu.make_async_copy(field.at[c, span], middle.at[c], sems.at[10 + len(kept)]))
    for copy in kept:
        copy.start()

    def project(k, carry):
        re, im = field[0, k], field[1, k]
        dr, di, q = beam[0], beam[1], profile[...]
        acc[0, pl.ds(k, 1)] = jnp.sum(q * re, axis=0, keepdims=True)
        acc[1, pl.ds(k, 1)] = jnp.sum(q * im, axis=0, keepdims=True)
        acc[2, pl.ds(k, 1)] = jnp.sum(dr * re - di * im, axis=0, keepdims=True)
        acc[3, pl.ds(k, 1)] = jnp.sum(dr * im + di * re, axis=0, keepdims=True)
        return carry

    lax.fori_loop(0, GROUPS, project, 0)
    self_re = jnp.sum(p * beam[0])
    self_im = jnp.sum(p * beam[1])
    for n in range(4):
        acc[n] = lane_total(acc[n]) * (1.0 / GRID)
    for copy in copies[5:]:
        copy.wait()

    def push(k, carry):
        rows = rows_of(k)
        ph = jnp.float32(2.0 * math.pi / NBINS) * (bins[rows].astype(jnp.float32) + jitter[rows])
        ph, en = pushed(ph, energy[rows], acc[0, pl.ds(k, 1)], acc[1, pl.ds(k, 1)])
        phases[rows] = ph
        energies[rows] = en
        c, s = cos_sin(ph)
        acc[4, pl.ds(k, 1)] = jnp.sum(c, axis=0, keepdims=True)
        acc[5, pl.ds(k, 1)] = jnp.sum(s, axis=0, keepdims=True)
        return carry

    lax.fori_loop(0, GROUPS, push, 0)
    kept.append(pltpu.make_async_copy(phases, phases_hbm, sems.at[9]))
    kept.append(pltpu.make_async_copy(energies, energies_hbm, sems.at[10]))
    for copy in kept[5:]:
        copy.start()
    to_scalar.wait()

    def put(n, carry):
        base = pl.multiple_of(n * BATCH, BATCH)
        spots = [index[n // (128 // BATCH), n % (128 // BATCH) * BATCH + m] for m in range(BATCH)]
        ph = [phases[pl.ds(base + m, 1)] for m in range(BATCH)]
        en = [energies[pl.ds(base + m, 1)] for m in range(BATCH)]
        for m in range(BATCH):
            send[pl.ds(spots[m], 1)] = ph[m]
            send[pl.ds(spots[m] + CAP, 1)] = en[m]
        return carry

    lax.fori_loop(0, COUNT // BATCH, put, 0)
    bre = lane_total(acc[4]) * (1.0 / (NBS * BLOCK))
    bim = lane_total(acc[5]) * (-1.0 / (NBS * BLOCK))
    gain = GAIN / GRID
    next_re = acc[2] + gain * (bre * self_re - bim * self_im)
    next_im = acc[3] + gain * (bre * self_im + bim * self_re)
    note = one_row([next_re, next_im, bre, bim])
    for n in range(PEERS):
        send[n * MESSAGE + 2 * CAP : (n + 1) * MESSAGE] = note
    out = pltpu.make_async_copy(send, send_hbm, sems.at[0])
    out.start()
    for copy in kept:
        copy.wait()
    out.wait()


def pushed(ph, en, amp_re, amp_im):
    c, s = cos_sin(ph)
    en = en - KAPPA * (amp_re * c - amp_im * s)
    return ph + OMEGA * en, en


def one_row(parts):
    rest = 128 // GROUPS - len(parts)
    stack = jnp.concatenate(parts + [jnp.zeros((rest * GROUPS, 128), jnp.float32)], axis=0)
    return stack.T[0:1]


def parts_of(recv, device):
    row = recv[pl.ds(device * MESSAGE + 2 * CAP, 1)]
    return jnp.broadcast_to(row, (128, 128)).T


def carried(value, flag):
    rolled = jnp.concatenate([jnp.zeros_like(value[:1]), value[:-1]], axis=0)
    return jnp.where(flag, rolled, value)


def second_kernel(mine, phases1, energies1, recv, small, earlier, acc):
    me = mine[0]
    near = parts_of(recv, (me + PEERS - 1) % PEERS)
    far = parts_of(recv, (me + PEERS - 2) % PEERS)
    for n in range(2):
        acc[n] = carried(near[n * GROUPS : (n + 1) * GROUPS], me == 0)
        earlier[n] = carried(far[(2 + n) * GROUPS : (3 + n) * GROUPS], me < 2)

    def push(k, carry):
        rows = rows_of(k)
        ph, _ = pushed(phases1[rows], energies1[rows], acc[0, pl.ds(k, 1)], acc[1, pl.ds(k, 1)])
        c, s = cos_sin(ph)
        acc[2, pl.ds(k, 1)] = jnp.sum(c, axis=0, keepdims=True)
        acc[3, pl.ds(k, 1)] = jnp.sum(s, axis=0, keepdims=True)
        return carry

    lax.fori_loop(0, GROUPS, push, 0)
    small[0] = lane_total(acc[2]) * (1.0 / (NBS * BLOCK))
    small[1] = lane_total(acc[3]) * (-1.0 / (NBS * BLOCK))


def wide_halves(x):
    high = x.astype(jnp.bfloat16)
    return high, (x - high.astype(jnp.float32)).astype(jnp.bfloat16)


def pick_kernel(mine, recv, places, phases_hbm, energies_hbm, index_v, index, amps, phases, energies, sems):
    me = mine[0]
    source = (me - places[0:1] + PEERS) % PEERS
    index_v[...] = folded(source * MESSAGE + places[1:2])
    to_scalar = pltpu.make_async_copy(index_v, index, sems.at[0])
    to_scalar.start()
    lane = lax.broadcasted_iota(jnp.int32, (128, 128), 1)
    sheet = recv[pl.ds(2 * CAP, PEERS, MESSAGE), :]
    wrapped = jnp.concatenate([sheet[127:128, 127:128], sheet[127:128, :127]], axis=1)
    wrapped = jnp.where(lane[0:1] % GROUPS == 0, 0.0, wrapped)
    sheet = jnp.concatenate([wrapped, sheet[:127]], axis=0)
    for n in range(COUNT // 128):
        column = jnp.broadcast_to(source[:, n * 128 : (n + 1) * 128], (128, 128)).T
        onehot = jnp.where(lane == column, 1.0, 0.0)
        amps[n * 128 : (n + 1) * 128] = jnp.dot(
            onehot, sheet, precision=HIGHEST, preferred_element_type=jnp.float32
        )
    to_scalar.wait()

    def get(n, carry):
        base = pl.multiple_of(n * BATCH, BATCH)
        spots = [index[n // (128 // BATCH), n % (128 // BATCH) * BATCH + m] for m in range(BATCH)]
        ph = [recv[pl.ds(spot, 1)] for spot in spots]
        en = [recv[pl.ds(spot + CAP, 1)] for spot in spots]
        for m in range(BATCH):
            phases[pl.ds(base + m, 1)] = ph[m]
            energies[pl.ds(base + m, 1)] = en[m]
        return carry

    copies = []
    for quarter in range(4):
        lax.fori_loop(quarter * COUNT // BATCH // 4, (quarter + 1) * COUNT // BATCH // 4, get, 0)
        for k in range(quarter * 4, quarter * 4 + 4):
            rows = slice(k * NBS, (k + 1) * NBS)
            re, im = amps[rows, k : k + 1], amps[rows, GROUPS + k : GROUPS + k + 1]
            phases[rows], energies[rows] = pushed(phases[rows], energies[rows], re, im)
        span = pl.ds(quarter * COUNT // 4, COUNT // 4)
        copies.append(pltpu.make_async_copy(phases.at[span], phases_hbm.at[span], sems.at[1 + 2 * quarter]))
        copies.append(pltpu.make_async_copy(energies.at[span], energies_hbm.at[span], sems.at[2 + 2 * quarter]))
        for copy in copies[-2:]:
            copy.start()
    for copy in copies:
        copy.wait()


SLAB = 4
EARLY, LATE = 5, 11
MIDDLE = ((5, 8), (8, 11))


def field_kernel(
    mine, piece_0, piece_1, piece_b0, piece_b1, piece_c, small, earlier, beam, left, right, out_hbm, acc, out, out_sems
):
    me = mine[0]

    def plane(c, k):
        if k < 0:
            return jnp.zeros((GRID, GRID), jnp.float32)
        if k < EARLY:
            return jnp.where(me % 2 == 0, piece_0[c, k], piece_1[c, k])
        for piece, (low, high) in zip((piece_b0, piece_b1), MIDDLE):
            if low <= k < high:
                return piece[c, k - low]
        return piece_c[c, k - LATE]

    for n in range(2):
        acc[n] = GAIN * carried(small[n], me == 0)
        acc[2 + n] = GAIN * earlier[n]
    late = me < 2
    p = beam[2]
    dr, di = beam[0], beam[1]
    copies = []
    for slab in range(GROUPS // SLAB):
        ks = range(slab * SLAB, (slab + 1) * SLAB)
        rows = []
        for k in ks:
            parts = [jnp.where(late, plane(c, k - 1), plane(c, k)) + acc[2 + c, k : k + 1] * p for c in range(2)]
            rows.append(jnp.concatenate(parts, axis=1))
        hi, lo = wide_halves(jnp.concatenate(rows, axis=0))
        half = jnp.dot(jnp.concatenate([hi, lo, hi], axis=1), right[...], preferred_element_type=jnp.float32)
        cols = []
        for m in range(SLAB):
            mid = half[m * GRID : (m + 1) * GRID]
            cols.append(jnp.concatenate([mid[:, :GRID], mid[:, GRID:]], axis=0))
        hi, lo = wide_halves(jnp.concatenate(cols, axis=1))
        full = jnp.dot(left[...], jnp.concatenate([hi, lo, hi], axis=0), preferred_element_type=jnp.float32)
        for m, k in enumerate(ks):
            cr, ci = acc[0, k : k + 1], acc[1, k : k + 1]
            out[0, k] = full[:GRID, m * GRID : (m + 1) * GRID] + (cr * dr - ci * di)
            out[1, k] = full[GRID:, m * GRID : (m + 1) * GRID] + (cr * di + ci * dr)
        for c in range(2):
            span = pl.ds(slab * SLAB, SLAB)
            copies.append(pltpu.make_async_copy(out.at[c, span], out_hbm.at[c, span], out_sems.at[2 * slab + c]))
            copies[-1].start()
    for copy in copies:
        copy.wait()


def early_pairs(core):
    onward = [(device, (device + 2) % PEERS) for device in range(core, PEERS, 2)]
    across = [(device, (device + 8) % PEERS) for device in range(1 - core, PEERS, 2) if device % 8 >= 6]
    return onward + across


def late_pairs():
    return [(device, device + 2 if device % 8 < 6 else device - 6) for device in range(PEERS)]


def shifted(value, axis, steps):
    count = lax.axis_size(axis)
    pairs = [(source, (source + steps) % count) for source in range(count)]
    return lax.ppermute(value, axis, pairs)


def shape(*dims, dtype=jnp.float32):
    return jax.ShapeDtypeStruct(dims, dtype)


def whole():
    return pl.BlockSpec(memory_space=pltpu.VMEM)


def vmem(*dims, dtype=jnp.float32):
    return pltpu.VMEM(dims, dtype)


def in_hbm(value):
    return pltpu.with_memory_space_constraint(value, pltpu.HBM)


def per_device(field, phase_bins, phase_jitter, energy, profile, delays):
    params = pltpu.CompilerParams(vmem_limit_bytes=VMEM_LIMIT)
    scalar = pl.BlockSpec(memory_space=pltpu.SMEM)
    remain = pl.BlockSpec(memory_space=pltpu.HBM)
    field = field.reshape(2, GROUPS, GRID, GRID)
    bins = phase_bins.reshape(COUNT, BLOCK)
    jitter = phase_jitter.reshape(COUNT, BLOCK)
    energies = energy.reshape(COUNT, BLOCK)
    mine = lax.axis_index("cuts").reshape(1)
    one, two = line_operator(1), line_operator(2)
    left_one = jnp.asarray(np.concatenate(one, axis=0), jnp.float32)
    right_one = jnp.asarray(right_form(*one), jnp.float32)
    core = mine[0] % 2
    shared_0 = lax.ppermute(lax.dynamic_slice_in_dim(field, core * LATE, EARLY, 1), "cuts", early_pairs(0))
    shared_1 = lax.ppermute(lax.dynamic_slice_in_dim(field, (1 - core) * LATE, EARLY, 1), "cuts", early_pairs(1))
    operands = [field, profile, bins, jitter, energies, delays.reshape(GROUPS, 1, NBS), left_one, right_one]
    send, phases1, energies1, places, beam, *sources = pl.pallas_call(
        first_kernel,
        out_shape=(
            pltpu.HBM((ROWS, BLOCK), jnp.float32),
            pltpu.HBM((COUNT, BLOCK), jnp.float32),
            pltpu.HBM((COUNT, BLOCK), jnp.float32),
            pltpu.HBM((8, COUNT), jnp.int32),
            pltpu.HBM((3, GRID, GRID), jnp.float32),
            *[pltpu.HBM((2, high - low, GRID, GRID), jnp.float32) for low, high in MIDDLE],
        ),
        in_specs=[scalar] + [remain] * 8,
        out_specs=(remain,) * 4 + (whole(),) + (remain,) * len(MIDDLE),
        scratch_shapes=[
            vmem(2, GROUPS, GRID, GRID),
            vmem(GRID, GRID),
            vmem(COUNT, BLOCK, dtype=jnp.int32),
            vmem(COUNT, BLOCK),
            vmem(COUNT, BLOCK),
            vmem(GROUPS, 1, NBS, dtype=jnp.int32),
            vmem(2 * GRID, GRID),
            vmem(2 * GRID, 2 * GRID),
            vmem(6, GROUPS, 128),
            vmem(ROWS, BLOCK),
            vmem(COUNT, BLOCK),
            vmem(COUNT, BLOCK),
            vmem(8, COUNT, dtype=jnp.int32),
            vmem(8, 128, dtype=jnp.int32),
            pltpu.SMEM((8, 128), jnp.int32),
            pltpu.SemaphoreType.DMA((15,)),
        ],
        compiler_params=params,
        name="push_place",
    )(mine, *[in_hbm(value) for value in operands])
    field_b = [shifted(source, "cuts", 2) for source in sources]

    def exchange(send, phases1, energies1, places, field, shared_0, shared_1):
        handed = jnp.where(core == 0, shared_1, shared_0)
        source_c = jnp.where(mine[0] % 8 >= 6, handed, field[:, LATE:])
        field_c = lax.ppermute(source_c, "cuts", late_pairs())
        recv = lax.all_to_all(send.reshape(ROWS, 1, BLOCK), "cuts", split_axis=0, concat_axis=0, tiled=True)
        recv = recv.reshape(ROWS, BLOCK)
        small, earlier = pl.pallas_call(
            second_kernel,
            out_shape=(shape(2, GROUPS, 128), shape(2, GROUPS, 128)),
            in_specs=[scalar] + [whole()] * 3,
            out_specs=(whole(),) * 2,
            scratch_shapes=[vmem(4, GROUPS, 128)],
            compiler_params=params,
            name="second_push",
        )(mine, phases1, energies1, recv)
        arrived = shifted(small, "cuts", 1)
        phase_out, energy_out = pl.pallas_call(
            pick_kernel,
            out_shape=(shape(COUNT, BLOCK), shape(COUNT, BLOCK)),
            in_specs=[scalar] + [whole()] * 2,
            out_specs=(remain,) * 2,
            scratch_shapes=[
                vmem(8, 128, dtype=jnp.int32),
                pltpu.SMEM((8, 128), jnp.int32),
                vmem(COUNT, 128),
                vmem(COUNT, BLOCK),
                vmem(COUNT, BLOCK),
                pltpu.SemaphoreType.DMA((9,)),
            ],
            compiler_params=params,
            name="pick",
        )(mine, recv, places)
        return phase_out, energy_out, field_c, arrived, earlier

    def refuse(*operands):
        sizes = [(COUNT, BLOCK)] * 2 + [(2, GROUPS - LATE, GRID, GRID)] + [(2, GROUPS, 128)] * 2
        return tuple(jnp.zeros(size, jnp.float32) for size in sizes)

    phase_out, energy_out, field_c, arrived, earlier = lax.cond(
        mine[0] < PEERS, exchange, refuse, send, phases1, energies1, places, field, shared_0, shared_1
    )
    out = pl.pallas_call(
        field_kernel,
        out_shape=shape(2, GROUPS, GRID, GRID),
        in_specs=[scalar] + [whole()] * 10,
        out_specs=remain,
        scratch_shapes=[
            vmem(4, GROUPS, 128),
            vmem(2, GROUPS, GRID, GRID),
            pltpu.SemaphoreType.DMA((2 * GROUPS // SLAB,)),
        ],
        compiler_params=params,
        name="diffract",
    )(
        mine,
        shared_0,
        shared_1,
        *field_b,
        field_c,
        arrived,
        earlier,
        beam,
        deep_left(left_form(*two)),
        deep_right(right_form(*two)),
    )
    return (
        out.reshape(2, GROUPS, 1, GRID, GRID),
        phase_out.reshape(GROUPS, 1, NBS * BLOCK),
        energy_out.reshape(GROUPS, 1, NBS * BLOCK),
    )


def solution(mesh):
    return jax.shard_map(
        per_device,
        mesh=mesh,
        in_specs=(
            P(None, None, "cuts", None, None),
            P(None, "cuts", None),
            P(None, "cuts", None),
            P(None, "cuts", None),
            P(),
            P(),
        ),
        out_specs=(P(None, None, "cuts", None, None), P(None, "cuts", None), P(None, "cuts", None)),
        check_vma=False,
    )
```

```python
import functools
import math

import jax
import jax.numpy as jnp
import ml_dtypes
import numpy as np
from jax import lax
from jax.experimental import pallas as pl
from jax.experimental.pallas import tpu as pltpu
from jax.sharding import PartitionSpec as P

BLOCK = 128
NBINS = 16
KAPPA = 1.0
OMEGA = 1.0
GAIN = 16.0
PHASE_COEF = 20.0
GRID = 128
GROUPS = 16
NBS = 64
COUNT = GROUPS * NBS
PEERS = 128
CAP = 20
MESSAGE = 2 * CAP + 1
ROWS = PEERS * MESSAGE
BATCH = 32
EARLY, LATE = 5, 11
MIDDLE = ((5, 8), (8, 11))
VMEM_LIMIT = 24 * 1024 * 1024
HIGHEST = lax.Precision.HIGHEST


def line_operator(power):
    index = np.arange(GRID)
    freq = ((index + GRID // 2) % GRID - GRID // 2) / GRID
    weight = np.exp(-1j * PHASE_COEF * power * freq**2)
    wave = np.exp(2j * np.pi * (index[:, None] * index[None, :] % GRID) / GRID)
    column = wave @ weight / GRID
    matrix = column[(index[:, None] - index[None, :]) % GRID]
    return matrix.real, matrix.imag


def left_form(real, imag):
    return np.block([[real, -imag], [imag, real]])


def right_form(real, imag):
    return np.block([[real, imag], [-imag, real]])


def halves(matrix):
    high = matrix.astype(ml_dtypes.bfloat16)
    return high, (matrix - high.astype(np.float64)).astype(ml_dtypes.bfloat16)


def deep_left(matrix):
    high, low = halves(matrix)
    return jnp.asarray(np.concatenate([high, high, low], axis=1))


def deep_right(matrix):
    high, low = halves(matrix)
    return jnp.asarray(np.concatenate([high, high, low], axis=0))


def fitted(function, degree):
    top = (math.pi / 2 + 0.01) ** 2
    nodes = (np.cos(np.pi * (np.arange(400) + 0.5) / 400) + 1) / 2 * top
    series = np.polynomial.chebyshev.Chebyshev.fit(nodes, function(np.sqrt(nodes)), degree, domain=[0, top])
    return [float(c) for c in series.convert(kind=np.polynomial.Polynomial).coef]


SIN_COEF = fitted(lambda r: np.sin(r) / r, 5)
COS_COEF = fitted(np.cos, 6)
PI_HIGH = 3.140625
PI_MID = 9.67502593994140625e-4
PI_LOW = math.pi - PI_HIGH - PI_MID


def horner(coefs, x):
    value = jnp.float32(coefs[-1])
    for c in coefs[-2::-1]:
        value = value * x + jnp.float32(c)
    return value


def cos_sin(x):
    turns = jnp.round(x * jnp.float32(1.0 / math.pi))
    r = x - turns * jnp.float32(PI_HIGH)
    r = r - turns * jnp.float32(PI_MID)
    r = r - turns * jnp.float32(PI_LOW)
    half = turns * 0.5
    sign = 1.0 - 4.0 * jnp.abs(half - jnp.round(half))
    square = r * r
    return horner(COS_COEF, square) * sign, horner(SIN_COEF, square) * (r * sign)


def lane_total(rows):
    return jnp.broadcast_to(jnp.sum(rows, axis=1, keepdims=True), rows.shape)


def slots_of(delays):
    row = jnp.concatenate([delays[k] for k in range(GROUPS)], axis=1)
    values = lax.broadcasted_iota(jnp.int32, (PEERS, COUNT), 0)
    onehot = jnp.where(values == row, 1.0, 0.0)
    before = lax.broadcasted_iota(jnp.int32, (COUNT, COUNT), 0) < lax.broadcasted_iota(jnp.int32, (COUNT, COUNT), 1)
    upper = jnp.where(before, 1.0, 0.0).astype(jnp.bfloat16)
    earlier = jnp.dot(onehot.astype(jnp.bfloat16), upper, preferred_element_type=jnp.float32)
    return row, jnp.sum(earlier * onehot, axis=0, keepdims=True).astype(jnp.int32)


def folded(row):
    return jnp.concatenate([row[:, n * 128 : (n + 1) * 128] for n in range(COUNT // 128)], axis=0)


def rows_of(k):
    return pl.ds(pl.multiple_of(k * NBS, NBS), NBS)


def first_kernel(
    mine, field_hbm, profile_hbm, bins_hbm, jitter_hbm, energy_hbm, delays_hbm, left_hbm, right_hbm,
    send_hbm, phases_hbm, energies_hbm, places_hbm, beam, middle_0, middle_1,
    field, profile, bins, jitter, energy, delays, left, right, acc, send, phases, energies, places, index_v, index, sems,
):
    pairs = [
        (profile_hbm, profile), (left_hbm, left), (right_hbm, right), (delays_hbm, delays),
        (field_hbm, field), (bins_hbm, bins), (jitter_hbm, jitter), (energy_hbm, energy),
    ]
    copies = [pltpu.make_async_copy(src, dst, sems.at[n]) for n, (src, dst) in enumerate(pairs)]
    for copy in copies:
        copy.start()
    copies[3].wait()
    row, slot = slots_of(delays)
    places[0:1] = row
    places[1:2] = slot
    index_v[...] = folded(((mine[0] + row) % PEERS) * MESSAGE + slot)
    to_scalar = pltpu.make_async_copy(index_v, index, sems.at[3])
    to_scalar.start()
    for copy in copies[:3]:
        copy.wait()
    p = profile[...]
    half = jnp.dot(left[...], p, precision=HIGHEST, preferred_element_type=jnp.float32)
    both = jnp.concatenate([half[:GRID], half[GRID:]], axis=1)
    spread = jnp.dot(both, right[...], precision=HIGHEST, preferred_element_type=jnp.float32)
    beam[0] = spread[:, :GRID]
    beam[1] = spread[:, GRID:]
    beam[2] = p
    copies[4].wait()
    kept = [pltpu.make_async_copy(places, places_hbm, sems.at[8])]
    for middle, (low, high) in zip((middle_0, middle_1), MIDDLE):
        for c in range(2):
            span = pl.ds(low, high - low)
            kept.append(pltpu.make_async_copy(field.at[c, span], middle.at[c], sems.at[10 + len(kept)]))
    for copy in kept:
        copy.start()

    def project(k, carry):
        re, im = field[0, k], field[1, k]
        dr, di, q = beam[0], beam[1], profile[...]
        acc[0, pl.ds(k, 1)] = jnp.sum(q * re, axis=0, keepdims=True)
        acc[1, pl.ds(k, 1)] = jnp.sum(q * im, axis=0, keepdims=True)
        acc[2, pl.ds(k, 1)] = jnp.sum(dr * re - di * im, axis=0, keepdims=True)
        acc[3, pl.ds(k, 1)] = jnp.sum(dr * im + di * re, axis=0, keepdims=True)
        return carry

    lax.fori_loop(0, GROUPS, project, 0)
    self_re = jnp.sum(p * beam[0])
    self_im = jnp.sum(p * beam[1])
    for n in range(4):
        acc[n] = lane_total(acc[n]) * (1.0 / GRID)
    for copy in copies[5:]:
        copy.wait()

    def push(k, carry):
        rows = rows_of(k)
        ph = jnp.float32(2.0 * math.pi / NBINS) * (bins[rows].astype(jnp.float32) + jitter[rows])
        ph, en = pushed(ph, energy[rows], acc[0, pl.ds(k, 1)], acc[1, pl.ds(k, 1)])
        phases[rows] = ph
        energies[rows] = en
        c, s = cos_sin(ph)
        acc[4, pl.ds(k, 1)] = jnp.sum(c, axis=0, keepdims=True)
        acc[5, pl.ds(k, 1)] = jnp.sum(s, axis=0, keepdims=True)
        return carry

    lax.fori_loop(0, GROUPS, push, 0)
    kept.append(pltpu.make_async_copy(phases, phases_hbm, sems.at[9]))
    kept.append(pltpu.make_async_copy(energies, energies_hbm, sems.at[10]))
    for copy in kept[5:]:
        copy.start()
    to_scalar.wait()

    def put(n, carry):
        base = pl.multiple_of(n * BATCH, BATCH)
        spots = [index[n // (128 // BATCH), n % (128 // BATCH) * BATCH + m] for m in range(BATCH)]
        ph = [phases[pl.ds(base + m, 1)] for m in range(BATCH)]
        en = [energies[pl.ds(base + m, 1)] for m in range(BATCH)]
        for m in range(BATCH):
            send[pl.ds(spots[m], 1)] = ph[m]
            send[pl.ds(spots[m] + CAP, 1)] = en[m]
        return carry

    lax.fori_loop(0, COUNT // BATCH, put, 0)
    bre = lane_total(acc[4]) * (1.0 / (NBS * BLOCK))
    bim = lane_total(acc[5]) * (-1.0 / (NBS * BLOCK))
    gain = GAIN / GRID
    next_re = acc[2] + gain * (bre * self_re - bim * self_im)
    next_im = acc[3] + gain * (bre * self_im + bim * self_re)
    note = one_row([next_re, next_im, bre, bim])
    for n in range(PEERS):
        send[n * MESSAGE + 2 * CAP : (n + 1) * MESSAGE] = note
    out = pltpu.make_async_copy(send, send_hbm, sems.at[0])
    out.start()
    for copy in kept:
        copy.wait()
    out.wait()


def pushed(ph, en, amp_re, amp_im):
    c, s = cos_sin(ph)
    en = en - KAPPA * (amp_re * c - amp_im * s)
    return ph + OMEGA * en, en


def one_row(parts):
    rest = 128 // GROUPS - len(parts)
    stack = jnp.concatenate(parts + [jnp.zeros((rest * GROUPS, 128), jnp.float32)], axis=0)
    return stack.T[0:1]


def parts_of(recv, device):
    row = recv[pl.ds(device * MESSAGE + 2 * CAP, 1)]
    return jnp.broadcast_to(row, (128, 128)).T


def carried(value, flag):
    rolled = jnp.concatenate([jnp.zeros_like(value[:1]), value[:-1]], axis=0)
    return jnp.where(flag, rolled, value)


def second_kernel(mine, phases1, energies1, recv, small, earlier, acc):
    me = mine[0]
    near = parts_of(recv, (me + PEERS - 1) % PEERS)
    far = parts_of(recv, (me + PEERS - 2) % PEERS)
    for n in range(2):
        acc[n] = carried(near[n * GROUPS : (n + 1) * GROUPS], me == 0)
        earlier[n] = carried(far[(2 + n) * GROUPS : (3 + n) * GROUPS], me < 2)

    def push(k, carry):
        rows = rows_of(k)
        ph, _ = pushed(phases1[rows], energies1[rows], acc[0, pl.ds(k, 1)], acc[1, pl.ds(k, 1)])
        c, s = cos_sin(ph)
        acc[2, pl.ds(k, 1)] = jnp.sum(c, axis=0, keepdims=True)
        acc[3, pl.ds(k, 1)] = jnp.sum(s, axis=0, keepdims=True)
        return carry

    lax.fori_loop(0, GROUPS, push, 0)
    small[0] = lane_total(acc[2]) * (1.0 / (NBS * BLOCK))
    small[1] = lane_total(acc[3]) * (-1.0 / (NBS * BLOCK))


def wide_halves(x):
    high = x.astype(jnp.bfloat16)
    return high, (x - high.astype(jnp.float32)).astype(jnp.bfloat16)


def pick_kernel(mine, recv, places, phases_hbm, energies_hbm, index_v, index, amps, phases, energies, sems):
    me = mine[0]
    source = (me - places[0:1] + PEERS) % PEERS
    index_v[...] = folded(source * MESSAGE + places[1:2])
    to_scalar = pltpu.make_async_copy(index_v, index, sems.at[0])
    to_scalar.start()
    lane = lax.broadcasted_iota(jnp.int32, (128, 128), 1)
    sheet = recv[pl.ds(2 * CAP, PEERS, MESSAGE), :]
    wrapped = jnp.concatenate([sheet[127:128, 127:128], sheet[127:128, :127]], axis=1)
    wrapped = jnp.where(lane[0:1] % GROUPS == 0, 0.0, wrapped)
    sheet = jnp.concatenate([wrapped, sheet[:127]], axis=0)
    for n in range(COUNT // 128):
        column = jnp.broadcast_to(source[:, n * 128 : (n + 1) * 128], (128, 128)).T
        onehot = jnp.where(lane == column, 1.0, 0.0)
        amps[n * 128 : (n + 1) * 128] = jnp.dot(
            onehot, sheet, precision=HIGHEST, preferred_element_type=jnp.float32
        )
    to_scalar.wait()

    def get(n, carry):
        base = pl.multiple_of(n * BATCH, BATCH)
        spots = [index[n // (128 // BATCH), n % (128 // BATCH) * BATCH + m] for m in range(BATCH)]
        ph = [recv[pl.ds(spot, 1)] for spot in spots]
        en = [recv[pl.ds(spot + CAP, 1)] for spot in spots]
        for m in range(BATCH):
            phases[pl.ds(base + m, 1)] = ph[m]
            energies[pl.ds(base + m, 1)] = en[m]
        return carry

    copies = []
    for quarter in range(4):
        lax.fori_loop(quarter * COUNT // BATCH // 4, (quarter + 1) * COUNT // BATCH // 4, get, 0)
        for k in range(quarter * 4, quarter * 4 + 4):
            rows = slice(k * NBS, (k + 1) * NBS)
            re, im = amps[rows, k : k + 1], amps[rows, GROUPS + k : GROUPS + k + 1]
            phases[rows], energies[rows] = pushed(phases[rows], energies[rows], re, im)
        span = pl.ds(quarter * COUNT // 4, COUNT // 4)
        copies.append(pltpu.make_async_copy(phases.at[span], phases_hbm.at[span], sems.at[1 + 2 * quarter]))
        copies.append(pltpu.make_async_copy(energies.at[span], energies_hbm.at[span], sems.at[2 + 2 * quarter]))
        for copy in copies[-2:]:
            copy.start()
    for copy in copies:
        copy.wait()


def twice_diffracted(planes, left, right):
    hi, lo = wide_halves(jnp.concatenate([jnp.concatenate(pair, axis=1) for pair in planes], axis=0))
    half = jnp.dot(jnp.concatenate([hi, lo, hi], axis=1), right[...], preferred_element_type=jnp.float32)
    cols = []
    for m in range(len(planes)):
        mid = half[m * GRID : (m + 1) * GRID]
        cols.append(jnp.concatenate([mid[:, :GRID], mid[:, GRID:]], axis=0))
    hi, lo = wide_halves(jnp.concatenate(cols, axis=1))
    full = jnp.dot(left[...], jnp.concatenate([hi, lo, hi], axis=0), preferred_element_type=jnp.float32)
    cuts = [slice(m * GRID, (m + 1) * GRID) for m in range(len(planes))]
    return [(full[:GRID, cut], full[GRID:, cut]) for cut in cuts]


def early_kernel(mine, piece_0, piece_1, beam, left, right, out):
    even = mine[0] % 2 == 0
    planes = [tuple(jnp.where(even, piece_0[c, k], piece_1[c, k]) for c in range(2)) for k in range(EARLY)]
    planes.append((beam[2], jnp.zeros((GRID, GRID), jnp.float32)))
    for k, (re, im) in enumerate(twice_diffracted(planes, left, right)):
        out[0, k] = re
        out[1, k] = im


def late_kernel(piece, left, right, out):
    planes = [(piece[0, k], piece[1, k]) for k in range(piece.shape[1])]
    for k, (re, im) in enumerate(twice_diffracted(planes, left, right)):
        out[0, k] = re
        out[1, k] = im


def last_kernel(mine, early, piece_b0, piece_b1, late, small, earlier, beam, left, right, out_hbm, acc, middle, out, sems):
    me = mine[0]
    for n in range(2):
        acc[n] = GAIN * carried(small[n], me == 0)
        acc[2 + n] = GAIN * earlier[n]
    copies = []

    def plane(c, k):
        if k < 0:
            return jnp.zeros((GRID, GRID), jnp.float32)
        if k < EARLY:
            return early[c, k]
        return middle[c, k - EARLY] if k < LATE else late[c, k - LATE]

    def finish(low, high):
        for k in range(low, high):
            cr, ci, br, bi = (acc[n, k : k + 1] for n in range(4))
            re, im = (jnp.where(me < 2, plane(c, k - 1), plane(c, k)) for c in range(2))
            out[0, k] = re + (br * early[0, EARLY] - bi * early[1, EARLY]) + (cr * beam[0] - ci * beam[1])
            out[1, k] = im + (br * early[1, EARLY] + bi * early[0, EARLY]) + (cr * beam[1] + ci * beam[0])
        span = pl.ds(low, high - low)
        for c in range(2):
            copies.append(pltpu.make_async_copy(out.at[c, span], out_hbm.at[c, span], sems.at[len(copies)]))
            copies[-1].start()

    finish(0, EARLY)
    planes = [(piece[0, k], piece[1, k]) for piece in (piece_b0, piece_b1) for k in range(piece.shape[1])]
    for k, (re, im) in enumerate(twice_diffracted(planes, left, right)):
        middle[0, k] = re
        middle[1, k] = im
    finish(EARLY, LATE)
    finish(LATE, GROUPS)
    for copy in copies:
        copy.wait()


def early_pairs(core):
    onward = [(device, (device + 2) % PEERS) for device in range(core, PEERS, 2)]
    across = [(device, (device + 8) % PEERS) for device in range(1 - core, PEERS, 2) if device % 8 >= 6]
    return onward + across


def late_pairs():
    return [(device, device + 2 if device % 8 < 6 else device - 6) for device in range(PEERS)]


def shifted(value, axis, steps):
    count = lax.axis_size(axis)
    pairs = [(source, (source + steps) % count) for source in range(count)]
    return lax.ppermute(value, axis, pairs)


def shape(*dims, dtype=jnp.float32):
    return jax.ShapeDtypeStruct(dims, dtype)


def whole():
    return pl.BlockSpec(memory_space=pltpu.VMEM)


def vmem(*dims, dtype=jnp.float32):
    return pltpu.VMEM(dims, dtype)


def in_hbm(value):
    return pltpu.with_memory_space_constraint(value, pltpu.HBM)


def per_device(field, phase_bins, phase_jitter, energy, profile, delays):
    params = pltpu.CompilerParams(vmem_limit_bytes=VMEM_LIMIT)
    scalar = pl.BlockSpec(memory_space=pltpu.SMEM)
    remain = pl.BlockSpec(memory_space=pltpu.HBM)
    field = field.reshape(2, GROUPS, GRID, GRID)
    bins = phase_bins.reshape(COUNT, BLOCK)
    jitter = phase_jitter.reshape(COUNT, BLOCK)
    energies = energy.reshape(COUNT, BLOCK)
    mine = lax.axis_index("cuts").reshape(1)
    one, two = line_operator(1), line_operator(2)
    left_one = jnp.asarray(np.concatenate(one, axis=0), jnp.float32)
    right_one = jnp.asarray(right_form(*one), jnp.float32)
    core = mine[0] % 2
    shared_0 = lax.ppermute(lax.dynamic_slice_in_dim(field, core * LATE, EARLY, 1), "cuts", early_pairs(0))
    shared_1 = lax.ppermute(lax.dynamic_slice_in_dim(field, (1 - core) * LATE, EARLY, 1), "cuts", early_pairs(1))
    operands = [field, profile, bins, jitter, energies, delays.reshape(GROUPS, 1, NBS), left_one, right_one]
    send, phases1, energies1, places, beam, *sources = pl.pallas_call(
        first_kernel,
        out_shape=(
            pltpu.HBM((ROWS, BLOCK), jnp.float32),
            pltpu.HBM((COUNT, BLOCK), jnp.float32),
            pltpu.HBM((COUNT, BLOCK), jnp.float32),
            pltpu.HBM((8, COUNT), jnp.int32),
            pltpu.HBM((3, GRID, GRID), jnp.float32),
            *[pltpu.HBM((2, high - low, GRID, GRID), jnp.float32) for low, high in MIDDLE],
        ),
        in_specs=[scalar] + [remain] * 8,
        out_specs=(remain,) * 4 + (whole(),) + (remain,) * len(MIDDLE),
        scratch_shapes=[
            vmem(2, GROUPS, GRID, GRID),
            vmem(GRID, GRID),
            vmem(COUNT, BLOCK, dtype=jnp.int32),
            vmem(COUNT, BLOCK),
            vmem(COUNT, BLOCK),
            vmem(GROUPS, 1, NBS, dtype=jnp.int32),
            vmem(2 * GRID, GRID),
            vmem(2 * GRID, 2 * GRID),
            vmem(6, GROUPS, 128),
            vmem(ROWS, BLOCK),
            vmem(COUNT, BLOCK),
            vmem(COUNT, BLOCK),
            vmem(8, COUNT, dtype=jnp.int32),
            vmem(8, 128, dtype=jnp.int32),
            pltpu.SMEM((8, 128), jnp.int32),
            pltpu.SemaphoreType.DMA((15,)),
        ],
        compiler_params=params,
        name="push_place",
    )(mine, *[in_hbm(value) for value in operands])
    field_b = [shifted(source, "cuts", 2) for source in sources]

    left_two, right_two = deep_left(left_form(*two)), deep_right(right_form(*two))

    def exchange(send, phases1, energies1, places, field, shared_0, shared_1, beam):
        early = pl.pallas_call(
            early_kernel,
            out_shape=shape(2, EARLY + 1, GRID, GRID),
            in_specs=[scalar] + [whole()] * 5,
            out_specs=whole(),
            compiler_params=params,
            name="early_field",
        )(mine, shared_0, shared_1, beam, left_two, right_two)
        handed = jnp.where(core == 0, shared_1, shared_0)
        source_c = jnp.where(mine[0] % 8 >= 6, handed, field[:, LATE:])
        field_c = lax.ppermute(source_c, "cuts", late_pairs())
        late = pl.pallas_call(
            late_kernel,
            out_shape=shape(2, GROUPS - LATE, GRID, GRID),
            in_specs=[whole()] * 3,
            out_specs=whole(),
            compiler_params=params,
            name="late_field",
        )(field_c, left_two, right_two)
        recv = lax.all_to_all(send.reshape(ROWS, 1, BLOCK), "cuts", split_axis=0, concat_axis=0, tiled=True)
        recv = recv.reshape(ROWS, BLOCK)
        small, earlier = pl.pallas_call(
            second_kernel,
            out_shape=(shape(2, GROUPS, 128), shape(2, GROUPS, 128)),
            in_specs=[scalar] + [whole()] * 3,
            out_specs=(whole(),) * 2,
            scratch_shapes=[vmem(4, GROUPS, 128)],
            compiler_params=params,
            name="second_push",
        )(mine, phases1, energies1, recv)
        arrived = shifted(small, "cuts", 1)
        phase_out, energy_out = pl.pallas_call(
            pick_kernel,
            out_shape=(shape(COUNT, BLOCK), shape(COUNT, BLOCK)),
            in_specs=[scalar] + [whole()] * 2,
            out_specs=(remain,) * 2,
            scratch_shapes=[
                vmem(8, 128, dtype=jnp.int32),
                pltpu.SMEM((8, 128), jnp.int32),
                vmem(COUNT, 128),
                vmem(COUNT, BLOCK),
                vmem(COUNT, BLOCK),
                pltpu.SemaphoreType.DMA((9,)),
            ],
            compiler_params=params,
            name="pick",
        )(mine, recv, places)
        return phase_out, energy_out, early, late, arrived, earlier

    def refuse(*operands):
        sizes = [(COUNT, BLOCK)] * 2 + [(2, n, GRID, GRID) for n in (EARLY + 1, GROUPS - LATE)] + [(2, GROUPS, 128)] * 2
        return tuple(jnp.zeros(size, jnp.float32) for size in sizes)

    phase_out, energy_out, early, late, arrived, earlier = lax.cond(
        mine[0] < PEERS, exchange, refuse, send, phases1, energies1, places, field, shared_0, shared_1, beam
    )
    out = pl.pallas_call(
        last_kernel,
        out_shape=shape(2, GROUPS, GRID, GRID),
        in_specs=[scalar] + [whole()] * 9,
        out_specs=remain,
        scratch_shapes=[
            vmem(4, GROUPS, 128),
            vmem(2, LATE - EARLY, GRID, GRID),
            vmem(2, GROUPS, GRID, GRID),
            pltpu.SemaphoreType.DMA((6,)),
        ],
        compiler_params=params,
        name="last_field",
    )(mine, early, *field_b, late, arrived, earlier, in_hbm(beam), left_two, right_two)
    return (
        out.reshape(2, GROUPS, 1, GRID, GRID),
        phase_out.reshape(GROUPS, 1, NBS * BLOCK),
        energy_out.reshape(GROUPS, 1, NBS * BLOCK),
    )


def solution(mesh):
    return jax.shard_map(
        per_device,
        mesh=mesh,
        in_specs=(
            P(None, None, "cuts", None, None),
            P(None, "cuts", None),
            P(None, "cuts", None),
            P(None, "cuts", None),
            P(),
            P(),
        ),
        out_specs=(P(None, None, "cuts", None, None), P(None, "cuts", None), P(None, "cuts", None)),
        check_vma=False,
    )
```

```python
import functools
import math

import jax
import jax.numpy as jnp
import ml_dtypes
import numpy as np
from jax import lax
from jax.experimental import pallas as pl
from jax.experimental.pallas import tpu as pltpu
from jax.sharding import PartitionSpec as P

BLOCK = 128
NBINS = 16
KAPPA = 1.0
OMEGA = 1.0
GAIN = 16.0
PHASE_COEF = 20.0
GRID = 128
GROUPS = 16
NBS = 64
COUNT = GROUPS * NBS
PEERS = 128
CAP = 20
MESSAGE = 2 * CAP + 1
ROWS = PEERS * MESSAGE
BATCH = 32
EARLY, LATE = 5, 11
MIDDLE = ((5, 8), (8, 11))
VMEM_LIMIT = 24 * 1024 * 1024
HIGHEST = lax.Precision.HIGHEST


def line_operator(power):
    index = np.arange(GRID)
    freq = ((index + GRID // 2) % GRID - GRID // 2) / GRID
    weight = np.exp(-1j * PHASE_COEF * power * freq**2)
    wave = np.exp(2j * np.pi * (index[:, None] * index[None, :] % GRID) / GRID)
    column = wave @ weight / GRID
    matrix = column[(index[:, None] - index[None, :]) % GRID]
    return matrix.real, matrix.imag


def left_form(real, imag):
    return np.block([[real, -imag], [imag, real]])


def right_form(real, imag):
    return np.block([[real, imag], [-imag, real]])


def halves(matrix):
    high = matrix.astype(ml_dtypes.bfloat16)
    return high, (matrix - high.astype(np.float64)).astype(ml_dtypes.bfloat16)


def deep_left(matrix):
    high, low = halves(matrix)
    return jnp.asarray(np.concatenate([high, high, low], axis=1))


def deep_right(matrix):
    high, low = halves(matrix)
    return jnp.asarray(np.concatenate([high, high, low], axis=0))


def fitted(function, degree):
    top = (math.pi / 2 + 0.01) ** 2
    nodes = (np.cos(np.pi * (np.arange(400) + 0.5) / 400) + 1) / 2 * top
    series = np.polynomial.chebyshev.Chebyshev.fit(nodes, function(np.sqrt(nodes)), degree, domain=[0, top])
    return [float(c) for c in series.convert(kind=np.polynomial.Polynomial).coef]


SIN_COEF = fitted(lambda r: np.sin(r) / r, 5)
COS_COEF = fitted(np.cos, 6)
PI_HIGH = 3.140625
PI_MID = 9.67502593994140625e-4
PI_LOW = math.pi - PI_HIGH - PI_MID


def horner(coefs, x):
    value = jnp.float32(coefs[-1])
    for c in coefs[-2::-1]:
        value = value * x + jnp.float32(c)
    return value


def cos_sin(x):
    turns = jnp.round(x * jnp.float32(1.0 / math.pi))
    r = x - turns * jnp.float32(PI_HIGH)
    r = r - turns * jnp.float32(PI_MID)
    r = r - turns * jnp.float32(PI_LOW)
    half = turns * 0.5
    sign = 1.0 - 4.0 * jnp.abs(half - jnp.round(half))
    square = r * r
    return horner(COS_COEF, square) * sign, horner(SIN_COEF, square) * (r * sign)


def lane_total(rows):
    return jnp.broadcast_to(jnp.sum(rows, axis=1, keepdims=True), rows.shape)


def slots_of(delays):
    row = jnp.concatenate([delays[k] for k in range(GROUPS)], axis=1)
    values = lax.broadcasted_iota(jnp.int32, (PEERS, COUNT), 0)
    onehot = jnp.where(values == row, 1.0, 0.0)
    before = lax.broadcasted_iota(jnp.int32, (COUNT, COUNT), 0) < lax.broadcasted_iota(jnp.int32, (COUNT, COUNT), 1)
    upper = jnp.where(before, 1.0, 0.0).astype(jnp.bfloat16)
    earlier = jnp.dot(onehot.astype(jnp.bfloat16), upper, preferred_element_type=jnp.float32)
    return row, jnp.sum(earlier * onehot, axis=0, keepdims=True).astype(jnp.int32)


def folded(row):
    return jnp.concatenate([row[:, n * 128 : (n + 1) * 128] for n in range(COUNT // 128)], axis=0)


def rows_of(k):
    return pl.ds(pl.multiple_of(k * NBS, NBS), NBS)


def first_kernel(
    mine, field_hbm, profile_hbm, bins_hbm, jitter_hbm, energy_hbm, delays_hbm, left_hbm, right_hbm,
    send_hbm, phases_hbm, energies_hbm, places_hbm, beam, middle_0, middle_1,
    field, profile, bins, jitter, energy, delays, left, right, acc, send, phases, energies, places, index_v, index, sems,
):
    pairs = [
        (profile_hbm, profile), (left_hbm, left), (right_hbm, right), (delays_hbm, delays),
        (field_hbm, field), (bins_hbm, bins), (jitter_hbm, jitter), (energy_hbm, energy),
    ]
    copies = [pltpu.make_async_copy(src, dst, sems.at[n]) for n, (src, dst) in enumerate(pairs)]
    for copy in copies:
        copy.start()
    copies[3].wait()
    row, slot = slots_of(delays)
    places[0:1] = row
    places[1:2] = slot
    index_v[...] = folded(((mine[0] + row) % PEERS) * MESSAGE + slot)
    to_scalar = pltpu.make_async_copy(index_v, index, sems.at[3])
    to_scalar.start()
    for copy in copies[:3]:
        copy.wait()
    p = profile[...]
    half = jnp.dot(left[...], p, precision=HIGHEST, preferred_element_type=jnp.float32)
    both = jnp.concatenate([half[:GRID], half[GRID:]], axis=1)
    spread = jnp.dot(both, right[...], precision=HIGHEST, preferred_element_type=jnp.float32)
    beam[0] = spread[:, :GRID]
    beam[1] = spread[:, GRID:]
    beam[2] = p
    copies[4].wait()
    kept = [pltpu.make_async_copy(places, places_hbm, sems.at[8])]
    for middle, (low, high) in zip((middle_0, middle_1), MIDDLE):
        for c in range(2):
            span = pl.ds(low, high - low)
            kept.append(pltpu.make_async_copy(field.at[c, span], middle.at[c], sems.at[10 + len(kept)]))
    for copy in kept:
        copy.start()

    def project(k, carry):
        re, im = field[0, k], field[1, k]
        dr, di, q = beam[0], beam[1], profile[...]
        acc[0, pl.ds(k, 1)] = jnp.sum(q * re, axis=0, keepdims=True)
        acc[1, pl.ds(k, 1)] = jnp.sum(q * im, axis=0, keepdims=True)
        acc[2, pl.ds(k, 1)] = jnp.sum(dr * re - di * im, axis=0, keepdims=True)
        acc[3, pl.ds(k, 1)] = jnp.sum(dr * im + di * re, axis=0, keepdims=True)
        return carry

    lax.fori_loop(0, GROUPS, project, 0)
    self_re = jnp.sum(p * beam[0])
    self_im = jnp.sum(p * beam[1])
    for n in range(4):
        acc[n] = lane_total(acc[n]) * (1.0 / GRID)
    for copy in copies[5:]:
        copy.wait()

    def push(k, carry):
        rows = rows_of(k)
        ph = jnp.float32(2.0 * math.pi / NBINS) * (bins[rows].astype(jnp.float32) + jitter[rows])
        ph, en = pushed(ph, energy[rows], acc[0, pl.ds(k, 1)], acc[1, pl.ds(k, 1)])
        phases[rows] = ph
        energies[rows] = en
        c, s = cos_sin(ph)
        acc[4, pl.ds(k, 1)] = jnp.sum(c, axis=0, keepdims=True)
        acc[5, pl.ds(k, 1)] = jnp.sum(s, axis=0, keepdims=True)
        return carry

    lax.fori_loop(0, GROUPS, push, 0)
    kept.append(pltpu.make_async_copy(phases, phases_hbm, sems.at[9]))
    kept.append(pltpu.make_async_copy(energies, energies_hbm, sems.at[10]))
    for copy in kept[5:]:
        copy.start()
    to_scalar.wait()

    def put(n, carry):
        base = pl.multiple_of(n * BATCH, BATCH)
        spots = [index[n // (128 // BATCH), n % (128 // BATCH) * BATCH + m] for m in range(BATCH)]
        ph = [phases[pl.ds(base + m, 1)] for m in range(BATCH)]
        en = [energies[pl.ds(base + m, 1)] for m in range(BATCH)]
        for m in range(BATCH):
            send[pl.ds(spots[m], 1)] = ph[m]
            send[pl.ds(spots[m] + CAP, 1)] = en[m]
        return carry

    lax.fori_loop(0, COUNT // BATCH, put, 0)
    bre = lane_total(acc[4]) * (1.0 / (NBS * BLOCK))
    bim = lane_total(acc[5]) * (-1.0 / (NBS * BLOCK))
    gain = GAIN / GRID
    next_re = acc[2] + gain * (bre * self_re - bim * self_im)
    next_im = acc[3] + gain * (bre * self_im + bim * self_re)
    note = one_row([next_re, next_im, bre, bim])
    for n in range(PEERS):
        send[n * MESSAGE + 2 * CAP : (n + 1) * MESSAGE] = note
    out = pltpu.make_async_copy(send, send_hbm, sems.at[0])
    out.start()
    for copy in kept:
        copy.wait()
    out.wait()


def pushed(ph, en, amp_re, amp_im):
    c, s = cos_sin(ph)
    en = en - KAPPA * (amp_re * c - amp_im * s)
    return ph + OMEGA * en, en


def one_row(parts):
    rest = 128 // GROUPS - len(parts)
    stack = jnp.concatenate(parts + [jnp.zeros((rest * GROUPS, 128), jnp.float32)], axis=0)
    return stack.T[0:1]


def parts_of(recv, device):
    row = recv[pl.ds(device * MESSAGE + 2 * CAP, 1)]
    return jnp.broadcast_to(row, (128, 128)).T


def carried(value, flag):
    rolled = jnp.concatenate([jnp.zeros_like(value[:1]), value[:-1]], axis=0)
    return jnp.where(flag, rolled, value)


def second_kernel(mine, phases1, energies1, recv, small, earlier, acc):
    me = mine[0]
    near = parts_of(recv, (me + PEERS - 1) % PEERS)
    far = parts_of(recv, (me + PEERS - 2) % PEERS)
    for n in range(2):
        acc[n] = carried(near[n * GROUPS : (n + 1) * GROUPS], me == 0)
        earlier[n] = carried(far[(2 + n) * GROUPS : (3 + n) * GROUPS], me < 2)

    def push(k, carry):
        rows = rows_of(k)
        ph, _ = pushed(phases1[rows], energies1[rows], acc[0, pl.ds(k, 1)], acc[1, pl.ds(k, 1)])
        c, s = cos_sin(ph)
        acc[2, pl.ds(k, 1)] = jnp.sum(c, axis=0, keepdims=True)
        acc[3, pl.ds(k, 1)] = jnp.sum(s, axis=0, keepdims=True)
        return carry

    lax.fori_loop(0, GROUPS, push, 0)
    small[0] = lane_total(acc[2]) * (1.0 / (NBS * BLOCK))
    small[1] = lane_total(acc[3]) * (-1.0 / (NBS * BLOCK))


def wide_halves(x):
    high = x.astype(jnp.bfloat16)
    return high, (x - high.astype(jnp.float32)).astype(jnp.bfloat16)


def pick_kernel(mine, recv, places, phases_hbm, energies_hbm, index_v, index, amps, phases, energies, sems):
    me = mine[0]
    source = (me - places[0:1] + PEERS) % PEERS
    index_v[...] = folded(source * MESSAGE + places[1:2])
    to_scalar = pltpu.make_async_copy(index_v, index, sems.at[0])
    to_scalar.start()
    lane = lax.broadcasted_iota(jnp.int32, (128, 128), 1)
    sheet = recv[pl.ds(2 * CAP, PEERS, MESSAGE), :]
    wrapped = jnp.concatenate([sheet[127:128, 127:128], sheet[127:128, :127]], axis=1)
    wrapped = jnp.where(lane[0:1] % GROUPS == 0, 0.0, wrapped)
    sheet = jnp.concatenate([wrapped, sheet[:127]], axis=0)
    for n in range(COUNT // 128):
        column = jnp.broadcast_to(source[:, n * 128 : (n + 1) * 128], (128, 128)).T
        onehot = jnp.where(lane == column, 1.0, 0.0)
        amps[n * 128 : (n + 1) * 128] = jnp.dot(
            onehot, sheet, precision=HIGHEST, preferred_element_type=jnp.float32
        )
    to_scalar.wait()

    def get(n, carry):
        base = pl.multiple_of(n * BATCH, BATCH)
        spots = [index[n // (128 // BATCH), n % (128 // BATCH) * BATCH + m] for m in range(BATCH)]
        ph = [recv[pl.ds(spot, 1)] for spot in spots]
        en = [recv[pl.ds(spot + CAP, 1)] for spot in spots]
        for m in range(BATCH):
            phases[pl.ds(base + m, 1)] = ph[m]
            energies[pl.ds(base + m, 1)] = en[m]
        return carry

    copies = []
    for quarter in range(4):
        lax.fori_loop(quarter * COUNT // BATCH // 4, (quarter + 1) * COUNT // BATCH // 4, get, 0)
        for k in range(quarter * 4, quarter * 4 + 4):
            rows = slice(k * NBS, (k + 1) * NBS)
            re, im = amps[rows, k : k + 1], amps[rows, GROUPS + k : GROUPS + k + 1]
            phases[rows], energies[rows] = pushed(phases[rows], energies[rows], re, im)
        span = pl.ds(quarter * COUNT // 4, COUNT // 4)
        copies.append(pltpu.make_async_copy(phases.at[span], phases_hbm.at[span], sems.at[1 + 2 * quarter]))
        copies.append(pltpu.make_async_copy(energies.at[span], energies_hbm.at[span], sems.at[2 + 2 * quarter]))
        for copy in copies[-2:]:
            copy.start()
    for copy in copies:
        copy.wait()


def twice_diffracted(planes, left, right):
    hi, lo = wide_halves(jnp.concatenate([jnp.concatenate(pair, axis=1) for pair in planes], axis=0))
    half = jnp.dot(jnp.concatenate([hi, lo, hi], axis=1), right[...], preferred_element_type=jnp.float32)
    cols = []
    for m in range(len(planes)):
        mid = half[m * GRID : (m + 1) * GRID]
        cols.append(jnp.concatenate([mid[:, :GRID], mid[:, GRID:]], axis=0))
    hi, lo = wide_halves(jnp.concatenate(cols, axis=1))
    full = jnp.dot(left[...], jnp.concatenate([hi, lo, hi], axis=0), preferred_element_type=jnp.float32)
    cuts = [slice(m * GRID, (m + 1) * GRID) for m in range(len(planes))]
    return [(full[:GRID, cut], full[GRID:, cut]) for cut in cuts]


def early_kernel(mine, piece_0, piece_1, beam, left, right, out):
    even = mine[0] % 2 == 0
    planes = [tuple(jnp.where(even, piece_0[c, k], piece_1[c, k]) for c in range(2)) for k in range(EARLY)]
    planes.append((beam[2], jnp.zeros((GRID, GRID), jnp.float32)))
    for k, (re, im) in enumerate(twice_diffracted(planes, left, right)):
        out[0, k] = re
        out[1, k] = im


def late_kernel(piece, left, right, out):
    planes = [(piece[0, k], piece[1, k]) for k in range(piece.shape[1])]
    for k, (re, im) in enumerate(twice_diffracted(planes, left, right)):
        out[0, k] = re
        out[1, k] = im


def last_kernel(
    mine, early_hbm, piece_b0, piece_b1, late_hbm, small, earlier, beam, left, right,
    out_hbm, acc, early, raw, late, middle, out, fetch_sems, sems,
):
    me = mine[0]
    pairs = [(early_hbm, early), (late_hbm, late)]
    for piece, (low, high) in zip((piece_b0, piece_b1), MIDDLE):
        span = pl.ds(low - EARLY, high - low)
        pairs += [(piece.at[c], raw.at[c, span]) for c in range(2)]
    fetches = [pltpu.make_async_copy(src, dst, fetch_sems.at[n]) for n, (src, dst) in enumerate(pairs)]
    for fetch in fetches:
        fetch.start()
    for n in range(2):
        acc[n] = GAIN * carried(small[n], me == 0)
        acc[2 + n] = GAIN * earlier[n]
    copies = []

    def plane(c, k):
        if k < 0:
            return jnp.zeros((GRID, GRID), jnp.float32)
        if k < EARLY:
            return early[c, k]
        return middle[c, k - EARLY] if k < LATE else late[c, k - LATE]

    def finish(low, high):
        for k in range(low, high):
            cr, ci, br, bi = (acc[n, k : k + 1] for n in range(4))
            re, im = (jnp.where(me < 2, plane(c, k - 1), plane(c, k)) for c in range(2))
            out[0, k] = re + (br * early[0, EARLY] - bi * early[1, EARLY]) + (cr * beam[0] - ci * beam[1])
            out[1, k] = im + (br * early[1, EARLY] + bi * early[0, EARLY]) + (cr * beam[1] + ci * beam[0])
        span = pl.ds(low, high - low)
        for c in range(2):
            copies.append(pltpu.make_async_copy(out.at[c, span], out_hbm.at[c, span], sems.at[len(copies)]))
            copies[-1].start()

    for fetch in fetches:
        fetch.wait()
    finish(0, EARLY)
    planes = [(raw[0, k], raw[1, k]) for k in range(LATE - EARLY)]
    for k, (re, im) in enumerate(twice_diffracted(planes, left, right)):
        middle[0, k] = re
        middle[1, k] = im
    finish(EARLY, LATE)
    finish(LATE, GROUPS)
    for copy in copies:
        copy.wait()


def early_pairs(core):
    onward = [(device, (device + 2) % PEERS) for device in range(core, PEERS, 2)]
    across = [(device, (device + 8) % PEERS) for device in range(1 - core, PEERS, 2) if device % 8 >= 6]
    return onward + across


def late_pairs():
    return [(device, device + 2 if device % 8 < 6 else device - 6) for device in range(PEERS)]


def shifted(value, axis, steps):
    count = lax.axis_size(axis)
    pairs = [(source, (source + steps) % count) for source in range(count)]
    return lax.ppermute(value, axis, pairs)


def shape(*dims, dtype=jnp.float32):
    return jax.ShapeDtypeStruct(dims, dtype)


def whole():
    return pl.BlockSpec(memory_space=pltpu.VMEM)


def vmem(*dims, dtype=jnp.float32):
    return pltpu.VMEM(dims, dtype)


def in_hbm(value):
    return pltpu.with_memory_space_constraint(value, pltpu.HBM)


def per_device(field, phase_bins, phase_jitter, energy, profile, delays):
    params = pltpu.CompilerParams(vmem_limit_bytes=VMEM_LIMIT)
    scalar = pl.BlockSpec(memory_space=pltpu.SMEM)
    remain = pl.BlockSpec(memory_space=pltpu.HBM)
    field = field.reshape(2, GROUPS, GRID, GRID)
    bins = phase_bins.reshape(COUNT, BLOCK)
    jitter = phase_jitter.reshape(COUNT, BLOCK)
    energies = energy.reshape(COUNT, BLOCK)
    mine = lax.axis_index("cuts").reshape(1)
    one, two = line_operator(1), line_operator(2)
    left_one = jnp.asarray(np.concatenate(one, axis=0), jnp.float32)
    right_one = jnp.asarray(right_form(*one), jnp.float32)
    core = mine[0] % 2
    shared_0 = lax.ppermute(lax.dynamic_slice_in_dim(field, core * LATE, EARLY, 1), "cuts", early_pairs(0))
    shared_1 = lax.ppermute(lax.dynamic_slice_in_dim(field, (1 - core) * LATE, EARLY, 1), "cuts", early_pairs(1))
    operands = [field, profile, bins, jitter, energies, delays.reshape(GROUPS, 1, NBS), left_one, right_one]
    send, phases1, energies1, places, beam, *sources = pl.pallas_call(
        first_kernel,
        out_shape=(
            pltpu.HBM((ROWS, BLOCK), jnp.float32),
            pltpu.HBM((COUNT, BLOCK), jnp.float32),
            pltpu.HBM((COUNT, BLOCK), jnp.float32),
            pltpu.HBM((8, COUNT), jnp.int32),
            pltpu.HBM((3, GRID, GRID), jnp.float32),
            *[pltpu.HBM((2, high - low, GRID, GRID), jnp.float32) for low, high in MIDDLE],
        ),
        in_specs=[scalar] + [remain] * 8,
        out_specs=(remain,) * 4 + (whole(),) + (remain,) * len(MIDDLE),
        scratch_shapes=[
            vmem(2, GROUPS, GRID, GRID),
            vmem(GRID, GRID),
            vmem(COUNT, BLOCK, dtype=jnp.int32),
            vmem(COUNT, BLOCK),
            vmem(COUNT, BLOCK),
            vmem(GROUPS, 1, NBS, dtype=jnp.int32),
            vmem(2 * GRID, GRID),
            vmem(2 * GRID, 2 * GRID),
            vmem(6, GROUPS, 128),
            vmem(ROWS, BLOCK),
            vmem(COUNT, BLOCK),
            vmem(COUNT, BLOCK),
            vmem(8, COUNT, dtype=jnp.int32),
            vmem(8, 128, dtype=jnp.int32),
            pltpu.SMEM((8, 128), jnp.int32),
            pltpu.SemaphoreType.DMA((15,)),
        ],
        compiler_params=params,
        name="push_place",
    )(mine, *[in_hbm(value) for value in operands])
    field_b = [shifted(source, "cuts", 2) for source in sources]

    left_two, right_two = deep_left(left_form(*two)), deep_right(right_form(*two))

    def exchange(send, phases1, energies1, places, field, shared_0, shared_1, beam):
        early = pl.pallas_call(
            early_kernel,
            out_shape=shape(2, EARLY + 1, GRID, GRID),
            in_specs=[scalar] + [whole()] * 5,
            out_specs=whole(),
            compiler_params=params,
            name="early_field",
        )(mine, shared_0, shared_1, beam, left_two, right_two)
        handed = jnp.where(core == 0, shared_1, shared_0)
        source_c = jnp.where(mine[0] % 8 >= 6, handed, field[:, LATE:])
        field_c = lax.ppermute(source_c, "cuts", late_pairs())
        recv = lax.all_to_all(send.reshape(ROWS, 1, BLOCK), "cuts", split_axis=0, concat_axis=0, tiled=True)
        recv, early = lax.optimization_barrier((recv.reshape(ROWS, BLOCK), early))
        small, earlier = pl.pallas_call(
            second_kernel,
            out_shape=(shape(2, GROUPS, 128), shape(2, GROUPS, 128)),
            in_specs=[scalar] + [whole()] * 3,
            out_specs=(whole(),) * 2,
            scratch_shapes=[vmem(4, GROUPS, 128)],
            compiler_params=params,
            name="second_push",
        )(mine, phases1, energies1, recv)
        arrived = shifted(small, "cuts", 1)
        phase_out, energy_out = pl.pallas_call(
            pick_kernel,
            out_shape=(shape(COUNT, BLOCK), shape(COUNT, BLOCK)),
            in_specs=[scalar] + [whole()] * 2,
            out_specs=(remain,) * 2,
            scratch_shapes=[
                vmem(8, 128, dtype=jnp.int32),
                pltpu.SMEM((8, 128), jnp.int32),
                vmem(COUNT, 128),
                vmem(COUNT, BLOCK),
                vmem(COUNT, BLOCK),
                pltpu.SemaphoreType.DMA((9,)),
            ],
            compiler_params=params,
            name="pick",
        )(mine, recv, places)
        phase_out, energy_out, field_c = lax.optimization_barrier((phase_out, energy_out, field_c))
        late = pl.pallas_call(
            late_kernel,
            out_shape=shape(2, GROUPS - LATE, GRID, GRID),
            in_specs=[whole()] * 3,
            out_specs=whole(),
            compiler_params=params,
            name="late_field",
        )(field_c, left_two, right_two)
        return phase_out, energy_out, early, late, arrived, earlier

    def refuse(*operands):
        sizes = [(COUNT, BLOCK)] * 2 + [(2, n, GRID, GRID) for n in (EARLY + 1, GROUPS - LATE)] + [(2, GROUPS, 128)] * 2
        return tuple(jnp.zeros(size, jnp.float32) for size in sizes)

    phase_out, energy_out, early, late, arrived, earlier = lax.cond(
        mine[0] < PEERS, exchange, refuse, send, phases1, energies1, places, field, shared_0, shared_1, beam
    )
    out = pl.pallas_call(
        last_kernel,
        out_shape=shape(2, GROUPS, GRID, GRID),
        in_specs=[scalar] + [remain] * 4 + [whole()] * 5,
        out_specs=remain,
        scratch_shapes=[
            vmem(4, GROUPS, 128),
            vmem(2, EARLY + 1, GRID, GRID),
            vmem(2, LATE - EARLY, GRID, GRID),
            vmem(2, GROUPS - LATE, GRID, GRID),
            vmem(2, LATE - EARLY, GRID, GRID),
            vmem(2, GROUPS, GRID, GRID),
            pltpu.SemaphoreType.DMA((6,)),
            pltpu.SemaphoreType.DMA((6,)),
        ],
        compiler_params=params,
        name="last_field",
    )(mine, early, *field_b, late, arrived, earlier, in_hbm(beam), left_two, right_two)
    return (
        out.reshape(2, GROUPS, 1, GRID, GRID),
        phase_out.reshape(GROUPS, 1, NBS * BLOCK),
        energy_out.reshape(GROUPS, 1, NBS * BLOCK),
    )


def solution(mesh):
    return jax.shard_map(
        per_device,
        mesh=mesh,
        in_specs=(
            P(None, None, "cuts", None, None),
            P(None, "cuts", None),
            P(None, "cuts", None),
            P(None, "cuts", None),
            P(),
            P(),
        ),
        out_specs=(P(None, None, "cuts", None, None), P(None, "cuts", None), P(None, "cuts", None)),
        check_vma=False,
    )
```

```python
import functools
import math

import jax
import jax.numpy as jnp
import ml_dtypes
import numpy as np
from jax import lax
from jax.experimental import pallas as pl
from jax.experimental.pallas import tpu as pltpu
from jax.sharding import PartitionSpec as P

BLOCK = 128
NBINS = 16
KAPPA = 1.0
OMEGA = 1.0
GAIN = 16.0
PHASE_COEF = 20.0
GRID = 128
GROUPS = 16
NBS = 64
COUNT = GROUPS * NBS
PEERS = 128
CAP = 20
MESSAGE = 2 * CAP + 1
ROWS = PEERS * MESSAGE
BATCH = 32
EARLY, LATE = 5, 11
MIDDLE = ((5, 7), (7, 9), (9, 11))
VMEM_LIMIT = 24 * 1024 * 1024
HIGHEST = lax.Precision.HIGHEST


def line_operator(power):
    index = np.arange(GRID)
    freq = ((index + GRID // 2) % GRID - GRID // 2) / GRID
    weight = np.exp(-1j * PHASE_COEF * power * freq**2)
    wave = np.exp(2j * np.pi * (index[:, None] * index[None, :] % GRID) / GRID)
    column = wave @ weight / GRID
    matrix = column[(index[:, None] - index[None, :]) % GRID]
    return matrix.real, matrix.imag


def left_form(real, imag):
    return np.block([[real, -imag], [imag, real]])


def right_form(real, imag):
    return np.block([[real, imag], [-imag, real]])


def halves(matrix):
    high = matrix.astype(ml_dtypes.bfloat16)
    return high, (matrix - high.astype(np.float64)).astype(ml_dtypes.bfloat16)


def deep_left(matrix):
    high, low = halves(matrix)
    return jnp.asarray(np.concatenate([high, high, low], axis=1))


def deep_right(matrix):
    high, low = halves(matrix)
    return jnp.asarray(np.concatenate([high, high, low], axis=0))


def fitted(function, degree):
    top = (math.pi / 2 + 0.01) ** 2
    nodes = (np.cos(np.pi * (np.arange(400) + 0.5) / 400) + 1) / 2 * top
    series = np.polynomial.chebyshev.Chebyshev.fit(nodes, function(np.sqrt(nodes)), degree, domain=[0, top])
    return [float(c) for c in series.convert(kind=np.polynomial.Polynomial).coef]


SIN_COEF = fitted(lambda r: np.sin(r) / r, 5)
COS_COEF = fitted(np.cos, 6)
PI_HIGH = 3.140625
PI_MID = 9.67502593994140625e-4
PI_LOW = math.pi - PI_HIGH - PI_MID


def horner(coefs, x):
    value = jnp.float32(coefs[-1])
    for c in coefs[-2::-1]:
        value = value * x + jnp.float32(c)
    return value


def cos_sin(x):
    turns = jnp.round(x * jnp.float32(1.0 / math.pi))
    r = x - turns * jnp.float32(PI_HIGH)
    r = r - turns * jnp.float32(PI_MID)
    r = r - turns * jnp.float32(PI_LOW)
    half = turns * 0.5
    sign = 1.0 - 4.0 * jnp.abs(half - jnp.round(half))
    square = r * r
    return horner(COS_COEF, square) * sign, horner(SIN_COEF, square) * (r * sign)


def lane_total(rows):
    return jnp.broadcast_to(jnp.sum(rows, axis=1, keepdims=True), rows.shape)


def slots_of(delays):
    row = jnp.concatenate([delays[k] for k in range(GROUPS)], axis=1)
    values = lax.broadcasted_iota(jnp.int32, (PEERS, COUNT), 0)
    onehot = jnp.where(values == row, 1.0, 0.0)
    before = lax.broadcasted_iota(jnp.int32, (COUNT, COUNT), 0) < lax.broadcasted_iota(jnp.int32, (COUNT, COUNT), 1)
    upper = jnp.where(before, 1.0, 0.0).astype(jnp.bfloat16)
    earlier = jnp.dot(onehot.astype(jnp.bfloat16), upper, preferred_element_type=jnp.float32)
    return row, jnp.sum(earlier * onehot, axis=0, keepdims=True).astype(jnp.int32)


def folded(row):
    return jnp.concatenate([row[:, n * 128 : (n + 1) * 128] for n in range(COUNT // 128)], axis=0)


def rows_of(k):
    return pl.ds(pl.multiple_of(k * NBS, NBS), NBS)


def first_kernel(
    mine, field_hbm, profile_hbm, bins_hbm, jitter_hbm, energy_hbm, delays_hbm, left_hbm, right_hbm,
    send_hbm, phases_hbm, energies_hbm, places_hbm, beam, small, middle_0, middle_1, middle_2,
    field, profile, bins, jitter, energy, delays, left, right, acc, send, phases, energies, places, index_v, index, sems,
):
    pairs = [
        (profile_hbm, profile), (left_hbm, left), (right_hbm, right), (delays_hbm, delays),
        (field_hbm, field), (bins_hbm, bins), (jitter_hbm, jitter), (energy_hbm, energy),
    ]
    copies = [pltpu.make_async_copy(src, dst, sems.at[n]) for n, (src, dst) in enumerate(pairs)]
    for copy in copies:
        copy.start()
    copies[3].wait()
    row, slot = slots_of(delays)
    places[0:1] = row
    places[1:2] = slot
    index_v[...] = folded(((mine[0] + row) % PEERS) * MESSAGE + slot)
    to_scalar = pltpu.make_async_copy(index_v, index, sems.at[3])
    to_scalar.start()
    for copy in copies[:3]:
        copy.wait()
    p = profile[...]
    half = jnp.dot(left[...], p, precision=HIGHEST, preferred_element_type=jnp.float32)
    both = jnp.concatenate([half[:GRID], half[GRID:]], axis=1)
    spread = jnp.dot(both, right[...], precision=HIGHEST, preferred_element_type=jnp.float32)
    beam[0] = spread[:, :GRID]
    beam[1] = spread[:, GRID:]
    beam[2] = p
    copies[4].wait()
    kept = [pltpu.make_async_copy(places, places_hbm, sems.at[8])]
    for middle, (low, high) in zip((middle_0, middle_1, middle_2), MIDDLE):
        for c in range(2):
            span = pl.ds(low, high - low)
            kept.append(pltpu.make_async_copy(field.at[c, span], middle.at[c], sems.at[10 + len(kept)]))
    for copy in kept:
        copy.start()

    def project(k, carry):
        re, im = field[0, k], field[1, k]
        dr, di, q = beam[0], beam[1], profile[...]
        acc[0, pl.ds(k, 1)] = jnp.sum(q * re, axis=0, keepdims=True)
        acc[1, pl.ds(k, 1)] = jnp.sum(q * im, axis=0, keepdims=True)
        acc[2, pl.ds(k, 1)] = jnp.sum(dr * re - di * im, axis=0, keepdims=True)
        acc[3, pl.ds(k, 1)] = jnp.sum(dr * im + di * re, axis=0, keepdims=True)
        return carry

    lax.fori_loop(0, GROUPS, project, 0)
    self_re = jnp.sum(p * beam[0])
    self_im = jnp.sum(p * beam[1])
    for n in range(4):
        acc[n] = lane_total(acc[n]) * (1.0 / GRID)
    for copy in copies[5:]:
        copy.wait()

    def push(k, carry):
        rows = rows_of(k)
        ph = jnp.float32(2.0 * math.pi / NBINS) * (bins[rows].astype(jnp.float32) + jitter[rows])
        ph, en = pushed(ph, energy[rows], acc[0, pl.ds(k, 1)], acc[1, pl.ds(k, 1)])
        phases[rows] = ph
        energies[rows] = en
        c, s = cos_sin(ph)
        acc[4, pl.ds(k, 1)] = jnp.sum(c, axis=0, keepdims=True)
        acc[5, pl.ds(k, 1)] = jnp.sum(s, axis=0, keepdims=True)
        return carry

    lax.fori_loop(0, GROUPS, push, 0)
    kept.append(pltpu.make_async_copy(phases, phases_hbm, sems.at[9]))
    kept.append(pltpu.make_async_copy(energies, energies_hbm, sems.at[10]))
    for copy in kept[7:]:
        copy.start()
    to_scalar.wait()

    def put(n, carry):
        base = pl.multiple_of(n * BATCH, BATCH)
        spots = [index[n // (128 // BATCH), n % (128 // BATCH) * BATCH + m] for m in range(BATCH)]
        ph = [phases[pl.ds(base + m, 1)] for m in range(BATCH)]
        en = [energies[pl.ds(base + m, 1)] for m in range(BATCH)]
        for m in range(BATCH):
            send[pl.ds(spots[m], 1)] = ph[m]
            send[pl.ds(spots[m] + CAP, 1)] = en[m]
        return carry

    lax.fori_loop(0, COUNT // BATCH, put, 0)
    bre = lane_total(acc[4]) * (1.0 / (NBS * BLOCK))
    bim = lane_total(acc[5]) * (-1.0 / (NBS * BLOCK))
    gain = GAIN / GRID
    next_re = acc[2] + gain * (bre * self_re - bim * self_im)
    next_im = acc[3] + gain * (bre * self_im + bim * self_re)
    for n, part in enumerate((next_re, next_im, bre, bim)):
        small[n] = part
    note = one_row([next_re, next_im])
    for n in range(PEERS):
        send[n * MESSAGE + 2 * CAP : (n + 1) * MESSAGE] = note
    out = pltpu.make_async_copy(send, send_hbm, sems.at[0])
    out.start()
    for copy in kept:
        copy.wait()
    out.wait()


def pushed(ph, en, amp_re, amp_im):
    c, s = cos_sin(ph)
    en = en - KAPPA * (amp_re * c - amp_im * s)
    return ph + OMEGA * en, en


def one_row(parts):
    rest = 128 // GROUPS - len(parts)
    stack = jnp.concatenate(parts + [jnp.zeros((rest * GROUPS, 128), jnp.float32)], axis=0)
    return stack.T[0:1]


def carried(value, flag):
    rolled = jnp.concatenate([jnp.zeros_like(value[:1]), value[:-1]], axis=0)
    return jnp.where(flag, rolled, value)


def second_kernel(mine, phases1, energies1, arrived, small, acc):
    for n in range(4):
        acc[n] = carried(arrived[n], mine[0] == 0)

    def push(k, carry):
        rows = rows_of(k)
        ph, _ = pushed(phases1[rows], energies1[rows], acc[0, pl.ds(k, 1)], acc[1, pl.ds(k, 1)])
        c, s = cos_sin(ph)
        small[0, pl.ds(k, 1)] = jnp.sum(c, axis=0, keepdims=True)
        small[1, pl.ds(k, 1)] = jnp.sum(s, axis=0, keepdims=True)
        return carry

    lax.fori_loop(0, GROUPS, push, 0)
    small[0] = lane_total(small[0]) * (1.0 / (NBS * BLOCK))
    small[1] = lane_total(small[1]) * (-1.0 / (NBS * BLOCK))
    small[2] = acc[2]
    small[3] = acc[3]


def wide_halves(x):
    high = x.astype(jnp.bfloat16)
    return high, (x - high.astype(jnp.float32)).astype(jnp.bfloat16)


def pick_kernel(mine, recv, places, phases_hbm, energies_hbm, index_v, index, amps, phases, energies, sems):
    me = mine[0]
    source = (me - places[0:1] + PEERS) % PEERS
    index_v[...] = folded(source * MESSAGE + places[1:2])
    to_scalar = pltpu.make_async_copy(index_v, index, sems.at[0])
    to_scalar.start()
    lane = lax.broadcasted_iota(jnp.int32, (128, 128), 1)
    sheet = recv[pl.ds(2 * CAP, PEERS, MESSAGE), :]
    wrapped = jnp.concatenate([sheet[127:128, 127:128], sheet[127:128, :127]], axis=1)
    wrapped = jnp.where(lane[0:1] % GROUPS == 0, 0.0, wrapped)
    sheet = jnp.concatenate([wrapped, sheet[:127]], axis=0)
    for n in range(COUNT // 128):
        column = jnp.broadcast_to(source[:, n * 128 : (n + 1) * 128], (128, 128)).T
        onehot = jnp.where(lane == column, 1.0, 0.0)
        amps[n * 128 : (n + 1) * 128] = jnp.dot(
            onehot, sheet, precision=HIGHEST, preferred_element_type=jnp.float32
        )
    to_scalar.wait()

    def get(n, carry):
        base = pl.multiple_of(n * BATCH, BATCH)
        spots = [index[n // (128 // BATCH), n % (128 // BATCH) * BATCH + m] for m in range(BATCH)]
        ph = [recv[pl.ds(spot, 1)] for spot in spots]
        en = [recv[pl.ds(spot + CAP, 1)] for spot in spots]
        for m in range(BATCH):
            phases[pl.ds(base + m, 1)] = ph[m]
            energies[pl.ds(base + m, 1)] = en[m]
        return carry

    copies = []
    for quarter in range(4):
        lax.fori_loop(quarter * COUNT // BATCH // 4, (quarter + 1) * COUNT // BATCH // 4, get, 0)
        for k in range(quarter * 4, quarter * 4 + 4):
            rows = slice(k * NBS, (k + 1) * NBS)
            re, im = amps[rows, k : k + 1], amps[rows, GROUPS + k : GROUPS + k + 1]
            phases[rows], energies[rows] = pushed(phases[rows], energies[rows], re, im)
        span = pl.ds(quarter * COUNT // 4, COUNT // 4)
        copies.append(pltpu.make_async_copy(phases.at[span], phases_hbm.at[span], sems.at[1 + 2 * quarter]))
        copies.append(pltpu.make_async_copy(energies.at[span], energies_hbm.at[span], sems.at[2 + 2 * quarter]))
        for copy in copies[-2:]:
            copy.start()
    for copy in copies:
        copy.wait()


def twice_diffracted(planes, left, right):
    hi, lo = wide_halves(jnp.concatenate([jnp.concatenate(pair, axis=1) for pair in planes], axis=0))
    half = jnp.dot(jnp.concatenate([hi, lo, hi], axis=1), right[...], preferred_element_type=jnp.float32)
    cols = []
    for m in range(len(planes)):
        mid = half[m * GRID : (m + 1) * GRID]
        cols.append(jnp.concatenate([mid[:, :GRID], mid[:, GRID:]], axis=0))
    hi, lo = wide_halves(jnp.concatenate(cols, axis=1))
    full = jnp.dot(left[...], jnp.concatenate([hi, lo, hi], axis=0), preferred_element_type=jnp.float32)
    cuts = [slice(m * GRID, (m + 1) * GRID) for m in range(len(planes))]
    return [(full[:GRID, cut], full[GRID:, cut]) for cut in cuts]


def early_kernel(mine, piece_0, piece_1, beam, left, right, out):
    even = mine[0] % 2 == 0
    planes = [tuple(jnp.where(even, piece_0[c, k], piece_1[c, k]) for c in range(2)) for k in range(EARLY)]
    planes.append((beam[2], jnp.zeros((GRID, GRID), jnp.float32)))
    for k, (re, im) in enumerate(twice_diffracted(planes, left, right)):
        out[0, k] = re
        out[1, k] = im


def last_kernel(
    mine, early, piece_b0, piece_b1, piece_b2, piece_c, small, beam, left, right, out_hbm, acc, rest, out, sems
):
    me = mine[0]
    for n in range(4):
        acc[n] = GAIN * carried(small[n], me == 0)
    copies = []

    def plane(c, k):
        if k < 0:
            return jnp.zeros((GRID, GRID), jnp.float32)
        return early[c, k] if k < EARLY else rest[c, k - EARLY]

    def finish(low, high):
        for k in range(low, high):
            cr, ci, br, bi = (acc[n, k : k + 1] for n in range(4))
            re, im = (jnp.where(me < 2, plane(c, k - 1), plane(c, k)) for c in range(2))
            out[0, k] = re + (br * early[0, EARLY] - bi * early[1, EARLY]) + (cr * beam[0] - ci * beam[1])
            out[1, k] = im + (br * early[1, EARLY] + bi * early[0, EARLY]) + (cr * beam[1] + ci * beam[0])
        span = pl.ds(low, high - low)
        for c in range(2):
            copies.append(pltpu.make_async_copy(out.at[c, span], out_hbm.at[c, span], sems.at[len(copies)]))
            copies[-1].start()

    finish(0, EARLY)
    planes = [(piece[0, k], piece[1, k]) for piece in (piece_b0, piece_b1, piece_b2) for k in range(piece.shape[1])]
    for k, (re, im) in enumerate(twice_diffracted(planes, left, right)):
        rest[0, k] = re
        rest[1, k] = im
    finish(EARLY, LATE)
    planes = [(piece_c[0, k], piece_c[1, k]) for k in range(piece_c.shape[1])]
    for k, (re, im) in enumerate(twice_diffracted(planes, left, right)):
        rest[0, LATE - EARLY + k] = re
        rest[1, LATE - EARLY + k] = im
    finish(LATE, GROUPS)
    for copy in copies:
        copy.wait()


def early_pairs(core):
    onward = [(device, (device + 2) % PEERS) for device in range(core, PEERS, 2)]
    across = [(device, (device + 8) % PEERS) for device in range(1 - core, PEERS, 2) if device % 8 >= 6]
    return onward + across


def late_pairs():
    return [(device, device + 2 if device % 8 < 6 else device - 6) for device in range(PEERS)]


def shifted(value, axis, steps):
    count = lax.axis_size(axis)
    pairs = [(source, (source + steps) % count) for source in range(count)]
    return lax.ppermute(value, axis, pairs)


def shape(*dims, dtype=jnp.float32):
    return jax.ShapeDtypeStruct(dims, dtype)


def whole():
    return pl.BlockSpec(memory_space=pltpu.VMEM)


def vmem(*dims, dtype=jnp.float32):
    return pltpu.VMEM(dims, dtype)


def in_hbm(value):
    return pltpu.with_memory_space_constraint(value, pltpu.HBM)


def per_device(field, phase_bins, phase_jitter, energy, profile, delays):
    params = pltpu.CompilerParams(vmem_limit_bytes=VMEM_LIMIT)
    scalar = pl.BlockSpec(memory_space=pltpu.SMEM)
    remain = pl.BlockSpec(memory_space=pltpu.HBM)
    field = field.reshape(2, GROUPS, GRID, GRID)
    bins = phase_bins.reshape(COUNT, BLOCK)
    jitter = phase_jitter.reshape(COUNT, BLOCK)
    energies = energy.reshape(COUNT, BLOCK)
    mine = lax.axis_index("cuts").reshape(1)
    one, two = line_operator(1), line_operator(2)
    left_one = jnp.asarray(np.concatenate(one, axis=0), jnp.float32)
    right_one = jnp.asarray(right_form(*one), jnp.float32)
    core = mine[0] % 2
    shared_0 = lax.ppermute(lax.dynamic_slice_in_dim(field, core * LATE, EARLY, 1), "cuts", early_pairs(0))
    shared_1 = lax.ppermute(lax.dynamic_slice_in_dim(field, (1 - core) * LATE, EARLY, 1), "cuts", early_pairs(1))
    operands = [field, profile, bins, jitter, energies, delays.reshape(GROUPS, 1, NBS), left_one, right_one]
    send, phases1, energies1, places, beam, small1, *sources = pl.pallas_call(
        first_kernel,
        out_shape=(
            pltpu.HBM((ROWS, BLOCK), jnp.float32),
            pltpu.HBM((COUNT, BLOCK), jnp.float32),
            pltpu.HBM((COUNT, BLOCK), jnp.float32),
            pltpu.HBM((8, COUNT), jnp.int32),
            pltpu.HBM((3, GRID, GRID), jnp.float32),
            shape(4, GROUPS, 128),
            *[pltpu.HBM((2, high - low, GRID, GRID), jnp.float32) for low, high in MIDDLE],
        ),
        in_specs=[scalar] + [remain] * 8,
        out_specs=(remain,) * 4 + (whole(),) * 2 + (remain,) * len(MIDDLE),
        scratch_shapes=[
            vmem(2, GROUPS, GRID, GRID),
            vmem(GRID, GRID),
            vmem(COUNT, BLOCK, dtype=jnp.int32),
            vmem(COUNT, BLOCK),
            vmem(COUNT, BLOCK),
            vmem(GROUPS, 1, NBS, dtype=jnp.int32),
            vmem(2 * GRID, GRID),
            vmem(2 * GRID, 2 * GRID),
            vmem(6, GROUPS, 128),
            vmem(ROWS, BLOCK),
            vmem(COUNT, BLOCK),
            vmem(COUNT, BLOCK),
            vmem(8, COUNT, dtype=jnp.int32),
            vmem(8, 128, dtype=jnp.int32),
            pltpu.SMEM((8, 128), jnp.int32),
            pltpu.SemaphoreType.DMA((17,)),
        ],
        compiler_params=params,
        name="push_place",
    )(mine, *[in_hbm(value) for value in operands])
    arrived1 = shifted(small1, "cuts", 1)
    small2 = pl.pallas_call(
        second_kernel,
        out_shape=shape(4, GROUPS, 128),
        in_specs=[scalar] + [whole()] * 3,
        out_specs=whole(),
        scratch_shapes=[vmem(4, GROUPS, 128)],
        compiler_params=params,
        name="second_push",
    )(mine, phases1, energies1, arrived1)
    field_b = [shifted(source, "cuts", 2) for source in sources]

    left_two, right_two = deep_left(left_form(*two)), deep_right(right_form(*two))

    def exchange(send, small2, places, field, shared_0, shared_1, beam):
        early = pl.pallas_call(
            early_kernel,
            out_shape=shape(2, EARLY + 1, GRID, GRID),
            in_specs=[scalar] + [whole()] * 5,
            out_specs=whole(),
            compiler_params=params,
            name="early_field",
        )(mine, shared_0, shared_1, beam, left_two, right_two)
        handed = jnp.where(core == 0, shared_1, shared_0)
        source_c = jnp.where(mine[0] % 8 >= 6, handed, field[:, LATE:])
        field_c = lax.ppermute(source_c, "cuts", late_pairs())
        recv = lax.all_to_all(send.reshape(ROWS, 1, BLOCK), "cuts", split_axis=0, concat_axis=0, tiled=True)
        recv, early = lax.optimization_barrier((recv.reshape(ROWS, BLOCK), early))
        arrived = shifted(small2, "cuts", 1)
        phase_out, energy_out = pl.pallas_call(
            pick_kernel,
            out_shape=(shape(COUNT, BLOCK), shape(COUNT, BLOCK)),
            in_specs=[scalar] + [whole()] * 2,
            out_specs=(remain,) * 2,
            scratch_shapes=[
                vmem(8, 128, dtype=jnp.int32),
                pltpu.SMEM((8, 128), jnp.int32),
                vmem(COUNT, 128),
                vmem(COUNT, BLOCK),
                vmem(COUNT, BLOCK),
                pltpu.SemaphoreType.DMA((9,)),
            ],
            compiler_params=params,
            name="pick",
        )(mine, recv, places)
        return phase_out, energy_out, early, field_c, arrived

    def refuse(*operands):
        sizes = [(COUNT, BLOCK)] * 2 + [(2, n, GRID, GRID) for n in (EARLY + 1, GROUPS - LATE)] + [(4, GROUPS, 128)]
        return tuple(jnp.zeros(size, jnp.float32) for size in sizes)

    phase_out, energy_out, early, field_c, arrived = lax.cond(
        mine[0] < PEERS, exchange, refuse, send, small2, places, field, shared_0, shared_1, beam
    )
    out = pl.pallas_call(
        last_kernel,
        out_shape=shape(2, GROUPS, GRID, GRID),
        in_specs=[scalar] + [whole()] * 9,
        out_specs=remain,
        scratch_shapes=[
            vmem(4, GROUPS, 128),
            vmem(2, GROUPS - EARLY, GRID, GRID),
            vmem(2, GROUPS, GRID, GRID),
            pltpu.SemaphoreType.DMA((6,)),
        ],
        compiler_params=params,
        name="last_field",
    )(mine, early, *field_b, field_c, arrived, in_hbm(beam), left_two, right_two)
    return (
        out.reshape(2, GROUPS, 1, GRID, GRID),
        phase_out.reshape(GROUPS, 1, NBS * BLOCK),
        energy_out.reshape(GROUPS, 1, NBS * BLOCK),
    )


def solution(mesh):
    return jax.shard_map(
        per_device,
        mesh=mesh,
        in_specs=(
            P(None, None, "cuts", None, None),
            P(None, "cuts", None),
            P(None, "cuts", None),
            P(None, "cuts", None),
            P(),
            P(),
        ),
        out_specs=(P(None, None, "cuts", None, None), P(None, "cuts", None), P(None, "cuts", None)),
        check_vma=False,
    )
```

```python
import functools
import math

import jax
import jax.numpy as jnp
import ml_dtypes
import numpy as np
from jax import lax
from jax.experimental import pallas as pl
from jax.experimental.pallas import tpu as pltpu
from jax.sharding import PartitionSpec as P

BLOCK = 128
NBINS = 16
KAPPA = 1.0
OMEGA = 1.0
GAIN = 16.0
PHASE_COEF = 20.0
GRID = 128
GROUPS = 16
NBS = 64
COUNT = GROUPS * NBS
PEERS = 128
CAP = 20
MESSAGE = 2 * CAP + 1
ROWS = PEERS * MESSAGE
BATCH = 32
EARLY, LATE = 5, 13
MIDDLE = ((5, 7), (7, 9), (9, 11), (11, 13))
VMEM_LIMIT = 24 * 1024 * 1024
HIGHEST = lax.Precision.HIGHEST


def line_operator(power):
    index = np.arange(GRID)
    freq = ((index + GRID // 2) % GRID - GRID // 2) / GRID
    weight = np.exp(-1j * PHASE_COEF * power * freq**2)
    wave = np.exp(2j * np.pi * (index[:, None] * index[None, :] % GRID) / GRID)
    column = wave @ weight / GRID
    matrix = column[(index[:, None] - index[None, :]) % GRID]
    return matrix.real, matrix.imag


def left_form(real, imag):
    return np.block([[real, -imag], [imag, real]])


def right_form(real, imag):
    return np.block([[real, imag], [-imag, real]])


def halves(matrix):
    high = matrix.astype(ml_dtypes.bfloat16)
    return high, (matrix - high.astype(np.float64)).astype(ml_dtypes.bfloat16)


def deep_left(matrix):
    high, low = halves(matrix)
    return jnp.asarray(np.concatenate([high, high, low], axis=1))


def deep_right(matrix):
    high, low = halves(matrix)
    return jnp.asarray(np.concatenate([high, high, low], axis=0))


def fitted(function, degree):
    top = (math.pi / 2 + 0.01) ** 2
    nodes = (np.cos(np.pi * (np.arange(400) + 0.5) / 400) + 1) / 2 * top
    series = np.polynomial.chebyshev.Chebyshev.fit(nodes, function(np.sqrt(nodes)), degree, domain=[0, top])
    return [float(c) for c in series.convert(kind=np.polynomial.Polynomial).coef]


SIN_COEF = fitted(lambda r: np.sin(r) / r, 5)
COS_COEF = fitted(np.cos, 6)
PI_HIGH = 3.140625
PI_MID = 9.67502593994140625e-4
PI_LOW = math.pi - PI_HIGH - PI_MID


def horner(coefs, x):
    value = jnp.float32(coefs[-1])
    for c in coefs[-2::-1]:
        value = value * x + jnp.float32(c)
    return value


def cos_sin(x):
    turns = jnp.round(x * jnp.float32(1.0 / math.pi))
    r = x - turns * jnp.float32(PI_HIGH)
    r = r - turns * jnp.float32(PI_MID)
    r = r - turns * jnp.float32(PI_LOW)
    half = turns * 0.5
    sign = 1.0 - 4.0 * jnp.abs(half - jnp.round(half))
    square = r * r
    return horner(COS_COEF, square) * sign, horner(SIN_COEF, square) * (r * sign)


def lane_total(rows):
    return jnp.broadcast_to(jnp.sum(rows, axis=1, keepdims=True), rows.shape)


def slots_of(delays):
    row = jnp.concatenate([delays[k] for k in range(GROUPS)], axis=1)
    values = lax.broadcasted_iota(jnp.int32, (PEERS, COUNT), 0)
    onehot = jnp.where(values == row, 1.0, 0.0)
    before = lax.broadcasted_iota(jnp.int32, (COUNT, COUNT), 0) < lax.broadcasted_iota(jnp.int32, (COUNT, COUNT), 1)
    upper = jnp.where(before, 1.0, 0.0).astype(jnp.bfloat16)
    earlier = jnp.dot(onehot.astype(jnp.bfloat16), upper, preferred_element_type=jnp.float32)
    return row, jnp.sum(earlier * onehot, axis=0, keepdims=True).astype(jnp.int32)


def folded(row):
    return jnp.concatenate([row[:, n * 128 : (n + 1) * 128] for n in range(COUNT // 128)], axis=0)


def rows_of(k):
    return pl.ds(pl.multiple_of(k * NBS, NBS), NBS)


def first_kernel(
    mine, field_hbm, profile_hbm, bins_hbm, jitter_hbm, energy_hbm, delays_hbm, left_hbm, right_hbm,
    send_hbm, phases, energies, places_hbm, beam, small, middle_0, middle_1, middle_2, middle_3,
    field, profile, bins, jitter, energy, delays, left, right, acc, send, places, index_v, index, sems,
):
    pairs = [
        (profile_hbm, profile), (left_hbm, left), (right_hbm, right), (delays_hbm, delays),
        (field_hbm, field), (bins_hbm, bins), (jitter_hbm, jitter), (energy_hbm, energy),
    ]
    copies = [pltpu.make_async_copy(src, dst, sems.at[n]) for n, (src, dst) in enumerate(pairs)]
    for copy in copies:
        copy.start()
    copies[3].wait()
    row, slot = slots_of(delays)
    places[0:1] = row
    places[1:2] = slot
    index_v[...] = folded(((mine[0] + row) % PEERS) * MESSAGE + slot)
    to_scalar = pltpu.make_async_copy(index_v, index, sems.at[3])
    to_scalar.start()
    for copy in copies[:3]:
        copy.wait()
    p = profile[...]
    half = jnp.dot(left[...], p, precision=HIGHEST, preferred_element_type=jnp.float32)
    both = jnp.concatenate([half[:GRID], half[GRID:]], axis=1)
    spread = jnp.dot(both, right[...], precision=HIGHEST, preferred_element_type=jnp.float32)
    beam[0] = spread[:, :GRID]
    beam[1] = spread[:, GRID:]
    beam[2] = p
    copies[4].wait()
    kept = [pltpu.make_async_copy(places, places_hbm, sems.at[8])]
    for middle, (low, high) in zip((middle_0, middle_1, middle_2, middle_3), MIDDLE):
        for c in range(2):
            span = pl.ds(low, high - low)
            kept.append(pltpu.make_async_copy(field.at[c, span], middle.at[c], sems.at[8 + len(kept)]))
    for copy in kept:
        copy.start()

    def project(k, carry):
        re, im = field[0, k], field[1, k]
        dr, di, q = beam[0], beam[1], profile[...]
        acc[0, pl.ds(k, 1)] = jnp.sum(q * re, axis=0, keepdims=True)
        acc[1, pl.ds(k, 1)] = jnp.sum(q * im, axis=0, keepdims=True)
        acc[2, pl.ds(k, 1)] = jnp.sum(dr * re - di * im, axis=0, keepdims=True)
        acc[3, pl.ds(k, 1)] = jnp.sum(dr * im + di * re, axis=0, keepdims=True)
        return carry

    lax.fori_loop(0, GROUPS, project, 0)
    self_re = jnp.sum(p * beam[0])
    self_im = jnp.sum(p * beam[1])
    for n in range(4):
        acc[n] = lane_total(acc[n]) * (1.0 / GRID)
    for copy in copies[5:]:
        copy.wait()

    def push(k, carry):
        rows = rows_of(k)
        ph = jnp.float32(2.0 * math.pi / NBINS) * (bins[rows].astype(jnp.float32) + jitter[rows])
        ph, en = pushed(ph, energy[rows], acc[0, pl.ds(k, 1)], acc[1, pl.ds(k, 1)])
        phases[rows] = ph
        energies[rows] = en
        c, s = cos_sin(ph)
        acc[4, pl.ds(k, 1)] = jnp.sum(c, axis=0, keepdims=True)
        acc[5, pl.ds(k, 1)] = jnp.sum(s, axis=0, keepdims=True)
        return carry

    lax.fori_loop(0, GROUPS, push, 0)
    to_scalar.wait()

    def put(n, carry):
        base = pl.multiple_of(n * BATCH, BATCH)
        spots = [index[n // (128 // BATCH), n % (128 // BATCH) * BATCH + m] for m in range(BATCH)]
        ph = [phases[pl.ds(base + m, 1)] for m in range(BATCH)]
        en = [energies[pl.ds(base + m, 1)] for m in range(BATCH)]
        for m in range(BATCH):
            send[spots[m]] = ph[m]
            send[spots[m] + CAP] = en[m]
        return carry

    lax.fori_loop(0, COUNT // BATCH, put, 0)
    bre = lane_total(acc[4]) * (1.0 / (NBS * BLOCK))
    bim = lane_total(acc[5]) * (-1.0 / (NBS * BLOCK))
    gain = GAIN / GRID
    next_re = acc[2] + gain * (bre * self_re - bim * self_im)
    next_im = acc[3] + gain * (bre * self_im + bim * self_re)
    for n, part in enumerate((next_re, next_im, bre, bim)):
        small[n] = part
    out = pltpu.make_async_copy(send, send_hbm, sems.at[0])
    out.start()
    for copy in kept:
        copy.wait()
    out.wait()


def pushed(ph, en, amp_re, amp_im):
    c, s = cos_sin(ph)
    en = en - KAPPA * (amp_re * c - amp_im * s)
    return ph + OMEGA * en, en


def one_row(parts):
    rest = 128 // GROUPS - len(parts)
    stack = jnp.concatenate(parts + [jnp.zeros((rest * GROUPS, 128), jnp.float32)], axis=0)
    return stack.T[0:1]


def carried(value, flag):
    rolled = jnp.concatenate([jnp.zeros_like(value[:1]), value[:-1]], axis=0)
    return jnp.where(flag, rolled, value)


def second_kernel(mine, phases1, energies1, arrived, own, send_in, send, acc, note, sems):
    del send_in
    for n in range(2):
        acc[n] = carried(arrived[n], mine[0] == 0)

    def push(k, carry):
        rows = rows_of(k)
        ph, _ = pushed(phases1[rows], energies1[rows], acc[0, pl.ds(k, 1)], acc[1, pl.ds(k, 1)])
        c, s = cos_sin(ph)
        acc[2, pl.ds(k, 1)] = jnp.sum(c, axis=0, keepdims=True)
        acc[3, pl.ds(k, 1)] = jnp.sum(s, axis=0, keepdims=True)
        return carry

    lax.fori_loop(0, GROUPS, push, 0)
    mean = 1.0 / (NBS * BLOCK)
    note[0] = one_row([own[n] for n in range(4)] + [lane_total(acc[2]) * mean, lane_total(acc[3]) * -mean])
    copies = [pltpu.make_async_copy(note.at[0], send.at[n * MESSAGE + 2 * CAP], sems.at[n]) for n in range(PEERS)]
    for copy in copies:
        copy.start()
    for copy in copies:
        copy.wait()


def wide_halves(x):
    high = x.astype(jnp.bfloat16)
    return high, (x - high.astype(jnp.float32)).astype(jnp.bfloat16)


def pick_kernel(mine, recv, places, phases_hbm, energies_hbm, small, index_v, index, amps, notes, phases, energies, sems):
    me = mine[0]
    source = (me - places[0:1] + PEERS) % PEERS
    index_v[...] = folded(source * MESSAGE + places[1:2])
    to_scalar = pltpu.make_async_copy(index_v, index, sems.at[0])
    to_scalar.start()
    lane = lax.broadcasted_iota(jnp.int32, (128, 128), 1)
    for n in range(PEERS):
        notes[n : n + 1] = recv[n * MESSAGE + 2 * CAP]
    sheet = notes[...]
    near = jnp.broadcast_to(notes[pl.ds((me + PEERS - 1) % PEERS, 1)], (128, 128)).T
    far = jnp.broadcast_to(notes[pl.ds((me + PEERS - 2) % PEERS, 1)], (128, 128)).T
    for n in range(2):
        small[n] = carried(near[(4 + n) * GROUPS : (5 + n) * GROUPS], me == 0)
        small[2 + n] = carried(far[(2 + n) * GROUPS : (3 + n) * GROUPS], me < 2)
    wrapped = jnp.concatenate([sheet[127:128, 127:128], sheet[127:128, :127]], axis=1)
    wrapped = jnp.where(lane[0:1] % GROUPS == 0, 0.0, wrapped)
    sheet = jnp.concatenate([wrapped, sheet[:127]], axis=0)
    for n in range(COUNT // 128):
        column = jnp.broadcast_to(source[:, n * 128 : (n + 1) * 128], (128, 128)).T
        onehot = jnp.where(lane == column, 1.0, 0.0)
        amps[n * 128 : (n + 1) * 128] = jnp.dot(
            onehot, sheet, precision=HIGHEST, preferred_element_type=jnp.float32
        )
    to_scalar.wait()

    def get(n, carry):
        base = pl.multiple_of(n * BATCH, BATCH)
        spots = [index[n // (128 // BATCH), n % (128 // BATCH) * BATCH + m] for m in range(BATCH)]
        ph = [recv[spot] for spot in spots]
        en = [recv[spot + CAP] for spot in spots]
        for m in range(BATCH):
            phases[pl.ds(base + m, 1)] = ph[m]
            energies[pl.ds(base + m, 1)] = en[m]
        return carry

    copies = []
    for quarter in range(4):
        lax.fori_loop(quarter * COUNT // BATCH // 4, (quarter + 1) * COUNT // BATCH // 4, get, 0)
        for k in range(quarter * 4, quarter * 4 + 4):
            rows = slice(k * NBS, (k + 1) * NBS)
            re, im = amps[rows, k : k + 1], amps[rows, GROUPS + k : GROUPS + k + 1]
            phases[rows], energies[rows] = pushed(phases[rows], energies[rows], re, im)
        span = pl.ds(quarter * COUNT // 4, COUNT // 4)
        copies.append(pltpu.make_async_copy(phases.at[span], phases_hbm.at[span], sems.at[1 + 2 * quarter]))
        copies.append(pltpu.make_async_copy(energies.at[span], energies_hbm.at[span], sems.at[2 + 2 * quarter]))
        for copy in copies[-2:]:
            copy.start()
    for copy in copies:
        copy.wait()


def twice_diffracted(planes, left, right):
    hi, lo = wide_halves(jnp.concatenate([jnp.concatenate(pair, axis=1) for pair in planes], axis=0))
    half = jnp.dot(jnp.concatenate([hi, lo, hi], axis=1), right[...], preferred_element_type=jnp.float32)
    cols = []
    for m in range(len(planes)):
        mid = half[m * GRID : (m + 1) * GRID]
        cols.append(jnp.concatenate([mid[:, :GRID], mid[:, GRID:]], axis=0))
    hi, lo = wide_halves(jnp.concatenate(cols, axis=1))
    full = jnp.dot(left[...], jnp.concatenate([hi, lo, hi], axis=0), preferred_element_type=jnp.float32)
    cuts = [slice(m * GRID, (m + 1) * GRID) for m in range(len(planes))]
    return [(full[:GRID, cut], full[GRID:, cut]) for cut in cuts]


def early_kernel(mine, piece_0, piece_1, beam, left, right, out):
    even = mine[0] % 2 == 0
    planes = [tuple(jnp.where(even, piece_0[c, k], piece_1[c, k]) for c in range(2)) for k in range(EARLY)]
    planes.append((beam[2], jnp.zeros((GRID, GRID), jnp.float32)))
    for k, (re, im) in enumerate(twice_diffracted(planes, left, right)):
        out[0, k] = re
        out[1, k] = im


def last_kernel(
    mine, early, piece_b0, piece_b1, piece_b2, piece_b3, piece_c, small, beam, left, right, out_hbm, acc, rest, out, sems
):
    me = mine[0]
    for n in range(4):
        acc[n] = GAIN * small[n]
    copies = []

    def plane(c, k):
        if k < 0:
            return jnp.zeros((GRID, GRID), jnp.float32)
        return early[c, k] if k < EARLY else rest[c, k - EARLY]

    def finish(low, high):
        for k in range(low, high):
            cr, ci, br, bi = (acc[n, k : k + 1] for n in range(4))
            re, im = (jnp.where(me < 2, plane(c, k - 1), plane(c, k)) for c in range(2))
            out[0, k] = re + (br * early[0, EARLY] - bi * early[1, EARLY]) + (cr * beam[0] - ci * beam[1])
            out[1, k] = im + (br * early[1, EARLY] + bi * early[0, EARLY]) + (cr * beam[1] + ci * beam[0])
        span = pl.ds(low, high - low)
        for c in range(2):
            copies.append(pltpu.make_async_copy(out.at[c, span], out_hbm.at[c, span], sems.at[len(copies)]))
            copies[-1].start()

    finish(0, EARLY)
    planes = [(piece[0, k], piece[1, k]) for piece in (piece_b0, piece_b1, piece_b2, piece_b3) for k in range(piece.shape[1])]
    for k, (re, im) in enumerate(twice_diffracted(planes, left, right)):
        rest[0, k] = re
        rest[1, k] = im
    finish(EARLY, LATE)
    planes = [(piece_c[0, k], piece_c[1, k]) for k in range(piece_c.shape[1])]
    for k, (re, im) in enumerate(twice_diffracted(planes, left, right)):
        rest[0, LATE - EARLY + k] = re
        rest[1, LATE - EARLY + k] = im
    finish(LATE, GROUPS)
    for copy in copies:
        copy.wait()


def early_pairs(core):
    onward = [(device, (device + 2) % PEERS) for device in range(core, PEERS, 2)]
    across = [(device, (device + 8) % PEERS) for device in range(1 - core, PEERS, 2) if device % 8 >= 6]
    return onward + across


def late_pairs():
    return [(device, device + 2 if device % 8 < 6 else device - 6) for device in range(PEERS)]


def shifted(value, axis, steps):
    count = lax.axis_size(axis)
    pairs = [(source, (source + steps) % count) for source in range(count)]
    return lax.ppermute(value, axis, pairs)


def shape(*dims, dtype=jnp.float32):
    return jax.ShapeDtypeStruct(dims, dtype)


def whole():
    return pl.BlockSpec(memory_space=pltpu.VMEM)


def vmem(*dims, dtype=jnp.float32):
    return pltpu.VMEM(dims, dtype)


def in_hbm(value):
    return pltpu.with_memory_space_constraint(value, pltpu.HBM)


def per_device(field, phase_bins, phase_jitter, energy, profile, delays):
    params = pltpu.CompilerParams(vmem_limit_bytes=VMEM_LIMIT)
    scalar = pl.BlockSpec(memory_space=pltpu.SMEM)
    remain = pl.BlockSpec(memory_space=pltpu.HBM)
    field = field.reshape(2, GROUPS, GRID, GRID)
    bins = phase_bins.reshape(COUNT, BLOCK)
    jitter = phase_jitter.reshape(COUNT, BLOCK)
    energies = energy.reshape(COUNT, BLOCK)
    mine = lax.axis_index("cuts").reshape(1)
    one, two = line_operator(1), line_operator(2)
    left_one = jnp.asarray(np.concatenate(one, axis=0), jnp.float32)
    right_one = jnp.asarray(right_form(*one), jnp.float32)
    core = mine[0] % 2
    shared_0 = lax.ppermute(lax.dynamic_slice_in_dim(field, core * (GROUPS - EARLY), EARLY, 1), "cuts", early_pairs(0))
    shared_1 = lax.ppermute(lax.dynamic_slice_in_dim(field, (1 - core) * (GROUPS - EARLY), EARLY, 1), "cuts", early_pairs(1))
    operands = [field, profile, bins, jitter, energies, delays.reshape(GROUPS, 1, NBS), left_one, right_one]
    send, phases1, energies1, places, beam, small1, *sources = pl.pallas_call(
        first_kernel,
        out_shape=(
            pltpu.HBM((ROWS, 1, BLOCK), jnp.float32),
            shape(COUNT, BLOCK),
            shape(COUNT, BLOCK),
            pltpu.HBM((8, COUNT), jnp.int32),
            pltpu.HBM((3, GRID, GRID), jnp.float32),
            shape(4, GROUPS, 128),
            *[pltpu.HBM((2, high - low, GRID, GRID), jnp.float32) for low, high in MIDDLE],
        ),
        in_specs=[scalar] + [remain] * 8,
        out_specs=(remain, whole(), whole(), remain, whole(), whole()) + (remain,) * len(MIDDLE),
        scratch_shapes=[
            vmem(2, GROUPS, GRID, GRID),
            vmem(GRID, GRID),
            vmem(COUNT, BLOCK, dtype=jnp.int32),
            vmem(COUNT, BLOCK),
            vmem(COUNT, BLOCK),
            vmem(GROUPS, 1, NBS, dtype=jnp.int32),
            vmem(2 * GRID, GRID),
            vmem(2 * GRID, 2 * GRID),
            vmem(6, GROUPS, 128),
            vmem(ROWS, 1, BLOCK),
            vmem(8, COUNT, dtype=jnp.int32),
            vmem(8, 128, dtype=jnp.int32),
            pltpu.SMEM((8, 128), jnp.int32),
            pltpu.SemaphoreType.DMA((17,)),
        ],
        compiler_params=params,
        name="push_place",
    )(mine, *[in_hbm(value) for value in operands])
    arrived1 = shifted(small1, "cuts", 1)
    send = pl.pallas_call(
        second_kernel,
        out_shape=pltpu.HBM((ROWS, 1, BLOCK), jnp.float32),
        in_specs=[scalar] + [whole()] * 4 + [remain],
        out_specs=remain,
        scratch_shapes=[vmem(4, GROUPS, 128), vmem(1, 1, 128), pltpu.SemaphoreType.DMA((PEERS,))],
        input_output_aliases={5: 0},
        compiler_params=params,
        name="second_push",
    )(mine, phases1, energies1, arrived1, small1, in_hbm(send))
    field_b = [shifted(source, "cuts", 2) for source in sources]

    left_two, right_two = deep_left(left_form(*two)), deep_right(right_form(*two))

    def exchange(send, places, field, shared_0, shared_1, beam):
        early = pl.pallas_call(
            early_kernel,
            out_shape=shape(2, EARLY + 1, GRID, GRID),
            in_specs=[scalar] + [whole()] * 5,
            out_specs=whole(),
            compiler_params=params,
            name="early_field",
        )(mine, shared_0, shared_1, beam, left_two, right_two)
        handed = jnp.where(core == 0, shared_1, shared_0)
        source_c = jnp.where(mine[0] % 8 >= 6, handed[:, LATE - GROUPS :], field[:, LATE:])
        field_c = lax.ppermute(source_c, "cuts", late_pairs())
        recv = lax.all_to_all(send, "cuts", split_axis=0, concat_axis=0, tiled=True)
        recv, early = lax.optimization_barrier((recv, early))
        phase_out, energy_out, small = pl.pallas_call(
            pick_kernel,
            out_shape=(shape(COUNT, BLOCK), shape(COUNT, BLOCK), shape(4, GROUPS, 128)),
            in_specs=[scalar] + [whole()] * 2,
            out_specs=(remain, remain, whole()),
            scratch_shapes=[
                vmem(8, 128, dtype=jnp.int32),
                pltpu.SMEM((8, 128), jnp.int32),
                vmem(COUNT, 128),
                vmem(PEERS, 128),
                vmem(COUNT, BLOCK),
                vmem(COUNT, BLOCK),
                pltpu.SemaphoreType.DMA((9,)),
            ],
            compiler_params=params,
            name="pick",
        )(mine, recv, places)
        return phase_out, energy_out, early, field_c, small

    def refuse(*operands):
        sizes = [(COUNT, BLOCK)] * 2 + [(2, n, GRID, GRID) for n in (EARLY + 1, GROUPS - LATE)] + [(4, GROUPS, 128)]
        return tuple(jnp.zeros(size, jnp.float32) for size in sizes)

    phase_out, energy_out, early, field_c, small = lax.cond(
        mine[0] < PEERS, exchange, refuse, send, places, field, shared_0, shared_1, beam
    )
    out = pl.pallas_call(
        last_kernel,
        out_shape=shape(2, GROUPS, GRID, GRID),
        in_specs=[scalar] + [whole()] * 10,
        out_specs=remain,
        scratch_shapes=[
            vmem(4, GROUPS, 128),
            vmem(2, GROUPS - EARLY, GRID, GRID),
            vmem(2, GROUPS, GRID, GRID),
            pltpu.SemaphoreType.DMA((6,)),
        ],
        compiler_params=params,
        name="last_field",
    )(mine, early, *field_b, field_c, small, in_hbm(beam), left_two, right_two)
    return (
        out.reshape(2, GROUPS, 1, GRID, GRID),
        phase_out.reshape(GROUPS, 1, NBS * BLOCK),
        energy_out.reshape(GROUPS, 1, NBS * BLOCK),
    )


def solution(mesh):
    return jax.shard_map(
        per_device,
        mesh=mesh,
        in_specs=(
            P(None, None, "cuts", None, None),
            P(None, "cuts", None),
            P(None, "cuts", None),
            P(None, "cuts", None),
            P(),
            P(),
        ),
        out_specs=(P(None, None, "cuts", None, None), P(None, "cuts", None), P(None, "cuts", None)),
        check_vma=False,
    )
```

```python
import functools
import math

import jax
import jax.numpy as jnp
import ml_dtypes
import numpy as np
from jax import lax
from jax.experimental import pallas as pl
from jax.experimental.pallas import tpu as pltpu
from jax.sharding import PartitionSpec as P

BLOCK = 128
NBINS = 16
KAPPA = 1.0
OMEGA = 1.0
GAIN = 16.0
PHASE_COEF = 20.0
GRID = 128
GROUPS = 16
NBS = 64
COUNT = GROUPS * NBS
PEERS = 128
CAP = 20
MESSAGE = 2 * CAP + 1
ROWS = PEERS * MESSAGE
BATCH = 16
EARLY, LATE = 5, 13
MIDDLE = ((5, 7), (7, 9), (9, 13))
VMEM_LIMIT = 16 * 1024 * 1024
HIGHEST = lax.Precision.HIGHEST


def line_operator(power):
    index = np.arange(GRID)
    freq = ((index + GRID // 2) % GRID - GRID // 2) / GRID
    weight = np.exp(-1j * PHASE_COEF * power * freq**2)
    wave = np.exp(2j * np.pi * (index[:, None] * index[None, :] % GRID) / GRID)
    column = wave @ weight / GRID
    matrix = column[(index[:, None] - index[None, :]) % GRID]
    return matrix.real, matrix.imag


def left_form(real, imag):
    return np.block([[real, -imag], [imag, real]])


def right_form(real, imag):
    return np.block([[real, imag], [-imag, real]])


def halves(matrix):
    high = matrix.astype(ml_dtypes.bfloat16)
    return high, (matrix - high.astype(np.float64)).astype(ml_dtypes.bfloat16)


def deep_left(matrix):
    high, low = halves(matrix)
    return jnp.asarray(np.concatenate([high, high, low], axis=1))


def deep_right(matrix):
    high, low = halves(matrix)
    return jnp.asarray(np.concatenate([high, high, low], axis=0))


def fitted(function, degree):
    top = (math.pi / 2 + 0.01) ** 2
    nodes = (np.cos(np.pi * (np.arange(400) + 0.5) / 400) + 1) / 2 * top
    series = np.polynomial.chebyshev.Chebyshev.fit(nodes, function(np.sqrt(nodes)), degree, domain=[0, top])
    return [float(c) for c in series.convert(kind=np.polynomial.Polynomial).coef]


SIN_COEF = fitted(lambda r: np.sin(r) / r, 5)
COS_COEF = fitted(np.cos, 6)
PI_HIGH = 3.140625
PI_MID = 9.67502593994140625e-4
PI_LOW = math.pi - PI_HIGH - PI_MID


def horner(coefs, x):
    value = jnp.float32(coefs[-1])
    for c in coefs[-2::-1]:
        value = value * x + jnp.float32(c)
    return value


def cos_sin(x):
    turns = jnp.round(x * jnp.float32(1.0 / math.pi))
    r = x - turns * jnp.float32(PI_HIGH)
    r = r - turns * jnp.float32(PI_MID)
    r = r - turns * jnp.float32(PI_LOW)
    half = turns * 0.5
    sign = 1.0 - 4.0 * jnp.abs(half - jnp.round(half))
    square = r * r
    return horner(COS_COEF, square) * sign, horner(SIN_COEF, square) * (r * sign)


def lane_total(rows):
    return jnp.broadcast_to(jnp.sum(rows, axis=1, keepdims=True), rows.shape)


def slots_of(delays):
    row = jnp.concatenate([delays[k] for k in range(GROUPS)], axis=1)
    values = lax.broadcasted_iota(jnp.int32, (PEERS, COUNT), 0)
    onehot = jnp.where(values == row, 1.0, 0.0)
    before = lax.broadcasted_iota(jnp.int32, (COUNT, COUNT), 0) < lax.broadcasted_iota(jnp.int32, (COUNT, COUNT), 1)
    upper = jnp.where(before, 1.0, 0.0).astype(jnp.bfloat16)
    earlier = jnp.dot(onehot.astype(jnp.bfloat16), upper, preferred_element_type=jnp.float32)
    return row, jnp.sum(earlier * onehot, axis=0, keepdims=True).astype(jnp.int32)


def folded(row):
    return jnp.concatenate([row[:, n * 128 : (n + 1) * 128] for n in range(COUNT // 128)], axis=0)


def rows_of(k):
    return pl.ds(pl.multiple_of(k * NBS, NBS), NBS)


def first_kernel(
    mine, field_hbm, profile_hbm, bins_hbm, jitter_hbm, energy_hbm, delays_hbm, left_hbm, right_hbm,
    send_hbm, phases, energies, places_hbm, beam, small, middle_0, middle_1, middle_2,
    field, profile, bins, jitter, energy, delays, left, right, acc, send, places, index_v, index, sems,
):
    pairs = [
        (profile_hbm, profile), (left_hbm, left), (right_hbm, right), (delays_hbm, delays),
        (field_hbm, field), (bins_hbm, bins), (jitter_hbm, jitter), (energy_hbm, energy),
    ]
    copies = [pltpu.make_async_copy(src, dst, sems.at[n]) for n, (src, dst) in enumerate(pairs)]
    for copy in copies:
        copy.start()
    copies[3].wait()
    row, slot = slots_of(delays)
    places[0:1] = row
    places[1:2] = slot
    index_v[...] = folded(((mine[0] + row) % PEERS) * MESSAGE + slot)
    to_scalar = pltpu.make_async_copy(index_v, index, sems.at[3])
    to_scalar.start()
    for copy in copies[:3]:
        copy.wait()
    p = profile[...]
    half = jnp.dot(left[...], p, precision=HIGHEST, preferred_element_type=jnp.float32)
    both = jnp.concatenate([half[:GRID], half[GRID:]], axis=1)
    spread = jnp.dot(both, right[...], precision=HIGHEST, preferred_element_type=jnp.float32)
    beam[0] = spread[:, :GRID]
    beam[1] = spread[:, GRID:]
    beam[2] = p
    copies[4].wait()
    kept = [pltpu.make_async_copy(places, places_hbm, sems.at[8])]
    for middle, (low, high) in zip((middle_0, middle_1, middle_2), MIDDLE):
        for c in range(2):
            span = pl.ds(low, high - low)
            kept.append(pltpu.make_async_copy(field.at[c, span], middle.at[c], sems.at[8 + len(kept)]))
    for copy in kept:
        copy.start()

    def project(k, carry):
        re, im = field[0, k], field[1, k]
        dr, di, q = beam[0], beam[1], profile[...]
        acc[0, pl.ds(k, 1)] = jnp.sum(q * re, axis=0, keepdims=True)
        acc[1, pl.ds(k, 1)] = jnp.sum(q * im, axis=0, keepdims=True)
        acc[2, pl.ds(k, 1)] = jnp.sum(dr * re - di * im, axis=0, keepdims=True)
        acc[3, pl.ds(k, 1)] = jnp.sum(dr * im + di * re, axis=0, keepdims=True)
        return carry

    lax.fori_loop(0, GROUPS, project, 0)
    self_re = jnp.sum(p * beam[0])
    self_im = jnp.sum(p * beam[1])
    for n in range(4):
        acc[n] = lane_total(acc[n]) * (1.0 / GRID)
    for copy in copies[5:]:
        copy.wait()

    def push(k, carry):
        rows = rows_of(k)
        ph = jnp.float32(2.0 * math.pi / NBINS) * (bins[rows].astype(jnp.float32) + jitter[rows])
        ph, en = pushed(ph, energy[rows], acc[0, pl.ds(k, 1)], acc[1, pl.ds(k, 1)])
        phases[rows] = ph
        energies[rows] = en
        c, s = cos_sin(ph)
        acc[4, pl.ds(k, 1)] = jnp.sum(c, axis=0, keepdims=True)
        acc[5, pl.ds(k, 1)] = jnp.sum(s, axis=0, keepdims=True)
        return carry

    lax.fori_loop(0, GROUPS, push, 0)
    to_scalar.wait()

    def put(n, carry):
        base = pl.multiple_of(n * BATCH, BATCH)
        spots = [index[n // (128 // BATCH), n % (128 // BATCH) * BATCH + m] for m in range(BATCH)]
        ph = [phases[pl.ds(base + m, 1)] for m in range(BATCH)]
        en = [energies[pl.ds(base + m, 1)] for m in range(BATCH)]
        for m in range(BATCH):
            send[spots[m]] = ph[m]
            send[spots[m] + CAP] = en[m]
        return carry

    lax.fori_loop(0, COUNT // BATCH, put, 0, unroll=4)
    bre = lane_total(acc[4]) * (1.0 / (NBS * BLOCK))
    bim = lane_total(acc[5]) * (-1.0 / (NBS * BLOCK))
    gain = GAIN / GRID
    next_re = acc[2] + gain * (bre * self_re - bim * self_im)
    next_im = acc[3] + gain * (bre * self_im + bim * self_re)
    for n, part in enumerate((next_re, next_im, bre, bim)):
        small[n] = part
    out = pltpu.make_async_copy(send, send_hbm, sems.at[0])
    out.start()
    for copy in kept:
        copy.wait()
    out.wait()


def pushed(ph, en, amp_re, amp_im):
    c, s = cos_sin(ph)
    en = en - KAPPA * (amp_re * c - amp_im * s)
    return ph + OMEGA * en, en


def one_row(parts):
    rest = 128 // GROUPS - len(parts)
    stack = jnp.concatenate(parts + [jnp.zeros((rest * GROUPS, 128), jnp.float32)], axis=0)
    return stack.T[0:1]


def carried(value, flag):
    rolled = jnp.concatenate([jnp.zeros_like(value[:1]), value[:-1]], axis=0)
    return jnp.where(flag, rolled, value)


def second_kernel(mine, phases1, energies1, arrived, own, send_in, send, acc, note, sem):
    del send_in
    for n in range(2):
        acc[n] = carried(arrived[n], mine[0] == 0)

    def push(k, carry):
        rows = rows_of(k)
        ph, _ = pushed(phases1[rows], energies1[rows], acc[0, pl.ds(k, 1)], acc[1, pl.ds(k, 1)])
        c, s = cos_sin(ph)
        acc[2, pl.ds(k, 1)] = jnp.sum(c, axis=0, keepdims=True)
        acc[3, pl.ds(k, 1)] = jnp.sum(s, axis=0, keepdims=True)
        return carry

    lax.fori_loop(0, GROUPS, push, 0)
    mean = 1.0 / (NBS * BLOCK)
    row = one_row([own[n] for n in range(4)] + [lane_total(acc[2]) * mean, lane_total(acc[3]) * -mean])
    note[...] = jnp.broadcast_to(row[None], (PEERS, 1, 128))
    copy = pltpu.make_async_copy(note, send.at[:, 2 * CAP], sem)
    copy.start()
    copy.wait()


def wide_halves(x):
    high = x.astype(jnp.bfloat16)
    return high, (x - high.astype(jnp.float32)).astype(jnp.bfloat16)


def pick_kernel(mine, recv, places, phases_hbm, energies_hbm, small, index_v, index, amps, notes, phases, energies, sems):
    me = mine[0]
    source = (me - places[0:1] + PEERS) % PEERS
    index_v[...] = folded(source * MESSAGE + places[1:2])
    to_scalar = pltpu.make_async_copy(index_v, index, sems.at[0])
    to_scalar.start()
    lane = lax.broadcasted_iota(jnp.int32, (128, 128), 1)
    for n in range(PEERS):
        notes[n : n + 1] = recv[n * MESSAGE + 2 * CAP]
    sheet = notes[...]
    near = jnp.broadcast_to(notes[pl.ds((me + PEERS - 1) % PEERS, 1)], (128, 128)).T
    far = jnp.broadcast_to(notes[pl.ds((me + PEERS - 2) % PEERS, 1)], (128, 128)).T
    for n in range(2):
        small[n] = carried(near[(4 + n) * GROUPS : (5 + n) * GROUPS], me == 0)
        small[2 + n] = carried(far[(2 + n) * GROUPS : (3 + n) * GROUPS], me < 2)
    wrapped = jnp.concatenate([sheet[127:128, 127:128], sheet[127:128, :127]], axis=1)
    wrapped = jnp.where(lane[0:1] % GROUPS == 0, 0.0, wrapped)
    sheet = jnp.concatenate([wrapped, sheet[:127]], axis=0)
    for n in range(COUNT // 128):
        column = jnp.broadcast_to(source[:, n * 128 : (n + 1) * 128], (128, 128)).T
        onehot = jnp.where(lane == column, 1.0, 0.0)
        amps[n * 128 : (n + 1) * 128] = jnp.dot(
            onehot, sheet, precision=HIGHEST, preferred_element_type=jnp.float32
        )
    to_scalar.wait()

    def get(n, carry):
        base = pl.multiple_of(n * BATCH, BATCH)
        spots = [index[n // (128 // BATCH), n % (128 // BATCH) * BATCH + m] for m in range(BATCH)]
        ph = [recv[spot] for spot in spots]
        en = [recv[spot + CAP] for spot in spots]
        for m in range(BATCH):
            phases[pl.ds(base + m, 1)] = ph[m]
            energies[pl.ds(base + m, 1)] = en[m]
        return carry

    copies = []
    for quarter in range(4):
        lax.fori_loop(quarter * COUNT // BATCH // 4, (quarter + 1) * COUNT // BATCH // 4, get, 0, unroll=4)
        for k in range(quarter * 4, quarter * 4 + 4):
            rows = slice(k * NBS, (k + 1) * NBS)
            re, im = amps[rows, k : k + 1], amps[rows, GROUPS + k : GROUPS + k + 1]
            phases[rows], energies[rows] = pushed(phases[rows], energies[rows], re, im)
        span = pl.ds(quarter * COUNT // 4, COUNT // 4)
        copies.append(pltpu.make_async_copy(phases.at[span], phases_hbm.at[span], sems.at[1 + 2 * quarter]))
        copies.append(pltpu.make_async_copy(energies.at[span], energies_hbm.at[span], sems.at[2 + 2 * quarter]))
        for copy in copies[-2:]:
            copy.start()
    for copy in copies:
        copy.wait()


def twice_diffracted(planes, left, right):
    hi, lo = wide_halves(jnp.concatenate([jnp.concatenate(pair, axis=1) for pair in planes], axis=0))
    half = jnp.dot(jnp.concatenate([hi, lo, hi], axis=1), right[...], preferred_element_type=jnp.float32)
    cols = []
    for m in range(len(planes)):
        mid = half[m * GRID : (m + 1) * GRID]
        cols.append(jnp.concatenate([mid[:, :GRID], mid[:, GRID:]], axis=0))
    hi, lo = wide_halves(jnp.concatenate(cols, axis=1))
    full = jnp.dot(left[...], jnp.concatenate([hi, lo, hi], axis=0), preferred_element_type=jnp.float32)
    cuts = [slice(m * GRID, (m + 1) * GRID) for m in range(len(planes))]
    return [(full[:GRID, cut], full[GRID:, cut]) for cut in cuts]


def early_kernel(mine, piece_0, piece_1, beam, left, right, out):
    even = mine[0] % 2 == 0
    planes = [tuple(jnp.where(even, piece_0[c, k], piece_1[c, k]) for c in range(2)) for k in range(EARLY)]
    planes.append((beam[2], jnp.zeros((GRID, GRID), jnp.float32)))
    for k, (re, im) in enumerate(twice_diffracted(planes, left, right)):
        out[0, k] = re
        out[1, k] = im


def last_kernel(
    mine, early, piece_b0, piece_b1, piece_b2, piece_c, small, beam, left, right, out_hbm, acc, rest, out, sems
):
    me = mine[0]
    for n in range(4):
        acc[n] = GAIN * small[n]
    copies = []

    def plane(c, k):
        if k < 0:
            return jnp.zeros((GRID, GRID), jnp.float32)
        return early[c, k] if k < EARLY else rest[c, k - EARLY]

    def finish(low, high):
        for k in range(low, high):
            cr, ci, br, bi = (acc[n, k : k + 1] for n in range(4))
            re, im = (jnp.where(me < 2, plane(c, k - 1), plane(c, k)) for c in range(2))
            out[0, k] = re + (br * early[0, EARLY] - bi * early[1, EARLY]) + (cr * beam[0] - ci * beam[1])
            out[1, k] = im + (br * early[1, EARLY] + bi * early[0, EARLY]) + (cr * beam[1] + ci * beam[0])
        span = pl.ds(low, high - low)
        for c in range(2):
            copies.append(pltpu.make_async_copy(out.at[c, span], out_hbm.at[c, span], sems.at[len(copies)]))
            copies[-1].start()

    finish(0, EARLY)
    planes = [(piece[0, k], piece[1, k]) for piece in (piece_b0, piece_b1, piece_b2) for k in range(piece.shape[1])]
    for k, (re, im) in enumerate(twice_diffracted(planes, left, right)):
        rest[0, k] = re
        rest[1, k] = im
    finish(EARLY, LATE)
    planes = [(piece_c[0, k], piece_c[1, k]) for k in range(piece_c.shape[1])]
    for k, (re, im) in enumerate(twice_diffracted(planes, left, right)):
        rest[0, LATE - EARLY + k] = re
        rest[1, LATE - EARLY + k] = im
    finish(LATE, GROUPS)
    for copy in copies:
        copy.wait()


def early_pairs(core):
    onward = [(device, (device + 2) % PEERS) for device in range(core, PEERS, 2)]
    across = [(device, (device + 8) % PEERS) for device in range(1 - core, PEERS, 2) if device % 8 >= 6]
    return onward + across


def late_pairs():
    return [(device, device + 2 if device % 8 < 6 else device - 6) for device in range(PEERS)]


def shifted(value, axis, steps):
    count = lax.axis_size(axis)
    pairs = [(source, (source + steps) % count) for source in range(count)]
    return lax.ppermute(value, axis, pairs)


def shape(*dims, dtype=jnp.float32):
    return jax.ShapeDtypeStruct(dims, dtype)


def whole():
    return pl.BlockSpec(memory_space=pltpu.VMEM)


def vmem(*dims, dtype=jnp.float32):
    return pltpu.VMEM(dims, dtype)


def in_hbm(value):
    return pltpu.with_memory_space_constraint(value, pltpu.HBM)


def per_device(field, phase_bins, phase_jitter, energy, profile, delays):
    params = pltpu.CompilerParams(vmem_limit_bytes=VMEM_LIMIT)
    scalar = pl.BlockSpec(memory_space=pltpu.SMEM)
    remain = pl.BlockSpec(memory_space=pltpu.HBM)
    field = field.reshape(2, GROUPS, GRID, GRID)
    bins = phase_bins.reshape(COUNT, BLOCK)
    jitter = phase_jitter.reshape(COUNT, BLOCK)
    energies = energy.reshape(COUNT, BLOCK)
    mine = lax.axis_index("cuts").reshape(1)
    one, two = line_operator(1), line_operator(2)
    left_one = jnp.asarray(np.concatenate(one, axis=0), jnp.float32)
    right_one = jnp.asarray(right_form(*one), jnp.float32)
    core = mine[0] % 2
    shared_0 = lax.ppermute(lax.dynamic_slice_in_dim(field, core * (GROUPS - EARLY), EARLY, 1), "cuts", early_pairs(0))
    shared_1 = lax.ppermute(lax.dynamic_slice_in_dim(field, (1 - core) * (GROUPS - EARLY), EARLY, 1), "cuts", early_pairs(1))
    operands = [field, profile, bins, jitter, energies, delays.reshape(GROUPS, 1, NBS), left_one, right_one]
    send, phases1, energies1, places, beam, small1, *sources = pl.pallas_call(
        first_kernel,
        out_shape=(
            pltpu.HBM((ROWS, 1, BLOCK), jnp.float32),
            shape(COUNT, BLOCK),
            shape(COUNT, BLOCK),
            pltpu.HBM((8, COUNT), jnp.int32),
            pltpu.HBM((3, GRID, GRID), jnp.float32),
            shape(4, GROUPS, 128),
            *[pltpu.HBM((2, high - low, GRID, GRID), jnp.float32) for low, high in MIDDLE],
        ),
        in_specs=[scalar] + [remain] * 8,
        out_specs=(remain, whole(), whole(), remain, whole(), whole()) + (remain,) * len(MIDDLE),
        scratch_shapes=[
            vmem(2, GROUPS, GRID, GRID),
            vmem(GRID, GRID),
            vmem(COUNT, BLOCK, dtype=jnp.int32),
            vmem(COUNT, BLOCK),
            vmem(COUNT, BLOCK),
            vmem(GROUPS, 1, NBS, dtype=jnp.int32),
            vmem(2 * GRID, GRID),
            vmem(2 * GRID, 2 * GRID),
            vmem(6, GROUPS, 128),
            vmem(ROWS, 1, BLOCK),
            vmem(8, COUNT, dtype=jnp.int32),
            vmem(8, 128, dtype=jnp.int32),
            pltpu.SMEM((8, 128), jnp.int32),
            pltpu.SemaphoreType.DMA((17,)),
        ],
        compiler_params=params,
        name="push_place",
    )(mine, *[in_hbm(value) for value in operands])
    arrived1 = shifted(small1, "cuts", 1)
    arrived1, sources[2] = lax.optimization_barrier((arrived1, sources[2]))
    send = pl.pallas_call(
        second_kernel,
        out_shape=pltpu.HBM((PEERS, MESSAGE, 1, BLOCK), jnp.float32),
        in_specs=[scalar] + [whole()] * 4 + [remain],
        out_specs=remain,
        scratch_shapes=[vmem(4, GROUPS, 128), vmem(PEERS, 1, 128), pltpu.SemaphoreType.DMA],
        input_output_aliases={5: 0},
        compiler_params=params,
        name="second_push",
    )(mine, phases1, energies1, arrived1, small1, in_hbm(send.reshape(PEERS, MESSAGE, 1, BLOCK)))
    field_b = [shifted(source, "cuts", 2) for source in sources]

    left_two, right_two = deep_left(left_form(*two)), deep_right(right_form(*two))

    def exchange(send, places, field, shared_0, shared_1, beam):
        early = pl.pallas_call(
            early_kernel,
            out_shape=shape(2, EARLY + 1, GRID, GRID),
            in_specs=[scalar] + [whole()] * 5,
            out_specs=whole(),
            compiler_params=params,
            name="early_field",
        )(mine, shared_0, shared_1, beam, left_two, right_two)
        handed = jnp.where(core == 0, shared_1, shared_0)
        source_c = jnp.where(mine[0] % 8 >= 6, handed[:, LATE - GROUPS :], field[:, LATE:])
        field_c = lax.ppermute(source_c, "cuts", late_pairs())
        recv = lax.all_to_all(send.reshape(ROWS, 1, BLOCK), "cuts", split_axis=0, concat_axis=0, tiled=True)
        recv, early = lax.optimization_barrier((recv, early))
        phase_out, energy_out, small = pl.pallas_call(
            pick_kernel,
            out_shape=(shape(COUNT, BLOCK), shape(COUNT, BLOCK), shape(4, GROUPS, 128)),
            in_specs=[scalar] + [whole()] * 2,
            out_specs=(remain, remain, whole()),
            scratch_shapes=[
                vmem(8, 128, dtype=jnp.int32),
                pltpu.SMEM((8, 128), jnp.int32),
                vmem(COUNT, 128),
                vmem(PEERS, 128),
                vmem(COUNT, BLOCK),
                vmem(COUNT, BLOCK),
                pltpu.SemaphoreType.DMA((9,)),
            ],
            compiler_params=params,
            name="pick",
        )(mine, recv, places)
        return phase_out, energy_out, early, field_c, small

    def refuse(*operands):
        sizes = [(COUNT, BLOCK)] * 2 + [(2, n, GRID, GRID) for n in (EARLY + 1, GROUPS - LATE)] + [(4, GROUPS, 128)]
        return tuple(jnp.zeros(size, jnp.float32) for size in sizes)

    phase_out, energy_out, early, field_c, small = lax.cond(
        mine[0] < PEERS, exchange, refuse, send, places, field, shared_0, shared_1, beam
    )
    out = pl.pallas_call(
        last_kernel,
        out_shape=shape(2, GROUPS, GRID, GRID),
        in_specs=[scalar] + [whole()] * 9,
        out_specs=remain,
        scratch_shapes=[
            vmem(4, GROUPS, 128),
            vmem(2, GROUPS - EARLY, GRID, GRID),
            vmem(2, GROUPS, GRID, GRID),
            pltpu.SemaphoreType.DMA((6,)),
        ],
        compiler_params=params,
        name="last_field",
    )(mine, early, *field_b, field_c, small, in_hbm(beam), left_two, right_two)
    return (
        out.reshape(2, GROUPS, 1, GRID, GRID),
        phase_out.reshape(GROUPS, 1, NBS * BLOCK),
        energy_out.reshape(GROUPS, 1, NBS * BLOCK),
    )


def solution(mesh):
    return jax.shard_map(
        per_device,
        mesh=mesh,
        in_specs=(
            P(None, None, "cuts", None, None),
            P(None, "cuts", None),
            P(None, "cuts", None),
            P(None, "cuts", None),
            P(),
            P(),
        ),
        out_specs=(P(None, None, "cuts", None, None), P(None, "cuts", None), P(None, "cuts", None)),
        check_vma=False,
    )
```

```python
import functools
import math

import jax
import jax.numpy as jnp
import ml_dtypes
import numpy as np
from jax import lax
from jax.experimental import pallas as pl
from jax.experimental.pallas import tpu as pltpu
from jax.sharding import PartitionSpec as P

BLOCK = 128
NBINS = 16
KAPPA = 1.0
OMEGA = 1.0
GAIN = 16.0
PHASE_COEF = 20.0
GRID = 128
GROUPS = 16
NBS = 64
COUNT = GROUPS * NBS
PEERS = 128
CAP = 20
MESSAGE = 2 * CAP + 1
ROWS = PEERS * MESSAGE
BATCH = 32
EARLY, LATE = 5, 13
MIDDLE = ((5, 7), (7, 9), (9, 11), (11, 13))
VMEM_LIMIT = 24 * 1024 * 1024
HIGHEST = lax.Precision.HIGHEST


def line_operator(power):
    index = np.arange(GRID)
    freq = ((index + GRID // 2) % GRID - GRID // 2) / GRID
    weight = np.exp(-1j * PHASE_COEF * power * freq**2)
    wave = np.exp(2j * np.pi * (index[:, None] * index[None, :] % GRID) / GRID)
    column = wave @ weight / GRID
    matrix = column[(index[:, None] - index[None, :]) % GRID]
    return matrix.real, matrix.imag


def left_form(real, imag):
    return np.block([[real, -imag], [imag, real]])


def right_form(real, imag):
    return np.block([[real, imag], [-imag, real]])


def halves(matrix):
    high = matrix.astype(ml_dtypes.bfloat16)
    return high, (matrix - high.astype(np.float64)).astype(ml_dtypes.bfloat16)


def deep_left(matrix):
    high, low = halves(matrix)
    return jnp.asarray(np.concatenate([high, high, low], axis=1))


def deep_right(matrix):
    high, low = halves(matrix)
    return jnp.asarray(np.concatenate([high, high, low], axis=0))


def fitted(function, degree):
    top = (math.pi / 2 + 0.01) ** 2
    nodes = (np.cos(np.pi * (np.arange(400) + 0.5) / 400) + 1) / 2 * top
    series = np.polynomial.chebyshev.Chebyshev.fit(nodes, function(np.sqrt(nodes)), degree, domain=[0, top])
    return [float(c) for c in series.convert(kind=np.polynomial.Polynomial).coef]


SIN_COEF = fitted(lambda r: np.sin(r) / r, 5)
COS_COEF = fitted(np.cos, 6)
PI_HIGH = 3.140625
PI_MID = 9.67502593994140625e-4
PI_LOW = math.pi - PI_HIGH - PI_MID


def horner(coefs, x):
    value = jnp.float32(coefs[-1])
    for c in coefs[-2::-1]:
        value = value * x + jnp.float32(c)
    return value


def cos_sin(x):
    turns = jnp.round(x * jnp.float32(1.0 / math.pi))
    r = x - turns * jnp.float32(PI_HIGH)
    r = r - turns * jnp.float32(PI_MID)
    r = r - turns * jnp.float32(PI_LOW)
    half = turns * 0.5
    sign = 1.0 - 4.0 * jnp.abs(half - jnp.round(half))
    square = r * r
    return horner(COS_COEF, square) * sign, horner(SIN_COEF, square) * (r * sign)


def lane_total(rows):
    return jnp.broadcast_to(jnp.sum(rows, axis=1, keepdims=True), rows.shape)


def slots_of(delays):
    row = jnp.concatenate([delays[k] for k in range(GROUPS)], axis=1)
    values = lax.broadcasted_iota(jnp.int32, (PEERS, COUNT), 0)
    onehot = jnp.where(values == row, 1.0, 0.0)
    before = lax.broadcasted_iota(jnp.int32, (COUNT, COUNT), 0) < lax.broadcasted_iota(jnp.int32, (COUNT, COUNT), 1)
    upper = jnp.where(before, 1.0, 0.0).astype(jnp.bfloat16)
    earlier = jnp.dot(onehot.astype(jnp.bfloat16), upper, preferred_element_type=jnp.float32)
    return row, jnp.sum(earlier * onehot, axis=0, keepdims=True).astype(jnp.int32)


def folded(row):
    return jnp.concatenate([row[:, n * 128 : (n + 1) * 128] for n in range(COUNT // 128)], axis=0)


def rows_of(k):
    return pl.ds(pl.multiple_of(k * NBS, NBS), NBS)


def first_kernel(
    mine, field_hbm, profile_hbm, bins_hbm, jitter_hbm, energy_hbm, delays_hbm, left_hbm, right_hbm,
    send_hbm, phases, energies, places_hbm, beam, small, middle_0, middle_1, middle_2, middle_3,
    field, profile, bins, jitter, energy, delays, left, right, acc, send, places, index_v, index, sems,
):
    pairs = [
        (profile_hbm, profile), (left_hbm, left), (right_hbm, right), (delays_hbm, delays),
        (field_hbm, field), (bins_hbm, bins), (jitter_hbm, jitter), (energy_hbm, energy),
    ]
    copies = [pltpu.make_async_copy(src, dst, sems.at[n]) for n, (src, dst) in enumerate(pairs)]
    for copy in copies:
        copy.start()
    copies[3].wait()
    row, slot = slots_of(delays)
    places[0:1] = row
    places[1:2] = slot
    index_v[...] = folded(((mine[0] + row) % PEERS) * MESSAGE + slot)
    to_scalar = pltpu.make_async_copy(index_v, index, sems.at[3])
    to_scalar.start()
    for copy in copies[:3]:
        copy.wait()
    p = profile[...]
    half = jnp.dot(left[...], p, precision=HIGHEST, preferred_element_type=jnp.float32)
    both = jnp.concatenate([half[:GRID], half[GRID:]], axis=1)
    spread = jnp.dot(both, right[...], precision=HIGHEST, preferred_element_type=jnp.float32)
    beam[0] = spread[:, :GRID]
    beam[1] = spread[:, GRID:]
    beam[2] = p
    copies[4].wait()
    kept = [pltpu.make_async_copy(places, places_hbm, sems.at[8])]
    for middle, (low, high) in zip((middle_0, middle_1, middle_2, middle_3), MIDDLE):
        for c in range(2):
            span = pl.ds(low, high - low)
            kept.append(pltpu.make_async_copy(field.at[c, span], middle.at[c], sems.at[8 + len(kept)]))
    for copy in kept:
        copy.start()

    def project(k, carry):
        re, im = field[0, k], field[1, k]
        dr, di, q = beam[0], beam[1], profile[...]
        acc[0, pl.ds(k, 1)] = jnp.sum(q * re, axis=0, keepdims=True)
        acc[1, pl.ds(k, 1)] = jnp.sum(q * im, axis=0, keepdims=True)
        acc[2, pl.ds(k, 1)] = jnp.sum(dr * re - di * im, axis=0, keepdims=True)
        acc[3, pl.ds(k, 1)] = jnp.sum(dr * im + di * re, axis=0, keepdims=True)
        return carry

    lax.fori_loop(0, GROUPS, project, 0)
    self_re = jnp.sum(p * beam[0])
    self_im = jnp.sum(p * beam[1])
    for n in range(4):
        acc[n] = lane_total(acc[n]) * (1.0 / GRID)
    for copy in copies[5:]:
        copy.wait()

    def push(k, carry):
        rows = rows_of(k)
        ph = jnp.float32(2.0 * math.pi / NBINS) * (bins[rows].astype(jnp.float32) + jitter[rows])
        ph, en = pushed(ph, energy[rows], acc[0, pl.ds(k, 1)], acc[1, pl.ds(k, 1)])
        phases[rows] = ph
        energies[rows] = en
        c, s = cos_sin(ph)
        acc[4, pl.ds(k, 1)] = jnp.sum(c, axis=0, keepdims=True)
        acc[5, pl.ds(k, 1)] = jnp.sum(s, axis=0, keepdims=True)
        return carry

    lax.fori_loop(0, GROUPS, push, 0)
    to_scalar.wait()

    def put(n, carry):
        base = pl.multiple_of(n * BATCH, BATCH)
        spots = [index[n // (128 // BATCH), n % (128 // BATCH) * BATCH + m] for m in range(BATCH)]
        ph = [phases[pl.ds(base + m, 1)] for m in range(BATCH)]
        en = [energies[pl.ds(base + m, 1)] for m in range(BATCH)]
        for m in range(BATCH):
            send[spots[m]] = ph[m]
            send[spots[m] + CAP] = en[m]
        return carry

    lax.fori_loop(0, COUNT // BATCH, put, 0)
    bre = lane_total(acc[4]) * (1.0 / (NBS * BLOCK))
    bim = lane_total(acc[5]) * (-1.0 / (NBS * BLOCK))
    gain = GAIN / GRID
    next_re = acc[2] + gain * (bre * self_re - bim * self_im)
    next_im = acc[3] + gain * (bre * self_im + bim * self_re)
    for n, part in enumerate((next_re, next_im, bre, bim)):
        small[n] = part
    out = pltpu.make_async_copy(send, send_hbm, sems.at[0])
    out.start()
    for copy in kept:
        copy.wait()
    out.wait()


def pushed(ph, en, amp_re, amp_im):
    c, s = cos_sin(ph)
    en = en - KAPPA * (amp_re * c - amp_im * s)
    return ph + OMEGA * en, en


def one_row(parts):
    rest = 128 // GROUPS - len(parts)
    stack = jnp.concatenate(parts + [jnp.zeros((rest * GROUPS, 128), jnp.float32)], axis=0)
    return stack.T[0:1]


def carried(value, flag):
    rolled = jnp.concatenate([jnp.zeros_like(value[:1]), value[:-1]], axis=0)
    return jnp.where(flag, rolled, value)


def second_kernel(mine, phases1, energies1, arrived, own, send_in, send, acc, note, sem):
    del send_in
    for n in range(2):
        acc[n] = carried(arrived[n], mine[0] == 0)

    def push(k, carry):
        rows = rows_of(k)
        ph, _ = pushed(phases1[rows], energies1[rows], acc[0, pl.ds(k, 1)], acc[1, pl.ds(k, 1)])
        c, s = cos_sin(ph)
        acc[2, pl.ds(k, 1)] = jnp.sum(c, axis=0, keepdims=True)
        acc[3, pl.ds(k, 1)] = jnp.sum(s, axis=0, keepdims=True)
        return carry

    lax.fori_loop(0, GROUPS, push, 0)
    mean = 1.0 / (NBS * BLOCK)
    row = one_row([own[n] for n in range(4)] + [lane_total(acc[2]) * mean, lane_total(acc[3]) * -mean])
    note[...] = jnp.broadcast_to(row[None], (PEERS, 1, 128))
    copy = pltpu.make_async_copy(note, send.at[:, 2 * CAP], sem)
    copy.start()
    copy.wait()


def wide_halves(x):
    high = x.astype(jnp.bfloat16)
    return high, (x - high.astype(jnp.float32)).astype(jnp.bfloat16)


def pick_kernel(mine, recv, places, phases_hbm, energies_hbm, small, index_v, index, amps, notes, phases, energies, sems):
    me = mine[0]
    source = (me - places[0:1] + PEERS) % PEERS
    index_v[...] = folded(source * MESSAGE + places[1:2])
    to_scalar = pltpu.make_async_copy(index_v, index, sems.at[0])
    to_scalar.start()
    lane = lax.broadcasted_iota(jnp.int32, (128, 128), 1)
    for n in range(PEERS):
        notes[n : n + 1] = recv[n * MESSAGE + 2 * CAP]
    sheet = notes[...]
    near = jnp.broadcast_to(notes[pl.ds((me + PEERS - 1) % PEERS, 1)], (128, 128)).T
    far = jnp.broadcast_to(notes[pl.ds((me + PEERS - 2) % PEERS, 1)], (128, 128)).T
    for n in range(2):
        small[n] = carried(near[(4 + n) * GROUPS : (5 + n) * GROUPS], me == 0)
        small[2 + n] = carried(far[(2 + n) * GROUPS : (3 + n) * GROUPS], me < 2)
    wrapped = jnp.concatenate([sheet[127:128, 127:128], sheet[127:128, :127]], axis=1)
    wrapped = jnp.where(lane[0:1] % GROUPS == 0, 0.0, wrapped)
    sheet = jnp.concatenate([wrapped, sheet[:127]], axis=0)
    for n in range(COUNT // 128):
        column = jnp.broadcast_to(source[:, n * 128 : (n + 1) * 128], (128, 128)).T
        onehot = jnp.where(lane == column, 1.0, 0.0)
        amps[n * 128 : (n + 1) * 128] = jnp.dot(
            onehot, sheet, precision=HIGHEST, preferred_element_type=jnp.float32
        )
    to_scalar.wait()

    def get(n, carry):
        base = pl.multiple_of(n * BATCH, BATCH)
        spots = [index[n // (128 // BATCH), n % (128 // BATCH) * BATCH + m] for m in range(BATCH)]
        ph = [recv[spot] for spot in spots]
        en = [recv[spot + CAP] for spot in spots]
        for m in range(BATCH):
            phases[pl.ds(base + m, 1)] = ph[m]
            energies[pl.ds(base + m, 1)] = en[m]
        return carry

    copies = []
    for quarter in range(4):
        lax.fori_loop(quarter * COUNT // BATCH // 4, (quarter + 1) * COUNT // BATCH // 4, get, 0)
        for k in range(quarter * 4, quarter * 4 + 4):
            rows = slice(k * NBS, (k + 1) * NBS)
            re, im = amps[rows, k : k + 1], amps[rows, GROUPS + k : GROUPS + k + 1]
            phases[rows], energies[rows] = pushed(phases[rows], energies[rows], re, im)
        span = pl.ds(quarter * COUNT // 4, COUNT // 4)
        copies.append(pltpu.make_async_copy(phases.at[span], phases_hbm.at[span], sems.at[1 + 2 * quarter]))
        copies.append(pltpu.make_async_copy(energies.at[span], energies_hbm.at[span], sems.at[2 + 2 * quarter]))
        for copy in copies[-2:]:
            copy.start()
    for copy in copies:
        copy.wait()


def twice_diffracted(planes, left, right):
    hi, lo = wide_halves(jnp.concatenate([jnp.concatenate(pair, axis=1) for pair in planes], axis=0))
    half = jnp.dot(jnp.concatenate([hi, lo, hi], axis=1), right[...], preferred_element_type=jnp.float32)
    cols = []
    for m in range(len(planes)):
        mid = half[m * GRID : (m + 1) * GRID]
        cols.append(jnp.concatenate([mid[:, :GRID], mid[:, GRID:]], axis=0))
    hi, lo = wide_halves(jnp.concatenate(cols, axis=1))
    full = jnp.dot(left[...], jnp.concatenate([hi, lo, hi], axis=0), preferred_element_type=jnp.float32)
    cuts = [slice(m * GRID, (m + 1) * GRID) for m in range(len(planes))]
    return [(full[:GRID, cut], full[GRID:, cut]) for cut in cuts]


def early_kernel(mine, piece_0, piece_1, beam, left, right, out):
    even = mine[0] % 2 == 0
    planes = [tuple(jnp.where(even, piece_0[c, k], piece_1[c, k]) for c in range(2)) for k in range(EARLY)]
    planes.append((beam[2], jnp.zeros((GRID, GRID), jnp.float32)))
    for k, (re, im) in enumerate(twice_diffracted(planes, left, right)):
        out[0, k] = re
        out[1, k] = im


def last_kernel(
    mine, early, piece_b0, piece_b1, piece_b2, piece_b3, piece_c, small, beam, left, right, out_hbm, acc, rest, out, sems
):
    me = mine[0]
    for n in range(4):
        acc[n] = GAIN * small[n]
    copies = []

    def plane(c, k):
        if k < 0:
            return jnp.zeros((GRID, GRID), jnp.float32)
        return early[c, k] if k < EARLY else rest[c, k - EARLY]

    def finish(low, high):
        for k in range(low, high):
            cr, ci, br, bi = (acc[n, k : k + 1] for n in range(4))
            re, im = (jnp.where(me < 2, plane(c, k - 1), plane(c, k)) for c in range(2))
            out[0, k] = re + (br * early[0, EARLY] - bi * early[1, EARLY]) + (cr * beam[0] - ci * beam[1])
            out[1, k] = im + (br * early[1, EARLY] + bi * early[0, EARLY]) + (cr * beam[1] + ci * beam[0])
        span = pl.ds(low, high - low)
        for c in range(2):
            copies.append(pltpu.make_async_copy(out.at[c, span], out_hbm.at[c, span], sems.at[len(copies)]))
            copies[-1].start()

    finish(0, EARLY)
    planes = [(piece[0, k], piece[1, k]) for piece in (piece_b0, piece_b1, piece_b2, piece_b3) for k in range(piece.shape[1])]
    for k, (re, im) in enumerate(twice_diffracted(planes, left, right)):
        rest[0, k] = re
        rest[1, k] = im
    finish(EARLY, LATE)
    planes = [(piece_c[0, k], piece_c[1, k]) for k in range(piece_c.shape[1])]
    for k, (re, im) in enumerate(twice_diffracted(planes, left, right)):
        rest[0, LATE - EARLY + k] = re
        rest[1, LATE - EARLY + k] = im
    finish(LATE, GROUPS)
    for copy in copies:
        copy.wait()


def early_pairs(core):
    onward = [(device, (device + 2) % PEERS) for device in range(core, PEERS, 2)]
    across = [(device, (device + 8) % PEERS) for device in range(1 - core, PEERS, 2) if device % 8 >= 6]
    return onward + across


def late_pairs():
    return [(device, device + 2 if device % 8 < 6 else device - 6) for device in range(PEERS)]


def shifted(value, axis, steps):
    count = lax.axis_size(axis)
    pairs = [(source, (source + steps) % count) for source in range(count)]
    return lax.ppermute(value, axis, pairs)


def shape(*dims, dtype=jnp.float32):
    return jax.ShapeDtypeStruct(dims, dtype)


def whole():
    return pl.BlockSpec(memory_space=pltpu.VMEM)


def vmem(*dims, dtype=jnp.float32):
    return pltpu.VMEM(dims, dtype)


def in_hbm(value):
    return pltpu.with_memory_space_constraint(value, pltpu.HBM)


def per_device(field, phase_bins, phase_jitter, energy, profile, delays):
    params = pltpu.CompilerParams(vmem_limit_bytes=VMEM_LIMIT)
    scalar = pl.BlockSpec(memory_space=pltpu.SMEM)
    remain = pl.BlockSpec(memory_space=pltpu.HBM)
    field = field.reshape(2, GROUPS, GRID, GRID)
    bins = phase_bins.reshape(COUNT, BLOCK)
    jitter = phase_jitter.reshape(COUNT, BLOCK)
    energies = energy.reshape(COUNT, BLOCK)
    mine = lax.axis_index("cuts").reshape(1)
    one, two = line_operator(1), line_operator(2)
    left_one = jnp.asarray(np.concatenate(one, axis=0), jnp.float32)
    right_one = jnp.asarray(right_form(*one), jnp.float32)
    core = mine[0] % 2
    shared_0 = lax.ppermute(lax.dynamic_slice_in_dim(field, core * (GROUPS - EARLY), EARLY, 1), "cuts", early_pairs(0))
    shared_1 = lax.ppermute(lax.dynamic_slice_in_dim(field, (1 - core) * (GROUPS - EARLY), EARLY, 1), "cuts", early_pairs(1))
    operands = [field, profile, bins, jitter, energies, delays.reshape(GROUPS, 1, NBS), left_one, right_one]
    send, phases1, energies1, places, beam, small1, *sources = pl.pallas_call(
        first_kernel,
        out_shape=(
            pltpu.HBM((ROWS, 1, BLOCK), jnp.float32),
            shape(COUNT, BLOCK),
            shape(COUNT, BLOCK),
            pltpu.HBM((8, COUNT), jnp.int32),
            pltpu.HBM((3, GRID, GRID), jnp.float32),
            shape(4, GROUPS, 128),
            *[pltpu.HBM((2, high - low, GRID, GRID), jnp.float32) for low, high in MIDDLE],
        ),
        in_specs=[scalar] + [remain] * 8,
        out_specs=(remain, whole(), whole(), remain, whole(), whole()) + (remain,) * len(MIDDLE),
        scratch_shapes=[
            vmem(2, GROUPS, GRID, GRID),
            vmem(GRID, GRID),
            vmem(COUNT, BLOCK, dtype=jnp.int32),
            vmem(COUNT, BLOCK),
            vmem(COUNT, BLOCK),
            vmem(GROUPS, 1, NBS, dtype=jnp.int32),
            vmem(2 * GRID, GRID),
            vmem(2 * GRID, 2 * GRID),
            vmem(6, GROUPS, 128),
            vmem(ROWS, 1, BLOCK),
            vmem(8, COUNT, dtype=jnp.int32),
            vmem(8, 128, dtype=jnp.int32),
            pltpu.SMEM((8, 128), jnp.int32),
            pltpu.SemaphoreType.DMA((17,)),
        ],
        compiler_params=params,
        name="push_place",
    )(mine, *[in_hbm(value) for value in operands])
    arrived1 = shifted(small1, "cuts", 1)
    send = pl.pallas_call(
        second_kernel,
        out_shape=pltpu.HBM((PEERS, MESSAGE, 1, BLOCK), jnp.float32),
        in_specs=[scalar] + [whole()] * 4 + [remain],
        out_specs=remain,
        scratch_shapes=[vmem(4, GROUPS, 128), vmem(PEERS, 1, 128), pltpu.SemaphoreType.DMA],
        input_output_aliases={5: 0},
        compiler_params=params,
        name="second_push",
    )(mine, phases1, energies1, arrived1, small1, in_hbm(send.reshape(PEERS, MESSAGE, 1, BLOCK)))
    field_b = [shifted(source, "cuts", 2) for source in sources]

    left_two, right_two = deep_left(left_form(*two)), deep_right(right_form(*two))

    def exchange(send, places, field, shared_0, shared_1, beam):
        early = pl.pallas_call(
            early_kernel,
            out_shape=shape(2, EARLY + 1, GRID, GRID),
            in_specs=[scalar] + [whole()] * 5,
            out_specs=whole(),
            compiler_params=params,
            name="early_field",
        )(mine, in_hbm(shared_0), in_hbm(shared_1), in_hbm(beam), left_two, right_two)
        handed = jnp.where(core == 0, shared_1, shared_0)
        source_c = jnp.where(mine[0] % 8 >= 6, handed[:, LATE - GROUPS :], field[:, LATE:])
        field_c = lax.ppermute(source_c, "cuts", late_pairs())
        recv = lax.all_to_all(send.reshape(ROWS, 1, BLOCK), "cuts", split_axis=0, concat_axis=0, tiled=True)
        recv, early = lax.optimization_barrier((recv, early))
        phase_out, energy_out, small = pl.pallas_call(
            pick_kernel,
            out_shape=(shape(COUNT, BLOCK), shape(COUNT, BLOCK), shape(4, GROUPS, 128)),
            in_specs=[scalar] + [whole()] * 2,
            out_specs=(remain, remain, whole()),
            scratch_shapes=[
                vmem(8, 128, dtype=jnp.int32),
                pltpu.SMEM((8, 128), jnp.int32),
                vmem(COUNT, 128),
                vmem(PEERS, 128),
                vmem(COUNT, BLOCK),
                vmem(COUNT, BLOCK),
                pltpu.SemaphoreType.DMA((9,)),
            ],
            compiler_params=params,
            name="pick",
        )(mine, recv, places)
        return phase_out, energy_out, early, field_c, small

    def refuse(*operands):
        sizes = [(COUNT, BLOCK)] * 2 + [(2, n, GRID, GRID) for n in (EARLY + 1, GROUPS - LATE)] + [(4, GROUPS, 128)]
        return tuple(jnp.zeros(size, jnp.float32) for size in sizes)

    phase_out, energy_out, early, field_c, small = lax.cond(
        mine[0] < PEERS, exchange, refuse, send, places, field, shared_0, shared_1, beam
    )
    out = pl.pallas_call(
        last_kernel,
        out_shape=shape(2, GROUPS, GRID, GRID),
        in_specs=[scalar] + [whole()] * 10,
        out_specs=remain,
        scratch_shapes=[
            vmem(4, GROUPS, 128),
            vmem(2, GROUPS - EARLY, GRID, GRID),
            vmem(2, GROUPS, GRID, GRID),
            pltpu.SemaphoreType.DMA((6,)),
        ],
        compiler_params=params,
        name="last_field",
    )(mine, early, *field_b, field_c, small, in_hbm(beam), left_two, right_two)
    return (
        out.reshape(2, GROUPS, 1, GRID, GRID),
        phase_out.reshape(GROUPS, 1, NBS * BLOCK),
        energy_out.reshape(GROUPS, 1, NBS * BLOCK),
    )


def solution(mesh):
    return jax.shard_map(
        per_device,
        mesh=mesh,
        in_specs=(
            P(None, None, "cuts", None, None),
            P(None, "cuts", None),
            P(None, "cuts", None),
            P(None, "cuts", None),
            P(),
            P(),
        ),
        out_specs=(P(None, None, "cuts", None, None), P(None, "cuts", None), P(None, "cuts", None)),
        check_vma=False,
    )
```

```python
import functools
import math

import jax
import jax.numpy as jnp
import ml_dtypes
import numpy as np
from jax import lax
from jax.experimental import pallas as pl
from jax.experimental.pallas import tpu as pltpu
from jax.sharding import PartitionSpec as P

BLOCK = 128
NBINS = 16
KAPPA = 1.0
OMEGA = 1.0
GAIN = 16.0
PHASE_COEF = 20.0
GRID = 128
GROUPS = 16
NBS = 64
COUNT = GROUPS * NBS
PEERS = 128
CAP = 20
MESSAGE = 2 * CAP + 1
ROWS = PEERS * MESSAGE
BATCH = 32
EARLY, LATE = 5, 13
MIDDLE = ((5, 7), (7, 9), (9, 11), (11, 13))
VMEM_LIMIT = 24 * 1024 * 1024
HIGHEST = lax.Precision.HIGHEST


def line_operator(power):
    index = np.arange(GRID)
    freq = ((index + GRID // 2) % GRID - GRID // 2) / GRID
    weight = np.exp(-1j * PHASE_COEF * power * freq**2)
    wave = np.exp(2j * np.pi * (index[:, None] * index[None, :] % GRID) / GRID)
    column = wave @ weight / GRID
    matrix = column[(index[:, None] - index[None, :]) % GRID]
    return matrix.real, matrix.imag


def right_form(real, imag):
    return np.block([[real, imag], [-imag, real]])


def halves(matrix):
    high = matrix.astype(ml_dtypes.bfloat16)
    return high, (matrix - high.astype(np.float64)).astype(ml_dtypes.bfloat16)


def quarters(real, imag):
    return jnp.asarray(np.stack(halves(real) + halves(imag)))


def lay_out(parts, left, right):
    for n, low in enumerate((0, 0, 1)):
        re, im = parts[low], parts[2 + low]
        rest = slice(n * 2 * GRID, n * 2 * GRID + GRID), slice(n * 2 * GRID + GRID, (n + 1) * 2 * GRID)
        left[:GRID, rest[0]], left[:GRID, rest[1]] = re, -im
        left[GRID:, rest[0]], left[GRID:, rest[1]] = im, re
        right[rest[0], :GRID], right[rest[0], GRID:] = re, im
        right[rest[1], :GRID], right[rest[1], GRID:] = -im, re


def fitted(function, degree):
    top = (math.pi / 2 + 0.01) ** 2
    nodes = (np.cos(np.pi * (np.arange(400) + 0.5) / 400) + 1) / 2 * top
    series = np.polynomial.chebyshev.Chebyshev.fit(nodes, function(np.sqrt(nodes)), degree, domain=[0, top])
    return [float(c) for c in series.convert(kind=np.polynomial.Polynomial).coef]


SIN_COEF = fitted(lambda r: np.sin(r) / r, 5)
COS_COEF = fitted(np.cos, 6)
PI_HIGH = 3.140625
PI_MID = 9.67502593994140625e-4
PI_LOW = math.pi - PI_HIGH - PI_MID


def horner(coefs, x):
    value = jnp.float32(coefs[-1])
    for c in coefs[-2::-1]:
        value = value * x + jnp.float32(c)
    return value


def cos_sin(x):
    turns = jnp.round(x * jnp.float32(1.0 / math.pi))
    r = x - turns * jnp.float32(PI_HIGH)
    r = r - turns * jnp.float32(PI_MID)
    r = r - turns * jnp.float32(PI_LOW)
    half = turns * 0.5
    sign = 1.0 - 4.0 * jnp.abs(half - jnp.round(half))
    square = r * r
    return horner(COS_COEF, square) * sign, horner(SIN_COEF, square) * (r * sign)


def lane_total(rows):
    return jnp.broadcast_to(jnp.sum(rows, axis=1, keepdims=True), rows.shape)


def slots_of(delays):
    row = jnp.concatenate([delays[k] for k in range(GROUPS)], axis=1)
    values = lax.broadcasted_iota(jnp.int32, (PEERS, COUNT), 0)
    onehot = jnp.where(values == row, 1.0, 0.0)
    before = lax.broadcasted_iota(jnp.int32, (COUNT, COUNT), 0) < lax.broadcasted_iota(jnp.int32, (COUNT, COUNT), 1)
    upper = jnp.where(before, 1.0, 0.0).astype(jnp.bfloat16)
    earlier = jnp.dot(onehot.astype(jnp.bfloat16), upper, preferred_element_type=jnp.float32)
    return row, jnp.sum(earlier * onehot, axis=0, keepdims=True).astype(jnp.int32)


def folded(row):
    return jnp.concatenate([row[:, n * 128 : (n + 1) * 128] for n in range(COUNT // 128)], axis=0)


def rows_of(k):
    return pl.ds(pl.multiple_of(k * NBS, NBS), NBS)


def first_kernel(
    mine, field_hbm, profile_hbm, bins_hbm, jitter_hbm, energy_hbm, delays_hbm, left_hbm, right_hbm,
    send_hbm, phases, energies, places_hbm, beam, small, middle_0, middle_1, middle_2, middle_3,
    field, profile, bins, jitter, energy, delays, left, right, acc, send, places, index_v, index, sems,
):
    pairs = [
        (profile_hbm, profile), (left_hbm, left), (right_hbm, right), (delays_hbm, delays),
        (field_hbm, field), (bins_hbm, bins), (jitter_hbm, jitter), (energy_hbm, energy),
    ]
    copies = [pltpu.make_async_copy(src, dst, sems.at[n]) for n, (src, dst) in enumerate(pairs)]
    for copy in copies:
        copy.start()
    copies[3].wait()
    row, slot = slots_of(delays)
    places[0:1] = row
    places[1:2] = slot
    index_v[...] = folded(((mine[0] + row) % PEERS) * MESSAGE + slot)
    to_scalar = pltpu.make_async_copy(index_v, index, sems.at[3])
    to_scalar.start()
    for copy in copies[:3]:
        copy.wait()
    p = profile[...]
    half = jnp.dot(left[...], p, precision=HIGHEST, preferred_element_type=jnp.float32)
    both = jnp.concatenate([half[:GRID], half[GRID:]], axis=1)
    spread = jnp.dot(both, right[...], precision=HIGHEST, preferred_element_type=jnp.float32)
    beam[0] = spread[:, :GRID]
    beam[1] = spread[:, GRID:]
    beam[2] = p
    copies[4].wait()
    kept = [pltpu.make_async_copy(places, places_hbm, sems.at[8])]
    for middle, (low, high) in zip((middle_0, middle_1, middle_2, middle_3), MIDDLE):
        for c in range(2):
            span = pl.ds(low, high - low)
            kept.append(pltpu.make_async_copy(field.at[c, span], middle.at[c], sems.at[8 + len(kept)]))
    for copy in kept:
        copy.start()

    def project(k, carry):
        re, im = field[0, k], field[1, k]
        dr, di, q = beam[0], beam[1], profile[...]
        acc[0, pl.ds(k, 1)] = jnp.sum(q * re, axis=0, keepdims=True)
        acc[1, pl.ds(k, 1)] = jnp.sum(q * im, axis=0, keepdims=True)
        acc[2, pl.ds(k, 1)] = jnp.sum(dr * re - di * im, axis=0, keepdims=True)
        acc[3, pl.ds(k, 1)] = jnp.sum(dr * im + di * re, axis=0, keepdims=True)
        return carry

    lax.fori_loop(0, GROUPS, project, 0)
    self_re = jnp.sum(p * beam[0])
    self_im = jnp.sum(p * beam[1])
    for n in range(4):
        acc[n] = lane_total(acc[n]) * (1.0 / GRID)
    for copy in copies[5:]:
        copy.wait()

    def push(k, carry):
        rows = rows_of(k)
        ph = jnp.float32(2.0 * math.pi / NBINS) * (bins[rows].astype(jnp.float32) + jitter[rows])
        ph, en = pushed(ph, energy[rows], acc[0, pl.ds(k, 1)], acc[1, pl.ds(k, 1)])
        phases[rows] = ph
        energies[rows] = en
        c, s = cos_sin(ph)
        acc[4, pl.ds(k, 1)] = jnp.sum(c, axis=0, keepdims=True)
        acc[5, pl.ds(k, 1)] = jnp.sum(s, axis=0, keepdims=True)
        return carry

    lax.fori_loop(0, GROUPS, push, 0)
    to_scalar.wait()

    def put(n, carry):
        base = pl.multiple_of(n * BATCH, BATCH)
        spots = [index[n // (128 // BATCH), n % (128 // BATCH) * BATCH + m] for m in range(BATCH)]
        ph = [phases[pl.ds(base + m, 1)] for m in range(BATCH)]
        en = [energies[pl.ds(base + m, 1)] for m in range(BATCH)]
        for m in range(BATCH):
            send[spots[m]] = ph[m]
            send[spots[m] + CAP] = en[m]
        return carry

    lax.fori_loop(0, COUNT // BATCH, put, 0)
    bre = lane_total(acc[4]) * (1.0 / (NBS * BLOCK))
    bim = lane_total(acc[5]) * (-1.0 / (NBS * BLOCK))
    gain = GAIN / GRID
    next_re = acc[2] + gain * (bre * self_re - bim * self_im)
    next_im = acc[3] + gain * (bre * self_im + bim * self_re)
    for n, part in enumerate((next_re, next_im, bre, bim)):
        small[n] = part
    out = pltpu.make_async_copy(send, send_hbm, sems.at[0])
    out.start()
    for copy in kept:
        copy.wait()
    out.wait()


def pushed(ph, en, amp_re, amp_im):
    c, s = cos_sin(ph)
    en = en - KAPPA * (amp_re * c - amp_im * s)
    return ph + OMEGA * en, en


def one_row(parts):
    rest = 128 // GROUPS - len(parts)
    stack = jnp.concatenate(parts + [jnp.zeros((rest * GROUPS, 128), jnp.float32)], axis=0)
    return stack.T[0:1]


def carried(value, flag):
    rolled = jnp.concatenate([jnp.zeros_like(value[:1]), value[:-1]], axis=0)
    return jnp.where(flag, rolled, value)


def second_kernel(mine, phases1, energies1, arrived, own, send_in, send, acc, note, sem):
    del send_in
    for n in range(2):
        acc[n] = carried(arrived[n], mine[0] == 0)

    def push(k, carry):
        rows = rows_of(k)
        ph, _ = pushed(phases1[rows], energies1[rows], acc[0, pl.ds(k, 1)], acc[1, pl.ds(k, 1)])
        c, s = cos_sin(ph)
        acc[2, pl.ds(k, 1)] = jnp.sum(c, axis=0, keepdims=True)
        acc[3, pl.ds(k, 1)] = jnp.sum(s, axis=0, keepdims=True)
        return carry

    lax.fori_loop(0, GROUPS, push, 0)
    mean = 1.0 / (NBS * BLOCK)
    row = one_row([own[n] for n in range(4)] + [lane_total(acc[2]) * mean, lane_total(acc[3]) * -mean])
    note[...] = jnp.broadcast_to(row[None], (PEERS, 1, 128))
    copy = pltpu.make_async_copy(note, send.at[:, 2 * CAP], sem)
    copy.start()
    copy.wait()


def wide_halves(x):
    high = x.astype(jnp.bfloat16)
    return high, (x - high.astype(jnp.float32)).astype(jnp.bfloat16)


def pick_kernel(mine, recv, places, phases_hbm, energies_hbm, small, index_v, index, amps, notes, phases, energies, sems):
    me = mine[0]
    source = (me - places[0:1] + PEERS) % PEERS
    index_v[...] = folded(source * MESSAGE + places[1:2])
    to_scalar = pltpu.make_async_copy(index_v, index, sems.at[0])
    to_scalar.start()
    lane = lax.broadcasted_iota(jnp.int32, (128, 128), 1)
    for n in range(PEERS):
        notes[n : n + 1] = recv[n * MESSAGE + 2 * CAP]
    sheet = notes[...]
    near = jnp.broadcast_to(notes[pl.ds((me + PEERS - 1) % PEERS, 1)], (128, 128)).T
    far = jnp.broadcast_to(notes[pl.ds((me + PEERS - 2) % PEERS, 1)], (128, 128)).T
    for n in range(2):
        small[n] = carried(near[(4 + n) * GROUPS : (5 + n) * GROUPS], me == 0)
        small[2 + n] = carried(far[(2 + n) * GROUPS : (3 + n) * GROUPS], me < 2)
    wrapped = jnp.concatenate([sheet[127:128, 127:128], sheet[127:128, :127]], axis=1)
    wrapped = jnp.where(lane[0:1] % GROUPS == 0, 0.0, wrapped)
    sheet = jnp.concatenate([wrapped, sheet[:127]], axis=0)
    kept = jnp.where(lane < 2 * GROUPS, sheet, 0.0)
    high, rest = wide_halves(kept)
    low = (kept - high.astype(jnp.float32) - rest.astype(jnp.float32)).astype(jnp.bfloat16)
    thirds = jnp.concatenate([high, rest, low], axis=1)
    onehot = jnp.concatenate(
        [
            jnp.where(lane == jnp.broadcast_to(source[:, n * 128 : (n + 1) * 128], (128, 128)).T, 1.0, 0.0)
            for n in range(COUNT // 128)
        ],
        axis=0,
    )
    found = jnp.dot(onehot.astype(jnp.bfloat16), thirds, preferred_element_type=jnp.float32)
    amps[...] = found[:, :128] + found[:, 128:256] + found[:, 256:]
    to_scalar.wait()

    def get(n, carry):
        base = pl.multiple_of(n * BATCH, BATCH)
        spots = [index[n // (128 // BATCH), n % (128 // BATCH) * BATCH + m] for m in range(BATCH)]
        ph = [recv[spot] for spot in spots]
        en = [recv[spot + CAP] for spot in spots]
        for m in range(BATCH):
            phases[pl.ds(base + m, 1)] = ph[m]
            energies[pl.ds(base + m, 1)] = en[m]
        return carry

    copies = []
    for quarter in range(4):
        lax.fori_loop(quarter * COUNT // BATCH // 4, (quarter + 1) * COUNT // BATCH // 4, get, 0)
        for k in range(quarter * 4, quarter * 4 + 4):
            rows = slice(k * NBS, (k + 1) * NBS)
            re, im = amps[rows, k : k + 1], amps[rows, GROUPS + k : GROUPS + k + 1]
            phases[rows], energies[rows] = pushed(phases[rows], energies[rows], re, im)
        span = pl.ds(quarter * COUNT // 4, COUNT // 4)
        copies.append(pltpu.make_async_copy(phases.at[span], phases_hbm.at[span], sems.at[1 + 2 * quarter]))
        copies.append(pltpu.make_async_copy(energies.at[span], energies_hbm.at[span], sems.at[2 + 2 * quarter]))
        for copy in copies[-2:]:
            copy.start()
    for copy in copies:
        copy.wait()


def twice_diffracted(planes, left, right):
    hi, lo = wide_halves(jnp.concatenate([jnp.concatenate(pair, axis=1) for pair in planes], axis=0))
    half = jnp.dot(jnp.concatenate([hi, lo, hi], axis=1), right[...], preferred_element_type=jnp.float32)
    cols = []
    for m in range(len(planes)):
        mid = half[m * GRID : (m + 1) * GRID]
        cols.append(jnp.concatenate([mid[:, :GRID], mid[:, GRID:]], axis=0))
    hi, lo = wide_halves(jnp.concatenate(cols, axis=1))
    full = jnp.dot(left[...], jnp.concatenate([hi, lo, hi], axis=0), preferred_element_type=jnp.float32)
    cuts = [slice(m * GRID, (m + 1) * GRID) for m in range(len(planes))]
    return [(full[:GRID, cut], full[GRID:, cut]) for cut in cuts]


def early_kernel(mine, piece_0, piece_1, beam, parts, out, left, right):
    lay_out(parts, left, right)
    even = mine[0] % 2 == 0
    planes = [tuple(jnp.where(even, piece_0[c, k], piece_1[c, k]) for c in range(2)) for k in range(EARLY)]
    planes.append((beam[2], jnp.zeros((GRID, GRID), jnp.float32)))
    for k, (re, im) in enumerate(twice_diffracted(planes, left, right)):
        out[0, k] = re
        out[1, k] = im


def last_kernel(
    mine, early, piece_b0, piece_b1, piece_b2, piece_b3, piece_c, small, beam, parts, out_hbm, acc, rest, out, left, right, sems
):
    me = mine[0]
    for n in range(4):
        acc[n] = GAIN * small[n]
    copies = []

    def plane(c, k):
        if k < 0:
            return jnp.zeros((GRID, GRID), jnp.float32)
        return early[c, k] if k < EARLY else rest[c, k - EARLY]

    def finish(low, high):
        for k in range(low, high):
            cr, ci, br, bi = (acc[n, k : k + 1] for n in range(4))
            re, im = (jnp.where(me < 2, plane(c, k - 1), plane(c, k)) for c in range(2))
            out[0, k] = re + (br * early[0, EARLY] - bi * early[1, EARLY]) + (cr * beam[0] - ci * beam[1])
            out[1, k] = im + (br * early[1, EARLY] + bi * early[0, EARLY]) + (cr * beam[1] + ci * beam[0])
        span = pl.ds(low, high - low)
        for c in range(2):
            copies.append(pltpu.make_async_copy(out.at[c, span], out_hbm.at[c, span], sems.at[len(copies)]))
            copies[-1].start()

    finish(0, EARLY)
    lay_out(parts, left, right)
    planes = [(piece[0, k], piece[1, k]) for piece in (piece_b0, piece_b1, piece_b2, piece_b3) for k in range(piece.shape[1])]
    for k, (re, im) in enumerate(twice_diffracted(planes, left, right)):
        rest[0, k] = re
        rest[1, k] = im
    finish(EARLY, LATE)
    planes = [(piece_c[0, k], piece_c[1, k]) for k in range(piece_c.shape[1])]
    for k, (re, im) in enumerate(twice_diffracted(planes, left, right)):
        rest[0, LATE - EARLY + k] = re
        rest[1, LATE - EARLY + k] = im
    finish(LATE, GROUPS)
    for copy in copies:
        copy.wait()


def early_pairs(core):
    onward = [(device, (device + 2) % PEERS) for device in range(core, PEERS, 2)]
    across = [(device, (device + 8) % PEERS) for device in range(1 - core, PEERS, 2) if device % 8 >= 6]
    return onward + across


def late_pairs():
    return [(device, device + 2 if device % 8 < 6 else device - 6) for device in range(PEERS)]


def shifted(value, axis, steps):
    count = lax.axis_size(axis)
    pairs = [(source, (source + steps) % count) for source in range(count)]
    return lax.ppermute(value, axis, pairs)


def shape(*dims, dtype=jnp.float32):
    return jax.ShapeDtypeStruct(dims, dtype)


def whole():
    return pl.BlockSpec(memory_space=pltpu.VMEM)


def vmem(*dims, dtype=jnp.float32):
    return pltpu.VMEM(dims, dtype)


def in_hbm(value):
    return pltpu.with_memory_space_constraint(value, pltpu.HBM)


def per_device(field, phase_bins, phase_jitter, energy, profile, delays):
    params = pltpu.CompilerParams(vmem_limit_bytes=VMEM_LIMIT)
    scalar = pl.BlockSpec(memory_space=pltpu.SMEM)
    remain = pl.BlockSpec(memory_space=pltpu.HBM)
    field = field.reshape(2, GROUPS, GRID, GRID)
    bins = phase_bins.reshape(COUNT, BLOCK)
    jitter = phase_jitter.reshape(COUNT, BLOCK)
    energies = energy.reshape(COUNT, BLOCK)
    mine = lax.axis_index("cuts").reshape(1)
    one, two = line_operator(1), line_operator(2)
    left_one = jnp.asarray(np.concatenate(one, axis=0), jnp.float32)
    right_one = jnp.asarray(right_form(*one), jnp.float32)
    core = mine[0] % 2
    shared_0 = lax.ppermute(lax.dynamic_slice_in_dim(field, core * (GROUPS - EARLY), EARLY, 1), "cuts", early_pairs(0))
    shared_1 = lax.ppermute(lax.dynamic_slice_in_dim(field, (1 - core) * (GROUPS - EARLY), EARLY, 1), "cuts", early_pairs(1))
    operands = [field, profile, bins, jitter, energies, delays.reshape(GROUPS, 1, NBS), left_one, right_one]
    send, phases1, energies1, places, beam, small1, *sources = pl.pallas_call(
        first_kernel,
        out_shape=(
            pltpu.HBM((ROWS, 1, BLOCK), jnp.float32),
            shape(COUNT, BLOCK),
            shape(COUNT, BLOCK),
            pltpu.HBM((8, COUNT), jnp.int32),
            pltpu.HBM((3, GRID, GRID), jnp.float32),
            shape(4, GROUPS, 128),
            *[pltpu.HBM((2, high - low, GRID, GRID), jnp.float32) for low, high in MIDDLE],
        ),
        in_specs=[scalar] + [remain] * 8,
        out_specs=(remain, whole(), whole(), remain, whole(), whole()) + (remain,) * len(MIDDLE),
        scratch_shapes=[
            vmem(2, GROUPS, GRID, GRID),
            vmem(GRID, GRID),
            vmem(COUNT, BLOCK, dtype=jnp.int32),
            vmem(COUNT, BLOCK),
            vmem(COUNT, BLOCK),
            vmem(GROUPS, 1, NBS, dtype=jnp.int32),
            vmem(2 * GRID, GRID),
            vmem(2 * GRID, 2 * GRID),
            vmem(6, GROUPS, 128),
            vmem(ROWS, 1, BLOCK),
            vmem(8, COUNT, dtype=jnp.int32),
            vmem(8, 128, dtype=jnp.int32),
            pltpu.SMEM((8, 128), jnp.int32),
            pltpu.SemaphoreType.DMA((17,)),
        ],
        compiler_params=params,
        name="push_place",
    )(mine, *[in_hbm(value) for value in operands])
    arrived1 = shifted(small1, "cuts", 1)
    send = pl.pallas_call(
        second_kernel,
        out_shape=pltpu.HBM((PEERS, MESSAGE, 1, BLOCK), jnp.float32),
        in_specs=[scalar] + [whole()] * 4 + [remain],
        out_specs=remain,
        scratch_shapes=[vmem(4, GROUPS, 128), vmem(PEERS, 1, 128), pltpu.SemaphoreType.DMA],
        input_output_aliases={5: 0},
        compiler_params=params,
        name="second_push",
    )(mine, phases1, energies1, arrived1, small1, in_hbm(send.reshape(PEERS, MESSAGE, 1, BLOCK)))
    field_b = [shifted(source, "cuts", 2) for source in sources]

    operator = quarters(*two)
    tables = [vmem(2 * GRID, 6 * GRID, dtype=jnp.bfloat16), vmem(6 * GRID, 2 * GRID, dtype=jnp.bfloat16)]

    def exchange(send, places, field, shared_0, shared_1, beam):
        early = pl.pallas_call(
            early_kernel,
            out_shape=shape(2, EARLY + 1, GRID, GRID),
            in_specs=[scalar] + [whole()] * 4,
            out_specs=whole(),
            scratch_shapes=tables,
            compiler_params=params,
            name="early_field",
        )(mine, in_hbm(shared_0), in_hbm(shared_1), in_hbm(beam), operator)
        handed = jnp.where(core == 0, shared_1, shared_0)
        source_c = jnp.where(mine[0] % 8 >= 6, handed[:, LATE - GROUPS :], field[:, LATE:])
        field_c = lax.ppermute(source_c, "cuts", late_pairs())
        recv = lax.all_to_all(send.reshape(ROWS, 1, BLOCK), "cuts", split_axis=0, concat_axis=0, tiled=True)
        recv, early = lax.optimization_barrier((recv, early))
        phase_out, energy_out, small = pl.pallas_call(
            pick_kernel,
            out_shape=(shape(COUNT, BLOCK), shape(COUNT, BLOCK), shape(4, GROUPS, 128)),
            in_specs=[scalar] + [whole()] * 2,
            out_specs=(remain, remain, whole()),
            scratch_shapes=[
                vmem(8, 128, dtype=jnp.int32),
                pltpu.SMEM((8, 128), jnp.int32),
                vmem(COUNT, 128),
                vmem(PEERS, 128),
                vmem(COUNT, BLOCK),
                vmem(COUNT, BLOCK),
                pltpu.SemaphoreType.DMA((9,)),
            ],
            compiler_params=params,
            name="pick",
        )(mine, recv, places)
        return phase_out, energy_out, early, field_c, small

    def refuse(*operands):
        sizes = [(COUNT, BLOCK)] * 2 + [(2, n, GRID, GRID) for n in (EARLY + 1, GROUPS - LATE)] + [(4, GROUPS, 128)]
        return tuple(jnp.zeros(size, jnp.float32) for size in sizes)

    phase_out, energy_out, early, field_c, small = lax.cond(
        mine[0] < PEERS, exchange, refuse, send, places, field, shared_0, shared_1, beam
    )
    out = pl.pallas_call(
        last_kernel,
        out_shape=shape(2, GROUPS, GRID, GRID),
        in_specs=[scalar] + [whole()] * 9,
        out_specs=remain,
        scratch_shapes=[
            vmem(4, GROUPS, 128),
            vmem(2, GROUPS - EARLY, GRID, GRID),
            vmem(2, GROUPS, GRID, GRID),
            *tables,
            pltpu.SemaphoreType.DMA((6,)),
        ],
        compiler_params=params,
        name="last_field",
    )(mine, early, *field_b, field_c, small, in_hbm(beam), operator)
    return (
        out.reshape(2, GROUPS, 1, GRID, GRID),
        phase_out.reshape(GROUPS, 1, NBS * BLOCK),
        energy_out.reshape(GROUPS, 1, NBS * BLOCK),
    )


def solution(mesh):
    return jax.shard_map(
        per_device,
        mesh=mesh,
        in_specs=(
            P(None, None, "cuts", None, None),
            P(None, "cuts", None),
            P(None, "cuts", None),
            P(None, "cuts", None),
            P(),
            P(),
        ),
        out_specs=(P(None, None, "cuts", None, None), P(None, "cuts", None), P(None, "cuts", None)),
        check_vma=False,
    )
```

```python
import functools
import math

import jax
import jax.numpy as jnp
import ml_dtypes
import numpy as np
from jax import lax
from jax.experimental import pallas as pl
from jax.experimental.pallas import tpu as pltpu
from jax.sharding import PartitionSpec as P

BLOCK = 128
NBINS = 16
KAPPA = 1.0
OMEGA = 1.0
GAIN = 16.0
PHASE_COEF = 20.0
GRID = 128
GROUPS = 16
NBS = 64
COUNT = GROUPS * NBS
PEERS = 128
CAP = 20
MESSAGE = 2 * CAP + 1
ROWS = PEERS * MESSAGE
BATCH = 32
EARLY, LATE = 5, 11
MIDDLE = ((5, 7), (7, 9), (9, 11))
VMEM_LIMIT = 24 * 1024 * 1024
HIGHEST = lax.Precision.HIGHEST


def line_operator(power):
    index = np.arange(GRID)
    freq = ((index + GRID // 2) % GRID - GRID // 2) / GRID
    weight = np.exp(-1j * PHASE_COEF * power * freq**2)
    wave = np.exp(2j * np.pi * (index[:, None] * index[None, :] % GRID) / GRID)
    column = wave @ weight / GRID
    matrix = column[(index[:, None] - index[None, :]) % GRID]
    return matrix.real, matrix.imag


def right_form(real, imag):
    return np.block([[real, imag], [-imag, real]])


def halves(matrix):
    high = matrix.astype(ml_dtypes.bfloat16)
    return high, (matrix - high.astype(np.float64)).astype(ml_dtypes.bfloat16)


def quarters(real, imag):
    return jnp.asarray(np.stack(halves(real) + halves(imag)))


def lay_out(parts, left, right):
    for n, low in enumerate((0, 0, 1)):
        re, im = parts[low], parts[2 + low]
        rest = slice(n * 2 * GRID, n * 2 * GRID + GRID), slice(n * 2 * GRID + GRID, (n + 1) * 2 * GRID)
        left[:GRID, rest[0]], left[:GRID, rest[1]] = re, -im
        left[GRID:, rest[0]], left[GRID:, rest[1]] = im, re
        right[rest[0], :GRID], right[rest[0], GRID:] = re, im
        right[rest[1], :GRID], right[rest[1], GRID:] = -im, re


def fitted(function, degree):
    top = (math.pi / 2 + 0.01) ** 2
    nodes = (np.cos(np.pi * (np.arange(400) + 0.5) / 400) + 1) / 2 * top
    series = np.polynomial.chebyshev.Chebyshev.fit(nodes, function(np.sqrt(nodes)), degree, domain=[0, top])
    return [float(c) for c in series.convert(kind=np.polynomial.Polynomial).coef]


SIN_COEF = fitted(lambda r: np.sin(r) / r, 5)
COS_COEF = fitted(np.cos, 6)
PI_HIGH = 3.140625
PI_MID = 9.67502593994140625e-4
PI_LOW = math.pi - PI_HIGH - PI_MID


def horner(coefs, x):
    value = jnp.float32(coefs[-1])
    for c in coefs[-2::-1]:
        value = value * x + jnp.float32(c)
    return value


def cos_sin(x):
    turns = jnp.round(x * jnp.float32(1.0 / math.pi))
    r = x - turns * jnp.float32(PI_HIGH)
    r = r - turns * jnp.float32(PI_MID)
    r = r - turns * jnp.float32(PI_LOW)
    half = turns * 0.5
    sign = 1.0 - 4.0 * jnp.abs(half - jnp.round(half))
    square = r * r
    return horner(COS_COEF, square) * sign, horner(SIN_COEF, square) * (r * sign)


def lane_total(rows):
    return jnp.broadcast_to(jnp.sum(rows, axis=1, keepdims=True), rows.shape)


def slots_of(delays):
    row = jnp.concatenate([delays[k] for k in range(GROUPS)], axis=1)
    values = lax.broadcasted_iota(jnp.int32, (PEERS, COUNT), 0)
    onehot = jnp.where(values == row, 1.0, 0.0)
    before = lax.broadcasted_iota(jnp.int32, (COUNT, COUNT), 0) < lax.broadcasted_iota(jnp.int32, (COUNT, COUNT), 1)
    upper = jnp.where(before, 1.0, 0.0).astype(jnp.bfloat16)
    earlier = jnp.dot(onehot.astype(jnp.bfloat16), upper, preferred_element_type=jnp.float32)
    return row, jnp.sum(earlier * onehot, axis=0, keepdims=True).astype(jnp.int32)


def folded(row):
    return jnp.concatenate([row[:, n * 128 : (n + 1) * 128] for n in range(COUNT // 128)], axis=0)


def rows_of(k):
    return pl.ds(pl.multiple_of(k * NBS, NBS), NBS)


def first_kernel(
    mine, field_hbm, profile_hbm, bins_hbm, jitter_hbm, energy_hbm, delays_hbm, left_hbm, right_hbm,
    send_hbm, phases, energies, places_hbm, beam, small, middle_0, middle_1, middle_2,
    field, profile, bins, jitter, energy, delays, left, right, acc, send, places, index_v, index, sems,
):
    pairs = [
        (profile_hbm, profile), (left_hbm, left), (right_hbm, right), (delays_hbm, delays),
        (field_hbm, field), (bins_hbm, bins), (jitter_hbm, jitter), (energy_hbm, energy),
    ]
    copies = [pltpu.make_async_copy(src, dst, sems.at[n]) for n, (src, dst) in enumerate(pairs)]
    for copy in copies:
        copy.start()
    copies[3].wait()
    row, slot = slots_of(delays)
    places[0:1] = row
    places[1:2] = slot
    index_v[...] = folded(((mine[0] + row) % PEERS) * MESSAGE + slot)
    to_scalar = pltpu.make_async_copy(index_v, index, sems.at[3])
    to_scalar.start()
    for copy in copies[:3]:
        copy.wait()
    p = profile[...]
    half = jnp.dot(left[...], p, precision=HIGHEST, preferred_element_type=jnp.float32)
    both = jnp.concatenate([half[:GRID], half[GRID:]], axis=1)
    spread = jnp.dot(both, right[...], precision=HIGHEST, preferred_element_type=jnp.float32)
    beam[0] = spread[:, :GRID]
    beam[1] = spread[:, GRID:]
    beam[2] = p
    copies[4].wait()
    kept = [pltpu.make_async_copy(places, places_hbm, sems.at[8])]
    for middle, (low, high) in zip((middle_0, middle_1, middle_2), MIDDLE):
        for c in range(2):
            span = pl.ds(low, high - low)
            kept.append(pltpu.make_async_copy(field.at[c, span], middle.at[c], sems.at[8 + len(kept)]))
    for copy in kept:
        copy.start()

    def project(k, carry):
        re, im = field[0, k], field[1, k]
        dr, di, q = beam[0], beam[1], profile[...]
        acc[0, pl.ds(k, 1)] = jnp.sum(q * re, axis=0, keepdims=True)
        acc[1, pl.ds(k, 1)] = jnp.sum(q * im, axis=0, keepdims=True)
        acc[2, pl.ds(k, 1)] = jnp.sum(dr * re - di * im, axis=0, keepdims=True)
        acc[3, pl.ds(k, 1)] = jnp.sum(dr * im + di * re, axis=0, keepdims=True)
        return carry

    lax.fori_loop(0, GROUPS, project, 0)
    self_re = jnp.sum(p * beam[0])
    self_im = jnp.sum(p * beam[1])
    for n in range(4):
        acc[n] = lane_total(acc[n]) * (1.0 / GRID)
    for copy in copies[5:]:
        copy.wait()

    def push(k, carry):
        rows = rows_of(k)
        ph = jnp.float32(2.0 * math.pi / NBINS) * (bins[rows].astype(jnp.float32) + jitter[rows])
        ph, en = pushed(ph, energy[rows], acc[0, pl.ds(k, 1)], acc[1, pl.ds(k, 1)])
        phases[rows] = ph
        energies[rows] = en
        c, s = cos_sin(ph)
        acc[4, pl.ds(k, 1)] = jnp.sum(c, axis=0, keepdims=True)
        acc[5, pl.ds(k, 1)] = jnp.sum(s, axis=0, keepdims=True)
        return carry

    lax.fori_loop(0, GROUPS, push, 0)
    to_scalar.wait()

    def put(n, carry):
        base = pl.multiple_of(n * BATCH, BATCH)
        spots = [index[n // (128 // BATCH), n % (128 // BATCH) * BATCH + m] for m in range(BATCH)]
        ph = [phases[pl.ds(base + m, 1)] for m in range(BATCH)]
        en = [energies[pl.ds(base + m, 1)] for m in range(BATCH)]
        for m in range(BATCH):
            send[spots[m]] = ph[m]
            send[spots[m] + CAP] = en[m]
        return carry

    lax.fori_loop(0, COUNT // BATCH, put, 0)
    bre = lane_total(acc[4]) * (1.0 / (NBS * BLOCK))
    bim = lane_total(acc[5]) * (-1.0 / (NBS * BLOCK))
    gain = GAIN / GRID
    next_re = acc[2] + gain * (bre * self_re - bim * self_im)
    next_im = acc[3] + gain * (bre * self_im + bim * self_re)
    for n, part in enumerate((next_re, next_im, bre, bim)):
        small[n] = part
    out = pltpu.make_async_copy(send, send_hbm, sems.at[0])
    out.start()
    for copy in kept:
        copy.wait()
    out.wait()


def pushed(ph, en, amp_re, amp_im):
    c, s = cos_sin(ph)
    en = en - KAPPA * (amp_re * c - amp_im * s)
    return ph + OMEGA * en, en


def one_row(parts):
    rest = 128 // GROUPS - len(parts)
    stack = jnp.concatenate(parts + [jnp.zeros((rest * GROUPS, 128), jnp.float32)], axis=0)
    return stack.T[0:1]


def carried(value, flag):
    rolled = jnp.concatenate([jnp.zeros_like(value[:1]), value[:-1]], axis=0)
    return jnp.where(flag, rolled, value)


def second_kernel(mine, phases1, energies1, arrived, own, send_in, send, acc, note, sem):
    del send_in
    for n in range(2):
        acc[n] = carried(arrived[n], mine[0] == 0)

    def push(k, carry):
        rows = rows_of(k)
        ph, _ = pushed(phases1[rows], energies1[rows], acc[0, pl.ds(k, 1)], acc[1, pl.ds(k, 1)])
        c, s = cos_sin(ph)
        acc[2, pl.ds(k, 1)] = jnp.sum(c, axis=0, keepdims=True)
        acc[3, pl.ds(k, 1)] = jnp.sum(s, axis=0, keepdims=True)
        return carry

    lax.fori_loop(0, GROUPS, push, 0)
    mean = 1.0 / (NBS * BLOCK)
    row = one_row([own[n] for n in range(4)] + [lane_total(acc[2]) * mean, lane_total(acc[3]) * -mean])
    note[...] = jnp.broadcast_to(row[None], (PEERS, 1, 128))
    copy = pltpu.make_async_copy(note, send.at[:, 2 * CAP], sem)
    copy.start()
    copy.wait()


def wide_halves(x):
    high = x.astype(jnp.bfloat16)
    return high, (x - high.astype(jnp.float32)).astype(jnp.bfloat16)


def pick_kernel(mine, recv, places, phases_hbm, energies_hbm, small, index_v, index, amps, notes, phases, energies, sems):
    me = mine[0]
    source = (me - places[0:1] + PEERS) % PEERS
    index_v[...] = folded(source * MESSAGE + places[1:2])
    to_scalar = pltpu.make_async_copy(index_v, index, sems.at[0])
    to_scalar.start()
    lane = lax.broadcasted_iota(jnp.int32, (128, 128), 1)
    for n in range(PEERS):
        notes[n : n + 1] = recv[n * MESSAGE + 2 * CAP]
    sheet = notes[...]
    near = jnp.broadcast_to(notes[pl.ds((me + PEERS - 1) % PEERS, 1)], (128, 128)).T
    far = jnp.broadcast_to(notes[pl.ds((me + PEERS - 2) % PEERS, 1)], (128, 128)).T
    for n in range(2):
        small[n] = carried(near[(4 + n) * GROUPS : (5 + n) * GROUPS], me == 0)
        small[2 + n] = carried(far[(2 + n) * GROUPS : (3 + n) * GROUPS], me < 2)
    wrapped = jnp.concatenate([sheet[127:128, 127:128], sheet[127:128, :127]], axis=1)
    wrapped = jnp.where(lane[0:1] % GROUPS == 0, 0.0, wrapped)
    sheet = jnp.concatenate([wrapped, sheet[:127]], axis=0)
    kept = jnp.where(lane < 2 * GROUPS, sheet, 0.0)
    high, rest = wide_halves(kept)
    low = (kept - high.astype(jnp.float32) - rest.astype(jnp.float32)).astype(jnp.bfloat16)
    thirds = jnp.concatenate([high, rest, low], axis=1)
    onehot = jnp.concatenate(
        [
            jnp.where(lane == jnp.broadcast_to(source[:, n * 128 : (n + 1) * 128], (128, 128)).T, 1.0, 0.0)
            for n in range(COUNT // 128)
        ],
        axis=0,
    )
    found = jnp.dot(onehot.astype(jnp.bfloat16), thirds, preferred_element_type=jnp.float32)
    amps[...] = found[:, :128] + found[:, 128:256] + found[:, 256:]
    to_scalar.wait()

    def get(n, carry):
        base = pl.multiple_of(n * BATCH, BATCH)
        spots = [index[n // (128 // BATCH), n % (128 // BATCH) * BATCH + m] for m in range(BATCH)]
        ph = [recv[spot] for spot in spots]
        en = [recv[spot + CAP] for spot in spots]
        for m in range(BATCH):
            phases[pl.ds(base + m, 1)] = ph[m]
            energies[pl.ds(base + m, 1)] = en[m]
        return carry

    copies = []
    for quarter in range(4):
        lax.fori_loop(quarter * COUNT // BATCH // 4, (quarter + 1) * COUNT // BATCH // 4, get, 0)
        for k in range(quarter * 4, quarter * 4 + 4):
            rows = slice(k * NBS, (k + 1) * NBS)
            re, im = amps[rows, k : k + 1], amps[rows, GROUPS + k : GROUPS + k + 1]
            phases[rows], energies[rows] = pushed(phases[rows], energies[rows], re, im)
        span = pl.ds(quarter * COUNT // 4, COUNT // 4)
        copies.append(pltpu.make_async_copy(phases.at[span], phases_hbm.at[span], sems.at[1 + 2 * quarter]))
        copies.append(pltpu.make_async_copy(energies.at[span], energies_hbm.at[span], sems.at[2 + 2 * quarter]))
        for copy in copies[-2:]:
            copy.start()
    for copy in copies:
        copy.wait()


def twice_diffracted(planes, left, right):
    hi, lo = wide_halves(jnp.concatenate([jnp.concatenate(pair, axis=1) for pair in planes], axis=0))
    half = jnp.dot(jnp.concatenate([hi, lo, hi], axis=1), right[...], preferred_element_type=jnp.float32)
    cols = []
    for m in range(len(planes)):
        mid = half[m * GRID : (m + 1) * GRID]
        cols.append(jnp.concatenate([mid[:, :GRID], mid[:, GRID:]], axis=0))
    hi, lo = wide_halves(jnp.concatenate(cols, axis=1))
    full = jnp.dot(left[...], jnp.concatenate([hi, lo, hi], axis=0), preferred_element_type=jnp.float32)
    cuts = [slice(m * GRID, (m + 1) * GRID) for m in range(len(planes))]
    return [(full[:GRID, cut], full[GRID:, cut]) for cut in cuts]


def early_kernel(mine, piece_0, piece_1, beam, parts, out, left, right):
    lay_out(parts, left, right)
    even = mine[0] % 2 == 0
    planes = [tuple(jnp.where(even, piece_0[c, k], piece_1[c, k]) for c in range(2)) for k in range(EARLY)]
    planes.append((beam[2], jnp.zeros((GRID, GRID), jnp.float32)))
    for k, (re, im) in enumerate(twice_diffracted(planes, left, right)):
        out[0, k] = re
        out[1, k] = im


def last_kernel(
    mine, early, piece_b0, piece_b1, piece_b2, piece_c, small, beam, parts, out_hbm, acc, rest, out, left, right, sems
):
    me = mine[0]
    for n in range(4):
        acc[n] = GAIN * small[n]
    copies = []

    def plane(c, k):
        if k < 0:
            return jnp.zeros((GRID, GRID), jnp.float32)
        return early[c, k] if k < EARLY else rest[c, k - EARLY]

    def finish(low, high):
        for k in range(low, high):
            cr, ci, br, bi = (acc[n, k : k + 1] for n in range(4))
            re, im = (jnp.where(me < 2, plane(c, k - 1), plane(c, k)) for c in range(2))
            out[0, k] = re + (br * early[0, EARLY] - bi * early[1, EARLY]) + (cr * beam[0] - ci * beam[1])
            out[1, k] = im + (br * early[1, EARLY] + bi * early[0, EARLY]) + (cr * beam[1] + ci * beam[0])
        span = pl.ds(low, high - low)
        for c in range(2):
            copies.append(pltpu.make_async_copy(out.at[c, span], out_hbm.at[c, span], sems.at[len(copies)]))
            copies[-1].start()

    finish(0, EARLY)
    lay_out(parts, left, right)
    planes = [(piece[0, k], piece[1, k]) for piece in (piece_b0, piece_b1, piece_b2) for k in range(piece.shape[1])]
    for k, (re, im) in enumerate(twice_diffracted(planes, left, right)):
        rest[0, k] = re
        rest[1, k] = im
    finish(EARLY, LATE)
    planes = [(piece_c[0, k], piece_c[1, k]) for k in range(piece_c.shape[1])]
    for k, (re, im) in enumerate(twice_diffracted(planes, left, right)):
        rest[0, LATE - EARLY + k] = re
        rest[1, LATE - EARLY + k] = im
    finish(LATE, GROUPS)
    for copy in copies:
        copy.wait()


def early_pairs(core):
    onward = [(device, (device + 2) % PEERS) for device in range(core, PEERS, 2)]
    across = [(device, (device + 8) % PEERS) for device in range(1 - core, PEERS, 2) if device % 8 >= 6]
    return onward + across


def late_pairs():
    return [(device, device + 2 if device % 8 < 6 else device - 6) for device in range(PEERS)]


def shifted(value, axis, steps):
    count = lax.axis_size(axis)
    pairs = [(source, (source + steps) % count) for source in range(count)]
    return lax.ppermute(value, axis, pairs)


def shape(*dims, dtype=jnp.float32):
    return jax.ShapeDtypeStruct(dims, dtype)


def whole():
    return pl.BlockSpec(memory_space=pltpu.VMEM)


def vmem(*dims, dtype=jnp.float32):
    return pltpu.VMEM(dims, dtype)


def in_hbm(value):
    return pltpu.with_memory_space_constraint(value, pltpu.HBM)


def per_device(field, phase_bins, phase_jitter, energy, profile, delays):
    params = pltpu.CompilerParams(vmem_limit_bytes=VMEM_LIMIT)
    scalar = pl.BlockSpec(memory_space=pltpu.SMEM)
    remain = pl.BlockSpec(memory_space=pltpu.HBM)
    field = field.reshape(2, GROUPS, GRID, GRID)
    bins = phase_bins.reshape(COUNT, BLOCK)
    jitter = phase_jitter.reshape(COUNT, BLOCK)
    energies = energy.reshape(COUNT, BLOCK)
    mine = lax.axis_index("cuts").reshape(1)
    one, two = line_operator(1), line_operator(2)
    left_one = jnp.asarray(np.concatenate(one, axis=0), jnp.float32)
    right_one = jnp.asarray(right_form(*one), jnp.float32)
    core = mine[0] % 2
    shared_0 = lax.ppermute(lax.dynamic_slice_in_dim(field, core * (GROUPS - EARLY), EARLY, 1), "cuts", early_pairs(0))
    shared_1 = lax.ppermute(lax.dynamic_slice_in_dim(field, (1 - core) * (GROUPS - EARLY), EARLY, 1), "cuts", early_pairs(1))
    operands = [field, profile, bins, jitter, energies, delays.reshape(GROUPS, 1, NBS), left_one, right_one]
    send, phases1, energies1, places, beam, small1, *sources = pl.pallas_call(
        first_kernel,
        out_shape=(
            pltpu.HBM((ROWS, 1, BLOCK), jnp.float32),
            shape(COUNT, BLOCK),
            shape(COUNT, BLOCK),
            pltpu.HBM((8, COUNT), jnp.int32),
            pltpu.HBM((3, GRID, GRID), jnp.float32),
            shape(4, GROUPS, 128),
            *[pltpu.HBM((2, high - low, GRID, GRID), jnp.float32) for low, high in MIDDLE],
        ),
        in_specs=[scalar] + [remain] * 8,
        out_specs=(remain, whole(), whole(), remain, whole(), whole()) + (remain,) * len(MIDDLE),
        scratch_shapes=[
            vmem(2, GROUPS, GRID, GRID),
            vmem(GRID, GRID),
            vmem(COUNT, BLOCK, dtype=jnp.int32),
            vmem(COUNT, BLOCK),
            vmem(COUNT, BLOCK),
            vmem(GROUPS, 1, NBS, dtype=jnp.int32),
            vmem(2 * GRID, GRID),
            vmem(2 * GRID, 2 * GRID),
            vmem(6, GROUPS, 128),
            vmem(ROWS, 1, BLOCK),
            vmem(8, COUNT, dtype=jnp.int32),
            vmem(8, 128, dtype=jnp.int32),
            pltpu.SMEM((8, 128), jnp.int32),
            pltpu.SemaphoreType.DMA((17,)),
        ],
        compiler_params=params,
        name="push_place",
    )(mine, *[in_hbm(value) for value in operands])
    arrived1 = shifted(small1, "cuts", 1)
    send = pl.pallas_call(
        second_kernel,
        out_shape=pltpu.HBM((PEERS, MESSAGE, 1, BLOCK), jnp.float32),
        in_specs=[scalar] + [whole()] * 4 + [remain],
        out_specs=remain,
        scratch_shapes=[vmem(4, GROUPS, 128), vmem(PEERS, 1, 128), pltpu.SemaphoreType.DMA],
        input_output_aliases={5: 0},
        compiler_params=params,
        name="second_push",
    )(mine, phases1, energies1, arrived1, small1, in_hbm(send.reshape(PEERS, MESSAGE, 1, BLOCK)))
    field_b = [shifted(source, "cuts", 2) for source in sources]

    operator = quarters(*two)
    tables = [vmem(2 * GRID, 6 * GRID, dtype=jnp.bfloat16), vmem(6 * GRID, 2 * GRID, dtype=jnp.bfloat16)]

    def exchange(send, places, field, shared_0, shared_1, beam):
        early = pl.pallas_call(
            early_kernel,
            out_shape=shape(2, EARLY + 1, GRID, GRID),
            in_specs=[scalar] + [whole()] * 4,
            out_specs=whole(),
            scratch_shapes=tables,
            compiler_params=params,
            name="early_field",
        )(mine, in_hbm(shared_0), in_hbm(shared_1), in_hbm(beam), operator)
        handed = jnp.where(core == 0, shared_1, shared_0)
        source_c = jnp.where(mine[0] % 8 >= 6, handed[:, LATE - GROUPS :], field[:, LATE:])
        field_c = lax.ppermute(source_c, "cuts", late_pairs())
        recv = lax.all_to_all(send.reshape(ROWS, 1, BLOCK), "cuts", split_axis=0, concat_axis=0, tiled=True)
        recv, early = lax.optimization_barrier((recv, early))
        phase_out, energy_out, small = pl.pallas_call(
            pick_kernel,
            out_shape=(shape(COUNT, BLOCK), shape(COUNT, BLOCK), shape(4, GROUPS, 128)),
            in_specs=[scalar] + [whole()] * 2,
            out_specs=(remain, remain, whole()),
            scratch_shapes=[
                vmem(8, 128, dtype=jnp.int32),
                pltpu.SMEM((8, 128), jnp.int32),
                vmem(COUNT, 128),
                vmem(PEERS, 128),
                vmem(COUNT, BLOCK),
                vmem(COUNT, BLOCK),
                pltpu.SemaphoreType.DMA((9,)),
            ],
            compiler_params=params,
            name="pick",
        )(mine, recv, places)
        return phase_out, energy_out, early, field_c, small

    def refuse(*operands):
        sizes = [(COUNT, BLOCK)] * 2 + [(2, n, GRID, GRID) for n in (EARLY + 1, GROUPS - LATE)] + [(4, GROUPS, 128)]
        return tuple(jnp.zeros(size, jnp.float32) for size in sizes)

    phase_out, energy_out, early, field_c, small = lax.cond(
        mine[0] < PEERS, exchange, refuse, send, places, field, shared_0, shared_1, beam
    )
    out = pl.pallas_call(
        last_kernel,
        out_shape=shape(2, GROUPS, GRID, GRID),
        in_specs=[scalar] + [whole()] * 8,
        out_specs=remain,
        scratch_shapes=[
            vmem(4, GROUPS, 128),
            vmem(2, GROUPS - EARLY, GRID, GRID),
            vmem(2, GROUPS, GRID, GRID),
            *tables,
            pltpu.SemaphoreType.DMA((6,)),
        ],
        compiler_params=params,
        name="last_field",
    )(mine, early, *field_b, field_c, small, in_hbm(beam), operator)
    return (
        out.reshape(2, GROUPS, 1, GRID, GRID),
        phase_out.reshape(GROUPS, 1, NBS * BLOCK),
        energy_out.reshape(GROUPS, 1, NBS * BLOCK),
    )


def solution(mesh):
    return jax.shard_map(
        per_device,
        mesh=mesh,
        in_specs=(
            P(None, None, "cuts", None, None),
            P(None, "cuts", None),
            P(None, "cuts", None),
            P(None, "cuts", None),
            P(),
            P(),
        ),
        out_specs=(P(None, None, "cuts", None, None), P(None, "cuts", None), P(None, "cuts", None)),
        check_vma=False,
    )
```

```python
import functools
import math

import jax
import jax.numpy as jnp
import ml_dtypes
import numpy as np
from jax import lax
from jax.experimental import pallas as pl
from jax.experimental.pallas import tpu as pltpu
from jax.sharding import PartitionSpec as P

BLOCK = 128
NBINS = 16
KAPPA = 1.0
OMEGA = 1.0
GAIN = 16.0
PHASE_COEF = 20.0
GRID = 128
GROUPS = 16
NBS = 64
COUNT = GROUPS * NBS
PEERS = 128
CAP = 20
MESSAGE = 2 * CAP + 1
ROWS = PEERS * MESSAGE
BATCH = 32
EARLY, LATE = 4, 12
MIDDLE = ((4, 6), (6, 8), (8, 10), (10, 12))
VMEM_LIMIT = 24 * 1024 * 1024
HIGHEST = lax.Precision.HIGHEST


def line_operator(power):
    index = np.arange(GRID)
    freq = ((index + GRID // 2) % GRID - GRID // 2) / GRID
    weight = np.exp(-1j * PHASE_COEF * power * freq**2)
    wave = np.exp(2j * np.pi * (index[:, None] * index[None, :] % GRID) / GRID)
    column = wave @ weight / GRID
    matrix = column[(index[:, None] - index[None, :]) % GRID]
    return matrix.real, matrix.imag


def right_form(real, imag):
    return np.block([[real, imag], [-imag, real]])


def halves(matrix):
    high = matrix.astype(ml_dtypes.bfloat16)
    return high, (matrix - high.astype(np.float64)).astype(ml_dtypes.bfloat16)


def quarters(real, imag):
    return jnp.asarray(np.stack(halves(real) + halves(imag)))


def lay_out(parts, left, right):
    for n, low in enumerate((0, 0, 1)):
        re, im = parts[low], parts[2 + low]
        rest = slice(n * 2 * GRID, n * 2 * GRID + GRID), slice(n * 2 * GRID + GRID, (n + 1) * 2 * GRID)
        left[:GRID, rest[0]], left[:GRID, rest[1]] = re, -im
        left[GRID:, rest[0]], left[GRID:, rest[1]] = im, re
        right[rest[0], :GRID], right[rest[0], GRID:] = re, im
        right[rest[1], :GRID], right[rest[1], GRID:] = -im, re


def fitted(function, degree):
    top = (math.pi / 2 + 0.01) ** 2
    nodes = (np.cos(np.pi * (np.arange(400) + 0.5) / 400) + 1) / 2 * top
    series = np.polynomial.chebyshev.Chebyshev.fit(nodes, function(np.sqrt(nodes)), degree, domain=[0, top])
    return [float(c) for c in series.convert(kind=np.polynomial.Polynomial).coef]


SIN_COEF = fitted(lambda r: np.sin(r) / r, 5)
COS_COEF = fitted(np.cos, 6)
PI_HIGH = 3.140625
PI_MID = 9.67502593994140625e-4
PI_LOW = math.pi - PI_HIGH - PI_MID


def horner(coefs, x):
    value = jnp.float32(coefs[-1])
    for c in coefs[-2::-1]:
        value = value * x + jnp.float32(c)
    return value


def cos_sin(x):
    turns = jnp.round(x * jnp.float32(1.0 / math.pi))
    r = x - turns * jnp.float32(PI_HIGH)
    r = r - turns * jnp.float32(PI_MID)
    r = r - turns * jnp.float32(PI_LOW)
    half = turns * 0.5
    sign = 1.0 - 4.0 * jnp.abs(half - jnp.round(half))
    square = r * r
    return horner(COS_COEF, square) * sign, horner(SIN_COEF, square) * (r * sign)


def lane_total(rows):
    return jnp.broadcast_to(jnp.sum(rows, axis=1, keepdims=True), rows.shape)


def slots_of(delays):
    row = jnp.concatenate([delays[k] for k in range(GROUPS)], axis=1)
    values = lax.broadcasted_iota(jnp.int32, (PEERS, COUNT), 0)
    onehot = jnp.where(values == row, 1.0, 0.0)
    before = lax.broadcasted_iota(jnp.int32, (COUNT, COUNT), 0) < lax.broadcasted_iota(jnp.int32, (COUNT, COUNT), 1)
    upper = jnp.where(before, 1.0, 0.0).astype(jnp.bfloat16)
    earlier = jnp.dot(onehot.astype(jnp.bfloat16), upper, preferred_element_type=jnp.float32)
    return row, jnp.sum(earlier * onehot, axis=0, keepdims=True).astype(jnp.int32)


def folded(row):
    return jnp.concatenate([row[:, n * 128 : (n + 1) * 128] for n in range(COUNT // 128)], axis=0)


def rows_of(k):
    return pl.ds(pl.multiple_of(k * NBS, NBS), NBS)


def first_kernel(
    mine, field_hbm, profile_hbm, bins_hbm, jitter_hbm, energy_hbm, delays_hbm, left_hbm, right_hbm,
    send_hbm, phases, energies, places_hbm, beam, small, middle_0, middle_1, middle_2, middle_3,
    field, profile, bins, jitter, energy, delays, left, right, acc, send, places, index_v, index, sems,
):
    pairs = [
        (profile_hbm, profile), (left_hbm, left), (right_hbm, right), (delays_hbm, delays),
        (field_hbm, field), (bins_hbm, bins), (jitter_hbm, jitter), (energy_hbm, energy),
    ]
    copies = [pltpu.make_async_copy(src, dst, sems.at[n]) for n, (src, dst) in enumerate(pairs)]
    for copy in copies:
        copy.start()
    copies[3].wait()
    row, slot = slots_of(delays)
    places[0:1] = row
    places[1:2] = slot
    index_v[...] = folded(((mine[0] + row) % PEERS) * MESSAGE + slot)
    to_scalar = pltpu.make_async_copy(index_v, index, sems.at[3])
    to_scalar.start()
    for copy in copies[:3]:
        copy.wait()
    p = profile[...]
    half = jnp.dot(left[...], p, precision=HIGHEST, preferred_element_type=jnp.float32)
    both = jnp.concatenate([half[:GRID], half[GRID:]], axis=1)
    spread = jnp.dot(both, right[...], precision=HIGHEST, preferred_element_type=jnp.float32)
    beam[0] = spread[:, :GRID]
    beam[1] = spread[:, GRID:]
    beam[2] = p
    copies[4].wait()
    kept = [pltpu.make_async_copy(places, places_hbm, sems.at[8])]
    for middle, (low, high) in zip((middle_0, middle_1, middle_2, middle_3), MIDDLE):
        for c in range(2):
            span = pl.ds(low, high - low)
            kept.append(pltpu.make_async_copy(field.at[c, span], middle.at[c], sems.at[8 + len(kept)]))
    for copy in kept:
        copy.start()

    def project(k, carry):
        re, im = field[0, k], field[1, k]
        dr, di, q = beam[0], beam[1], profile[...]
        acc[0, pl.ds(k, 1)] = jnp.sum(q * re, axis=0, keepdims=True)
        acc[1, pl.ds(k, 1)] = jnp.sum(q * im, axis=0, keepdims=True)
        acc[2, pl.ds(k, 1)] = jnp.sum(dr * re - di * im, axis=0, keepdims=True)
        acc[3, pl.ds(k, 1)] = jnp.sum(dr * im + di * re, axis=0, keepdims=True)
        return carry

    lax.fori_loop(0, GROUPS, project, 0)
    self_re = jnp.sum(p * beam[0])
    self_im = jnp.sum(p * beam[1])
    for n in range(4):
        acc[n] = lane_total(acc[n]) * (1.0 / GRID)
    for copy in copies[5:]:
        copy.wait()

    def push(k, carry):
        rows = rows_of(k)
        ph = jnp.float32(2.0 * math.pi / NBINS) * (bins[rows].astype(jnp.float32) + jitter[rows])
        ph, en = pushed(ph, energy[rows], acc[0, pl.ds(k, 1)], acc[1, pl.ds(k, 1)])
        phases[rows] = ph
        energies[rows] = en
        c, s = cos_sin(ph)
        acc[4, pl.ds(k, 1)] = jnp.sum(c, axis=0, keepdims=True)
        acc[5, pl.ds(k, 1)] = jnp.sum(s, axis=0, keepdims=True)
        return carry

    lax.fori_loop(0, GROUPS, push, 0)
    to_scalar.wait()

    def put(n, carry):
        base = pl.multiple_of(n * BATCH, BATCH)
        spots = [index[n // (128 // BATCH), n % (128 // BATCH) * BATCH + m] for m in range(BATCH)]
        ph = [phases[pl.ds(base + m, 1)] for m in range(BATCH)]
        en = [energies[pl.ds(base + m, 1)] for m in range(BATCH)]
        for m in range(BATCH):
            send[spots[m]] = ph[m]
            send[spots[m] + CAP] = en[m]
        return carry

    lax.fori_loop(0, COUNT // BATCH, put, 0)
    bre = lane_total(acc[4]) * (1.0 / (NBS * BLOCK))
    bim = lane_total(acc[5]) * (-1.0 / (NBS * BLOCK))
    gain = GAIN / GRID
    next_re = acc[2] + gain * (bre * self_re - bim * self_im)
    next_im = acc[3] + gain * (bre * self_im + bim * self_re)
    for n, part in enumerate((next_re, next_im, bre, bim)):
        small[n] = part
    out = pltpu.make_async_copy(send, send_hbm, sems.at[0])
    out.start()
    for copy in kept:
        copy.wait()
    out.wait()


def pushed(ph, en, amp_re, amp_im):
    c, s = cos_sin(ph)
    en = en - KAPPA * (amp_re * c - amp_im * s)
    return ph + OMEGA * en, en


def one_row(parts):
    rest = 128 // GROUPS - len(parts)
    stack = jnp.concatenate(parts + [jnp.zeros((rest * GROUPS, 128), jnp.float32)], axis=0)
    return stack.T[0:1]


def carried(value, flag):
    rolled = jnp.concatenate([jnp.zeros_like(value[:1]), value[:-1]], axis=0)
    return jnp.where(flag, rolled, value)


def second_kernel(mine, phases1, energies1, arrived, own, send_in, send, acc, note, sem):
    del send_in
    for n in range(2):
        acc[n] = carried(arrived[n], mine[0] == 0)

    def push(k, carry):
        rows = rows_of(k)
        ph, _ = pushed(phases1[rows], energies1[rows], acc[0, pl.ds(k, 1)], acc[1, pl.ds(k, 1)])
        c, s = cos_sin(ph)
        acc[2, pl.ds(k, 1)] = jnp.sum(c, axis=0, keepdims=True)
        acc[3, pl.ds(k, 1)] = jnp.sum(s, axis=0, keepdims=True)
        return carry

    lax.fori_loop(0, GROUPS, push, 0)
    mean = 1.0 / (NBS * BLOCK)
    row = one_row([own[n] for n in range(4)] + [lane_total(acc[2]) * mean, lane_total(acc[3]) * -mean])
    note[...] = jnp.broadcast_to(row[None], (PEERS, 1, 128))
    copy = pltpu.make_async_copy(note, send.at[:, 2 * CAP], sem)
    copy.start()
    copy.wait()


def wide_halves(x):
    high = x.astype(jnp.bfloat16)
    return high, (x - high.astype(jnp.float32)).astype(jnp.bfloat16)


def pick_kernel(mine, recv, places, phases_hbm, energies_hbm, small, index_v, index, amps, notes, phases, energies, sems):
    me = mine[0]
    source = (me - places[0:1] + PEERS) % PEERS
    index_v[...] = folded(source * MESSAGE + places[1:2])
    to_scalar = pltpu.make_async_copy(index_v, index, sems.at[0])
    to_scalar.start()
    lane = lax.broadcasted_iota(jnp.int32, (128, 128), 1)
    for n in range(PEERS):
        notes[n : n + 1] = recv[n * MESSAGE + 2 * CAP]
    sheet = notes[...]
    near = jnp.broadcast_to(notes[pl.ds((me + PEERS - 1) % PEERS, 1)], (128, 128)).T
    far = jnp.broadcast_to(notes[pl.ds((me + PEERS - 2) % PEERS, 1)], (128, 128)).T
    for n in range(2):
        small[n] = carried(near[(4 + n) * GROUPS : (5 + n) * GROUPS], me == 0)
        small[2 + n] = carried(far[(2 + n) * GROUPS : (3 + n) * GROUPS], me < 2)
    wrapped = jnp.concatenate([sheet[127:128, 127:128], sheet[127:128, :127]], axis=1)
    wrapped = jnp.where(lane[0:1] % GROUPS == 0, 0.0, wrapped)
    sheet = jnp.concatenate([wrapped, sheet[:127]], axis=0)
    kept = jnp.where(lane < 2 * GROUPS, sheet, 0.0)
    high, rest = wide_halves(kept)
    low = (kept - high.astype(jnp.float32) - rest.astype(jnp.float32)).astype(jnp.bfloat16)
    thirds = jnp.concatenate([high, rest, low], axis=1)
    onehot = jnp.concatenate(
        [
            jnp.where(lane == jnp.broadcast_to(source[:, n * 128 : (n + 1) * 128], (128, 128)).T, 1.0, 0.0)
            for n in range(COUNT // 128)
        ],
        axis=0,
    )
    found = jnp.dot(onehot.astype(jnp.bfloat16), thirds, preferred_element_type=jnp.float32)
    amps[...] = found[:, :128] + found[:, 128:256] + found[:, 256:]
    to_scalar.wait()

    def get(n, carry):
        base = pl.multiple_of(n * BATCH, BATCH)
        spots = [index[n // (128 // BATCH), n % (128 // BATCH) * BATCH + m] for m in range(BATCH)]
        ph = [recv[spot] for spot in spots]
        en = [recv[spot + CAP] for spot in spots]
        for m in range(BATCH):
            phases[pl.ds(base + m, 1)] = ph[m]
            energies[pl.ds(base + m, 1)] = en[m]
        return carry

    copies = []
    for quarter in range(4):
        lax.fori_loop(quarter * COUNT // BATCH // 4, (quarter + 1) * COUNT // BATCH // 4, get, 0)
        for k in range(quarter * 4, quarter * 4 + 4):
            rows = slice(k * NBS, (k + 1) * NBS)
            re, im = amps[rows, k : k + 1], amps[rows, GROUPS + k : GROUPS + k + 1]
            phases[rows], energies[rows] = pushed(phases[rows], energies[rows], re, im)
        span = pl.ds(quarter * COUNT // 4, COUNT // 4)
        copies.append(pltpu.make_async_copy(phases.at[span], phases_hbm.at[span], sems.at[1 + 2 * quarter]))
        copies.append(pltpu.make_async_copy(energies.at[span], energies_hbm.at[span], sems.at[2 + 2 * quarter]))
        for copy in copies[-2:]:
            copy.start()
    for copy in copies:
        copy.wait()


def twice_diffracted(planes, left, right):
    hi, lo = wide_halves(jnp.concatenate([jnp.concatenate(pair, axis=1) for pair in planes], axis=0))
    half = jnp.dot(jnp.concatenate([hi, lo, hi], axis=1), right[...], preferred_element_type=jnp.float32)
    cols = []
    for m in range(len(planes)):
        mid = half[m * GRID : (m + 1) * GRID]
        cols.append(jnp.concatenate([mid[:, :GRID], mid[:, GRID:]], axis=0))
    hi, lo = wide_halves(jnp.concatenate(cols, axis=1))
    full = jnp.dot(left[...], jnp.concatenate([hi, lo, hi], axis=0), preferred_element_type=jnp.float32)
    cuts = [slice(m * GRID, (m + 1) * GRID) for m in range(len(planes))]
    return [(full[:GRID, cut], full[GRID:, cut]) for cut in cuts]


def early_kernel(mine, piece_0, piece_1, beam, parts, out, left, right):
    lay_out(parts, left, right)
    even = mine[0] % 2 == 0
    planes = [tuple(jnp.where(even, piece_0[c, k], piece_1[c, k]) for c in range(2)) for k in range(EARLY)]
    planes.append((beam[2], jnp.zeros((GRID, GRID), jnp.float32)))
    for k, (re, im) in enumerate(twice_diffracted(planes, left, right)):
        out[0, k] = re
        out[1, k] = im


def last_kernel(
    mine, early, piece_b0, piece_b1, piece_b2, piece_b3, piece_c, small, beam, parts, out_hbm, acc, rest, out, left, right, sems
):
    me = mine[0]
    for n in range(4):
        acc[n] = GAIN * small[n]
    copies = []

    def plane(c, k):
        if k < 0:
            return jnp.zeros((GRID, GRID), jnp.float32)
        return early[c, k] if k < EARLY else rest[c, k - EARLY]

    def finish(low, high):
        for k in range(low, high):
            cr, ci, br, bi = (acc[n, k : k + 1] for n in range(4))
            re, im = (jnp.where(me < 2, plane(c, k - 1), plane(c, k)) for c in range(2))
            out[0, k] = re + (br * early[0, EARLY] - bi * early[1, EARLY]) + (cr * beam[0] - ci * beam[1])
            out[1, k] = im + (br * early[1, EARLY] + bi * early[0, EARLY]) + (cr * beam[1] + ci * beam[0])
        span = pl.ds(low, high - low)
        for c in range(2):
            copies.append(pltpu.make_async_copy(out.at[c, span], out_hbm.at[c, span], sems.at[len(copies)]))
            copies[-1].start()

    finish(0, EARLY)
    lay_out(parts, left, right)
    planes = [(piece[0, k], piece[1, k]) for piece in (piece_b0, piece_b1, piece_b2, piece_b3) for k in range(piece.shape[1])]
    for k, (re, im) in enumerate(twice_diffracted(planes, left, right)):
        rest[0, k] = re
        rest[1, k] = im
    finish(EARLY, LATE)
    planes = [(piece_c[0, k], piece_c[1, k]) for k in range(piece_c.shape[1])]
    for k, (re, im) in enumerate(twice_diffracted(planes, left, right)):
        rest[0, LATE - EARLY + k] = re
        rest[1, LATE - EARLY + k] = im
    finish(LATE, GROUPS)
    for copy in copies:
        copy.wait()


def early_pairs(core):
    onward = [(device, (device + 2) % PEERS) for device in range(core, PEERS, 2)]
    across = [(device, (device + 8) % PEERS) for device in range(1 - core, PEERS, 2) if device % 8 >= 6]
    return onward + across


def late_pairs():
    return [(device, device + 2 if device % 8 < 6 else device - 6) for device in range(PEERS)]


def shifted(value, axis, steps):
    count = lax.axis_size(axis)
    pairs = [(source, (source + steps) % count) for source in range(count)]
    return lax.ppermute(value, axis, pairs)


def shape(*dims, dtype=jnp.float32):
    return jax.ShapeDtypeStruct(dims, dtype)


def whole():
    return pl.BlockSpec(memory_space=pltpu.VMEM)


def vmem(*dims, dtype=jnp.float32):
    return pltpu.VMEM(dims, dtype)


def in_hbm(value):
    return pltpu.with_memory_space_constraint(value, pltpu.HBM)


def per_device(field, phase_bins, phase_jitter, energy, profile, delays):
    params = pltpu.CompilerParams(vmem_limit_bytes=VMEM_LIMIT)
    scalar = pl.BlockSpec(memory_space=pltpu.SMEM)
    remain = pl.BlockSpec(memory_space=pltpu.HBM)
    field = field.reshape(2, GROUPS, GRID, GRID)
    bins = phase_bins.reshape(COUNT, BLOCK)
    jitter = phase_jitter.reshape(COUNT, BLOCK)
    energies = energy.reshape(COUNT, BLOCK)
    mine = lax.axis_index("cuts").reshape(1)
    one, two = line_operator(1), line_operator(2)
    left_one = jnp.asarray(np.concatenate(one, axis=0), jnp.float32)
    right_one = jnp.asarray(right_form(*one), jnp.float32)
    core = mine[0] % 2
    shared_0 = lax.ppermute(lax.dynamic_slice_in_dim(field, core * (GROUPS - EARLY), EARLY, 1), "cuts", early_pairs(0))
    shared_1 = lax.ppermute(lax.dynamic_slice_in_dim(field, (1 - core) * (GROUPS - EARLY), EARLY, 1), "cuts", early_pairs(1))
    operands = [field, profile, bins, jitter, energies, delays.reshape(GROUPS, 1, NBS), left_one, right_one]
    send, phases1, energies1, places, beam, small1, *sources = pl.pallas_call(
        first_kernel,
        out_shape=(
            pltpu.HBM((ROWS, 1, BLOCK), jnp.float32),
            shape(COUNT, BLOCK),
            shape(COUNT, BLOCK),
            pltpu.HBM((8, COUNT), jnp.int32),
            pltpu.HBM((3, GRID, GRID), jnp.float32),
            shape(4, GROUPS, 128),
            *[pltpu.HBM((2, high - low, GRID, GRID), jnp.float32) for low, high in MIDDLE],
        ),
        in_specs=[scalar] + [remain] * 8,
        out_specs=(remain, whole(), whole(), remain, whole(), whole()) + (remain,) * len(MIDDLE),
        scratch_shapes=[
            vmem(2, GROUPS, GRID, GRID),
            vmem(GRID, GRID),
            vmem(COUNT, BLOCK, dtype=jnp.int32),
            vmem(COUNT, BLOCK),
            vmem(COUNT, BLOCK),
            vmem(GROUPS, 1, NBS, dtype=jnp.int32),
            vmem(2 * GRID, GRID),
            vmem(2 * GRID, 2 * GRID),
            vmem(6, GROUPS, 128),
            vmem(ROWS, 1, BLOCK),
            vmem(8, COUNT, dtype=jnp.int32),
            vmem(8, 128, dtype=jnp.int32),
            pltpu.SMEM((8, 128), jnp.int32),
            pltpu.SemaphoreType.DMA((17,)),
        ],
        compiler_params=params,
        name="push_place",
    )(mine, *[in_hbm(value) for value in operands])
    arrived1 = shifted(small1, "cuts", 1)
    send = pl.pallas_call(
        second_kernel,
        out_shape=pltpu.HBM((PEERS, MESSAGE, 1, BLOCK), jnp.float32),
        in_specs=[scalar] + [whole()] * 4 + [remain],
        out_specs=remain,
        scratch_shapes=[vmem(4, GROUPS, 128), vmem(PEERS, 1, 128), pltpu.SemaphoreType.DMA],
        input_output_aliases={5: 0},
        compiler_params=params,
        name="second_push",
    )(mine, phases1, energies1, arrived1, small1, in_hbm(send.reshape(PEERS, MESSAGE, 1, BLOCK)))
    field_b = [shifted(source, "cuts", 2) for source in sources]

    operator = quarters(*two)
    tables = [vmem(2 * GRID, 6 * GRID, dtype=jnp.bfloat16), vmem(6 * GRID, 2 * GRID, dtype=jnp.bfloat16)]

    def exchange(send, places, field, shared_0, shared_1, beam):
        early = pl.pallas_call(
            early_kernel,
            out_shape=shape(2, EARLY + 1, GRID, GRID),
            in_specs=[scalar] + [whole()] * 4,
            out_specs=whole(),
            scratch_shapes=tables,
            compiler_params=params,
            name="early_field",
        )(mine, in_hbm(shared_0), in_hbm(shared_1), in_hbm(beam), operator)
        handed = jnp.where(core == 0, shared_1, shared_0)
        source_c = jnp.where(mine[0] % 8 >= 6, handed[:, LATE - GROUPS :], field[:, LATE:])
        field_c = lax.ppermute(source_c, "cuts", late_pairs())
        recv = lax.all_to_all(send.reshape(ROWS, 1, BLOCK), "cuts", split_axis=0, concat_axis=0, tiled=True)
        recv, early = lax.optimization_barrier((recv, early))
        phase_out, energy_out, small = pl.pallas_call(
            pick_kernel,
            out_shape=(shape(COUNT, BLOCK), shape(COUNT, BLOCK), shape(4, GROUPS, 128)),
            in_specs=[scalar] + [whole()] * 2,
            out_specs=(remain, remain, whole()),
            scratch_shapes=[
                vmem(8, 128, dtype=jnp.int32),
                pltpu.SMEM((8, 128), jnp.int32),
                vmem(COUNT, 128),
                vmem(PEERS, 128),
                vmem(COUNT, BLOCK),
                vmem(COUNT, BLOCK),
                pltpu.SemaphoreType.DMA((9,)),
            ],
            compiler_params=params,
            name="pick",
        )(mine, recv, places)
        return phase_out, energy_out, early, field_c, small

    def refuse(*operands):
        sizes = [(COUNT, BLOCK)] * 2 + [(2, n, GRID, GRID) for n in (EARLY + 1, GROUPS - LATE)] + [(4, GROUPS, 128)]
        return tuple(jnp.zeros(size, jnp.float32) for size in sizes)

    phase_out, energy_out, early, field_c, small = lax.cond(
        mine[0] < PEERS, exchange, refuse, send, places, field, shared_0, shared_1, beam
    )
    out = pl.pallas_call(
        last_kernel,
        out_shape=shape(2, GROUPS, GRID, GRID),
        in_specs=[scalar] + [whole()] * 9,
        out_specs=remain,
        scratch_shapes=[
            vmem(4, GROUPS, 128),
            vmem(2, GROUPS - EARLY, GRID, GRID),
            vmem(2, GROUPS, GRID, GRID),
            *tables,
            pltpu.SemaphoreType.DMA((6,)),
        ],
        compiler_params=params,
        name="last_field",
    )(mine, early, *field_b, field_c, small, in_hbm(beam), operator)
    return (
        out.reshape(2, GROUPS, 1, GRID, GRID),
        phase_out.reshape(GROUPS, 1, NBS * BLOCK),
        energy_out.reshape(GROUPS, 1, NBS * BLOCK),
    )


def solution(mesh):
    return jax.shard_map(
        per_device,
        mesh=mesh,
        in_specs=(
            P(None, None, "cuts", None, None),
            P(None, "cuts", None),
            P(None, "cuts", None),
            P(None, "cuts", None),
            P(),
            P(),
        ),
        out_specs=(P(None, None, "cuts", None, None), P(None, "cuts", None), P(None, "cuts", None)),
        check_vma=False,
    )
```

```python
import functools
import math

import jax
import jax.numpy as jnp
import ml_dtypes
import numpy as np
from jax import lax
from jax.experimental import pallas as pl
from jax.experimental.pallas import tpu as pltpu
from jax.sharding import PartitionSpec as P

BLOCK = 128
NBINS = 16
KAPPA = 1.0
OMEGA = 1.0
GAIN = 16.0
PHASE_COEF = 20.0
GRID = 128
GROUPS = 16
NBS = 64
COUNT = GROUPS * NBS
PEERS = 128
CAP = 20
MESSAGE = 2 * CAP + 1
ROWS = PEERS * MESSAGE
BATCH = 32
EARLY, LATE = 4, 12
MIDDLE = ((4, 6), (6, 8), (8, 10), (10, 12))
VMEM_LIMIT = 24 * 1024 * 1024
HIGHEST = lax.Precision.HIGHEST


def line_operator(power):
    index = np.arange(GRID)
    freq = ((index + GRID // 2) % GRID - GRID // 2) / GRID
    weight = np.exp(-1j * PHASE_COEF * power * freq**2)
    wave = np.exp(2j * np.pi * (index[:, None] * index[None, :] % GRID) / GRID)
    column = wave @ weight / GRID
    matrix = column[(index[:, None] - index[None, :]) % GRID]
    return matrix.real, matrix.imag


def right_form(real, imag):
    return np.block([[real, imag], [-imag, real]])


def halves(matrix):
    high = matrix.astype(ml_dtypes.bfloat16)
    return high, (matrix - high.astype(np.float64)).astype(ml_dtypes.bfloat16)


def quarters(real, imag):
    return jnp.asarray(np.stack(halves(real) + halves(imag)))


def lay_out(parts, left, right):
    for n, low in enumerate((0, 0, 1)):
        re, im = parts[low], parts[2 + low]
        rest = slice(n * 2 * GRID, n * 2 * GRID + GRID), slice(n * 2 * GRID + GRID, (n + 1) * 2 * GRID)
        left[:GRID, rest[0]], left[:GRID, rest[1]] = re, -im
        left[GRID:, rest[0]], left[GRID:, rest[1]] = im, re
        right[rest[0], :GRID], right[rest[0], GRID:] = re, im
        right[rest[1], :GRID], right[rest[1], GRID:] = -im, re


def fitted(function, degree):
    top = (math.pi / 2 + 0.01) ** 2
    nodes = (np.cos(np.pi * (np.arange(400) + 0.5) / 400) + 1) / 2 * top
    series = np.polynomial.chebyshev.Chebyshev.fit(nodes, function(np.sqrt(nodes)), degree, domain=[0, top])
    return [float(c) for c in series.convert(kind=np.polynomial.Polynomial).coef]


SIN_COEF = fitted(lambda r: np.sin(r) / r, 5)
COS_COEF = fitted(np.cos, 6)
PI_HIGH = 3.140625
PI_MID = 9.67502593994140625e-4
PI_LOW = math.pi - PI_HIGH - PI_MID


def horner(coefs, x):
    value = jnp.float32(coefs[-1])
    for c in coefs[-2::-1]:
        value = value * x + jnp.float32(c)
    return value


def cos_sin(x):
    turns = jnp.round(x * jnp.float32(1.0 / math.pi))
    r = x - turns * jnp.float32(PI_HIGH)
    r = r - turns * jnp.float32(PI_MID)
    r = r - turns * jnp.float32(PI_LOW)
    half = turns * 0.5
    sign = 1.0 - 4.0 * jnp.abs(half - jnp.round(half))
    square = r * r
    return horner(COS_COEF, square) * sign, horner(SIN_COEF, square) * (r * sign)


def lane_total(rows):
    return jnp.broadcast_to(jnp.sum(rows, axis=1, keepdims=True), rows.shape)


def slots_of(delays):
    row = jnp.concatenate([delays[k] for k in range(GROUPS)], axis=1)
    values = lax.broadcasted_iota(jnp.int32, (PEERS, COUNT), 0)
    onehot = jnp.where(values == row, 1.0, 0.0)
    before = lax.broadcasted_iota(jnp.int32, (COUNT, COUNT), 0) < lax.broadcasted_iota(jnp.int32, (COUNT, COUNT), 1)
    upper = jnp.where(before, 1.0, 0.0).astype(jnp.bfloat16)
    earlier = jnp.dot(onehot.astype(jnp.bfloat16), upper, preferred_element_type=jnp.float32)
    return row, jnp.sum(earlier * onehot, axis=0, keepdims=True).astype(jnp.int32)


def folded(row):
    return jnp.concatenate([row[:, n * 128 : (n + 1) * 128] for n in range(COUNT // 128)], axis=0)


def rows_of(k):
    return pl.ds(pl.multiple_of(k * NBS, NBS), NBS)


def first_kernel(
    mine, field_hbm, profile_hbm, bins_hbm, jitter_hbm, energy_hbm, delays_hbm, left_hbm, right_hbm,
    send_hbm, phases, energies, places_hbm, beam, small, middle_0, middle_1, middle_2, middle_3,
    field, profile, bins, jitter, energy, delays, left, right, acc, send, places, index_v, index, sems,
):
    pairs = [
        (profile_hbm, profile), (left_hbm, left), (right_hbm, right), (delays_hbm, delays),
        (field_hbm, field), (bins_hbm, bins), (jitter_hbm, jitter), (energy_hbm, energy),
    ]
    copies = [pltpu.make_async_copy(src, dst, sems.at[n]) for n, (src, dst) in enumerate(pairs)]
    for copy in copies:
        copy.start()
    copies[3].wait()
    row, slot = slots_of(delays)
    places[0:1] = row
    places[1:2] = slot
    index_v[...] = folded(((mine[0] + row) % PEERS) * MESSAGE + slot)
    to_scalar = pltpu.make_async_copy(index_v, index, sems.at[3])
    to_scalar.start()
    for copy in copies[:3]:
        copy.wait()
    p = profile[...]
    half = jnp.dot(left[...], p, precision=HIGHEST, preferred_element_type=jnp.float32)
    both = jnp.concatenate([half[:GRID], half[GRID:]], axis=1)
    spread = jnp.dot(both, right[...], precision=HIGHEST, preferred_element_type=jnp.float32)
    beam[0] = spread[:, :GRID]
    beam[1] = spread[:, GRID:]
    beam[2] = p
    copies[4].wait()
    kept = [pltpu.make_async_copy(places, places_hbm, sems.at[8])]
    for middle, (low, high) in zip((middle_0, middle_1, middle_2, middle_3), MIDDLE):
        for c in range(2):
            span = pl.ds(low, high - low)
            kept.append(pltpu.make_async_copy(field.at[c, span], middle.at[c], sems.at[8 + len(kept)]))
    for copy in kept:
        copy.start()

    def project(k, carry):
        re, im = field[0, k], field[1, k]
        dr, di, q = beam[0], beam[1], profile[...]
        acc[0, pl.ds(k, 1)] = jnp.sum(q * re, axis=0, keepdims=True)
        acc[1, pl.ds(k, 1)] = jnp.sum(q * im, axis=0, keepdims=True)
        acc[2, pl.ds(k, 1)] = jnp.sum(dr * re - di * im, axis=0, keepdims=True)
        acc[3, pl.ds(k, 1)] = jnp.sum(dr * im + di * re, axis=0, keepdims=True)
        return carry

    lax.fori_loop(0, GROUPS, project, 0)
    self_re = jnp.sum(p * beam[0])
    self_im = jnp.sum(p * beam[1])
    for n in range(4):
        acc[n] = lane_total(acc[n]) * (1.0 / GRID)
    for copy in copies[5:]:
        copy.wait()

    def push(k, carry):
        rows = rows_of(k)
        ph = jnp.float32(2.0 * math.pi / NBINS) * (bins[rows].astype(jnp.float32) + jitter[rows])
        ph, en = pushed(ph, energy[rows], acc[0, pl.ds(k, 1)], acc[1, pl.ds(k, 1)])
        phases[rows] = ph
        energies[rows] = en
        c, s = cos_sin(ph)
        acc[4, pl.ds(k, 1)] = jnp.sum(c, axis=0, keepdims=True)
        acc[5, pl.ds(k, 1)] = jnp.sum(s, axis=0, keepdims=True)
        return carry

    lax.fori_loop(0, GROUPS, push, 0)
    to_scalar.wait()

    def put_rows(rows, offset):
        def put(n, carry):
            base = pl.multiple_of(n * BATCH, BATCH)
            spots = [index[n // (128 // BATCH), n % (128 // BATCH) * BATCH + m] for m in range(BATCH)]
            taken = [rows[pl.ds(base + m, 1)] for m in range(BATCH)]
            for m in range(BATCH):
                send[spots[m] + offset] = taken[m]
            return carry

        lax.fori_loop(0, COUNT // BATCH, put, 0)
        part = send.reshape(PEERS, MESSAGE, 1, BLOCK).at[:, pl.ds(offset, CAP)]
        kept.append(pltpu.make_async_copy(part, send_hbm.at[:, pl.ds(offset, CAP)], sems.at[offset // CAP]))
        kept[-1].start()

    put_rows(phases, 0)
    put_rows(energies, CAP)
    bre = lane_total(acc[4]) * (1.0 / (NBS * BLOCK))
    bim = lane_total(acc[5]) * (-1.0 / (NBS * BLOCK))
    gain = GAIN / GRID
    next_re = acc[2] + gain * (bre * self_re - bim * self_im)
    next_im = acc[3] + gain * (bre * self_im + bim * self_re)
    for n, part in enumerate((next_re, next_im, bre, bim)):
        small[n] = part
    for copy in kept:
        copy.wait()


def pushed(ph, en, amp_re, amp_im):
    c, s = cos_sin(ph)
    en = en - KAPPA * (amp_re * c - amp_im * s)
    return ph + OMEGA * en, en


def one_row(parts):
    rest = 128 // GROUPS - len(parts)
    stack = jnp.concatenate(parts + [jnp.zeros((rest * GROUPS, 128), jnp.float32)], axis=0)
    return stack.T[0:1]


def carried(value, flag):
    rolled = jnp.concatenate([jnp.zeros_like(value[:1]), value[:-1]], axis=0)
    return jnp.where(flag, rolled, value)


def second_kernel(mine, phases1, energies1, arrived, own, send_in, send, acc, note, sem):
    del send_in
    for n in range(2):
        acc[n] = carried(arrived[n], mine[0] == 0)

    def push(k, carry):
        rows = rows_of(k)
        ph, _ = pushed(phases1[rows], energies1[rows], acc[0, pl.ds(k, 1)], acc[1, pl.ds(k, 1)])
        c, s = cos_sin(ph)
        acc[2, pl.ds(k, 1)] = jnp.sum(c, axis=0, keepdims=True)
        acc[3, pl.ds(k, 1)] = jnp.sum(s, axis=0, keepdims=True)
        return carry

    lax.fori_loop(0, GROUPS, push, 0)
    mean = 1.0 / (NBS * BLOCK)
    row = one_row([own[n] for n in range(4)] + [lane_total(acc[2]) * mean, lane_total(acc[3]) * -mean])
    note[...] = jnp.broadcast_to(row[None], (PEERS, 1, 128))
    copy = pltpu.make_async_copy(note, send.at[:, 2 * CAP], sem)
    copy.start()
    copy.wait()


def wide_halves(x):
    high = x.astype(jnp.bfloat16)
    return high, (x - high.astype(jnp.float32)).astype(jnp.bfloat16)


def pick_kernel(mine, recv, places, phases_hbm, energies_hbm, small, index_v, index, amps, notes, phases, energies, sems):
    me = mine[0]
    source = (me - places[0:1] + PEERS) % PEERS
    index_v[...] = folded(source * MESSAGE + places[1:2])
    to_scalar = pltpu.make_async_copy(index_v, index, sems.at[0])
    to_scalar.start()
    lane = lax.broadcasted_iota(jnp.int32, (128, 128), 1)
    for n in range(PEERS):
        notes[n : n + 1] = recv[n * MESSAGE + 2 * CAP]
    sheet = notes[...]
    near = jnp.broadcast_to(notes[pl.ds((me + PEERS - 1) % PEERS, 1)], (128, 128)).T
    far = jnp.broadcast_to(notes[pl.ds((me + PEERS - 2) % PEERS, 1)], (128, 128)).T
    for n in range(2):
        small[n] = carried(near[(4 + n) * GROUPS : (5 + n) * GROUPS], me == 0)
        small[2 + n] = carried(far[(2 + n) * GROUPS : (3 + n) * GROUPS], me < 2)
    wrapped = jnp.concatenate([sheet[127:128, 127:128], sheet[127:128, :127]], axis=1)
    wrapped = jnp.where(lane[0:1] % GROUPS == 0, 0.0, wrapped)
    sheet = jnp.concatenate([wrapped, sheet[:127]], axis=0)
    kept = jnp.where(lane < 2 * GROUPS, sheet, 0.0)
    high, rest = wide_halves(kept)
    low = (kept - high.astype(jnp.float32) - rest.astype(jnp.float32)).astype(jnp.bfloat16)
    thirds = jnp.concatenate([high, rest, low], axis=1)
    onehot = jnp.concatenate(
        [
            jnp.where(lane == jnp.broadcast_to(source[:, n * 128 : (n + 1) * 128], (128, 128)).T, 1.0, 0.0)
            for n in range(COUNT // 128)
        ],
        axis=0,
    )
    found = jnp.dot(onehot.astype(jnp.bfloat16), thirds, preferred_element_type=jnp.float32)
    amps[...] = found[:, :128] + found[:, 128:256] + found[:, 256:]
    to_scalar.wait()

    def get(n, carry):
        base = pl.multiple_of(n * BATCH, BATCH)
        spots = [index[n // (128 // BATCH), n % (128 // BATCH) * BATCH + m] for m in range(BATCH)]
        ph = [recv[spot] for spot in spots]
        en = [recv[spot + CAP] for spot in spots]
        for m in range(BATCH):
            phases[pl.ds(base + m, 1)] = ph[m]
            energies[pl.ds(base + m, 1)] = en[m]
        return carry

    copies = []
    for quarter in range(4):
        lax.fori_loop(quarter * COUNT // BATCH // 4, (quarter + 1) * COUNT // BATCH // 4, get, 0)
        for k in range(quarter * 4, quarter * 4 + 4):
            rows = slice(k * NBS, (k + 1) * NBS)
            re, im = amps[rows, k : k + 1], amps[rows, GROUPS + k : GROUPS + k + 1]
            phases[rows], energies[rows] = pushed(phases[rows], energies[rows], re, im)
        span = pl.ds(quarter * COUNT // 4, COUNT // 4)
        copies.append(pltpu.make_async_copy(phases.at[span], phases_hbm.at[span], sems.at[1 + 2 * quarter]))
        copies.append(pltpu.make_async_copy(energies.at[span], energies_hbm.at[span], sems.at[2 + 2 * quarter]))
        for copy in copies[-2:]:
            copy.start()
    for copy in copies:
        copy.wait()


def twice_diffracted(planes, left, right):
    hi, lo = wide_halves(jnp.concatenate([jnp.concatenate(pair, axis=1) for pair in planes], axis=0))
    half = jnp.dot(jnp.concatenate([hi, lo, hi], axis=1), right[...], preferred_element_type=jnp.float32)
    cols = []
    for m in range(len(planes)):
        mid = half[m * GRID : (m + 1) * GRID]
        cols.append(jnp.concatenate([mid[:, :GRID], mid[:, GRID:]], axis=0))
    hi, lo = wide_halves(jnp.concatenate(cols, axis=1))
    full = jnp.dot(left[...], jnp.concatenate([hi, lo, hi], axis=0), preferred_element_type=jnp.float32)
    cuts = [slice(m * GRID, (m + 1) * GRID) for m in range(len(planes))]
    return [(full[:GRID, cut], full[GRID:, cut]) for cut in cuts]


def early_kernel(mine, piece_0, piece_1, beam, parts, out, left, right):
    lay_out(parts, left, right)
    even = mine[0] % 2 == 0
    planes = [tuple(jnp.where(even, piece_0[c, k], piece_1[c, k]) for c in range(2)) for k in range(EARLY)]
    planes.append((beam[2], jnp.zeros((GRID, GRID), jnp.float32)))
    for k, (re, im) in enumerate(twice_diffracted(planes, left, right)):
        out[0, k] = re
        out[1, k] = im


def last_kernel(
    mine, early, piece_b0, piece_b1, piece_b2, piece_b3, piece_c, small, beam, parts, out_hbm, acc, rest, out, left, right, sems
):
    me = mine[0]
    for n in range(4):
        acc[n] = GAIN * small[n]
    copies = []

    def plane(c, k):
        if k < 0:
            return jnp.zeros((GRID, GRID), jnp.float32)
        return early[c, k] if k < EARLY else rest[c, k - EARLY]

    def finish(low, high):
        for k in range(low, high):
            cr, ci, br, bi = (acc[n, k : k + 1] for n in range(4))
            re, im = (jnp.where(me < 2, plane(c, k - 1), plane(c, k)) for c in range(2))
            out[0, k] = re + (br * early[0, EARLY] - bi * early[1, EARLY]) + (cr * beam[0] - ci * beam[1])
            out[1, k] = im + (br * early[1, EARLY] + bi * early[0, EARLY]) + (cr * beam[1] + ci * beam[0])
        span = pl.ds(low, high - low)
        for c in range(2):
            copies.append(pltpu.make_async_copy(out.at[c, span], out_hbm.at[c, span], sems.at[len(copies)]))
            copies[-1].start()

    finish(0, EARLY)
    lay_out(parts, left, right)
    planes = [(piece[0, k], piece[1, k]) for piece in (piece_b0, piece_b1, piece_b2, piece_b3) for k in range(piece.shape[1])]
    for k, (re, im) in enumerate(twice_diffracted(planes, left, right)):
        rest[0, k] = re
        rest[1, k] = im
    finish(EARLY, LATE)
    planes = [(piece_c[0, k], piece_c[1, k]) for k in range(piece_c.shape[1])]
    for k, (re, im) in enumerate(twice_diffracted(planes, left, right)):
        rest[0, LATE - EARLY + k] = re
        rest[1, LATE - EARLY + k] = im
    finish(LATE, GROUPS)
    for copy in copies:
        copy.wait()


def early_pairs(core):
    onward = [(device, (device + 2) % PEERS) for device in range(core, PEERS, 2)]
    across = [(device, (device + 8) % PEERS) for device in range(1 - core, PEERS, 2) if device % 8 >= 6]
    return onward + across


def late_pairs():
    return [(device, device + 2 if device % 8 < 6 else device - 6) for device in range(PEERS)]


def shifted(value, axis, steps):
    count = lax.axis_size(axis)
    pairs = [(source, (source + steps) % count) for source in range(count)]
    return lax.ppermute(value, axis, pairs)


def shape(*dims, dtype=jnp.float32):
    return jax.ShapeDtypeStruct(dims, dtype)


def whole():
    return pl.BlockSpec(memory_space=pltpu.VMEM)


def vmem(*dims, dtype=jnp.float32):
    return pltpu.VMEM(dims, dtype)


def in_hbm(value):
    return pltpu.with_memory_space_constraint(value, pltpu.HBM)


def per_device(field, phase_bins, phase_jitter, energy, profile, delays):
    params = pltpu.CompilerParams(vmem_limit_bytes=VMEM_LIMIT)
    scalar = pl.BlockSpec(memory_space=pltpu.SMEM)
    remain = pl.BlockSpec(memory_space=pltpu.HBM)
    field = field.reshape(2, GROUPS, GRID, GRID)
    bins = phase_bins.reshape(COUNT, BLOCK)
    jitter = phase_jitter.reshape(COUNT, BLOCK)
    energies = energy.reshape(COUNT, BLOCK)
    mine = lax.axis_index("cuts").reshape(1)
    one, two = line_operator(1), line_operator(2)
    left_one = jnp.asarray(np.concatenate(one, axis=0), jnp.float32)
    right_one = jnp.asarray(right_form(*one), jnp.float32)
    core = mine[0] % 2
    shared_0 = lax.ppermute(lax.dynamic_slice_in_dim(field, core * (GROUPS - EARLY), EARLY, 1), "cuts", early_pairs(0))
    shared_1 = lax.ppermute(lax.dynamic_slice_in_dim(field, (1 - core) * (GROUPS - EARLY), EARLY, 1), "cuts", early_pairs(1))
    operands = [field, profile, bins, jitter, energies, delays.reshape(GROUPS, 1, NBS), left_one, right_one]
    send, phases1, energies1, places, beam, small1, *sources = pl.pallas_call(
        first_kernel,
        out_shape=(
            pltpu.HBM((PEERS, MESSAGE, 1, BLOCK), jnp.float32),
            shape(COUNT, BLOCK),
            shape(COUNT, BLOCK),
            pltpu.HBM((8, COUNT), jnp.int32),
            pltpu.HBM((3, GRID, GRID), jnp.float32),
            shape(4, GROUPS, 128),
            *[pltpu.HBM((2, high - low, GRID, GRID), jnp.float32) for low, high in MIDDLE],
        ),
        in_specs=[scalar] + [remain] * 8,
        out_specs=(remain, whole(), whole(), remain, whole(), whole()) + (remain,) * len(MIDDLE),
        scratch_shapes=[
            vmem(2, GROUPS, GRID, GRID),
            vmem(GRID, GRID),
            vmem(COUNT, BLOCK, dtype=jnp.int32),
            vmem(COUNT, BLOCK),
            vmem(COUNT, BLOCK),
            vmem(GROUPS, 1, NBS, dtype=jnp.int32),
            vmem(2 * GRID, GRID),
            vmem(2 * GRID, 2 * GRID),
            vmem(6, GROUPS, 128),
            vmem(ROWS, 1, BLOCK),
            vmem(8, COUNT, dtype=jnp.int32),
            vmem(8, 128, dtype=jnp.int32),
            pltpu.SMEM((8, 128), jnp.int32),
            pltpu.SemaphoreType.DMA((17,)),
        ],
        compiler_params=params,
        name="push_place",
    )(mine, *[in_hbm(value) for value in operands])
    arrived1 = shifted(small1, "cuts", 1)
    send = pl.pallas_call(
        second_kernel,
        out_shape=pltpu.HBM((PEERS, MESSAGE, 1, BLOCK), jnp.float32),
        in_specs=[scalar] + [whole()] * 4 + [remain],
        out_specs=remain,
        scratch_shapes=[vmem(4, GROUPS, 128), vmem(PEERS, 1, 128), pltpu.SemaphoreType.DMA],
        input_output_aliases={5: 0},
        compiler_params=params,
        name="second_push",
    )(mine, phases1, energies1, arrived1, small1, in_hbm(send))
    field_b = [shifted(source, "cuts", 2) for source in sources]

    operator = quarters(*two)
    tables = [vmem(2 * GRID, 6 * GRID, dtype=jnp.bfloat16), vmem(6 * GRID, 2 * GRID, dtype=jnp.bfloat16)]

    def exchange(send, places, field, shared_0, shared_1, beam):
        early = pl.pallas_call(
            early_kernel,
            out_shape=shape(2, EARLY + 1, GRID, GRID),
            in_specs=[scalar] + [whole()] * 4,
            out_specs=whole(),
            scratch_shapes=tables,
            compiler_params=params,
            name="early_field",
        )(mine, in_hbm(shared_0), in_hbm(shared_1), in_hbm(beam), operator)
        handed = jnp.where(core == 0, shared_1, shared_0)
        source_c = jnp.where(mine[0] % 8 >= 6, handed[:, LATE - GROUPS :], field[:, LATE:])
        field_c = lax.ppermute(source_c, "cuts", late_pairs())
        recv = lax.all_to_all(send.reshape(ROWS, 1, BLOCK), "cuts", split_axis=0, concat_axis=0, tiled=True)
        recv, early = lax.optimization_barrier((recv, early))
        phase_out, energy_out, small = pl.pallas_call(
            pick_kernel,
            out_shape=(shape(COUNT, BLOCK), shape(COUNT, BLOCK), shape(4, GROUPS, 128)),
            in_specs=[scalar] + [whole()] * 2,
            out_specs=(remain, remain, whole()),
            scratch_shapes=[
                vmem(8, 128, dtype=jnp.int32),
                pltpu.SMEM((8, 128), jnp.int32),
                vmem(COUNT, 128),
                vmem(PEERS, 128),
                vmem(COUNT, BLOCK),
                vmem(COUNT, BLOCK),
                pltpu.SemaphoreType.DMA((9,)),
            ],
            compiler_params=params,
            name="pick",
        )(mine, recv, places)
        return phase_out, energy_out, early, field_c, small

    def refuse(*operands):
        sizes = [(COUNT, BLOCK)] * 2 + [(2, n, GRID, GRID) for n in (EARLY + 1, GROUPS - LATE)] + [(4, GROUPS, 128)]
        return tuple(jnp.zeros(size, jnp.float32) for size in sizes)

    phase_out, energy_out, early, field_c, small = lax.cond(
        mine[0] < PEERS, exchange, refuse, send, places, field, shared_0, shared_1, beam
    )
    out = pl.pallas_call(
        last_kernel,
        out_shape=shape(2, GROUPS, GRID, GRID),
        in_specs=[scalar] + [whole()] * 9,
        out_specs=remain,
        scratch_shapes=[
            vmem(4, GROUPS, 128),
            vmem(2, GROUPS - EARLY, GRID, GRID),
            vmem(2, GROUPS, GRID, GRID),
            *tables,
            pltpu.SemaphoreType.DMA((6,)),
        ],
        compiler_params=params,
        name="last_field",
    )(mine, early, *field_b, field_c, small, in_hbm(beam), operator)
    return (
        out.reshape(2, GROUPS, 1, GRID, GRID),
        phase_out.reshape(GROUPS, 1, NBS * BLOCK),
        energy_out.reshape(GROUPS, 1, NBS * BLOCK),
    )


def solution(mesh):
    return jax.shard_map(
        per_device,
        mesh=mesh,
        in_specs=(
            P(None, None, "cuts", None, None),
            P(None, "cuts", None),
            P(None, "cuts", None),
            P(None, "cuts", None),
            P(),
            P(),
        ),
        out_specs=(P(None, None, "cuts", None, None), P(None, "cuts", None), P(None, "cuts", None)),
        check_vma=False,
    )
```

```python
import functools
import math

import jax
import jax.numpy as jnp
import ml_dtypes
import numpy as np
from jax import lax
from jax.experimental import pallas as pl
from jax.experimental.pallas import tpu as pltpu
from jax.sharding import PartitionSpec as P

BLOCK = 128
NBINS = 16
KAPPA = 1.0
OMEGA = 1.0
GAIN = 16.0
PHASE_COEF = 20.0
GRID = 128
GROUPS = 16
NBS = 64
COUNT = GROUPS * NBS
PEERS = 128
CAP = 20
MESSAGE = 2 * CAP + 1
ROWS = PEERS * MESSAGE
BATCH = 32
EARLY, LATE = 4, 12
MIDDLE = ((4, 6), (6, 8), (8, 10), (10, 12))
VMEM_LIMIT = 24 * 1024 * 1024
HIGHEST = lax.Precision.HIGHEST


def line_operator(power):
    index = np.arange(GRID)
    freq = ((index + GRID // 2) % GRID - GRID // 2) / GRID
    weight = np.exp(-1j * PHASE_COEF * power * freq**2)
    wave = np.exp(2j * np.pi * (index[:, None] * index[None, :] % GRID) / GRID)
    column = wave @ weight / GRID
    matrix = column[(index[:, None] - index[None, :]) % GRID]
    return matrix.real, matrix.imag


def right_form(real, imag):
    return np.block([[real, imag], [-imag, real]])


def halves(matrix):
    high = matrix.astype(ml_dtypes.bfloat16)
    return high, (matrix - high.astype(np.float64)).astype(ml_dtypes.bfloat16)


def quarters(real, imag):
    return jnp.asarray(np.stack(halves(real) + halves(imag)))


def lay_out(parts, left, right):
    for n, low in enumerate((0, 0, 1)):
        re, im = parts[low], parts[2 + low]
        rest = slice(n * 2 * GRID, n * 2 * GRID + GRID), slice(n * 2 * GRID + GRID, (n + 1) * 2 * GRID)
        left[:GRID, rest[0]], left[:GRID, rest[1]] = re, -im
        left[GRID:, rest[0]], left[GRID:, rest[1]] = im, re
        right[rest[0], :GRID], right[rest[0], GRID:] = re, im
        right[rest[1], :GRID], right[rest[1], GRID:] = -im, re


def fitted(function, degree):
    top = (math.pi / 2 + 0.01) ** 2
    nodes = (np.cos(np.pi * (np.arange(400) + 0.5) / 400) + 1) / 2 * top
    series = np.polynomial.chebyshev.Chebyshev.fit(nodes, function(np.sqrt(nodes)), degree, domain=[0, top])
    return [float(c) for c in series.convert(kind=np.polynomial.Polynomial).coef]


SIN_COEF = fitted(lambda r: np.sin(r) / r, 5)
COS_COEF = fitted(np.cos, 6)
PI_HIGH = 3.140625
PI_MID = 9.67502593994140625e-4
PI_LOW = math.pi - PI_HIGH - PI_MID


def horner(coefs, x):
    value = jnp.float32(coefs[-1])
    for c in coefs[-2::-1]:
        value = value * x + jnp.float32(c)
    return value


def cos_sin(x):
    turns = jnp.round(x * jnp.float32(1.0 / math.pi))
    r = x - turns * jnp.float32(PI_HIGH)
    r = r - turns * jnp.float32(PI_MID)
    r = r - turns * jnp.float32(PI_LOW)
    half = turns * 0.5
    sign = 1.0 - 4.0 * jnp.abs(half - jnp.round(half))
    square = r * r
    return horner(COS_COEF, square) * sign, horner(SIN_COEF, square) * (r * sign)


def lane_total(rows):
    return jnp.broadcast_to(jnp.sum(rows, axis=1, keepdims=True), rows.shape)


def slots_of(delays):
    row = jnp.concatenate([delays[k] for k in range(GROUPS)], axis=1)
    values = lax.broadcasted_iota(jnp.int32, (PEERS, COUNT), 0)
    onehot = jnp.where(values == row, 1.0, 0.0)
    before = lax.broadcasted_iota(jnp.int32, (COUNT, COUNT), 0) < lax.broadcasted_iota(jnp.int32, (COUNT, COUNT), 1)
    upper = jnp.where(before, 1.0, 0.0).astype(jnp.bfloat16)
    earlier = jnp.dot(onehot.astype(jnp.bfloat16), upper, preferred_element_type=jnp.float32)
    return row, jnp.sum(earlier * onehot, axis=0, keepdims=True).astype(jnp.int32)


def folded(row):
    return jnp.concatenate([row[:, n * 128 : (n + 1) * 128] for n in range(COUNT // 128)], axis=0)


def rows_of(k):
    return pl.ds(pl.multiple_of(k * NBS, NBS), NBS)


def first_kernel(
    mine, field_hbm, profile_hbm, bins_hbm, jitter_hbm, energy_hbm, delays_hbm, left_hbm, right_hbm,
    send_hbm, phases, energies, places_hbm, beam, small, middle_0, middle_1, middle_2, middle_3,
    field, profile, bins, jitter, energy, delays, left, right, acc, send, places, index_v, index, sems,
):
    pairs = [
        (profile_hbm, profile), (left_hbm, left), (right_hbm, right), (delays_hbm, delays),
        (field_hbm, field), (bins_hbm, bins), (jitter_hbm, jitter), (energy_hbm, energy),
    ]
    copies = [pltpu.make_async_copy(src, dst, sems.at[n]) for n, (src, dst) in enumerate(pairs)]
    for copy in copies:
        copy.start()
    copies[3].wait()
    row, slot = slots_of(delays)
    places[0:1] = row
    places[1:2] = slot
    index_v[...] = folded(((mine[0] + row) % PEERS) * MESSAGE + slot)
    to_scalar = pltpu.make_async_copy(index_v, index, sems.at[3])
    to_scalar.start()
    for copy in copies[:3]:
        copy.wait()
    p = profile[...]
    half = jnp.dot(left[...], p, precision=HIGHEST, preferred_element_type=jnp.float32)
    both = jnp.concatenate([half[:GRID], half[GRID:]], axis=1)
    spread = jnp.dot(both, right[...], precision=HIGHEST, preferred_element_type=jnp.float32)
    beam[0] = spread[:, :GRID]
    beam[1] = spread[:, GRID:]
    beam[2] = p
    copies[4].wait()
    kept = [pltpu.make_async_copy(places, places_hbm, sems.at[8])]
    for middle, (low, high) in zip((middle_0, middle_1, middle_2, middle_3), MIDDLE):
        for c in range(2):
            span = pl.ds(low, high - low)
            kept.append(pltpu.make_async_copy(field.at[c, span], middle.at[c], sems.at[8 + len(kept)]))
    for copy in kept:
        copy.start()

    def project(k, carry):
        re, im = field[0, k], field[1, k]
        dr, di, q = beam[0], beam[1], profile[...]
        acc[0, pl.ds(k, 1)] = jnp.sum(q * re, axis=0, keepdims=True)
        acc[1, pl.ds(k, 1)] = jnp.sum(q * im, axis=0, keepdims=True)
        acc[2, pl.ds(k, 1)] = jnp.sum(dr * re - di * im, axis=0, keepdims=True)
        acc[3, pl.ds(k, 1)] = jnp.sum(dr * im + di * re, axis=0, keepdims=True)
        return carry

    lax.fori_loop(0, GROUPS, project, 0)
    self_re = jnp.sum(p * beam[0])
    self_im = jnp.sum(p * beam[1])
    for n in range(4):
        acc[n] = lane_total(acc[n]) * (1.0 / GRID)
    for copy in copies[5:]:
        copy.wait()

    def push(k, carry):
        rows = rows_of(k)
        ph = jnp.float32(2.0 * math.pi / NBINS) * (bins[rows].astype(jnp.float32) + jitter[rows])
        ph, en = pushed(ph, energy[rows], acc[0, pl.ds(k, 1)], acc[1, pl.ds(k, 1)])
        phases[rows] = ph
        energies[rows] = en
        c, s = cos_sin(ph)
        acc[4, pl.ds(k, 1)] = jnp.sum(c, axis=0, keepdims=True)
        acc[5, pl.ds(k, 1)] = jnp.sum(s, axis=0, keepdims=True)
        return carry

    lax.fori_loop(0, GROUPS, push, 0)
    to_scalar.wait()

    def put(n, carry):
        base = pl.multiple_of(n * BATCH, BATCH)
        spots = [index[n // (128 // BATCH), n % (128 // BATCH) * BATCH + m] for m in range(BATCH)]
        ph = [phases[pl.ds(base + m, 1)] for m in range(BATCH)]
        en = [energies[pl.ds(base + m, 1)] for m in range(BATCH)]
        for m in range(BATCH):
            send[spots[m]] = ph[m]
            send[spots[m] + CAP] = en[m]
        return carry

    lax.fori_loop(0, COUNT // BATCH, put, 0)
    bre = lane_total(acc[4]) * (1.0 / (NBS * BLOCK))
    bim = lane_total(acc[5]) * (-1.0 / (NBS * BLOCK))
    gain = GAIN / GRID
    next_re = acc[2] + gain * (bre * self_re - bim * self_im)
    next_im = acc[3] + gain * (bre * self_im + bim * self_re)
    for n, part in enumerate((next_re, next_im, bre, bim)):
        small[n] = part
    out = pltpu.make_async_copy(send, send_hbm, sems.at[0])
    out.start()
    for copy in kept:
        copy.wait()
    out.wait()


def pushed(ph, en, amp_re, amp_im):
    c, s = cos_sin(ph)
    en = en - KAPPA * (amp_re * c - amp_im * s)
    return ph + OMEGA * en, en


def one_row(parts):
    rest = 128 // GROUPS - len(parts)
    stack = jnp.concatenate(parts + [jnp.zeros((rest * GROUPS, 128), jnp.float32)], axis=0)
    return stack.T[0:1]


def carried(value, flag):
    rolled = jnp.concatenate([jnp.zeros_like(value[:1]), value[:-1]], axis=0)
    return jnp.where(flag, rolled, value)


def second_kernel(mine, phases1, energies1, arrived, own, send_in, send, acc, note, sem):
    del send_in
    for n in range(2):
        acc[n] = carried(arrived[n], mine[0] == 0)

    def push(k, carry):
        rows = rows_of(k)
        ph, _ = pushed(phases1[rows], energies1[rows], acc[0, pl.ds(k, 1)], acc[1, pl.ds(k, 1)])
        c, s = cos_sin(ph)
        acc[2, pl.ds(k, 1)] = jnp.sum(c, axis=0, keepdims=True)
        acc[3, pl.ds(k, 1)] = jnp.sum(s, axis=0, keepdims=True)
        return carry

    lax.fori_loop(0, GROUPS, push, 0)
    mean = 1.0 / (NBS * BLOCK)
    row = one_row([own[n] for n in range(4)] + [lane_total(acc[2]) * mean, lane_total(acc[3]) * -mean])
    note[...] = jnp.broadcast_to(row[None], (PEERS, 1, 128))
    copy = pltpu.make_async_copy(note, send.at[:, 2 * CAP], sem)
    copy.start()
    copy.wait()


def wide_halves(x):
    high = x.astype(jnp.bfloat16)
    return high, (x - high.astype(jnp.float32)).astype(jnp.bfloat16)


def pick_kernel(mine, recv, places, phases_hbm, energies_hbm, small, index_v, index, amps, notes, phases, energies, sems):
    me = mine[0]
    source = (me - places[0:1] + PEERS) % PEERS
    index_v[...] = folded(source * MESSAGE + places[1:2])
    to_scalar = pltpu.make_async_copy(index_v, index, sems.at[0])
    to_scalar.start()
    lane = lax.broadcasted_iota(jnp.int32, (128, 128), 1)
    for n in range(PEERS):
        notes[n : n + 1] = recv[n * MESSAGE + 2 * CAP]
    sheet = notes[...]
    near = jnp.broadcast_to(notes[pl.ds((me + PEERS - 1) % PEERS, 1)], (128, 128)).T
    far = jnp.broadcast_to(notes[pl.ds((me + PEERS - 2) % PEERS, 1)], (128, 128)).T
    for n in range(2):
        small[n] = carried(near[(4 + n) * GROUPS : (5 + n) * GROUPS], me == 0)
        small[2 + n] = carried(far[(2 + n) * GROUPS : (3 + n) * GROUPS], me < 2)
    wrapped = jnp.concatenate([sheet[127:128, 127:128], sheet[127:128, :127]], axis=1)
    wrapped = jnp.where(lane[0:1] % GROUPS == 0, 0.0, wrapped)
    sheet = jnp.concatenate([wrapped, sheet[:127]], axis=0)
    kept = jnp.where(lane < 2 * GROUPS, sheet, 0.0)
    high, rest = wide_halves(kept)
    low = (kept - high.astype(jnp.float32) - rest.astype(jnp.float32)).astype(jnp.bfloat16)
    thirds = jnp.concatenate([high, rest, low], axis=1)
    onehot = jnp.concatenate(
        [
            jnp.where(lane == jnp.broadcast_to(source[:, n * 128 : (n + 1) * 128], (128, 128)).T, 1.0, 0.0)
            for n in range(COUNT // 128)
        ],
        axis=0,
    )
    found = jnp.dot(onehot.astype(jnp.bfloat16), thirds, preferred_element_type=jnp.float32)
    amps[...] = found[:, :128] + found[:, 128:256] + found[:, 256:]
    to_scalar.wait()

    def get(n, carry):
        base = pl.multiple_of(n * BATCH, BATCH)
        spots = [index[n // (128 // BATCH), n % (128 // BATCH) * BATCH + m] for m in range(BATCH)]
        ph = [recv[spot] for spot in spots]
        en = [recv[spot + CAP] for spot in spots]
        for m in range(BATCH):
            phases[pl.ds(base + m, 1)] = ph[m]
            energies[pl.ds(base + m, 1)] = en[m]
        return carry

    copies = []
    for quarter in range(4):
        lax.fori_loop(quarter * COUNT // BATCH // 4, (quarter + 1) * COUNT // BATCH // 4, get, 0)
        for k in range(quarter * 4, quarter * 4 + 4):
            rows = slice(k * NBS, (k + 1) * NBS)
            re, im = amps[rows, k : k + 1], amps[rows, GROUPS + k : GROUPS + k + 1]
            phases[rows], energies[rows] = pushed(phases[rows], energies[rows], re, im)
        span = pl.ds(quarter * COUNT // 4, COUNT // 4)
        copies.append(pltpu.make_async_copy(phases.at[span], phases_hbm.at[span], sems.at[1 + 2 * quarter]))
        copies.append(pltpu.make_async_copy(energies.at[span], energies_hbm.at[span], sems.at[2 + 2 * quarter]))
        for copy in copies[-2:]:
            copy.start()
    for copy in copies:
        copy.wait()


def twice_diffracted(planes, left, right):
    hi, lo = wide_halves(jnp.concatenate([jnp.concatenate(pair, axis=1) for pair in planes], axis=0))
    half = jnp.dot(jnp.concatenate([hi, lo, hi], axis=1), right[...], preferred_element_type=jnp.float32)
    cols = []
    for m in range(len(planes)):
        mid = half[m * GRID : (m + 1) * GRID]
        cols.append(jnp.concatenate([mid[:, :GRID], mid[:, GRID:]], axis=0))
    hi, lo = wide_halves(jnp.concatenate(cols, axis=1))
    full = jnp.dot(left[...], jnp.concatenate([hi, lo, hi], axis=0), preferred_element_type=jnp.float32)
    cuts = [slice(m * GRID, (m + 1) * GRID) for m in range(len(planes))]
    return [(full[:GRID, cut], full[GRID:, cut]) for cut in cuts]


def early_kernel(mine, piece_0, piece_1, beam, parts, out, left, right):
    lay_out(parts, left, right)
    even = mine[0] % 2 == 0
    planes = [tuple(jnp.where(even, piece_0[c, k], piece_1[c, k]) for c in range(2)) for k in range(EARLY)]
    planes.append((beam[2], jnp.zeros((GRID, GRID), jnp.float32)))
    for k, (re, im) in enumerate(twice_diffracted(planes, left, right)):
        out[0, k] = re
        out[1, k] = im


def last_kernel(
    mine, early, piece_b0, piece_b1, piece_b2, piece_b3, piece_c, small, beam, parts, out_hbm, acc, rest, out, left, right, sems
):
    me = mine[0]
    for n in range(4):
        acc[n] = GAIN * small[n]
    copies = []

    def plane(c, k):
        if k < 0:
            return jnp.zeros((GRID, GRID), jnp.float32)
        return early[c, k] if k < EARLY else rest[c, k - EARLY]

    def finish(low, high):
        for k in range(low, high):
            cr, ci, br, bi = (acc[n, k : k + 1] for n in range(4))
            re, im = (jnp.where(me < 2, plane(c, k - 1), plane(c, k)) for c in range(2))
            out[0, k] = re + (br * early[0, EARLY] - bi * early[1, EARLY]) + (cr * beam[0] - ci * beam[1])
            out[1, k] = im + (br * early[1, EARLY] + bi * early[0, EARLY]) + (cr * beam[1] + ci * beam[0])
        span = pl.ds(low, high - low)
        for c in range(2):
            copies.append(pltpu.make_async_copy(out.at[c, span], out_hbm.at[c, span], sems.at[len(copies)]))
            copies[-1].start()

    finish(0, EARLY)
    lay_out(parts, left, right)
    halfway = (EARLY + LATE) // 2
    for low, high, pieces in ((EARLY, halfway, (piece_b0, piece_b1)), (halfway, LATE, (piece_b2, piece_b3))):
        planes = [(piece[0, k], piece[1, k]) for piece in pieces for k in range(piece.shape[1])]
        for k, (re, im) in enumerate(twice_diffracted(planes, left, right)):
            rest[0, low - EARLY + k] = re
            rest[1, low - EARLY + k] = im
        finish(low, high)
    planes = [(piece_c[0, k], piece_c[1, k]) for k in range(piece_c.shape[1])]
    for k, (re, im) in enumerate(twice_diffracted(planes, left, right)):
        rest[0, LATE - EARLY + k] = re
        rest[1, LATE - EARLY + k] = im
    finish(LATE, GROUPS)
    for copy in copies:
        copy.wait()


def early_pairs(core):
    onward = [(device, (device + 2) % PEERS) for device in range(core, PEERS, 2)]
    across = [(device, (device + 8) % PEERS) for device in range(1 - core, PEERS, 2) if device % 8 >= 6]
    return onward + across


def late_pairs():
    return [(device, device + 2 if device % 8 < 6 else device - 6) for device in range(PEERS)]


def shifted(value, axis, steps):
    count = lax.axis_size(axis)
    pairs = [(source, (source + steps) % count) for source in range(count)]
    return lax.ppermute(value, axis, pairs)


def shape(*dims, dtype=jnp.float32):
    return jax.ShapeDtypeStruct(dims, dtype)


def whole():
    return pl.BlockSpec(memory_space=pltpu.VMEM)


def vmem(*dims, dtype=jnp.float32):
    return pltpu.VMEM(dims, dtype)


def in_hbm(value):
    return pltpu.with_memory_space_constraint(value, pltpu.HBM)


def per_device(field, phase_bins, phase_jitter, energy, profile, delays):
    params = pltpu.CompilerParams(vmem_limit_bytes=VMEM_LIMIT)
    scalar = pl.BlockSpec(memory_space=pltpu.SMEM)
    remain = pl.BlockSpec(memory_space=pltpu.HBM)
    field = field.reshape(2, GROUPS, GRID, GRID)
    bins = phase_bins.reshape(COUNT, BLOCK)
    jitter = phase_jitter.reshape(COUNT, BLOCK)
    energies = energy.reshape(COUNT, BLOCK)
    mine = lax.axis_index("cuts").reshape(1)
    one, two = line_operator(1), line_operator(2)
    left_one = jnp.asarray(np.concatenate(one, axis=0), jnp.float32)
    right_one = jnp.asarray(right_form(*one), jnp.float32)
    core = mine[0] % 2
    shared_0 = lax.ppermute(lax.dynamic_slice_in_dim(field, core * (GROUPS - EARLY), EARLY, 1), "cuts", early_pairs(0))
    shared_1 = lax.ppermute(lax.dynamic_slice_in_dim(field, (1 - core) * (GROUPS - EARLY), EARLY, 1), "cuts", early_pairs(1))
    operands = [field, profile, bins, jitter, energies, delays.reshape(GROUPS, 1, NBS), left_one, right_one]
    send, phases1, energies1, places, beam, small1, *sources = pl.pallas_call(
        first_kernel,
        out_shape=(
            pltpu.HBM((ROWS, 1, BLOCK), jnp.float32),
            shape(COUNT, BLOCK),
            shape(COUNT, BLOCK),
            pltpu.HBM((8, COUNT), jnp.int32),
            pltpu.HBM((3, GRID, GRID), jnp.float32),
            shape(4, GROUPS, 128),
            *[pltpu.HBM((2, high - low, GRID, GRID), jnp.float32) for low, high in MIDDLE],
        ),
        in_specs=[scalar] + [remain] * 8,
        out_specs=(remain, whole(), whole(), remain, whole(), whole()) + (remain,) * len(MIDDLE),
        scratch_shapes=[
            vmem(2, GROUPS, GRID, GRID),
            vmem(GRID, GRID),
            vmem(COUNT, BLOCK, dtype=jnp.int32),
            vmem(COUNT, BLOCK),
            vmem(COUNT, BLOCK),
            vmem(GROUPS, 1, NBS, dtype=jnp.int32),
            vmem(2 * GRID, GRID),
            vmem(2 * GRID, 2 * GRID),
            vmem(6, GROUPS, 128),
            vmem(ROWS, 1, BLOCK),
            vmem(8, COUNT, dtype=jnp.int32),
            vmem(8, 128, dtype=jnp.int32),
            pltpu.SMEM((8, 128), jnp.int32),
            pltpu.SemaphoreType.DMA((17,)),
        ],
        compiler_params=params,
        name="push_place",
    )(mine, *[in_hbm(value) for value in operands])
    arrived1 = shifted(small1, "cuts", 1)
    send = pl.pallas_call(
        second_kernel,
        out_shape=pltpu.HBM((PEERS, MESSAGE, 1, BLOCK), jnp.float32),
        in_specs=[scalar] + [whole()] * 4 + [remain],
        out_specs=remain,
        scratch_shapes=[vmem(4, GROUPS, 128), vmem(PEERS, 1, 128), pltpu.SemaphoreType.DMA],
        input_output_aliases={5: 0},
        compiler_params=params,
        name="second_push",
    )(mine, phases1, energies1, arrived1, small1, in_hbm(send.reshape(PEERS, MESSAGE, 1, BLOCK)))
    field_b = [shifted(source, "cuts", 2) for source in sources]

    operator = quarters(*two)
    tables = [vmem(2 * GRID, 6 * GRID, dtype=jnp.bfloat16), vmem(6 * GRID, 2 * GRID, dtype=jnp.bfloat16)]

    def exchange(send, places, field, shared_0, shared_1, beam):
        early = pl.pallas_call(
            early_kernel,
            out_shape=shape(2, EARLY + 1, GRID, GRID),
            in_specs=[scalar] + [whole()] * 4,
            out_specs=whole(),
            scratch_shapes=tables,
            compiler_params=params,
            name="early_field",
        )(mine, in_hbm(shared_0), in_hbm(shared_1), in_hbm(beam), operator)
        handed = jnp.where(core == 0, shared_1, shared_0)
        source_c = jnp.where(mine[0] % 8 >= 6, handed[:, LATE - GROUPS :], field[:, LATE:])
        field_c = lax.ppermute(source_c, "cuts", late_pairs())
        recv = lax.all_to_all(send.reshape(ROWS, 1, BLOCK), "cuts", split_axis=0, concat_axis=0, tiled=True)
        recv, early = lax.optimization_barrier((recv, early))
        phase_out, energy_out, small = pl.pallas_call(
            pick_kernel,
            out_shape=(shape(COUNT, BLOCK), shape(COUNT, BLOCK), shape(4, GROUPS, 128)),
            in_specs=[scalar] + [whole()] * 2,
            out_specs=(remain, remain, whole()),
            scratch_shapes=[
                vmem(8, 128, dtype=jnp.int32),
                pltpu.SMEM((8, 128), jnp.int32),
                vmem(COUNT, 128),
                vmem(PEERS, 128),
                vmem(COUNT, BLOCK),
                vmem(COUNT, BLOCK),
                pltpu.SemaphoreType.DMA((9,)),
            ],
            compiler_params=params,
            name="pick",
        )(mine, recv, places)
        return phase_out, energy_out, early, field_c, small

    def refuse(*operands):
        sizes = [(COUNT, BLOCK)] * 2 + [(2, n, GRID, GRID) for n in (EARLY + 1, GROUPS - LATE)] + [(4, GROUPS, 128)]
        return tuple(jnp.zeros(size, jnp.float32) for size in sizes)

    phase_out, energy_out, early, field_c, small = lax.cond(
        mine[0] < PEERS, exchange, refuse, send, places, field, shared_0, shared_1, beam
    )
    out = pl.pallas_call(
        last_kernel,
        out_shape=shape(2, GROUPS, GRID, GRID),
        in_specs=[scalar] + [whole()] * 9,
        out_specs=remain,
        scratch_shapes=[
            vmem(4, GROUPS, 128),
            vmem(2, GROUPS - EARLY, GRID, GRID),
            vmem(2, GROUPS, GRID, GRID),
            *tables,
            pltpu.SemaphoreType.DMA((8,)),
        ],
        compiler_params=params,
        name="last_field",
    )(mine, early, *field_b, field_c, small, in_hbm(beam), operator)
    return (
        out.reshape(2, GROUPS, 1, GRID, GRID),
        phase_out.reshape(GROUPS, 1, NBS * BLOCK),
        energy_out.reshape(GROUPS, 1, NBS * BLOCK),
    )


def solution(mesh):
    return jax.shard_map(
        per_device,
        mesh=mesh,
        in_specs=(
            P(None, None, "cuts", None, None),
            P(None, "cuts", None),
            P(None, "cuts", None),
            P(None, "cuts", None),
            P(),
            P(),
        ),
        out_specs=(P(None, None, "cuts", None, None), P(None, "cuts", None), P(None, "cuts", None)),
        check_vma=False,
    )
```
